32 devices in a mesh: parts: 2 (over y), tile: 4 (over z), slab: 2 (over x), rep: 2 (over core).
Axes of the slice: x: 2, y: 2, z: 4, core: 2. Of those that a mesh axis runs over, the one named last changes fastest.
Arguments:
- volume: float32 [16, 16384], P(('parts', 'slab'), 'tile'), parts along dimension 0, may hold values from -6 to 6
- split_var: float32 [3, 16, 16384], P(None, ('parts', 'slab'), 'tile'), parts along dimension 1, may hold values from -6 to 6
- dual_var: float32 [3, 16, 16384], P(None, ('parts', 'slab'), 'tile'), parts along dimension 1, may hold values from -6 to 6
- sinogram: float32 [32, 16, 128], P(('tile', 'rep'), ('parts', 'slab')), parts along dimension 1, may hold values from -6 to 6
- proj_tiles: bfloat16 [2048, 64, 128], P(('tile', 'rep')), may hold values from -0.125 to 0.125
- ray_index: int32 [2048], P(('tile', 'rep')), may hold values from 0 to 31
- voxel_index: int32 [2048], P(('tile', 'rep')), may hold values from 0 to 63
- tile_count: int32 [8], P(('tile', 'rep')), may hold values from 1 to 256, 1024 in all
- rho: float32 [1], replicated, may hold values from 0.5 to 2
Outputs:
- new_volume: float32 [16, 16384], P(('parts', 'slab'), 'tile'), parts along dimension 0
- new_split: float32 [3, 16, 16384], P(None, ('parts', 'slab'), 'tile'), parts along dimension 1
- new_dual: float32 [3, 16, 16384], P(None, ('parts', 'slab'), 'tile'), parts along dimension 1
The draws below stay inside these ranges and needn't reach their ends.
There are 2 independent parts, one for each index of `parts`. The reference program is written for one: setup_inputs(seed, part) draws one part's arguments, and reference() takes and returns one part's arrays. A program takes and returns all parts, laid end to end along the dimension named above; an argument that names none is the same for every part. Nothing has to cross between parts.
Inputs may be any that keep to these rules, and one draw needn't show every extreme that they name: `tile_count`: slots at or beyond a device's count are unused; some device uses all 256 slots.
All inputs are finite; a program needn't handle non-finite values.
Results may differ from the reference program's by a relative error of at most 0.0017.
Values may be sent and summed in bfloat16 or wider, within the bound.
No kernel may reach another device: no remote copies, remote signals or barrier semaphores. Data moves between devices by JAX's collectives and lax.ppermute only.
A program may use at most 64 MiB of HBM per device.

```python
import math
import jax
import jax.numpy as jnp
import numpy as np

TV = 64
TR = 128
VT_DEV = 64
RT_DEV = 4
NT_DEV = 256
GROUP = 8
RT_ALL = 32
NT_ALL = 2048
STACK = 8
VOXELS = 16384
N_TILE = 4
N_REP = 2


def plant(drawn, rng, low, largest):
    spot = [jax.random.randint(jax.random.fold_in(rng, axis), (), 0, length) for axis, length in enumerate(drawn.shape)]
    longest = drawn.shape.index(max(drawn.shape))
    beside = spot[:longest] + [(spot[longest] + 1) % drawn.shape[longest]] + spot[longest + 1:]
    return drawn.at[tuple(spot)].set(low).at[tuple(beside)].set(largest)


def block_levels(stream_key, extent, split, least, largest):
    factor_of = 1.0
    for axis_at, shards_of in split:
        steps = jax.random.uniform(jax.random.fold_in(jax.random.fold_in(stream_key, 6), axis_at), (shards_of,), jnp.float32, least / len(split), largest / len(split))
        factor_of = factor_of * jnp.repeat(jnp.exp(steps), extent[axis_at] // shards_of).reshape((-1,) + (1,) * (len(extent) - 1 - axis_at))
    return factor_of


def split_up(number_of, total, most, lean):
    weights = [(1 << 20) // math.isqrt(standing ** lean) + 1 for standing in range(2, number_of + 1)]
    surplus, given = total - most - (number_of - 1), [1] * (number_of - 1)
    while surplus > 0:
        free = [i for i in range(number_of - 1) if given[i] < most]
        pool, budget = sum([weights[i] for i in free]), surplus
        for i in free:
            extra = min(most - given[i], max(1, budget * weights[i] // pool), surplus)
            given[i] = given[i] + extra
            surplus = surplus - extra
    return np.array([most] + given)


def ragged(stream_key, amount, total, reach, slope):
    if amount == 2:
        one = jax.random.randint(stream_key, (), max(1, total - reach), min(reach, total - 1) + 1)
        return jnp.stack([one, total - one])
    tallies = jnp.asarray(split_up(amount, total, reach, slope), jnp.int32)
    pairs = (amount - 1) // 2
    source_of, taker = tallies[1:1 + 2 * pairs:2], tallies[2:2 + 2 * pairs:2]
    margin = jnp.minimum(source_of - 1, reach - taker)
    moved = jax.random.randint(jax.random.fold_in(stream_key, 1), (pairs,), 0, 1 << 20) % (margin + 1)
    tallies = tallies.at[1:1 + 2 * pairs:2].set(source_of - moved).at[2:2 + 2 * pairs:2].set(taker + moved)
    return tallies[jax.random.permutation(jax.random.fold_in(stream_key, 2), amount)]


def scatter_about(rng, extent, deviation, reach, split=(), kind=jnp.bfloat16):
    result = jax.random.normal(rng, extent, jnp.float32) * deviation
    if len(split) > 0:
        result = block_levels(rng, extent, split, -0.22, 0.18) * result
    return jnp.clip(result, min=-reach, max=reach).astype(kind)


def setup_inputs(seed: int = 0, part: int = 0) -> dict:
    key_of = jax.random.split(jax.random.key(seed), 10)
    part_splits = jax.random.split(jax.random.fold_in(key_of[9], part), 10)
    return {
        "volume": scatter_about(part_splits[0], (STACK, VOXELS), 1.0, 6.0, ((0, 2), (1, 4)), jnp.float32),
        "split_var": scatter_about(part_splits[1], (3, STACK, VOXELS), 1.0, 6.0, ((1, 2), (2, 4)), jnp.float32),
        "dual_var": scatter_about(part_splits[2], (3, STACK, VOXELS), 1.0, 6.0, ((1, 2), (2, 4)), jnp.float32),
        "sinogram": scatter_about(part_splits[3], (RT_ALL, STACK, TR), 1.0, 6.0, ((0, 8), (1, 2)), jnp.float32),
        "proj_tiles": scatter_about(key_of[4], (NT_ALL, TV, TR), (TV * NT_DEV // (2 * RT_DEV)) ** -0.5, 0.125, ((0, 8),)),
        "ray_index": plant(jax.random.randint(key_of[5], (NT_ALL,), 0, RT_ALL), jax.random.fold_in(key_of[5], 1), 0, RT_ALL - 1).astype(jnp.int32),
        "voxel_index": plant(jax.random.randint(key_of[6], (NT_ALL,), 0, VT_DEV), jax.random.fold_in(key_of[6], 1), 0, VT_DEV - 1).astype(jnp.int32),
        "tile_count": ragged(key_of[7], GROUP, N_TILE * N_REP * NT_DEV // 2, NT_DEV, 2).astype(jnp.int32),
        "rho": jnp.clip(jax.random.uniform(key_of[8], (1,), jnp.float32, 0.5, 2.0), 0.5, 2.0),
    }


TAU = 0.5

def plane_grad(field):
    cells = field.reshape(field.shape[:-1] + (-1, 8, 8))
    across = jnp.concatenate([cells[..., 1:, :] - cells[..., :-1, :], jnp.zeros_like(cells[..., :1, :])], axis=-2)
    along = jnp.concatenate([cells[..., :, 1:] - cells[..., :, :-1], jnp.zeros_like(cells[..., :, :1])], axis=-1)
    return (across.reshape(field.shape), along.reshape(field.shape))

def plane_masks(width):
    place = jnp.arange(width, dtype=jnp.int32) % TV
    return (place // 8 < 7, place % 8 < 7)

def plane_adjoint(across, along):
    shape = across.shape
    cells_a = across.reshape(shape[:-1] + (-1, 8, 8))
    cells_b = along.reshape(shape[:-1] + (-1, 8, 8))
    part_a = jnp.concatenate([jnp.zeros_like(cells_a[..., :1, :]), cells_a[..., :-1, :]], axis=-2) - cells_a
    part_b = jnp.concatenate([jnp.zeros_like(cells_b[..., :, :1]), cells_b[..., :, :-1]], axis=-1) - cells_b
    return (part_a + part_b).reshape(shape)

def depth_grad(field):
    return jnp.concatenate([field[1:] - field[:-1], jnp.zeros_like(field[:1])], axis=0)

def reference(volume, split_var, dual_var, sinogram, proj_tiles, ray_index, voxel_index, tile_count, rho):
    penalty = rho[0]
    slots = ray_index.shape[0]
    entry = jnp.arange(slots, dtype=jnp.int32)
    owner = entry // NT_DEV
    used = entry % NT_DEV < tile_count[owner]
    whole_tile = owner // N_REP * VT_DEV + voxel_index
    stack = volume.shape[0]
    tiles_all = volume.shape[1] // TV
    vol_b = volume.astype(jnp.bfloat16)
    tiles = proj_tiles.astype(jnp.float32)
    picked = vol_b.reshape(stack, tiles_all, TV)[:, whole_tile].astype(jnp.float32)
    forward = jnp.einsum('snv,nvr->nsr', picked, tiles)
    forward = jnp.where(used[:, None, None], forward, 0.0)
    ray_sums = jax.ops.segment_sum(forward, ray_index, num_segments=sinogram.shape[0])
    resid = (ray_sums - sinogram).astype(jnp.bfloat16)
    rows = resid[ray_index].astype(jnp.float32)
    backward = jnp.einsum('nsr,nvr->nsv', rows, tiles)
    backward = jnp.where(used[:, None, None], backward, 0.0)
    grad_tiles = jax.ops.segment_sum(backward, whole_tile, num_segments=tiles_all)
    grad = grad_tiles.transpose(1, 0, 2).reshape(stack, tiles_all * TV)
    keep = jnp.arange(stack, dtype=jnp.int32) < stack - 1
    row_mask, col_mask = plane_masks(volume.shape[1])
    across, along = plane_grad(volume)
    w_depth = jnp.where(keep[:, None], depth_grad(volume) - split_var[0] + dual_var[0], 0.0)
    w_across = jnp.where(row_mask, across - split_var[1] + dual_var[1], 0.0)
    w_along = jnp.where(col_mask, along - split_var[2] + dual_var[2], 0.0)
    adjoint = jnp.concatenate([jnp.zeros_like(w_depth[:1]), w_depth[:-1]], axis=0) - w_depth
    adjoint = adjoint + plane_adjoint(w_across, w_along)
    new_volume = volume - TAU * (grad + penalty * adjoint)
    across2, along2 = plane_grad(new_volume)
    mixed = jnp.stack([depth_grad(new_volume), across2, along2]) + dual_var
    limit = 1.0 / penalty
    new_dual = jnp.clip(mixed, -limit, limit)
    new_split = mixed - new_dual
    return (new_volume, new_split, new_dual)
```

```python
import jax
import jax.numpy as jnp
from jax import lax
from jax.experimental import pallas as pl
from jax.experimental.pallas import tpu as pltpu
from jax.sharding import PartitionSpec as P

TV = 64
TR = 128
TAU = 0.5
GROUP = 4
CHUNKS = 8
VMEM_LIMIT = 48 * 1024 * 1024


def iotas(shape):
    row = lax.broadcasted_iota(jnp.int32, shape, 0)
    lane = lax.broadcasted_iota(jnp.int32, shape, 1)
    return row, lane


def start_tiles(proj_hbm, tiles, sems):
    per = proj_hbm.shape[0] // CHUNKS
    copies = []
    for c in range(CHUNKS):
        part = pl.ds(c * per, per)
        copy = pltpu.make_async_copy(proj_hbm.at[part], tiles.at[part], sems.at[c])
        copy.start()
        copies.append(copy)
    return copies


def plane_masks(lane):
    return (lane % TV) // 8 < 7, lane % 8 < 7


def forward_kernel(
    count, ray, voxel, rho, vol_hbm, split_hbm, dual_hbm, proj_hbm,
    partial_out, base_out, halo_out,
    vol, split, dual, tiles, double, table, acc0, acc1, acc2, acc3, sems, tile_sems,
):
    slots = proj_hbm.shape[0]
    rays = acc0.shape[0] - 1
    width = vol.shape[1]
    loads = [
        pltpu.make_async_copy(vol_hbm, vol, sems.at[0]),
        pltpu.make_async_copy(split_hbm, split, sems.at[1]),
        pltpu.make_async_copy(dual_hbm, dual, sems.at[2]),
    ]
    for load in loads:
        load.start()
    copies = start_tiles(proj_hbm, tiles, tile_sems)
    accs = (acc0, acc1, acc2, acc3)
    for acc in accs:
        acc[...] = jnp.zeros_like(acc)
    row, lane = iotas((8, 128))
    low, top = lane < TV, row < 4

    loads[0].wait()
    field = vol[...]
    double[0:4, :] = field
    double[4:8, :] = field
    for j in range(width // 128):
        x = double[:, 128 * j:128 * j + 128].astype(jnp.bfloat16).astype(jnp.float32)
        turned = pltpu.roll(x, TV, axis=1)
        zero = jnp.zeros_like(x)
        first = jnp.where(jnp.logical_and(top, low), x, zero)
        second = jnp.where(jnp.logical_and(top, low), turned, zero)
        other = jnp.logical_not(jnp.logical_or(top, low))
        table[2 * j] = jnp.where(other, turned, first)
        table[2 * j + 1] = jnp.where(other, x, second)

    loads[1].wait()
    loads[2].wait()
    factor = TAU * rho[0]
    row_mask, col_mask = plane_masks(lane)
    for j in range(width // 128):
        at = slice(128 * j, 128 * j + 128)
        x = double[:, at]
        gap = [
            jnp.concatenate([dual[k, :, at] - split[k, :, at]] * 2, axis=0) for k in range(3)
        ]
        depth = jnp.where(row < 3, pltpu.roll(x, 7, axis=0) - x + gap[0], 0.0)
        across = jnp.where(row_mask, pltpu.roll(x, 120, axis=1) - x + gap[1], 0.0)
        along = jnp.where(col_mask, pltpu.roll(x, 127, axis=1) - x + gap[2], 0.0)
        adjoint = pltpu.roll(depth, 1, axis=0) - depth
        adjoint += jnp.where((lane % TV) >= 8, pltpu.roll(across, 8, axis=1), 0.0) - across
        adjoint += jnp.where(lane % 8 >= 1, pltpu.roll(along, 1, axis=1), 0.0) - along
        base = x - factor * adjoint
        base_out[:, at] = base[0:4]
        halo_out[0:1, at] = (x - gap[0])[3:4]
        halo_out[1:2, at] = x[0:1]
        halo_out[2:3, at] = base[0:1]
        halo_out[3:4, at] = base[0:1]

    used = count[0]
    per = slots // CHUNKS
    for g in range(slots // GROUP):
        if GROUP * g % per == 0:
            copies[GROUP * g // per].wait()
        n = GROUP * g
        pairs = [
            jnp.where(top, table[voxel[n + 2 * i]], table[voxel[n + 2 * i + 1]]) for i in range(2)
        ]
        zero = jnp.zeros_like(pairs[0])
        left = jnp.concatenate([pairs[0], zero], axis=0).astype(jnp.bfloat16)
        right = jnp.concatenate([zero, pairs[1]], axis=0).astype(jnp.bfloat16)
        sums = jnp.dot(
            jnp.concatenate([left, right], axis=1),
            tiles[n:n + GROUP].reshape(GROUP * TV, TR),
            preferred_element_type=jnp.float32,
        )
        for i in range(GROUP):
            at = jnp.where(n + i < used, ray[n + i], rays)
            accs[i][at] += sums[8 * (i // 2):8 * (i // 2) + 8]
    for q in range(rays // 4):
        halves = []
        for r in (4 * q, 4 * q + 2):
            even = [acc0[r + k] + acc2[r + k] for k in range(2)]
            odd = [acc1[r + k] + acc3[r + k] for k in range(2)]
            halves.append(
                jnp.where(top, even[0], odd[1])
                + pltpu.roll(jnp.where(top, even[1], odd[0]), 4, axis=0)
            )
        partial_out[16 * q:16 * q + 16, :] = jnp.concatenate(halves, axis=0).astype(jnp.bfloat16)


def resid_kernel(parts, sinogram, out, total):
    total[...] = jnp.sum(parts[...].astype(jnp.float32), axis=0)
    for r in range(sinogram.shape[0]):
        at = pl.ds(4 * r, 4)
        total[at, :] = total[at, :] - sinogram[r]
    resid = total[...].astype(jnp.bfloat16)
    for copy in range(out.shape[0]):
        out[copy] = resid


def backward_kernel(
    count, ray, voxel, here, resid, proj_hbm, out,
    tiles, table, acc0, acc1, acc2, acc3, tile_sems,
):
    slots = proj_hbm.shape[0]
    rays = table.shape[0]
    voxel_tiles = acc0.shape[0] - 1
    copies = start_tiles(proj_hbm, tiles, tile_sems)
    accs = (acc0, acc1, acc2, acc3)
    for acc in accs:
        acc[...] = jnp.zeros_like(acc)
    row, lane = iotas((8, 128))
    low, top = lane < TV, row < 4
    mine = here[0]
    for q in range(rays // 4):
        own = resid[mine, 16 * q:16 * q + 16, :].astype(jnp.float32)
        following = resid[1 - mine, 16 * q:16 * q + 16, :].astype(jnp.float32)
        for k in range(2):
            a, b = own[8 * k:8 * k + 8], following[8 * k:8 * k + 8]
            table[4 * q + 2 * k] = jnp.where(top, a, pltpu.roll(b, 4, axis=0))
            table[4 * q + 2 * k + 1] = jnp.where(top, pltpu.roll(a, 4, axis=0), b)
    used = count[0]
    per = slots // CHUNKS
    for g in range(slots // GROUP):
        if GROUP * g % per == 0:
            copies[GROUP * g // per].wait()
        n = GROUP * g
        rows = jnp.concatenate([table[ray[n + i]] for i in range(GROUP)], axis=0)
        back = lax.dot_general(
            rows.astype(jnp.bfloat16),
            tiles[n:n + GROUP].reshape(GROUP * TV, TR),
            (((1,), (1,)), ((), ())),
            preferred_element_type=jnp.float32,
        )
        for i in range(GROUP):
            at = jnp.where(n + i < used, voxel[n + i], voxel_tiles)
            half = 128 * (i // 2)
            accs[i][at] += back[8 * i:8 * i + 8, half:half + 128]
    for j in range(voxel_tiles // 2):
        even = [acc0[2 * j + k] + acc2[2 * j + k] for k in range(2)]
        odd = [acc1[2 * j + k] + acc3[2 * j + k] for k in range(2)]
        out[:, 128 * j:128 * j + 128] = jnp.where(low, even[0], odd[1]) + pltpu.roll(
            jnp.where(low, even[1], odd[0]), TV, axis=1
        )


def update_kernel(
    rho, grad, grad_other, base, dual, halo, from_next, from_previous,
    new_volume, new_split, new_dual,
):
    slab, slabs = lax.axis_index("slab"), lax.axis_size("slab")
    first, last = slab == 0, slab == slabs - 1
    penalty = rho[0]
    factor = TAU * penalty
    limit = 1.0 / penalty
    row, lane = iotas((8, 128))
    row_mask, col_mask = plane_masks(lane)
    inner = jnp.logical_or(row < 3, jnp.logical_not(last))
    for j in range(dual.shape[2] // 128):
        at = slice(128 * j, 128 * j + 128)
        above = jnp.where(last, 0.0, factor * (from_next[1:2, at] - halo[0:1, at]))
        below = jnp.where(first, 0.0, factor * (halo[1:2, at] - from_previous[0:1, at]))
        own = jnp.concatenate([base[:, at]] * 2, axis=0)
        field = jnp.where(row < 4, own, from_next[2:3, at])
        field += jnp.where(
            row == 0, -below, jnp.where(row == 3, above, jnp.where(row == 4, -above, 0.0))
        )
        field -= TAU * (grad[:, at] + grad_other[:, at])
        new_volume[:, at] = field[0:4]
        steps = (
            jnp.where(inner, pltpu.roll(field, 7, axis=0) - field, 0.0),
            jnp.where(row_mask, pltpu.roll(field, 120, axis=1) - field, 0.0),
            jnp.where(col_mask, pltpu.roll(field, 127, axis=1) - field, 0.0),
        )
        for k in range(3):
            mixed = steps[k][0:4] + dual[k, :, at]
            clipped = jnp.clip(mixed, -limit, limit)
            new_dual[k, :, at] = clipped
            new_split[k, :, at] = mixed - clipped


def vmem():
    return pl.BlockSpec(memory_space=pltpu.VMEM)


def smem():
    return pl.BlockSpec(memory_space=pltpu.SMEM)


def anywhere():
    return pl.BlockSpec(memory_space=pl.ANY)


def params():
    return pltpu.CompilerParams(vmem_limit_bytes=VMEM_LIMIT)


def shards(
    volume, split_var, dual_var, sinogram, proj_tiles, ray_index, voxel_index, tile_count, rho
):
    f32, bf16 = jnp.float32, jnp.bfloat16
    slices, width = volume.shape
    slots = ray_index.shape[0]
    owned = sinogram.shape[0]
    group = lax.axis_size(("tile", "rep"))
    slabs = lax.axis_size("slab")
    rays = owned * group
    voxel_tiles = width // TV
    block = owned * slices

    partial, base, halo = pl.pallas_call(
        forward_kernel,
        out_shape=(
            jax.ShapeDtypeStruct((rays * slices, TR), bf16),
            jax.ShapeDtypeStruct((slices, width), f32),
            jax.ShapeDtypeStruct((4, width), f32),
        ),
        in_specs=[smem()] * 4 + [anywhere()] * 4,
        out_specs=(vmem(), vmem(), vmem()),
        scratch_shapes=[
            pltpu.VMEM((slices, width), f32),
            pltpu.VMEM((3, slices, width), f32),
            pltpu.VMEM((3, slices, width), f32),
            pltpu.VMEM(proj_tiles.shape, bf16),
            pltpu.VMEM((8, width), f32),
            pltpu.VMEM((voxel_tiles, 8, 128), f32),
        ]
        + [pltpu.VMEM((rays + 1, 8, 128), f32)] * 4
        + [pltpu.SemaphoreType.DMA((3,)), pltpu.SemaphoreType.DMA((CHUNKS,))],
        compiler_params=params(),
        name="forward",
    )(tile_count, ray_index, voxel_index, rho, volume, split_var, dual_var, proj_tiles)

    if slabs == 2:
        from_next = from_previous = lax.ppermute(halo, "slab", [(0, 1), (1, 0)])
    else:
        from_next = lax.ppermute(halo, "slab", [(i, i - 1) for i in range(1, slabs)])
        from_previous = lax.ppermute(halo, "slab", [(i, i + 1) for i in range(slabs - 1)])

    parts = lax.all_to_all(
        partial.reshape(group, block, TR), ("tile", "rep"), 0, 0, tiled=True
    )
    copies = group * (2 if slabs == 2 else 1)
    resid = pl.pallas_call(
        resid_kernel,
        out_shape=jax.ShapeDtypeStruct((copies, block, TR), bf16),
        in_specs=[vmem(), vmem()],
        out_specs=vmem(),
        scratch_shapes=[pltpu.VMEM((block, TR), f32)],
        compiler_params=params(),
        name="residual",
    )(parts, sinogram)
    if slabs == 2:
        both = lax.all_to_all(resid, ("slab", "tile", "rep"), 0, 0, tiled=True)
        both = both.reshape(2, rays * slices, TR)
        here = lax.axis_index("slab").reshape(1)
    else:
        own = lax.all_to_all(resid, ("tile", "rep"), 0, 0, tiled=True)
        following = lax.ppermute(own, "slab", [(i, i - 1) for i in range(1, slabs)])
        both = jnp.stack([own, following]).reshape(2, rays * slices, TR)
        here = jnp.zeros((1,), jnp.int32)

    grad = pl.pallas_call(
        backward_kernel,
        out_shape=jax.ShapeDtypeStruct((8, width), f32),
        in_specs=[smem()] * 4 + [vmem(), anywhere()],
        out_specs=vmem(),
        scratch_shapes=[
            pltpu.VMEM(proj_tiles.shape, bf16),
            pltpu.VMEM((rays, 8, 128), f32),
        ]
        + [pltpu.VMEM((voxel_tiles + 1, 8, 128), f32)] * 4
        + [pltpu.SemaphoreType.DMA((CHUNKS,))],
        compiler_params=params(),
        name="backward",
    )(tile_count, ray_index, voxel_index, here.astype(jnp.int32), both, proj_tiles)
    grad_other = lax.ppermute(grad, "rep", [(0, 1), (1, 0)])

    return pl.pallas_call(
        update_kernel,
        out_shape=(
            jax.ShapeDtypeStruct((slices, width), f32),
            jax.ShapeDtypeStruct((3, slices, width), f32),
            jax.ShapeDtypeStruct((3, slices, width), f32),
        ),
        in_specs=[smem()] + [vmem()] * 7,
        out_specs=(vmem(), vmem(), vmem()),
        compiler_params=params(),
        name="update",
    )(rho, grad, grad_other, base, dual_var, halo, from_next, from_previous)


def solution(mesh):
    return jax.shard_map(
        shards,
        mesh=mesh,
        in_specs=(
            P(("parts", "slab"), "tile"),
            P(None, ("parts", "slab"), "tile"),
            P(None, ("parts", "slab"), "tile"),
            P(("tile", "rep"), ("parts", "slab"), None),
            P(("tile", "rep"), None, None),
            P(("tile", "rep")),
            P(("tile", "rep")),
            P(("tile", "rep")),
            P(),
        ),
        out_specs=(
            P(("parts", "slab"), "tile"),
            P(None, ("parts", "slab"), "tile"),
            P(None, ("parts", "slab"), "tile"),
        ),
        check_vma=False,
    )
```

```python
import functools

import jax
import jax.numpy as jnp
from jax import lax
from jax.experimental import pallas as pl
from jax.experimental.pallas import tpu as pltpu
from jax.sharding import PartitionSpec as P

TV = 64
TR = 128
TAU = 0.5
GROUP = 4
CHUNKS = 8
VMEM_LIMIT = 16 * 1024 * 1024


def iotas(shape):
    row = lax.broadcasted_iota(jnp.int32, shape, 0)
    lane = lax.broadcasted_iota(jnp.int32, shape, 1)
    return row, lane


def start_tiles(proj_hbm, tiles, sems):
    per = proj_hbm.shape[0] // CHUNKS
    copies = []
    for c in range(CHUNKS):
        part = pl.ds(c * per, per)
        copy = pltpu.make_async_copy(proj_hbm.at[part], tiles.at[part], sems.at[c])
        copy.start()
        copies.append(copy)
    return copies


def plane_masks(lane):
    return (lane % TV) // 8 < 7, lane % 8 < 7


def forward_kernel(
    count, rho, ray_hbm, voxel_hbm, vol_hbm, split_hbm, dual_hbm, sino_hbm, proj_hbm,
    partial_out, base_out, halo_out,
    ray, voxel, vol, split, dual, sino, tiles, double, table, acc0, acc1, acc2, acc3,
    sems, tile_sems,
):
    slots = proj_hbm.shape[0]
    rays = acc0.shape[0] - 1
    owned = sino.shape[0]
    width = vol.shape[1]
    loads = [
        pltpu.make_async_copy(source, target, sems.at[i])
        for i, (source, target) in enumerate(
            [
                (vol_hbm, vol), (voxel_hbm, voxel), (ray_hbm, ray), (sino_hbm, sino),
                (split_hbm, split), (dual_hbm, dual),
            ]
        )
    ]
    for load in loads:
        load.start()
    copies = start_tiles(proj_hbm, tiles, tile_sems)
    accs = (acc0, acc1, acc2, acc3)
    for acc in accs:
        acc[...] = jnp.zeros_like(acc)
    row, lane = iotas((8, 128))
    low, top = lane < TV, row < 4

    loads[0].wait()
    field = vol[...]
    double[0:4, :] = field
    double[4:8, :] = field
    for j in range(width // 128):
        x = double[:, 128 * j:128 * j + 128].astype(jnp.bfloat16).astype(jnp.float32)
        turned = pltpu.roll(x, TV, axis=1)
        zero = jnp.zeros_like(x)
        first = jnp.where(jnp.logical_and(top, low), x, zero)
        second = jnp.where(jnp.logical_and(top, low), turned, zero)
        other = jnp.logical_not(jnp.logical_or(top, low))
        table[2 * j] = jnp.where(other, turned, first)
        table[2 * j + 1] = jnp.where(other, x, second)

    for load in loads[1:]:
        load.wait()
    mine = (lax.axis_index("tile") * lax.axis_size("rep") + lax.axis_index("rep")) * owned
    for r in range(owned):
        acc0[mine + r, 0:4, :] = -sino[r]
    factor = TAU * rho[0]
    row_mask, col_mask = plane_masks(lane)
    for j in range(width // 128):
        at = slice(128 * j, 128 * j + 128)
        x = double[:, at]
        gap = [
            jnp.concatenate([dual[k, :, at] - split[k, :, at]] * 2, axis=0) for k in range(3)
        ]
        depth = jnp.where(row < 3, pltpu.roll(x, 7, axis=0) - x + gap[0], 0.0)
        across = jnp.where(row_mask, pltpu.roll(x, 120, axis=1) - x + gap[1], 0.0)
        along = jnp.where(col_mask, pltpu.roll(x, 127, axis=1) - x + gap[2], 0.0)
        adjoint = pltpu.roll(depth, 1, axis=0) - depth
        adjoint += jnp.where((lane % TV) >= 8, pltpu.roll(across, 8, axis=1), 0.0) - across
        adjoint += jnp.where(lane % 8 >= 1, pltpu.roll(along, 1, axis=1), 0.0) - along
        base = x - factor * adjoint
        base_out[:, at] = base[0:4]
        halo_out[0:1, at] = (x - gap[0])[3:4]
        halo_out[1:2, at] = x[0:1]
        halo_out[2:3, at] = base[0:1]
        halo_out[3:4, at] = base[0:1]

    used = count[0]
    per = slots // CHUNKS
    for g in range(slots // GROUP):
        if GROUP * g % per == 0:
            copies[GROUP * g // per].wait()
        n = GROUP * g
        pairs = [
            jnp.where(top, table[voxel[n + 2 * i]], table[voxel[n + 2 * i + 1]]) for i in range(2)
        ]
        zero = jnp.zeros_like(pairs[0])
        left = jnp.concatenate([pairs[0], zero], axis=0).astype(jnp.bfloat16)
        right = jnp.concatenate([zero, pairs[1]], axis=0).astype(jnp.bfloat16)
        sums = jnp.dot(
            jnp.concatenate([left, right], axis=1),
            tiles[n:n + GROUP].reshape(GROUP * TV, TR),
            preferred_element_type=jnp.float32,
        )
        for i in range(GROUP):
            at = jnp.where(n + i < used, ray[n + i], rays)
            accs[i][at] += sums[8 * (i // 2):8 * (i // 2) + 8]
    for q in range(rays // 4):
        halves = []
        for r in (4 * q, 4 * q + 2):
            even = [acc0[r + k] + acc2[r + k] for k in range(2)]
            odd = [acc1[r + k] + acc3[r + k] for k in range(2)]
            halves.append(
                jnp.where(top, even[0], odd[1])
                + pltpu.roll(jnp.where(top, even[1], odd[0]), 4, axis=0)
            )
        partial_out[16 * q:16 * q + 16, :] = jnp.concatenate(halves, axis=0).astype(jnp.bfloat16)


def backward_kernel(parts_in, *refs):
    count, rho, ray_hbm, voxel_hbm, proj_hbm = refs[:5]
    parts = refs[5:5 + parts_in]
    base, halo, from_next, from_previous = refs[5 + parts_in:9 + parts_in]
    grad_out, first_out, base_out = refs[9 + parts_in:12 + parts_in]
    (
        ray, voxel, tiles, table, acc0, acc1, acc2, acc3, sems, tile_sems
    ) = refs[12 + parts_in:]
    slots = proj_hbm.shape[0]
    rays = table.shape[0]
    voxel_tiles = acc0.shape[0] - 1
    loads = [
        pltpu.make_async_copy(source, target, sems.at[i])
        for i, (source, target) in enumerate(
            [(voxel_hbm, voxel), (ray_hbm, ray)]
        )
    ]
    for load in loads:
        load.start()
    copies = start_tiles(proj_hbm, tiles, tile_sems)
    accs = (acc0, acc1, acc2, acc3)
    for acc in accs:
        acc[...] = jnp.zeros_like(acc)
    row, lane = iotas((8, 128))
    low, top = lane < TV, row < 4
    for q in range(rays // 4):
        at = slice(16 * q, 16 * q + 16)
        total = parts[0][at, :].astype(jnp.float32)
        for part in parts[1:]:
            total += part[at, :].astype(jnp.float32)
        for k in range(2):
            x = total[8 * k:8 * k + 8]
            turned = pltpu.roll(x, 4, axis=0)
            table[4 * q + 2 * k] = jnp.where(top, x, turned)
            table[4 * q + 2 * k + 1] = jnp.where(top, turned, x)

    for load in loads:
        load.wait()
    slab, slabs = lax.axis_index("slab"), lax.axis_size("slab")
    factor = TAU * rho[0]
    limit = 1.0 / rho[0]
    for j in range(voxel_tiles // 2):
        at = slice(128 * j, 128 * j + 128)
        above = factor * (from_next[1:2, at] - halo[0:1, at])
        above = jnp.where(slab == slabs - 1, 0.0, above)
        below = factor * (halo[1:2, at] - from_previous[0:1, at])
        below = jnp.where(slab == 0, 0.0, below)
        own = jnp.concatenate([base[:, at]] * 2, axis=0)
        field = jnp.where(top, own, from_next[2:3, at])
        field += jnp.where(
            row == 0, -below, jnp.where(row == 3, above, jnp.where(row == 4, -above, 0.0))
        )
        base_out[:, at] = jnp.where(row < 5, field, limit)

    used = count[0]
    per = slots // CHUNKS
    for g in range(slots // GROUP):
        if GROUP * g % per == 0:
            copies[GROUP * g // per].wait()
        n = GROUP * g
        rows = jnp.concatenate(
            [
                jnp.where(top, table[ray[n + 2 * i]], table[ray[n + 2 * i + 1]])
                for i in range(GROUP // 2)
            ],
            axis=0,
        )
        back = lax.dot_general(
            rows.astype(jnp.bfloat16),
            tiles[n:n + GROUP].reshape(GROUP * TV, TR),
            (((1,), (1,)), ((), ())),
            preferred_element_type=jnp.float32,
        )
        for i in range(GROUP):
            at = jnp.where(n + i < used, voxel[n + i], voxel_tiles)
            k = i // 2
            accs[i][at] += back[8 * k:8 * k + 8, 128 * k:128 * k + 128]
    for j in range(voxel_tiles // 2):
        at = slice(128 * j, 128 * j + 128)
        even = [acc0[2 * j + k] + acc2[2 * j + k] for k in range(2)]
        odd = [acc1[2 * j + k] + acc3[2 * j + k] for k in range(2)]
        turned = pltpu.roll(jnp.where(top, even[1], odd[0]), TV, axis=1)
        both = jnp.where(top == low, jnp.where(top, even[0], odd[1]), turned)
        grad = (both + pltpu.roll(both, 4, axis=0))[0:4]
        grad_out[:, at] = grad
        first_out[:, at] = grad[0:1]


def update_kernel(
    grad, grad_other, first_next, first_cross, base, dual,
    new_volume, new_split, new_dual,
):
    last = lax.axis_index("slab") == lax.axis_size("slab") - 1
    row, lane = iotas((8, 128))
    row_mask, col_mask = plane_masks(lane)
    inner = jnp.logical_or(row < 3, jnp.logical_not(last))
    for j in range(dual.shape[2] // 128):
        at = slice(128 * j, 128 * j + 128)
        slope = jnp.concatenate([grad[:, at] + grad_other[:, at]] * 2, axis=0)
        slope = jnp.where(row < 4, slope, first_next[:, at] + first_cross[:, at])
        limit = base[5:6, at]
        field = base[:, at] - TAU * slope
        new_volume[:, at] = field[0:4]
        steps = (
            jnp.where(inner, pltpu.roll(field, 7, axis=0) - field, 0.0),
            jnp.where(row_mask, pltpu.roll(field, 120, axis=1) - field, 0.0),
            jnp.where(col_mask, pltpu.roll(field, 127, axis=1) - field, 0.0),
        )
        for k in range(3):
            mixed = steps[k][0:4] + dual[k, :, at]
            clipped = jnp.clip(mixed, -limit, limit)
            new_dual[k, :, at] = clipped
            new_split[k, :, at] = mixed - clipped


def vmem():
    return pl.BlockSpec(memory_space=pltpu.VMEM)


def smem():
    return pl.BlockSpec(memory_space=pltpu.SMEM)


def hbm():
    return pl.BlockSpec(memory_space=pltpu.HBM)


def params():
    return pltpu.CompilerParams(vmem_limit_bytes=VMEM_LIMIT)


def shards(
    volume, split_var, dual_var, sinogram, proj_tiles, ray_index, voxel_index, tile_count, rho
):
    f32, bf16 = jnp.float32, jnp.bfloat16
    slices, width = volume.shape
    slots = ray_index.shape[0]
    owned = sinogram.shape[0]
    group = lax.axis_size(("tile", "rep"))
    reps = lax.axis_size("rep")
    slabs = lax.axis_size("slab")
    rays = owned * group
    voxel_tiles = width // TV
    dual_here = dual_var
    volume, split_var, dual_var, sinogram, proj_tiles, ray_index, voxel_index = (
        pltpu.with_memory_space_constraint(x, pltpu.HBM)
        for x in (
            volume, split_var, dual_var, sinogram, proj_tiles, ray_index, voxel_index
        )
    )

    partial, base, halo = pl.pallas_call(
        forward_kernel,
        out_shape=(
            jax.ShapeDtypeStruct((rays * slices, TR), bf16),
            jax.ShapeDtypeStruct((slices, width), f32),
            jax.ShapeDtypeStruct((4, width), f32),
        ),
        in_specs=[smem()] * 2 + [hbm()] * 7,
        out_specs=(vmem(), vmem(), vmem()),
        scratch_shapes=[
            pltpu.SMEM((slots,), jnp.int32),
            pltpu.SMEM((slots,), jnp.int32),
            pltpu.VMEM((slices, width), f32),
            pltpu.VMEM((3, slices, width), f32),
            pltpu.VMEM((3, slices, width), f32),
            pltpu.VMEM(sinogram.shape, f32),
            pltpu.VMEM(proj_tiles.shape, bf16),
            pltpu.VMEM((8, width), f32),
            pltpu.VMEM((voxel_tiles, 8, 128), f32),
        ]
        + [pltpu.VMEM((rays + 1, 8, 128), f32)] * 4
        + [pltpu.SemaphoreType.DMA((6,)), pltpu.SemaphoreType.DMA((CHUNKS,))],
        compiler_params=params(),
        name="forward",
    )(
        tile_count, rho, ray_index, voxel_index, volume, split_var, dual_var, sinogram, proj_tiles
    )

    down = [(i, i - 1) for i in range(1, slabs)]
    if slabs == 2:
        from_next = from_previous = lax.ppermute(halo, "slab", [(0, 1), (1, 0)])
    else:
        from_next = lax.ppermute(halo, "slab", down)
        from_previous = lax.ppermute(halo, "slab", [(i - 1, i) for i in range(1, slabs)])
    parts = [partial] + [
        lax.ppermute(partial, ("tile", "rep"), [(i, i ^ k) for i in range(group)])
        for k in reversed(range(1, group))
    ]

    grad, first, base = pl.pallas_call(
        functools.partial(backward_kernel, len(parts)),
        out_shape=(
            jax.ShapeDtypeStruct((slices, width), f32),
            jax.ShapeDtypeStruct((1, width), f32),
            jax.ShapeDtypeStruct((8, width), f32),
        ),
        in_specs=[smem()] * 2 + [hbm()] * 3 + [vmem()] * (len(parts) + 4),
        out_specs=(vmem(), vmem(), vmem()),
        scratch_shapes=[
            pltpu.SMEM((slots,), jnp.int32),
            pltpu.SMEM((slots,), jnp.int32),
            pltpu.VMEM(proj_tiles.shape, bf16),
            pltpu.VMEM((rays, 8, 128), f32),
        ]
        + [pltpu.VMEM((voxel_tiles + 1, 8, 128), f32)] * 4
        + [pltpu.SemaphoreType.DMA((2,)), pltpu.SemaphoreType.DMA((CHUNKS,))],
        compiler_params=params(),
        name="backward",
    )(
        tile_count, rho, ray_index, voxel_index, proj_tiles,
        *parts, base, halo, from_next, from_previous,
    )
    grad_other = lax.ppermute(grad, "rep", [(i, i ^ 1) for i in range(reps)])
    first_next = lax.ppermute(first, "slab", down)
    first_cross = lax.ppermute(
        first, ("slab", "rep"),
        [(i * reps + k, j * reps + 1 - k) for i, j in down for k in range(reps)],
    )

    return pl.pallas_call(
        update_kernel,
        out_shape=(
            jax.ShapeDtypeStruct((slices, width), f32),
            jax.ShapeDtypeStruct((3, slices, width), f32),
            jax.ShapeDtypeStruct((3, slices, width), f32),
        ),
        in_specs=[vmem()] * 6,
        out_specs=(vmem(), vmem(), vmem()),
        compiler_params=params(),
        name="update",
    )(grad, grad_other, first_next, first_cross, base, dual_here)


def solution(mesh):
    return jax.shard_map(
        shards,
        mesh=mesh,
        in_specs=(
            P(("parts", "slab"), "tile"),
            P(None, ("parts", "slab"), "tile"),
            P(None, ("parts", "slab"), "tile"),
            P(("tile", "rep"), ("parts", "slab"), None),
            P(("tile", "rep"), None, None),
            P(("tile", "rep")),
            P(("tile", "rep")),
            P(("tile", "rep")),
            P(),
        ),
        out_specs=(
            P(("parts", "slab"), "tile"),
            P(None, ("parts", "slab"), "tile"),
            P(None, ("parts", "slab"), "tile"),
        ),
        check_vma=False,
    )
```

```python
import functools

import jax
import jax.numpy as jnp
from jax import lax
from jax.experimental import pallas as pl
from jax.experimental.pallas import tpu as pltpu
from jax.sharding import PartitionSpec as P

TV = 64
TR = 128
TAU = 0.5
GROUP = 4
CHUNKS = 8
VMEM_LIMIT = 16 * 1024 * 1024


def iotas(shape):
    row = lax.broadcasted_iota(jnp.int32, shape, 0)
    lane = lax.broadcasted_iota(jnp.int32, shape, 1)
    return row, lane


def start_tiles(proj_hbm, tiles, sems):
    per = proj_hbm.shape[0] // CHUNKS
    copies = []
    for c in range(CHUNKS):
        part = pl.ds(c * per, per)
        copy = pltpu.make_async_copy(proj_hbm.at[part], tiles.at[part], sems.at[c])
        copy.start()
        copies.append(copy)
    return copies


def plane_masks(lane):
    return (lane % TV) // 8 < 7, lane % 8 < 7


def forward_kernel(
    count, ray_hbm, voxel_hbm, vol_hbm, split_hbm, dual_hbm, sino_hbm, proj_hbm,
    partial_out, adjoint_out, halo_out,
    ray, voxel, vol, split, dual, sino, tiles, double, table, acc0, acc1, acc2, acc3,
    sems, tile_sems,
):
    slots = proj_hbm.shape[0]
    rays = acc0.shape[0] - 1
    owned = sino.shape[0]
    width = vol.shape[1]
    loads = [
        pltpu.make_async_copy(source, target, sems.at[i])
        for i, (source, target) in enumerate(
            [
                (vol_hbm, vol), (voxel_hbm, voxel), (ray_hbm, ray), (sino_hbm, sino),
                (split_hbm, split), (dual_hbm, dual),
            ]
        )
    ]
    for load in loads:
        load.start()
    copies = start_tiles(proj_hbm, tiles, tile_sems)
    accs = (acc0, acc1, acc2, acc3)
    for acc in accs:
        acc[...] = jnp.zeros_like(acc)
    row, lane = iotas((8, 128))
    low, top = lane < TV, row < 4

    loads[0].wait()
    field = vol[...]
    double[0:4, :] = field
    double[4:8, :] = field
    for j in range(width // 128):
        x = double[:, 128 * j:128 * j + 128].astype(jnp.bfloat16).astype(jnp.float32)
        turned = pltpu.roll(x, TV, axis=1)
        zero = jnp.zeros_like(x)
        first = jnp.where(jnp.logical_and(top, low), x, zero)
        second = jnp.where(jnp.logical_and(top, low), turned, zero)
        other = jnp.logical_not(jnp.logical_or(top, low))
        table[2 * j] = jnp.where(other, turned, first)
        table[2 * j + 1] = jnp.where(other, x, second)

    for load in loads[1:]:
        load.wait()
    mine = (lax.axis_index("tile") * lax.axis_size("rep") + lax.axis_index("rep")) * owned
    for r in range(owned):
        acc0[mine + r, 0:4, :] = -sino[r]
    row_mask, col_mask = plane_masks(lane)
    for j in range(width // 128):
        at = slice(128 * j, 128 * j + 128)
        x = double[:, at]
        gap = [
            jnp.concatenate([dual[k, :, at] - split[k, :, at]] * 2, axis=0) for k in range(3)
        ]
        depth = jnp.where(row < 3, pltpu.roll(x, 7, axis=0) - x + gap[0], 0.0)
        across = jnp.where(row_mask, pltpu.roll(x, 120, axis=1) - x + gap[1], 0.0)
        along = jnp.where(col_mask, pltpu.roll(x, 127, axis=1) - x + gap[2], 0.0)
        adjoint = pltpu.roll(depth, 1, axis=0) - depth
        adjoint += jnp.where((lane % TV) >= 8, pltpu.roll(across, 8, axis=1), 0.0) - across
        adjoint += jnp.where(lane % 8 >= 1, pltpu.roll(along, 1, axis=1), 0.0) - along
        adjoint_out[:, at] = adjoint[0:4]
        halo_out[0:1, at] = (x - gap[0])[3:4]
        halo_out[1:2, at] = x[0:1]
        halo_out[2:3, at] = adjoint[0:1]
        halo_out[3:4, at] = adjoint[0:1]

    used = count[0]
    per = slots // CHUNKS
    for g in range(slots // GROUP):
        if GROUP * g % per == 0:
            copies[GROUP * g // per].wait()
        n = GROUP * g
        pairs = [
            jnp.where(top, table[voxel[n + 2 * i]], table[voxel[n + 2 * i + 1]]) for i in range(2)
        ]
        zero = jnp.zeros_like(pairs[0])
        left = jnp.concatenate([pairs[0], zero], axis=0).astype(jnp.bfloat16)
        right = jnp.concatenate([zero, pairs[1]], axis=0).astype(jnp.bfloat16)
        sums = jnp.dot(
            jnp.concatenate([left, right], axis=1),
            tiles[n:n + GROUP].reshape(GROUP * TV, TR),
            preferred_element_type=jnp.float32,
        )
        for i in range(GROUP):
            at = jnp.where(n + i < used, ray[n + i], rays)
            accs[i][at] += sums[8 * (i // 2):8 * (i // 2) + 8]
    for q in range(rays // 4):
        halves = []
        for r in (4 * q, 4 * q + 2):
            even = [acc0[r + k] + acc2[r + k] for k in range(2)]
            odd = [acc1[r + k] + acc3[r + k] for k in range(2)]
            halves.append(
                jnp.where(top, even[0], odd[1])
                + pltpu.roll(jnp.where(top, even[1], odd[0]), 4, axis=0)
            )
        partial_out[16 * q:16 * q + 16, :] = jnp.concatenate(halves, axis=0).astype(jnp.bfloat16)


def backward_kernel(parts_in, *refs):
    count, rho, ray_hbm, voxel_hbm, proj_hbm = refs[:5]
    parts = refs[5:5 + parts_in]
    vol, adjoint, halo, from_next, from_previous = refs[5 + parts_in:10 + parts_in]
    grad_out, first_out, base_out = refs[10 + parts_in:13 + parts_in]
    (
        ray, voxel, tiles, table, acc0, acc1, acc2, acc3, sems, tile_sems
    ) = refs[13 + parts_in:]
    slots = proj_hbm.shape[0]
    rays = table.shape[0]
    voxel_tiles = acc0.shape[0] - 1
    loads = [
        pltpu.make_async_copy(source, target, sems.at[i])
        for i, (source, target) in enumerate(
            [(voxel_hbm, voxel), (ray_hbm, ray)]
        )
    ]
    for load in loads:
        load.start()
    copies = start_tiles(proj_hbm, tiles, tile_sems)
    accs = (acc0, acc1, acc2, acc3)
    for acc in accs:
        acc[...] = jnp.zeros_like(acc)
    row, lane = iotas((8, 128))
    low, top = lane < TV, row < 4
    for q in range(rays // 4):
        at = slice(16 * q, 16 * q + 16)
        total = parts[0][at, :].astype(jnp.float32)
        for part in parts[1:]:
            total += part[at, :].astype(jnp.float32)
        for k in range(2):
            x = total[8 * k:8 * k + 8]
            turned = pltpu.roll(x, 4, axis=0)
            table[4 * q + 2 * k] = jnp.where(top, x, turned)
            table[4 * q + 2 * k + 1] = jnp.where(top, turned, x)

    for load in loads:
        load.wait()
    slab, slabs = lax.axis_index("slab"), lax.axis_size("slab")
    factor = TAU * rho[0]
    limit = 1.0 / rho[0]
    for j in range(voxel_tiles // 2):
        at = slice(128 * j, 128 * j + 128)
        above = jnp.where(slab == slabs - 1, 0.0, from_next[1:2, at] - halo[0:1, at])
        below = jnp.where(slab == 0, 0.0, halo[1:2, at] - from_previous[0:1, at])
        turn = jnp.where(top, jnp.concatenate([adjoint[:, at]] * 2, axis=0), from_next[2:3, at])
        turn += jnp.where(
            row == 0, below, jnp.where(row == 3, -above, jnp.where(row == 4, above, 0.0))
        )
        field = jnp.where(top, jnp.concatenate([vol[:, at]] * 2, axis=0), from_next[1:2, at])
        field -= factor * turn
        base_out[:, at] = jnp.where(row < 5, field, limit)

    used = count[0]
    per = slots // CHUNKS
    for g in range(slots // GROUP):
        if GROUP * g % per == 0:
            copies[GROUP * g // per].wait()
        n = GROUP * g
        rows = jnp.concatenate(
            [
                jnp.where(top, table[ray[n + 2 * i]], table[ray[n + 2 * i + 1]])
                for i in range(GROUP // 2)
            ],
            axis=0,
        )
        back = lax.dot_general(
            rows.astype(jnp.bfloat16),
            tiles[n:n + GROUP].reshape(GROUP * TV, TR),
            (((1,), (1,)), ((), ())),
            preferred_element_type=jnp.float32,
        )
        for i in range(GROUP):
            at = jnp.where(n + i < used, voxel[n + i], voxel_tiles)
            k = i // 2
            accs[i][at] += back[8 * k:8 * k + 8, 128 * k:128 * k + 128]
    for j in range(voxel_tiles // 2):
        at = slice(128 * j, 128 * j + 128)
        even = [acc0[2 * j + k] + acc2[2 * j + k] for k in range(2)]
        odd = [acc1[2 * j + k] + acc3[2 * j + k] for k in range(2)]
        turned = pltpu.roll(jnp.where(top, even[1], odd[0]), TV, axis=1)
        both = jnp.where(top == low, jnp.where(top, even[0], odd[1]), turned)
        grad = (both + pltpu.roll(both, 4, axis=0))[0:4]
        grad_out[:, at] = grad
        first_out[:, at] = grad[0:1]


def update_kernel(
    grad, grad_other, first_next, first_cross, base, dual,
    new_volume, new_split, new_dual,
):
    last = lax.axis_index("slab") == lax.axis_size("slab") - 1
    row, lane = iotas((8, 128))
    row_mask, col_mask = plane_masks(lane)
    inner = jnp.logical_or(row < 3, jnp.logical_not(last))
    for j in range(dual.shape[2] // 128):
        at = slice(128 * j, 128 * j + 128)
        slope = jnp.concatenate([grad[:, at] + grad_other[:, at]] * 2, axis=0)
        slope = jnp.where(row < 4, slope, first_next[:, at] + first_cross[:, at])
        limit = base[5:6, at]
        field = base[:, at] - TAU * slope
        new_volume[:, at] = field[0:4]
        steps = (
            jnp.where(inner, pltpu.roll(field, 7, axis=0) - field, 0.0),
            jnp.where(row_mask, pltpu.roll(field, 120, axis=1) - field, 0.0),
            jnp.where(col_mask, pltpu.roll(field, 127, axis=1) - field, 0.0),
        )
        for k in range(3):
            mixed = steps[k][0:4] + dual[k, :, at]
            clipped = jnp.clip(mixed, -limit, limit)
            new_dual[k, :, at] = clipped
            new_split[k, :, at] = mixed - clipped


def vmem():
    return pl.BlockSpec(memory_space=pltpu.VMEM)


def smem():
    return pl.BlockSpec(memory_space=pltpu.SMEM)


def hbm():
    return pl.BlockSpec(memory_space=pltpu.HBM)


def params():
    return pltpu.CompilerParams(vmem_limit_bytes=VMEM_LIMIT)


def shards(
    volume, split_var, dual_var, sinogram, proj_tiles, ray_index, voxel_index, tile_count, rho
):
    f32, bf16 = jnp.float32, jnp.bfloat16
    slices, width = volume.shape
    slots = ray_index.shape[0]
    owned = sinogram.shape[0]
    group = lax.axis_size(("tile", "rep"))
    reps = lax.axis_size("rep")
    slabs = lax.axis_size("slab")
    rays = owned * group
    voxel_tiles = width // TV
    volume_here, dual_here = volume, dual_var
    volume, split_var, dual_var, sinogram, proj_tiles, ray_index, voxel_index = (
        pltpu.with_memory_space_constraint(x, pltpu.HBM)
        for x in (
            volume, split_var, dual_var, sinogram, proj_tiles, ray_index, voxel_index
        )
    )

    partial, adjoint, halo = pl.pallas_call(
        forward_kernel,
        out_shape=(
            jax.ShapeDtypeStruct((rays * slices, TR), bf16),
            jax.ShapeDtypeStruct((slices, width), f32),
            jax.ShapeDtypeStruct((4, width), f32),
        ),
        in_specs=[smem()] + [hbm()] * 7,
        out_specs=(vmem(), vmem(), vmem()),
        scratch_shapes=[
            pltpu.SMEM((slots,), jnp.int32),
            pltpu.SMEM((slots,), jnp.int32),
            pltpu.VMEM((slices, width), f32),
            pltpu.VMEM((3, slices, width), f32),
            pltpu.VMEM((3, slices, width), f32),
            pltpu.VMEM(sinogram.shape, f32),
            pltpu.VMEM(proj_tiles.shape, bf16),
            pltpu.VMEM((8, width), f32),
            pltpu.VMEM((voxel_tiles, 8, 128), f32),
        ]
        + [pltpu.VMEM((rays + 1, 8, 128), f32)] * 4
        + [pltpu.SemaphoreType.DMA((6,)), pltpu.SemaphoreType.DMA((CHUNKS,))],
        compiler_params=params(),
        name="forward",
    )(
        tile_count, ray_index, voxel_index, volume, split_var, dual_var, sinogram, proj_tiles
    )

    down = [(i, i - 1) for i in range(1, slabs)]
    if slabs == 2:
        from_next = from_previous = lax.ppermute(halo, "slab", [(0, 1), (1, 0)])
    else:
        from_next = lax.ppermute(halo, "slab", down)
        from_previous = lax.ppermute(halo, "slab", [(i - 1, i) for i in range(1, slabs)])
    step = 1
    while True:
        moved = lax.ppermute(partial, ("tile", "rep"), [(i, i ^ step) for i in range(group)])
        step *= 2
        if step == group:
            break
        partial = (partial.astype(f32) + moved.astype(f32)).astype(bf16)
    parts = [partial, moved]

    grad, first, base = pl.pallas_call(
        functools.partial(backward_kernel, len(parts)),
        out_shape=(
            jax.ShapeDtypeStruct((slices, width), f32),
            jax.ShapeDtypeStruct((1, width), f32),
            jax.ShapeDtypeStruct((8, width), f32),
        ),
        in_specs=[smem()] * 2 + [hbm()] * 3 + [vmem()] * (len(parts) + 5),
        out_specs=(vmem(), vmem(), vmem()),
        scratch_shapes=[
            pltpu.SMEM((slots,), jnp.int32),
            pltpu.SMEM((slots,), jnp.int32),
            pltpu.VMEM(proj_tiles.shape, bf16),
            pltpu.VMEM((rays, 8, 128), f32),
        ]
        + [pltpu.VMEM((voxel_tiles + 1, 8, 128), f32)] * 4
        + [pltpu.SemaphoreType.DMA((2,)), pltpu.SemaphoreType.DMA((CHUNKS,))],
        compiler_params=params(),
        name="backward",
    )(
        tile_count, rho, ray_index, voxel_index, proj_tiles,
        *parts, volume_here, adjoint, halo, from_next, from_previous,
    )
    grad_other = lax.ppermute(grad, "rep", [(i, i ^ 1) for i in range(reps)])
    first_next = lax.ppermute(first, "slab", down)
    first_cross = lax.ppermute(first_next, "rep", [(i, i ^ 1) for i in range(reps)])

    return pl.pallas_call(
        update_kernel,
        out_shape=(
            jax.ShapeDtypeStruct((slices, width), f32),
            jax.ShapeDtypeStruct((3, slices, width), f32),
            jax.ShapeDtypeStruct((3, slices, width), f32),
        ),
        in_specs=[vmem()] * 6,
        out_specs=(vmem(), vmem(), vmem()),
        compiler_params=params(),
        name="update",
    )(grad, grad_other, first_next, first_cross, base, dual_here)


def solution(mesh):
    return jax.shard_map(
        shards,
        mesh=mesh,
        in_specs=(
            P(("parts", "slab"), "tile"),
            P(None, ("parts", "slab"), "tile"),
            P(None, ("parts", "slab"), "tile"),
            P(("tile", "rep"), ("parts", "slab"), None),
            P(("tile", "rep"), None, None),
            P(("tile", "rep")),
            P(("tile", "rep")),
            P(("tile", "rep")),
            P(),
        ),
        out_specs=(
            P(("parts", "slab"), "tile"),
            P(None, ("parts", "slab"), "tile"),
            P(None, ("parts", "slab"), "tile"),
        ),
        check_vma=False,
    )
```

```python
import jax
import jax.numpy as jnp
from jax import lax
from jax.experimental import pallas as pl
from jax.experimental.pallas import tpu as pltpu
from jax.sharding import PartitionSpec as P

TV = 64
TR = 128
TAU = 0.5
GROUP = 4
CHUNKS = 8
VMEM_LIMIT = 16 * 1024 * 1024


def iotas(shape):
    row = lax.broadcasted_iota(jnp.int32, shape, 0)
    lane = lax.broadcasted_iota(jnp.int32, shape, 1)
    return row, lane


def start_tiles(proj_hbm, tiles, sems):
    per = proj_hbm.shape[0] // CHUNKS
    copies = []
    for c in range(CHUNKS):
        part = pl.ds(c * per, per)
        copy = pltpu.make_async_copy(proj_hbm.at[part], tiles.at[part], sems.at[c])
        copy.start()
        copies.append(copy)
    return copies


def plane_masks(lane):
    return (lane % TV) // 8 < 7, lane % 8 < 7


def forward_kernel(
    count, ray_hbm, voxel_hbm, vol_hbm, split_hbm, dual_hbm, sino_hbm, proj_hbm,
    partial_out, adjoint_out, edge_out, first_out,
    ray, voxel, vol, split, dual, sino, tiles, double, table, acc0, acc1, acc2, acc3,
    sems, tile_sems,
):
    slots = proj_hbm.shape[0]
    rays = acc0.shape[0] - 1
    owned = sino.shape[0]
    width = vol.shape[1]
    loads = [
        pltpu.make_async_copy(source, target, sems.at[i])
        for i, (source, target) in enumerate(
            [
                (vol_hbm, vol), (voxel_hbm, voxel), (ray_hbm, ray), (sino_hbm, sino),
                (split_hbm, split), (dual_hbm, dual),
            ]
        )
    ]
    for load in loads:
        load.start()
    copies = start_tiles(proj_hbm, tiles, tile_sems)
    accs = (acc0, acc1, acc2, acc3)
    for acc in accs:
        acc[...] = jnp.zeros_like(acc)
    row, lane = iotas((8, 128))
    low, top = lane < TV, row < 4

    loads[0].wait()
    field = vol[...]
    double[0:4, :] = field
    double[4:8, :] = field
    for j in range(width // 128):
        x = double[:, 128 * j:128 * j + 128].astype(jnp.bfloat16).astype(jnp.float32)
        turned = pltpu.roll(x, TV, axis=1)
        zero = jnp.zeros_like(x)
        first = jnp.where(jnp.logical_and(top, low), x, zero)
        second = jnp.where(jnp.logical_and(top, low), turned, zero)
        other = jnp.logical_not(jnp.logical_or(top, low))
        table[2 * j] = jnp.where(other, turned, first)
        table[2 * j + 1] = jnp.where(other, x, second)

    for load in loads[1:]:
        load.wait()
    mine = (lax.axis_index("tile") * lax.axis_size("rep") + lax.axis_index("rep")) * owned
    for r in range(owned):
        acc0[mine + r, 0:4, :] = -sino[r]
    row_mask, col_mask = plane_masks(lane)
    for j in range(width // 128):
        at = slice(128 * j, 128 * j + 128)
        x = double[:, at]
        gap = [
            jnp.concatenate([dual[k, :, at] - split[k, :, at]] * 2, axis=0) for k in range(3)
        ]
        depth = jnp.where(row < 3, pltpu.roll(x, 7, axis=0) - x + gap[0], 0.0)
        across = jnp.where(row_mask, pltpu.roll(x, 120, axis=1) - x + gap[1], 0.0)
        along = jnp.where(col_mask, pltpu.roll(x, 127, axis=1) - x + gap[2], 0.0)
        adjoint = pltpu.roll(depth, 1, axis=0) - depth
        adjoint += jnp.where((lane % TV) >= 8, pltpu.roll(across, 8, axis=1), 0.0) - across
        adjoint += jnp.where(lane % 8 >= 1, pltpu.roll(along, 1, axis=1), 0.0) - along
        adjoint_out[:, at] = adjoint[0:4]
        edge_out[:, at] = (x - gap[0])[3:4]
        first_out[:, at] = x[0:1]

    used = count[0]
    per = slots // CHUNKS
    for g in range(slots // GROUP):
        if GROUP * g % per == 0:
            copies[GROUP * g // per].wait()
        n = GROUP * g
        pairs = [
            jnp.where(top, table[voxel[n + 2 * i]], table[voxel[n + 2 * i + 1]]) for i in range(2)
        ]
        zero = jnp.zeros_like(pairs[0])
        left = jnp.concatenate([pairs[0], zero], axis=0).astype(jnp.bfloat16)
        right = jnp.concatenate([zero, pairs[1]], axis=0).astype(jnp.bfloat16)
        sums = jnp.dot(
            jnp.concatenate([left, right], axis=1),
            tiles[n:n + GROUP].reshape(GROUP * TV, TR),
            preferred_element_type=jnp.float32,
        )
        for i in range(GROUP):
            at = jnp.where(n + i < used, ray[n + i], rays)
            accs[i][at] += sums[8 * (i // 2):8 * (i // 2) + 8]
    for q in range(rays // 4):
        halves = []
        for r in (4 * q, 4 * q + 2):
            even = [acc0[r + k] + acc2[r + k] for k in range(2)]
            odd = [acc1[r + k] + acc3[r + k] for k in range(2)]
            halves.append(
                jnp.where(top, even[0], odd[1])
                + pltpu.roll(jnp.where(top, even[1], odd[0]), 4, axis=0)
            )
        partial_out[16 * q:16 * q + 16, :] = jnp.concatenate(halves, axis=0).astype(jnp.bfloat16)


def backward_kernel(
    count, rho, ray_hbm, voxel_hbm, proj_hbm,
    total, shared, vol, adjoint, edge, from_next, from_previous,
    grad_out, base_out, limit_out,
    ray, voxel, tiles, table, acc0, acc1, acc2, acc3, sems, tile_sems,
):
    slots = proj_hbm.shape[0]
    rays = table.shape[0]
    voxel_tiles = acc0.shape[0] - 1
    loads = [
        pltpu.make_async_copy(source, target, sems.at[i])
        for i, (source, target) in enumerate(
            [(voxel_hbm, voxel), (ray_hbm, ray)]
        )
    ]
    for load in loads:
        load.start()
    copies = start_tiles(proj_hbm, tiles, tile_sems)
    accs = (acc0, acc1, acc2, acc3)
    for acc in accs:
        acc[...] = jnp.zeros_like(acc)
    row, lane = iotas((8, 128))
    low, top = lane < TV, row < 4
    holder = lax.axis_index("rep") == lax.axis_size("rep") - 1
    for q in range(rays // 4):
        at = slice(16 * q, 16 * q + 16)
        both = jnp.where(holder, total[at, :].astype(jnp.float32), shared[at, :].astype(jnp.float32))
        for k in range(2):
            x = both[8 * k:8 * k + 8]
            turned = pltpu.roll(x, 4, axis=0)
            table[4 * q + 2 * k] = jnp.where(top, x, turned)
            table[4 * q + 2 * k + 1] = jnp.where(top, turned, x)

    for load in loads:
        load.wait()
    slab, slabs = lax.axis_index("slab"), lax.axis_size("slab")
    factor = TAU * rho[0]
    limit = 1.0 / rho[0]
    short = lax.broadcasted_iota(jnp.int32, (4, 128), 0)
    for j in range(voxel_tiles // 2):
        at = slice(128 * j, 128 * j + 128)
        field = vol[:, at]
        above = jnp.where(slab == slabs - 1, 0.0, from_next[:, at] - edge[:, at])
        below = jnp.where(slab == 0, 0.0, field[0:1] - from_previous[:, at])
        turn = adjoint[:, at] + jnp.where(short == 0, below, jnp.where(short == 3, -above, 0.0))
        base_out[:, at] = field - factor * turn
        limit_out[:, at] = jnp.full((1, 128), limit, jnp.float32)

    used = count[0]
    per = slots // CHUNKS
    for g in range(slots // GROUP):
        if GROUP * g % per == 0:
            copies[GROUP * g // per].wait()
        n = GROUP * g
        rows = jnp.concatenate(
            [
                jnp.where(top, table[ray[n + 2 * i]], table[ray[n + 2 * i + 1]])
                for i in range(GROUP // 2)
            ],
            axis=0,
        )
        back = lax.dot_general(
            rows.astype(jnp.bfloat16),
            tiles[n:n + GROUP].reshape(GROUP * TV, TR),
            (((1,), (1,)), ((), ())),
            preferred_element_type=jnp.float32,
        )
        for i in range(GROUP):
            at = jnp.where(n + i < used, voxel[n + i], voxel_tiles)
            k = i // 2
            accs[i][at] += back[8 * k:8 * k + 8, 128 * k:128 * k + 128]
    for j in range(voxel_tiles // 2):
        at = slice(128 * j, 128 * j + 128)
        even = [acc0[2 * j + k] + acc2[2 * j + k] for k in range(2)]
        odd = [acc1[2 * j + k] + acc3[2 * j + k] for k in range(2)]
        turned = pltpu.roll(jnp.where(top, even[1], odd[0]), TV, axis=1)
        both = jnp.where(top == low, jnp.where(top, even[0], odd[1]), turned)
        grad = (both + pltpu.roll(both, 4, axis=0))[0:4]
        grad_out[:, at] = grad


def update_kernel(
    grad, grad_other, first_next, base, dual, limits,
    new_volume, new_split, new_dual,
):
    last = lax.axis_index("slab") == lax.axis_size("slab") - 1
    row, lane = iotas((8, 128))
    row_mask, col_mask = plane_masks(lane)
    inner = jnp.logical_or(row < 3, jnp.logical_not(last))
    for j in range(dual.shape[2] // 128):
        at = slice(128 * j, 128 * j + 128)
        limit = limits[:, at]
        own = base[:, at] - TAU * (grad[:, at] + grad_other[:, at])
        field = jnp.where(row < 4, jnp.concatenate([own] * 2, axis=0), first_next[:, at])
        new_volume[:, at] = own
        steps = (
            jnp.where(inner, pltpu.roll(field, 7, axis=0) - field, 0.0),
            jnp.where(row_mask, pltpu.roll(field, 120, axis=1) - field, 0.0),
            jnp.where(col_mask, pltpu.roll(field, 127, axis=1) - field, 0.0),
        )
        for k in range(3):
            mixed = steps[k][0:4] + dual[k, :, at]
            clipped = jnp.clip(mixed, -limit, limit)
            new_dual[k, :, at] = clipped
            new_split[k, :, at] = mixed - clipped


def vmem():
    return pl.BlockSpec(memory_space=pltpu.VMEM)


def smem():
    return pl.BlockSpec(memory_space=pltpu.SMEM)


def hbm():
    return pl.BlockSpec(memory_space=pltpu.HBM)


def params():
    return pltpu.CompilerParams(vmem_limit_bytes=VMEM_LIMIT)


def shards(
    volume, split_var, dual_var, sinogram, proj_tiles, ray_index, voxel_index, tile_count, rho
):
    f32, bf16 = jnp.float32, jnp.bfloat16
    slices, width = volume.shape
    slots = ray_index.shape[0]
    owned = sinogram.shape[0]
    group = lax.axis_size(("tile", "rep"))
    reps = lax.axis_size("rep")
    slabs = lax.axis_size("slab")
    rays = owned * group
    voxel_tiles = width // TV
    volume_here, dual_here = volume, dual_var
    volume, split_var, dual_var, sinogram, proj_tiles, ray_index, voxel_index = (
        pltpu.with_memory_space_constraint(x, pltpu.HBM)
        for x in (
            volume, split_var, dual_var, sinogram, proj_tiles, ray_index, voxel_index
        )
    )

    partial, adjoint, edge, first = pl.pallas_call(
        forward_kernel,
        out_shape=(
            jax.ShapeDtypeStruct((rays * slices, TR), bf16),
            jax.ShapeDtypeStruct((slices, width), f32),
            jax.ShapeDtypeStruct((1, width), f32),
            jax.ShapeDtypeStruct((1, width), f32),
        ),
        in_specs=[smem()] + [hbm()] * 7,
        out_specs=(vmem(),) * 4,
        scratch_shapes=[
            pltpu.SMEM((slots,), jnp.int32),
            pltpu.SMEM((slots,), jnp.int32),
            pltpu.VMEM((slices, width), f32),
            pltpu.VMEM((3, slices, width), f32),
            pltpu.VMEM((3, slices, width), f32),
            pltpu.VMEM(sinogram.shape, f32),
            pltpu.VMEM(proj_tiles.shape, bf16),
            pltpu.VMEM((8, width), f32),
            pltpu.VMEM((voxel_tiles, 8, 128), f32),
        ]
        + [pltpu.VMEM((rays + 1, 8, 128), f32)] * 4
        + [pltpu.SemaphoreType.DMA((6,)), pltpu.SemaphoreType.DMA((CHUNKS,))],
        compiler_params=params(),
        name="forward",
    )(
        tile_count, ray_index, voxel_index, volume, split_var, dual_var, sinogram, proj_tiles
    )

    down = [(i, i - 1) for i in range(1, slabs)]
    if slabs == 2:
        halo = jnp.where(lax.axis_index("slab") == 0, edge, first)
        from_next = from_previous = lax.ppermute(halo, "slab", [(0, 1), (1, 0)])
    else:
        from_next = lax.ppermute(first, "slab", down)
        from_previous = lax.ppermute(edge, "slab", [(i - 1, i) for i in range(1, slabs)])

    both = ("tile", "rep")
    holders = range(reps - 1, group, reps)
    moved = lax.ppermute(partial, "rep", [(0, 1)])
    total = (partial.astype(f32) + moved.astype(f32)).astype(bf16)
    step = reps
    while step < group:
        moved = lax.ppermute(total, both, [(i, i ^ step) for i in holders])
        if step == reps:
            moved, from_next, from_previous = lax.optimization_barrier(
                (moved, from_next, from_previous)
            )
        total = (total.astype(f32) + moved.astype(f32)).astype(bf16)
        step *= 2
    shared = lax.ppermute(total, "rep", [(1, 0)])

    grad, base, limits = pl.pallas_call(
        backward_kernel,
        out_shape=(
            jax.ShapeDtypeStruct((slices, width), f32),
            jax.ShapeDtypeStruct((slices, width), f32),
            jax.ShapeDtypeStruct((1, width), f32),
        ),
        in_specs=[smem()] * 2 + [hbm()] * 3 + [vmem()] * 7,
        out_specs=(vmem(), vmem(), vmem()),
        scratch_shapes=[
            pltpu.SMEM((slots,), jnp.int32),
            pltpu.SMEM((slots,), jnp.int32),
            pltpu.VMEM(proj_tiles.shape, bf16),
            pltpu.VMEM((rays, 8, 128), f32),
        ]
        + [pltpu.VMEM((voxel_tiles + 1, 8, 128), f32)] * 4
        + [pltpu.SemaphoreType.DMA((2,)), pltpu.SemaphoreType.DMA((CHUNKS,))],
        compiler_params=params(),
        name="backward",
    )(
        tile_count, rho, ray_index, voxel_index, proj_tiles,
        total, shared, volume_here, adjoint, edge, from_next, from_previous,
    )
    grad_other = lax.ppermute(grad, "rep", [(i, i ^ 1) for i in range(reps)])
    new_first = base[0:1] - TAU * (grad[0:1] + grad_other[0:1])
    first_next = lax.ppermute(new_first, "slab", down)

    return pl.pallas_call(
        update_kernel,
        out_shape=(
            jax.ShapeDtypeStruct((slices, width), f32),
            jax.ShapeDtypeStruct((3, slices, width), f32),
            jax.ShapeDtypeStruct((3, slices, width), f32),
        ),
        in_specs=[vmem()] * 6,
        out_specs=(vmem(), vmem(), vmem()),
        compiler_params=params(),
        name="update",
    )(grad, grad_other, first_next, base, dual_here, limits)


def solution(mesh):
    return jax.shard_map(
        shards,
        mesh=mesh,
        in_specs=(
            P(("parts", "slab"), "tile"),
            P(None, ("parts", "slab"), "tile"),
            P(None, ("parts", "slab"), "tile"),
            P(("tile", "rep"), ("parts", "slab"), None),
            P(("tile", "rep"), None, None),
            P(("tile", "rep")),
            P(("tile", "rep")),
            P(("tile", "rep")),
            P(),
        ),
        out_specs=(
            P(("parts", "slab"), "tile"),
            P(None, ("parts", "slab"), "tile"),
            P(None, ("parts", "slab"), "tile"),
        ),
        check_vma=False,
    )
```

```python
import jax
import jax.numpy as jnp
from jax import lax
from jax.experimental import pallas as pl
from jax.experimental.pallas import tpu as pltpu
from jax.sharding import PartitionSpec as P

TV = 64
TR = 128
TAU = 0.5
GROUP = 4
CHUNKS = 8
VMEM_LIMIT = 16 * 1024 * 1024


def iotas(shape):
    row = lax.broadcasted_iota(jnp.int32, shape, 0)
    lane = lax.broadcasted_iota(jnp.int32, shape, 1)
    return row, lane


def start_tiles(proj_hbm, tiles, sems):
    per = proj_hbm.shape[0] // CHUNKS
    copies = []
    for c in range(CHUNKS):
        part = pl.ds(c * per, per)
        copy = pltpu.make_async_copy(proj_hbm.at[part], tiles.at[part], sems.at[c])
        copy.start()
        copies.append(copy)
    return copies


def plane_masks(lane):
    return (lane % TV) // 8 < 7, lane % 8 < 7


def forward_kernel(
    count, ray_hbm, voxel_hbm, vol_hbm, split_hbm, dual_hbm, sino_hbm, proj_hbm,
    partial_out, adjoint_out, edge_out, first_out,
    ray, voxel, vol, split, dual, sino, tiles, double, table, acc0, acc1, acc2, acc3,
    sems, tile_sems,
):
    slots = proj_hbm.shape[0]
    rays = acc0.shape[0] - 1
    owned = sino.shape[0]
    width = vol.shape[1]
    loads = [
        pltpu.make_async_copy(source, target, sems.at[i])
        for i, (source, target) in enumerate(
            [
                (vol_hbm, vol), (voxel_hbm, voxel), (ray_hbm, ray), (sino_hbm, sino),
                (split_hbm, split), (dual_hbm, dual),
            ]
        )
    ]
    for load in loads:
        load.start()
    copies = start_tiles(proj_hbm, tiles, tile_sems)
    accs = (acc0, acc1, acc2, acc3)
    for acc in accs:
        acc[...] = jnp.zeros_like(acc)
    row, lane = iotas((8, 128))
    low, top = lane < TV, row < 4

    loads[0].wait()
    field = vol[...]
    double[0:4, :] = field
    double[4:8, :] = field
    for j in range(width // 128):
        x = double[:, 128 * j:128 * j + 128].astype(jnp.bfloat16).astype(jnp.float32)
        turned = pltpu.roll(x, TV, axis=1)
        zero = jnp.zeros_like(x)
        first = jnp.where(jnp.logical_and(top, low), x, zero)
        second = jnp.where(jnp.logical_and(top, low), turned, zero)
        other = jnp.logical_not(jnp.logical_or(top, low))
        table[2 * j] = jnp.where(other, turned, first)
        table[2 * j + 1] = jnp.where(other, x, second)

    for load in loads[1:]:
        load.wait()
    mine = (lax.axis_index("tile") * lax.axis_size("rep") + lax.axis_index("rep")) * owned
    for r in range(owned):
        acc0[mine + r, 0:4, :] = -sino[r]
    row_mask, col_mask = plane_masks(lane)
    for j in range(width // 128):
        at = slice(128 * j, 128 * j + 128)
        x = double[:, at]
        gap = [
            jnp.concatenate([dual[k, :, at] - split[k, :, at]] * 2, axis=0) for k in range(3)
        ]
        depth = jnp.where(row < 3, pltpu.roll(x, 7, axis=0) - x + gap[0], 0.0)
        across = jnp.where(row_mask, pltpu.roll(x, 120, axis=1) - x + gap[1], 0.0)
        along = jnp.where(col_mask, pltpu.roll(x, 127, axis=1) - x + gap[2], 0.0)
        adjoint = pltpu.roll(depth, 1, axis=0) - depth
        adjoint += jnp.where((lane % TV) >= 8, pltpu.roll(across, 8, axis=1), 0.0) - across
        adjoint += jnp.where(lane % 8 >= 1, pltpu.roll(along, 1, axis=1), 0.0) - along
        adjoint_out[:, at] = adjoint[0:4]
        edge_out[:, at] = (x - gap[0])[3:4]
        first_out[:, at] = x[0:1]

    used = count[0]
    per = slots // CHUNKS
    for g in range(slots // GROUP):
        if GROUP * g % per == 0:
            copies[GROUP * g // per].wait()
        n = GROUP * g
        pairs = [
            jnp.where(top, table[voxel[n + 2 * i]], table[voxel[n + 2 * i + 1]]) for i in range(2)
        ]
        zero = jnp.zeros_like(pairs[0])
        left = jnp.concatenate([pairs[0], zero], axis=0).astype(jnp.bfloat16)
        right = jnp.concatenate([zero, pairs[1]], axis=0).astype(jnp.bfloat16)
        sums = jnp.dot(
            jnp.concatenate([left, right], axis=1),
            tiles[n:n + GROUP].reshape(GROUP * TV, TR),
            preferred_element_type=jnp.float32,
        )
        for i in range(GROUP):
            at = jnp.where(n + i < used, ray[n + i], rays)
            accs[i][at] += sums[8 * (i // 2):8 * (i // 2) + 8]
    for q in range(rays // 4):
        halves = []
        for r in (4 * q, 4 * q + 2):
            even = [acc0[r + k] + acc2[r + k] for k in range(2)]
            odd = [acc1[r + k] + acc3[r + k] for k in range(2)]
            halves.append(
                jnp.where(top, even[0], odd[1])
                + pltpu.roll(jnp.where(top, even[1], odd[0]), 4, axis=0)
            )
        partial_out[16 * q:16 * q + 16, :] = jnp.concatenate(halves, axis=0).astype(jnp.bfloat16)


def backward_kernel(
    count, rho, ray_hbm, voxel_hbm, proj_hbm,
    part, moved, vol, adjoint, edge, from_next, from_previous,
    grad_out, base_out, limit_out,
    ray, voxel, tiles, table, acc0, acc1, acc2, acc3, sems, tile_sems,
):
    slots = proj_hbm.shape[0]
    rays = table.shape[0]
    voxel_tiles = acc0.shape[0] - 1
    loads = [
        pltpu.make_async_copy(source, target, sems.at[i])
        for i, (source, target) in enumerate(
            [(voxel_hbm, voxel), (ray_hbm, ray)]
        )
    ]
    for load in loads:
        load.start()
    copies = start_tiles(proj_hbm, tiles, tile_sems)
    accs = (acc0, acc1, acc2, acc3)
    for acc in accs:
        acc[...] = jnp.zeros_like(acc)
    row, lane = iotas((8, 128))
    low, top = lane < TV, row < 4
    for q in range(rays // 4):
        at = slice(16 * q, 16 * q + 16)
        both = part[at, :].astype(jnp.float32) + moved[at, :].astype(jnp.float32)
        for k in range(2):
            x = both[8 * k:8 * k + 8]
            turned = pltpu.roll(x, 4, axis=0)
            table[4 * q + 2 * k] = jnp.where(top, x, turned)
            table[4 * q + 2 * k + 1] = jnp.where(top, turned, x)

    for load in loads:
        load.wait()
    slab, slabs = lax.axis_index("slab"), lax.axis_size("slab")
    factor = TAU * rho[0]
    limit = 1.0 / rho[0]
    short = lax.broadcasted_iota(jnp.int32, (4, 128), 0)
    for j in range(voxel_tiles // 2):
        at = slice(128 * j, 128 * j + 128)
        field = vol[:, at]
        above = jnp.where(slab == slabs - 1, 0.0, from_next[:, at] - edge[:, at])
        below = jnp.where(slab == 0, 0.0, field[0:1] - from_previous[:, at])
        turn = adjoint[:, at] + jnp.where(short == 0, below, jnp.where(short == 3, -above, 0.0))
        base_out[:, at] = field - factor * turn
        limit_out[:, at] = jnp.full((1, 128), limit, jnp.float32)

    used = count[0]
    per = slots // CHUNKS
    for g in range(slots // GROUP):
        if GROUP * g % per == 0:
            copies[GROUP * g // per].wait()
        n = GROUP * g
        rows = jnp.concatenate(
            [
                jnp.where(top, table[ray[n + 2 * i]], table[ray[n + 2 * i + 1]])
                for i in range(GROUP // 2)
            ],
            axis=0,
        )
        back = lax.dot_general(
            rows.astype(jnp.bfloat16),
            tiles[n:n + GROUP].reshape(GROUP * TV, TR),
            (((1,), (1,)), ((), ())),
            preferred_element_type=jnp.float32,
        )
        for i in range(GROUP):
            at = jnp.where(n + i < used, voxel[n + i], voxel_tiles)
            k = i // 2
            accs[i][at] += back[8 * k:8 * k + 8, 128 * k:128 * k + 128]
    for j in range(voxel_tiles // 2):
        at = slice(128 * j, 128 * j + 128)
        even = [acc0[2 * j + k] + acc2[2 * j + k] for k in range(2)]
        odd = [acc1[2 * j + k] + acc3[2 * j + k] for k in range(2)]
        turned = pltpu.roll(jnp.where(top, even[1], odd[0]), TV, axis=1)
        both = jnp.where(top == low, jnp.where(top, even[0], odd[1]), turned)
        grad = (both + pltpu.roll(both, 4, axis=0))[0:4]
        grad_out[:, at] = grad


def update_kernel(
    grad, grad_other, first_next, base, dual, limits,
    new_volume, new_split, new_dual,
):
    last = lax.axis_index("slab") == lax.axis_size("slab") - 1
    row, lane = iotas((8, 128))
    row_mask, col_mask = plane_masks(lane)
    inner = jnp.logical_or(row < 3, jnp.logical_not(last))
    for j in range(dual.shape[2] // 128):
        at = slice(128 * j, 128 * j + 128)
        limit = limits[:, at]
        own = base[:, at] - TAU * (grad[:, at] + grad_other[:, at])
        field = jnp.where(row < 4, jnp.concatenate([own] * 2, axis=0), first_next[:, at])
        new_volume[:, at] = own
        steps = (
            jnp.where(inner, pltpu.roll(field, 7, axis=0) - field, 0.0),
            jnp.where(row_mask, pltpu.roll(field, 120, axis=1) - field, 0.0),
            jnp.where(col_mask, pltpu.roll(field, 127, axis=1) - field, 0.0),
        )
        for k in range(3):
            mixed = steps[k][0:4] + dual[k, :, at]
            clipped = jnp.clip(mixed, -limit, limit)
            new_dual[k, :, at] = clipped
            new_split[k, :, at] = mixed - clipped


def vmem():
    return pl.BlockSpec(memory_space=pltpu.VMEM)


def smem():
    return pl.BlockSpec(memory_space=pltpu.SMEM)


def hbm():
    return pl.BlockSpec(memory_space=pltpu.HBM)


def params():
    return pltpu.CompilerParams(vmem_limit_bytes=VMEM_LIMIT)


def shards(
    volume, split_var, dual_var, sinogram, proj_tiles, ray_index, voxel_index, tile_count, rho
):
    f32, bf16 = jnp.float32, jnp.bfloat16
    slices, width = volume.shape
    slots = ray_index.shape[0]
    owned = sinogram.shape[0]
    group = lax.axis_size(("tile", "rep"))
    reps = lax.axis_size("rep")
    slabs = lax.axis_size("slab")
    rays = owned * group
    voxel_tiles = width // TV
    volume_here, dual_here = volume, dual_var
    volume, split_var, dual_var, sinogram, proj_tiles, ray_index, voxel_index = (
        pltpu.with_memory_space_constraint(x, pltpu.HBM)
        for x in (
            volume, split_var, dual_var, sinogram, proj_tiles, ray_index, voxel_index
        )
    )

    partial, adjoint, edge, first = pl.pallas_call(
        forward_kernel,
        out_shape=(
            jax.ShapeDtypeStruct((rays * slices, TR), bf16),
            jax.ShapeDtypeStruct((slices, width), f32),
            jax.ShapeDtypeStruct((1, width), f32),
            jax.ShapeDtypeStruct((1, width), f32),
        ),
        in_specs=[smem()] + [hbm()] * 7,
        out_specs=(vmem(),) * 4,
        scratch_shapes=[
            pltpu.SMEM((slots,), jnp.int32),
            pltpu.SMEM((slots,), jnp.int32),
            pltpu.VMEM((slices, width), f32),
            pltpu.VMEM((3, slices, width), f32),
            pltpu.VMEM((3, slices, width), f32),
            pltpu.VMEM(sinogram.shape, f32),
            pltpu.VMEM(proj_tiles.shape, bf16),
            pltpu.VMEM((8, width), f32),
            pltpu.VMEM((voxel_tiles, 8, 128), f32),
        ]
        + [pltpu.VMEM((rays + 1, 8, 128), f32)] * 4
        + [pltpu.SemaphoreType.DMA((6,)), pltpu.SemaphoreType.DMA((CHUNKS,))],
        compiler_params=params(),
        name="forward",
    )(
        tile_count, ray_index, voxel_index, volume, split_var, dual_var, sinogram, proj_tiles
    )

    down = [(i, i - 1) for i in range(1, slabs)]
    swap = [(0, 1), (1, 0)]
    if slabs == 2:
        halo = jnp.where(lax.axis_index("slab") == 0, edge, first)
        from_next = from_previous = lax.ppermute(halo, "slab", swap)
    else:
        from_next = lax.ppermute(first, "slab", down)
        from_previous = lax.ppermute(edge, "slab", [(i - 1, i) for i in range(1, slabs)])

    both = ("tile", "rep")
    step = 1
    while True:
        moved = lax.ppermute(partial, both, [(i, i ^ step) for i in range(group)])
        if step == reps:
            moved, from_next, from_previous = lax.optimization_barrier(
                (moved, from_next, from_previous)
            )
        step *= 2
        if step == group:
            break
        partial = (partial.astype(f32) + moved.astype(f32)).astype(bf16)

    grad, base, limits = pl.pallas_call(
        backward_kernel,
        out_shape=(
            jax.ShapeDtypeStruct((slices, width), f32),
            jax.ShapeDtypeStruct((slices, width), f32),
            jax.ShapeDtypeStruct((1, width), f32),
        ),
        in_specs=[smem()] * 2 + [hbm()] * 3 + [vmem()] * 7,
        out_specs=(vmem(), vmem(), vmem()),
        scratch_shapes=[
            pltpu.SMEM((slots,), jnp.int32),
            pltpu.SMEM((slots,), jnp.int32),
            pltpu.VMEM(proj_tiles.shape, bf16),
            pltpu.VMEM((rays, 8, 128), f32),
        ]
        + [pltpu.VMEM((voxel_tiles + 1, 8, 128), f32)] * 4
        + [pltpu.SemaphoreType.DMA((2,)), pltpu.SemaphoreType.DMA((CHUNKS,))],
        compiler_params=params(),
        name="backward",
    )(
        tile_count, rho, ray_index, voxel_index, proj_tiles,
        partial, moved, volume_here, adjoint, edge, from_next, from_previous,
    )
    grad_other = lax.ppermute(grad, "rep", [(i, i ^ 1) for i in range(reps)])
    new_first = base[0:1] - TAU * (grad[0:1] + grad_other[0:1])
    first_next = lax.ppermute(new_first, "slab", swap if slabs == 2 else down)

    return pl.pallas_call(
        update_kernel,
        out_shape=(
            jax.ShapeDtypeStruct((slices, width), f32),
            jax.ShapeDtypeStruct((3, slices, width), f32),
            jax.ShapeDtypeStruct((3, slices, width), f32),
        ),
        in_specs=[vmem()] * 6,
        out_specs=(vmem(), vmem(), vmem()),
        compiler_params=params(),
        name="update",
    )(grad, grad_other, first_next, base, dual_here, limits)


def solution(mesh):
    return jax.shard_map(
        shards,
        mesh=mesh,
        in_specs=(
            P(("parts", "slab"), "tile"),
            P(None, ("parts", "slab"), "tile"),
            P(None, ("parts", "slab"), "tile"),
            P(("tile", "rep"), ("parts", "slab"), None),
            P(("tile", "rep"), None, None),
            P(("tile", "rep")),
            P(("tile", "rep")),
            P(("tile", "rep")),
            P(),
        ),
        out_specs=(
            P(("parts", "slab"), "tile"),
            P(None, ("parts", "slab"), "tile"),
            P(None, ("parts", "slab"), "tile"),
        ),
        check_vma=False,
    )
```

```python
import jax
import jax.numpy as jnp
from jax import lax
from jax.experimental import pallas as pl
from jax.experimental.pallas import tpu as pltpu
from jax.sharding import PartitionSpec as P

TV = 64
TR = 128
TAU = 0.5
GROUP = 4
CHUNKS = 8
VMEM_LIMIT = 16 * 1024 * 1024


def iotas(shape):
    row = lax.broadcasted_iota(jnp.int32, shape, 0)
    lane = lax.broadcasted_iota(jnp.int32, shape, 1)
    return row, lane


def start_tiles(proj_hbm, tiles, sems):
    per = proj_hbm.shape[0] // CHUNKS
    copies = []
    for c in range(CHUNKS):
        part = pl.ds(c * per, per)
        copy = pltpu.make_async_copy(proj_hbm.at[part], tiles.at[part], sems.at[c])
        copy.start()
        copies.append(copy)
    return copies


def plane_masks(lane):
    return (lane % TV) // 8 < 7, lane % 8 < 7


def forward_kernel(
    count, ray_hbm, voxel_hbm, vol_hbm, split_hbm, dual_hbm, sino_hbm, proj_hbm,
    partial_out, adjoint_out, edge_out, first_out,
    ray, voxel, vol, split, dual, sino, tiles, double, table, acc0, acc1, acc2, acc3,
    sems, tile_sems,
):
    slots = proj_hbm.shape[0]
    rays = acc0.shape[0] - 1
    owned = sino.shape[0]
    width = vol.shape[1]
    loads = [
        pltpu.make_async_copy(source, target, sems.at[i])
        for i, (source, target) in enumerate(
            [
                (vol_hbm, vol), (voxel_hbm, voxel), (ray_hbm, ray), (sino_hbm, sino),
                (split_hbm, split), (dual_hbm, dual),
            ]
        )
    ]
    for load in loads:
        load.start()
    copies = start_tiles(proj_hbm, tiles, tile_sems)
    accs = (acc0, acc1, acc2, acc3)
    for acc in accs:
        acc[...] = jnp.zeros_like(acc)
    row, lane = iotas((8, 128))
    low, top = lane < TV, row < 4

    loads[0].wait()
    field = vol[...]
    double[0:4, :] = field
    double[4:8, :] = field
    for j in range(width // 128):
        x = double[:, 128 * j:128 * j + 128].astype(jnp.bfloat16).astype(jnp.float32)
        turned = pltpu.roll(x, TV, axis=1)
        zero = jnp.zeros_like(x)
        first = jnp.where(jnp.logical_and(top, low), x, zero)
        second = jnp.where(jnp.logical_and(top, low), turned, zero)
        other = jnp.logical_not(jnp.logical_or(top, low))
        table[2 * j] = jnp.where(other, turned, first)
        table[2 * j + 1] = jnp.where(other, x, second)

    for load in loads[1:]:
        load.wait()
    mine = (lax.axis_index("tile") * lax.axis_size("rep") + lax.axis_index("rep")) * owned
    for r in range(owned):
        acc0[mine + r, 0:4, :] = -sino[r]
    row_mask, col_mask = plane_masks(lane)
    for j in range(width // 128):
        at = slice(128 * j, 128 * j + 128)
        x = double[:, at]
        gap = [
            jnp.concatenate([dual[k, :, at] - split[k, :, at]] * 2, axis=0) for k in range(3)
        ]
        depth = jnp.where(row < 3, pltpu.roll(x, 7, axis=0) - x + gap[0], 0.0)
        across = jnp.where(row_mask, pltpu.roll(x, 120, axis=1) - x + gap[1], 0.0)
        along = jnp.where(col_mask, pltpu.roll(x, 127, axis=1) - x + gap[2], 0.0)
        adjoint = pltpu.roll(depth, 1, axis=0) - depth
        adjoint += jnp.where((lane % TV) >= 8, pltpu.roll(across, 8, axis=1), 0.0) - across
        adjoint += jnp.where(lane % 8 >= 1, pltpu.roll(along, 1, axis=1), 0.0) - along
        adjoint_out[:, at] = adjoint[0:4]
        edge_out[:, at] = (x - gap[0])[3:4]
        first_out[:, at] = x[0:1]

    used = count[0]
    per = slots // CHUNKS
    for g in range(slots // GROUP):
        if GROUP * g % per == 0:
            copies[GROUP * g // per].wait()
        n = GROUP * g
        pairs = [
            jnp.where(top, table[voxel[n + 2 * i]], table[voxel[n + 2 * i + 1]]) for i in range(2)
        ]
        zero = jnp.zeros_like(pairs[0])
        left = jnp.concatenate([pairs[0], zero], axis=0).astype(jnp.bfloat16)
        right = jnp.concatenate([zero, pairs[1]], axis=0).astype(jnp.bfloat16)
        sums = jnp.dot(
            jnp.concatenate([left, right], axis=1),
            tiles[n:n + GROUP].reshape(GROUP * TV, TR),
            preferred_element_type=jnp.float32,
        )
        for i in range(GROUP):
            at = jnp.where(n + i < used, ray[n + i], rays)
            accs[i][at] += sums[8 * (i // 2):8 * (i // 2) + 8]
    for q in range(rays // 4):
        halves = []
        for r in (4 * q, 4 * q + 2):
            even = [acc0[r + k] + acc2[r + k] for k in range(2)]
            odd = [acc1[r + k] + acc3[r + k] for k in range(2)]
            halves.append(
                jnp.where(top, even[0], odd[1])
                + pltpu.roll(jnp.where(top, even[1], odd[0]), 4, axis=0)
            )
        partial_out[16 * q:16 * q + 16, :] = jnp.concatenate(halves, axis=0).astype(jnp.bfloat16)


def backward_kernel(
    count, rho, ray_hbm, voxel_hbm, proj_hbm,
    parts, vol, adjoint,
    grad_out, base_out, scale_out,
    ray, voxel, tiles, table, acc0, acc1, acc2, acc3, sems, tile_sems,
):
    slots = proj_hbm.shape[0]
    rays = table.shape[0]
    voxel_tiles = acc0.shape[0] - 1
    loads = [
        pltpu.make_async_copy(source, target, sems.at[i])
        for i, (source, target) in enumerate(
            [(voxel_hbm, voxel), (ray_hbm, ray)]
        )
    ]
    for load in loads:
        load.start()
    copies = start_tiles(proj_hbm, tiles, tile_sems)
    accs = (acc0, acc1, acc2, acc3)
    for acc in accs:
        acc[...] = jnp.zeros_like(acc)
    row, lane = iotas((8, 128))
    low, top = lane < TV, row < 4
    for q in range(rays // 4):
        at = slice(16 * q, 16 * q + 16)
        total = parts[0, at, :].astype(jnp.float32)
        for p in range(1, parts.shape[0]):
            total += parts[p, at, :].astype(jnp.float32)
        for k in range(2):
            x = total[8 * k:8 * k + 8]
            turned = pltpu.roll(x, 4, axis=0)
            table[4 * q + 2 * k] = jnp.where(top, x, turned)
            table[4 * q + 2 * k + 1] = jnp.where(top, turned, x)

    for load in loads:
        load.wait()
    factor = TAU * rho[0]
    limit = 1.0 / rho[0]
    for j in range(voxel_tiles // 2):
        at = slice(128 * j, 128 * j + 128)
        base_out[:, at] = vol[:, at] - factor * adjoint[:, at]
        scale_out[0:1, at] = jnp.full((1, 128), limit, jnp.float32)
        scale_out[1:2, at] = jnp.full((1, 128), factor, jnp.float32)

    used = count[0]
    per = slots // CHUNKS
    for g in range(slots // GROUP):
        if GROUP * g % per == 0:
            copies[GROUP * g // per].wait()
        n = GROUP * g
        rows = jnp.concatenate(
            [
                jnp.where(top, table[ray[n + 2 * i]], table[ray[n + 2 * i + 1]])
                for i in range(GROUP // 2)
            ],
            axis=0,
        )
        back = lax.dot_general(
            rows.astype(jnp.bfloat16),
            tiles[n:n + GROUP].reshape(GROUP * TV, TR),
            (((1,), (1,)), ((), ())),
            preferred_element_type=jnp.float32,
        )
        for i in range(GROUP):
            at = jnp.where(n + i < used, voxel[n + i], voxel_tiles)
            k = i // 2
            accs[i][at] += back[8 * k:8 * k + 8, 128 * k:128 * k + 128]
    for j in range(voxel_tiles // 2):
        at = slice(128 * j, 128 * j + 128)
        even = [acc0[2 * j + k] + acc2[2 * j + k] for k in range(2)]
        odd = [acc1[2 * j + k] + acc3[2 * j + k] for k in range(2)]
        turned = pltpu.roll(jnp.where(top, even[1], odd[0]), TV, axis=1)
        both = jnp.where(top == low, jnp.where(top, even[0], odd[1]), turned)
        grad = (both + pltpu.roll(both, 4, axis=0))[0:4]
        grad_out[:, at] = grad


def update_kernel(
    grad, grad_other, from_next, from_previous, base, edge, first, dual, scales,
    new_volume, new_split, new_dual,
):
    slab, slabs = lax.axis_index("slab"), lax.axis_size("slab")
    row, lane = iotas((8, 128))
    short = lax.broadcasted_iota(jnp.int32, (4, 128), 0)
    row_mask, col_mask = plane_masks(lane)
    inner = jnp.logical_or(row < 3, slab < slabs - 1)
    for j in range(dual.shape[2] // 128):
        at = slice(128 * j, 128 * j + 128)
        limit, factor = scales[0:1, at], scales[1:2, at]
        above = jnp.where(slab == slabs - 1, 0.0, factor * (from_next[1:2, at] - edge[:, at]))
        below = jnp.where(slab == 0, 0.0, factor * (first[:, at] - from_previous[0:1, at]))
        own = base[:, at] - TAU * (grad[:, at] + grad_other[:, at])
        own += jnp.where(short == 0, -below, jnp.where(short == 3, above, 0.0))
        ahead = from_next[0:1, at] - above
        field = jnp.where(row < 4, jnp.concatenate([own] * 2, axis=0), ahead)
        new_volume[:, at] = own
        steps = (
            jnp.where(inner, pltpu.roll(field, 7, axis=0) - field, 0.0),
            jnp.where(row_mask, pltpu.roll(field, 120, axis=1) - field, 0.0),
            jnp.where(col_mask, pltpu.roll(field, 127, axis=1) - field, 0.0),
        )
        for k in range(3):
            mixed = steps[k][0:4] + dual[k, :, at]
            clipped = jnp.clip(mixed, -limit, limit)
            new_dual[k, :, at] = clipped
            new_split[k, :, at] = mixed - clipped


def vmem():
    return pl.BlockSpec(memory_space=pltpu.VMEM)


def smem():
    return pl.BlockSpec(memory_space=pltpu.SMEM)


def hbm():
    return pl.BlockSpec(memory_space=pltpu.HBM)


def params():
    return pltpu.CompilerParams(vmem_limit_bytes=VMEM_LIMIT)


def shards(
    volume, split_var, dual_var, sinogram, proj_tiles, ray_index, voxel_index, tile_count, rho
):
    f32, bf16 = jnp.float32, jnp.bfloat16
    slices, width = volume.shape
    slots = ray_index.shape[0]
    owned = sinogram.shape[0]
    group = lax.axis_size(("tile", "rep"))
    reps = lax.axis_size("rep")
    slabs = lax.axis_size("slab")
    rays = owned * group
    voxel_tiles = width // TV
    volume_here, dual_here = volume, dual_var
    volume, split_var, dual_var, sinogram, proj_tiles, ray_index, voxel_index = (
        pltpu.with_memory_space_constraint(x, pltpu.HBM)
        for x in (
            volume, split_var, dual_var, sinogram, proj_tiles, ray_index, voxel_index
        )
    )

    partial, adjoint, edge, first = pl.pallas_call(
        forward_kernel,
        out_shape=(
            jax.ShapeDtypeStruct((rays * slices, TR), bf16),
            jax.ShapeDtypeStruct((slices, width), f32),
            jax.ShapeDtypeStruct((1, width), f32),
            jax.ShapeDtypeStruct((1, width), f32),
        ),
        in_specs=[smem()] + [hbm()] * 7,
        out_specs=(vmem(),) * 4,
        scratch_shapes=[
            pltpu.SMEM((slots,), jnp.int32),
            pltpu.SMEM((slots,), jnp.int32),
            pltpu.VMEM((slices, width), f32),
            pltpu.VMEM((3, slices, width), f32),
            pltpu.VMEM((3, slices, width), f32),
            pltpu.VMEM(sinogram.shape, f32),
            pltpu.VMEM(proj_tiles.shape, bf16),
            pltpu.VMEM((8, width), f32),
            pltpu.VMEM((voxel_tiles, 8, 128), f32),
        ]
        + [pltpu.VMEM((rays + 1, 8, 128), f32)] * 4
        + [pltpu.SemaphoreType.DMA((6,)), pltpu.SemaphoreType.DMA((CHUNKS,))],
        compiler_params=params(),
        name="forward",
    )(
        tile_count, ray_index, voxel_index, volume, split_var, dual_var, sinogram, proj_tiles
    )

    swap = [(i, i ^ 1) for i in range(reps)]
    moved = lax.ppermute(partial, "rep", swap)
    chip = (partial.astype(f32) + moved.astype(f32)).astype(bf16)
    parts = lax.all_to_all(
        jnp.broadcast_to(chip, (group // reps, *chip.shape)), "tile", 0, 0, tiled=True
    )

    grad, base, scales = pl.pallas_call(
        backward_kernel,
        out_shape=(
            jax.ShapeDtypeStruct((slices, width), f32),
            jax.ShapeDtypeStruct((slices, width), f32),
            jax.ShapeDtypeStruct((2, width), f32),
        ),
        in_specs=[smem()] * 2 + [hbm()] * 3 + [vmem()] * 3,
        out_specs=(vmem(), vmem(), vmem()),
        scratch_shapes=[
            pltpu.SMEM((slots,), jnp.int32),
            pltpu.SMEM((slots,), jnp.int32),
            pltpu.VMEM(proj_tiles.shape, bf16),
            pltpu.VMEM((rays, 8, 128), f32),
        ]
        + [pltpu.VMEM((voxel_tiles + 1, 8, 128), f32)] * 4
        + [pltpu.SemaphoreType.DMA((2,)), pltpu.SemaphoreType.DMA((CHUNKS,))],
        compiler_params=params(),
        name="backward",
    )(
        tile_count, rho, ray_index, voxel_index, proj_tiles,
        parts, volume_here, adjoint,
    )
    grad_other = lax.ppermute(grad, "rep", swap)
    ahead = jnp.concatenate([base[0:1] - TAU * (grad[0:1] + grad_other[0:1]), first], axis=0)
    behind = jnp.concatenate([edge, edge], axis=0)
    if slabs == 2:
        halo = jnp.where(lax.axis_index("slab") == 0, behind, ahead)
        from_next = from_previous = lax.ppermute(halo, "slab", [(0, 1), (1, 0)])
    else:
        from_next = lax.ppermute(ahead, "slab", [(i, i - 1) for i in range(1, slabs)])
        from_previous = lax.ppermute(behind, "slab", [(i - 1, i) for i in range(1, slabs)])

    return pl.pallas_call(
        update_kernel,
        out_shape=(
            jax.ShapeDtypeStruct((slices, width), f32),
            jax.ShapeDtypeStruct((3, slices, width), f32),
            jax.ShapeDtypeStruct((3, slices, width), f32),
        ),
        in_specs=[vmem()] * 9,
        out_specs=(vmem(), vmem(), vmem()),
        compiler_params=params(),
        name="update",
    )(grad, grad_other, from_next, from_previous, base, edge, first, dual_here, scales)


def solution(mesh):
    return jax.shard_map(
        shards,
        mesh=mesh,
        in_specs=(
            P(("parts", "slab"), "tile"),
            P(None, ("parts", "slab"), "tile"),
            P(None, ("parts", "slab"), "tile"),
            P(("tile", "rep"), ("parts", "slab"), None),
            P(("tile", "rep"), None, None),
            P(("tile", "rep")),
            P(("tile", "rep")),
            P(("tile", "rep")),
            P(),
        ),
        out_specs=(
            P(("parts", "slab"), "tile"),
            P(None, ("parts", "slab"), "tile"),
            P(None, ("parts", "slab"), "tile"),
        ),
        check_vma=False,
    )
```

```python
import jax
import jax.numpy as jnp
from jax import lax
from jax.experimental import pallas as pl
from jax.experimental.pallas import tpu as pltpu
from jax.sharding import PartitionSpec as P

TV = 64
TR = 128
TAU = 0.5
GROUP = 4
CHUNKS = 8
VMEM_LIMIT = 16 * 1024 * 1024


def iotas(shape):
    row = lax.broadcasted_iota(jnp.int32, shape, 0)
    lane = lax.broadcasted_iota(jnp.int32, shape, 1)
    return row, lane


def start_tiles(proj_hbm, tiles, sems):
    per = proj_hbm.shape[0] // CHUNKS
    copies = []
    for c in range(CHUNKS):
        part = pl.ds(c * per, per)
        copy = pltpu.make_async_copy(proj_hbm.at[part], tiles.at[part], sems.at[c])
        copy.start()
        copies.append(copy)
    return copies


def plane_masks(lane):
    return (lane % TV) // 8 < 7, lane % 8 < 7


def forward_kernel(
    count, ray_hbm, voxel_hbm, vol_hbm, split_hbm, dual_hbm, sino_hbm, proj_hbm,
    partial_out, adjoint_out, edge_out, first_out,
    ray, voxel, vol, split, dual, sino, tiles, double, table, acc0, acc1, acc2, acc3,
    sems, tile_sems,
):
    slots = proj_hbm.shape[0]
    rays = acc0.shape[0] - 1
    owned = sino.shape[0]
    width = vol.shape[1]
    loads = [
        pltpu.make_async_copy(source, target, sems.at[i])
        for i, (source, target) in enumerate(
            [
                (vol_hbm, vol), (voxel_hbm, voxel), (ray_hbm, ray), (sino_hbm, sino),
                (split_hbm, split), (dual_hbm, dual),
            ]
        )
    ]
    for load in loads:
        load.start()
    copies = start_tiles(proj_hbm, tiles, tile_sems)
    accs = (acc0, acc1, acc2, acc3)
    for acc in accs:
        acc[...] = jnp.zeros_like(acc)
    row, lane = iotas((8, 128))
    low, top = lane < TV, row < 4

    loads[0].wait()
    field = vol[...]
    double[0:4, :] = field
    double[4:8, :] = field
    for j in range(width // 128):
        x = double[:, 128 * j:128 * j + 128].astype(jnp.bfloat16).astype(jnp.float32)
        turned = pltpu.roll(x, TV, axis=1)
        zero = jnp.zeros_like(x)
        first = jnp.where(jnp.logical_and(top, low), x, zero)
        second = jnp.where(jnp.logical_and(top, low), turned, zero)
        other = jnp.logical_not(jnp.logical_or(top, low))
        table[2 * j] = jnp.where(other, turned, first)
        table[2 * j + 1] = jnp.where(other, x, second)

    for load in loads[1:]:
        load.wait()
    mine = (lax.axis_index("tile") * lax.axis_size("rep") + lax.axis_index("rep")) * owned
    for r in range(owned):
        acc0[mine + r, 0:4, :] = -sino[r]
    row_mask, col_mask = plane_masks(lane)
    for j in range(width // 128):
        at = slice(128 * j, 128 * j + 128)
        x = double[:, at]
        gap = [
            jnp.concatenate([dual[k, :, at] - split[k, :, at]] * 2, axis=0) for k in range(3)
        ]
        depth = jnp.where(row < 3, pltpu.roll(x, 7, axis=0) - x + gap[0], 0.0)
        across = jnp.where(row_mask, pltpu.roll(x, 120, axis=1) - x + gap[1], 0.0)
        along = jnp.where(col_mask, pltpu.roll(x, 127, axis=1) - x + gap[2], 0.0)
        adjoint = pltpu.roll(depth, 1, axis=0) - depth
        adjoint += jnp.where((lane % TV) >= 8, pltpu.roll(across, 8, axis=1), 0.0) - across
        adjoint += jnp.where(lane % 8 >= 1, pltpu.roll(along, 1, axis=1), 0.0) - along
        adjoint_out[:, at] = adjoint[0:4]
        edge_out[:, at] = (x - gap[0])[3:4]
        first_out[:, at] = x[0:1]

    used = count[0]
    per = slots // CHUNKS
    for g in range(slots // GROUP):
        if GROUP * g % per == 0:
            copies[GROUP * g // per].wait()
        n = GROUP * g
        pairs = [
            jnp.where(top, table[voxel[n + 2 * i]], table[voxel[n + 2 * i + 1]]) for i in range(2)
        ]
        zero = jnp.zeros_like(pairs[0])
        left = jnp.concatenate([pairs[0], zero], axis=0).astype(jnp.bfloat16)
        right = jnp.concatenate([zero, pairs[1]], axis=0).astype(jnp.bfloat16)
        sums = jnp.dot(
            jnp.concatenate([left, right], axis=1),
            tiles[n:n + GROUP].reshape(GROUP * TV, TR),
            preferred_element_type=jnp.float32,
        )
        for i in range(GROUP):
            at = jnp.where(n + i < used, ray[n + i], rays)
            accs[i][at] += sums[8 * (i // 2):8 * (i // 2) + 8]
    for q in range(rays // 4):
        halves = []
        for r in (4 * q, 4 * q + 2):
            even = [acc0[r + k] + acc2[r + k] for k in range(2)]
            odd = [acc1[r + k] + acc3[r + k] for k in range(2)]
            halves.append(
                jnp.where(top, even[0], odd[1])
                + pltpu.roll(jnp.where(top, even[1], odd[0]), 4, axis=0)
            )
        partial_out[16 * q:16 * q + 16, :] = jnp.concatenate(halves, axis=0).astype(jnp.bfloat16)


def backward_kernel(
    count, rho, ray_hbm, voxel_hbm, proj_hbm,
    part, moved, vol, adjoint,
    grad_out, base_out, scale_out,
    ray, voxel, tiles, table, acc0, acc1, acc2, acc3, sems, tile_sems,
):
    slots = proj_hbm.shape[0]
    rays = table.shape[0]
    voxel_tiles = acc0.shape[0] - 1
    loads = [
        pltpu.make_async_copy(source, target, sems.at[i])
        for i, (source, target) in enumerate(
            [(voxel_hbm, voxel), (ray_hbm, ray)]
        )
    ]
    for load in loads:
        load.start()
    copies = start_tiles(proj_hbm, tiles, tile_sems)
    accs = (acc0, acc1, acc2, acc3)
    for acc in accs:
        acc[...] = jnp.zeros_like(acc)
    row, lane = iotas((8, 128))
    low, top = lane < TV, row < 4
    for q in range(rays // 4):
        at = slice(16 * q, 16 * q + 16)
        total = part[at, :].astype(jnp.float32) + moved[at, :].astype(jnp.float32)
        for k in range(2):
            x = total[8 * k:8 * k + 8]
            turned = pltpu.roll(x, 4, axis=0)
            table[4 * q + 2 * k] = jnp.where(top, x, turned)
            table[4 * q + 2 * k + 1] = jnp.where(top, turned, x)

    for load in loads:
        load.wait()
    factor = TAU * rho[0]
    limit = 1.0 / rho[0]
    for j in range(voxel_tiles // 2):
        at = slice(128 * j, 128 * j + 128)
        base_out[:, at] = vol[:, at] - factor * adjoint[:, at]
        scale_out[0:1, at] = jnp.full((1, 128), limit, jnp.float32)
        scale_out[1:2, at] = jnp.full((1, 128), factor, jnp.float32)

    used = count[0]
    per = slots // CHUNKS
    for g in range(slots // GROUP):
        if GROUP * g % per == 0:
            copies[GROUP * g // per].wait()
        n = GROUP * g
        rows = jnp.concatenate(
            [
                jnp.where(top, table[ray[n + 2 * i]], table[ray[n + 2 * i + 1]])
                for i in range(GROUP // 2)
            ],
            axis=0,
        )
        back = lax.dot_general(
            rows.astype(jnp.bfloat16),
            tiles[n:n + GROUP].reshape(GROUP * TV, TR),
            (((1,), (1,)), ((), ())),
            preferred_element_type=jnp.float32,
        )
        for i in range(GROUP):
            at = jnp.where(n + i < used, voxel[n + i], voxel_tiles)
            k = i // 2
            accs[i][at] += back[8 * k:8 * k + 8, 128 * k:128 * k + 128]
    for j in range(voxel_tiles // 2):
        at = slice(128 * j, 128 * j + 128)
        even = [acc0[2 * j + k] + acc2[2 * j + k] for k in range(2)]
        odd = [acc1[2 * j + k] + acc3[2 * j + k] for k in range(2)]
        turned = pltpu.roll(jnp.where(top, even[1], odd[0]), TV, axis=1)
        both = jnp.where(top == low, jnp.where(top, even[0], odd[1]), turned)
        grad = (both + pltpu.roll(both, 4, axis=0))[0:4]
        grad_out[:, at] = grad


def update_kernel(
    grad, grad_other, from_next, from_previous, base, edge, first, dual, scales,
    new_volume, new_split, new_dual,
):
    slab, slabs = lax.axis_index("slab"), lax.axis_size("slab")
    row, lane = iotas((8, 128))
    short = lax.broadcasted_iota(jnp.int32, (4, 128), 0)
    row_mask, col_mask = plane_masks(lane)
    inner = jnp.logical_or(row < 3, slab < slabs - 1)
    for j in range(dual.shape[2] // 128):
        at = slice(128 * j, 128 * j + 128)
        limit, factor = scales[0:1, at], scales[1:2, at]
        above = jnp.where(slab == slabs - 1, 0.0, factor * (from_next[1:2, at] - edge[:, at]))
        below = jnp.where(slab == 0, 0.0, factor * (first[:, at] - from_previous[0:1, at]))
        own = base[:, at] - TAU * (grad[:, at] + grad_other[:, at])
        own += jnp.where(short == 0, -below, jnp.where(short == 3, above, 0.0))
        ahead = from_next[0:1, at] - above
        field = jnp.where(row < 4, jnp.concatenate([own] * 2, axis=0), ahead)
        new_volume[:, at] = own
        steps = (
            jnp.where(inner, pltpu.roll(field, 7, axis=0) - field, 0.0),
            jnp.where(row_mask, pltpu.roll(field, 120, axis=1) - field, 0.0),
            jnp.where(col_mask, pltpu.roll(field, 127, axis=1) - field, 0.0),
        )
        for k in range(3):
            mixed = steps[k][0:4] + dual[k, :, at]
            clipped = jnp.clip(mixed, -limit, limit)
            new_dual[k, :, at] = clipped
            new_split[k, :, at] = mixed - clipped


def vmem():
    return pl.BlockSpec(memory_space=pltpu.VMEM)


def smem():
    return pl.BlockSpec(memory_space=pltpu.SMEM)


def hbm():
    return pl.BlockSpec(memory_space=pltpu.HBM)


def params():
    return pltpu.CompilerParams(vmem_limit_bytes=VMEM_LIMIT)


def shards(
    volume, split_var, dual_var, sinogram, proj_tiles, ray_index, voxel_index, tile_count, rho
):
    f32, bf16 = jnp.float32, jnp.bfloat16
    slices, width = volume.shape
    slots = ray_index.shape[0]
    owned = sinogram.shape[0]
    group = lax.axis_size(("tile", "rep"))
    reps = lax.axis_size("rep")
    slabs = lax.axis_size("slab")
    rays = owned * group
    voxel_tiles = width // TV
    volume_here, dual_here = volume, dual_var
    volume, split_var, dual_var, sinogram, proj_tiles, ray_index, voxel_index = (
        pltpu.with_memory_space_constraint(x, pltpu.HBM)
        for x in (
            volume, split_var, dual_var, sinogram, proj_tiles, ray_index, voxel_index
        )
    )

    partial, adjoint, edge, first = pl.pallas_call(
        forward_kernel,
        out_shape=(
            jax.ShapeDtypeStruct((rays * slices, TR), bf16),
            jax.ShapeDtypeStruct((slices, width), f32),
            jax.ShapeDtypeStruct((1, width), f32),
            jax.ShapeDtypeStruct((1, width), f32),
        ),
        in_specs=[smem()] + [hbm()] * 7,
        out_specs=(vmem(),) * 4,
        scratch_shapes=[
            pltpu.SMEM((slots,), jnp.int32),
            pltpu.SMEM((slots,), jnp.int32),
            pltpu.VMEM((slices, width), f32),
            pltpu.VMEM((3, slices, width), f32),
            pltpu.VMEM((3, slices, width), f32),
            pltpu.VMEM(sinogram.shape, f32),
            pltpu.VMEM(proj_tiles.shape, bf16),
            pltpu.VMEM((8, width), f32),
            pltpu.VMEM((voxel_tiles, 8, 128), f32),
        ]
        + [pltpu.VMEM((rays + 1, 8, 128), f32)] * 4
        + [pltpu.SemaphoreType.DMA((6,)), pltpu.SemaphoreType.DMA((CHUNKS,))],
        compiler_params=params(),
        name="forward",
    )(
        tile_count, ray_index, voxel_index, volume, split_var, dual_var, sinogram, proj_tiles
    )

    swap = [(i, i ^ 1) for i in range(reps)]
    step = 1
    while True:
        moved = lax.ppermute(
            partial, ("tile", "rep"), [(i, i ^ step) for i in range(group)]
        )
        step *= 2
        if step == group:
            break
        partial = (partial.astype(f32) + moved.astype(f32)).astype(bf16)

    grad, base, scales = pl.pallas_call(
        backward_kernel,
        out_shape=(
            jax.ShapeDtypeStruct((slices, width), f32),
            jax.ShapeDtypeStruct((slices, width), f32),
            jax.ShapeDtypeStruct((2, width), f32),
        ),
        in_specs=[smem()] * 2 + [hbm()] * 3 + [vmem()] * 4,
        out_specs=(vmem(), vmem(), vmem()),
        scratch_shapes=[
            pltpu.SMEM((slots,), jnp.int32),
            pltpu.SMEM((slots,), jnp.int32),
            pltpu.VMEM(proj_tiles.shape, bf16),
            pltpu.VMEM((rays, 8, 128), f32),
        ]
        + [pltpu.VMEM((voxel_tiles + 1, 8, 128), f32)] * 4
        + [pltpu.SemaphoreType.DMA((2,)), pltpu.SemaphoreType.DMA((CHUNKS,))],
        compiler_params=params(),
        name="backward",
    )(
        tile_count, rho, ray_index, voxel_index, proj_tiles,
        partial, moved, volume_here, adjoint,
    )
    grad_other = lax.ppermute(grad, "rep", swap)
    ahead = jnp.concatenate([base[0:1] - TAU * (grad[0:1] + grad_other[0:1]), first], axis=0)
    behind = jnp.concatenate([edge, edge], axis=0)
    if slabs == 2:
        halo = jnp.where(lax.axis_index("slab") == 0, behind, ahead)
        from_next = from_previous = lax.ppermute(halo, "slab", [(0, 1), (1, 0)])
    else:
        from_next = lax.ppermute(ahead, "slab", [(i, i - 1) for i in range(1, slabs)])
        from_previous = lax.ppermute(behind, "slab", [(i - 1, i) for i in range(1, slabs)])

    return pl.pallas_call(
        update_kernel,
        out_shape=(
            jax.ShapeDtypeStruct((slices, width), f32),
            jax.ShapeDtypeStruct((3, slices, width), f32),
            jax.ShapeDtypeStruct((3, slices, width), f32),
        ),
        in_specs=[vmem()] * 9,
        out_specs=(vmem(), vmem(), vmem()),
        compiler_params=params(),
        name="update",
    )(grad, grad_other, from_next, from_previous, base, edge, first, dual_here, scales)


def solution(mesh):
    return jax.shard_map(
        shards,
        mesh=mesh,
        in_specs=(
            P(("parts", "slab"), "tile"),
            P(None, ("parts", "slab"), "tile"),
            P(None, ("parts", "slab"), "tile"),
            P(("tile", "rep"), ("parts", "slab"), None),
            P(("tile", "rep"), None, None),
            P(("tile", "rep")),
            P(("tile", "rep")),
            P(("tile", "rep")),
            P(),
        ),
        out_specs=(
            P(("parts", "slab"), "tile"),
            P(None, ("parts", "slab"), "tile"),
            P(None, ("parts", "slab"), "tile"),
        ),
        check_vma=False,
    )
```

```python
import jax
import jax.numpy as jnp
from jax import lax
from jax.experimental import pallas as pl
from jax.experimental.pallas import tpu as pltpu
from jax.sharding import PartitionSpec as P

TV = 64
TR = 128
TAU = 0.5
GROUP = 4
CHUNKS = 8
VMEM_LIMIT = 16 * 1024 * 1024


def iotas(shape):
    row = lax.broadcasted_iota(jnp.int32, shape, 0)
    lane = lax.broadcasted_iota(jnp.int32, shape, 1)
    return row, lane


def start_tiles(proj_hbm, tiles, sems):
    per = proj_hbm.shape[0] // CHUNKS
    copies = []
    for c in range(CHUNKS):
        part = pl.ds(c * per, per)
        copy = pltpu.make_async_copy(proj_hbm.at[part], tiles.at[part], sems.at[c])
        copy.start()
        copies.append(copy)
    return copies


def plane_masks(lane):
    return (lane % TV) // 8 < 7, lane % 8 < 7


def forward_kernel(
    count, ray_hbm, voxel_hbm, vol_hbm, split_hbm, dual_hbm, sino_hbm, proj_hbm,
    partial_out, adjoint_out, edge_out, first_out,
    ray, voxel, vol, split, dual, sino, tiles, double, table, acc0, acc1, acc2, acc3,
    sems, tile_sems,
):
    slots = proj_hbm.shape[0]
    rays = acc0.shape[0] - 1
    owned = sino.shape[0]
    width = vol.shape[1]
    loads = [
        pltpu.make_async_copy(source, target, sems.at[i])
        for i, (source, target) in enumerate(
            [
                (vol_hbm, vol), (voxel_hbm, voxel), (ray_hbm, ray), (sino_hbm, sino),
                (split_hbm, split), (dual_hbm, dual),
            ]
        )
    ]
    for load in loads:
        load.start()
    copies = start_tiles(proj_hbm, tiles, tile_sems)
    accs = (acc0, acc1, acc2, acc3)
    for acc in accs:
        acc[...] = jnp.zeros_like(acc)
    row, lane = iotas((8, 128))
    low, top = lane < TV, row < 4

    loads[0].wait()
    field = vol[...]
    double[0:4, :] = field
    double[4:8, :] = field
    for j in range(width // 128):
        x = double[:, 128 * j:128 * j + 128].astype(jnp.bfloat16).astype(jnp.float32)
        turned = pltpu.roll(x, TV, axis=1)
        zero = jnp.zeros_like(x)
        first = jnp.where(jnp.logical_and(top, low), x, zero)
        second = jnp.where(jnp.logical_and(top, low), turned, zero)
        other = jnp.logical_not(jnp.logical_or(top, low))
        table[2 * j] = jnp.where(other, turned, first)
        table[2 * j + 1] = jnp.where(other, x, second)

    for load in loads[1:]:
        load.wait()
    mine = (lax.axis_index("tile") * lax.axis_size("rep") + lax.axis_index("rep")) * owned
    for r in range(owned):
        acc0[mine + r, 0:4, :] = -sino[r]
    row_mask, col_mask = plane_masks(lane)
    for j in range(width // 128):
        at = slice(128 * j, 128 * j + 128)
        x = double[:, at]
        gap = [
            jnp.concatenate([dual[k, :, at] - split[k, :, at]] * 2, axis=0) for k in range(3)
        ]
        depth = jnp.where(row < 3, pltpu.roll(x, 7, axis=0) - x + gap[0], 0.0)
        across = jnp.where(row_mask, pltpu.roll(x, 120, axis=1) - x + gap[1], 0.0)
        along = jnp.where(col_mask, pltpu.roll(x, 127, axis=1) - x + gap[2], 0.0)
        adjoint = pltpu.roll(depth, 1, axis=0) - depth
        adjoint += jnp.where((lane % TV) >= 8, pltpu.roll(across, 8, axis=1), 0.0) - across
        adjoint += jnp.where(lane % 8 >= 1, pltpu.roll(along, 1, axis=1), 0.0) - along
        adjoint_out[:, at] = adjoint[0:4]
        edge_out[:, at] = (x - gap[0])[3:4]
        first_out[:, at] = x[0:1]

    used = count[0]
    per = slots // CHUNKS
    for g in range(slots // GROUP):
        if GROUP * g % per == 0:
            copies[GROUP * g // per].wait()
        n = GROUP * g
        pairs = [
            jnp.where(top, table[voxel[n + 2 * i]], table[voxel[n + 2 * i + 1]]) for i in range(2)
        ]
        zero = jnp.zeros_like(pairs[0])
        left = jnp.concatenate([pairs[0], zero], axis=0).astype(jnp.bfloat16)
        right = jnp.concatenate([zero, pairs[1]], axis=0).astype(jnp.bfloat16)
        sums = jnp.dot(
            jnp.concatenate([left, right], axis=1),
            tiles[n:n + GROUP].reshape(GROUP * TV, TR),
            preferred_element_type=jnp.float32,
        )
        for i in range(GROUP):
            at = jnp.where(n + i < used, ray[n + i], rays)
            accs[i][at] += sums[8 * (i // 2):8 * (i // 2) + 8]
    for q in range(rays // 4):
        halves = []
        for r in (4 * q, 4 * q + 2):
            even = [acc0[r + k] + acc2[r + k] for k in range(2)]
            odd = [acc1[r + k] + acc3[r + k] for k in range(2)]
            halves.append(
                jnp.where(top, even[0], odd[1])
                + pltpu.roll(jnp.where(top, even[1], odd[0]), 4, axis=0)
            )
        partial_out[16 * q:16 * q + 16, :] = jnp.concatenate(halves, axis=0).astype(jnp.bfloat16)


def backward_kernel(
    count, rho, ray_hbm, voxel_hbm, proj_hbm,
    held, shared, vol, adjoint,
    grad_out, base_out, scale_out,
    ray, voxel, tiles, table, acc0, acc1, acc2, acc3, sems, tile_sems,
):
    slots = proj_hbm.shape[0]
    rays = table.shape[0]
    voxel_tiles = acc0.shape[0] - 1
    loads = [
        pltpu.make_async_copy(source, target, sems.at[i])
        for i, (source, target) in enumerate(
            [(voxel_hbm, voxel), (ray_hbm, ray)]
        )
    ]
    for load in loads:
        load.start()
    copies = start_tiles(proj_hbm, tiles, tile_sems)
    accs = (acc0, acc1, acc2, acc3)
    for acc in accs:
        acc[...] = jnp.zeros_like(acc)
    row, lane = iotas((8, 128))
    low, top = lane < TV, row < 4
    holder = lax.axis_index("rep") == lax.axis_size("rep") - 1
    for q in range(rays // 4):
        at = slice(16 * q, 16 * q + 16)
        total = jnp.where(
            holder, held[at, :].astype(jnp.float32), shared[at, :].astype(jnp.float32)
        )
        for k in range(2):
            x = total[8 * k:8 * k + 8]
            turned = pltpu.roll(x, 4, axis=0)
            table[4 * q + 2 * k] = jnp.where(top, x, turned)
            table[4 * q + 2 * k + 1] = jnp.where(top, turned, x)

    for load in loads:
        load.wait()
    factor = TAU * rho[0]
    limit = 1.0 / rho[0]
    for j in range(voxel_tiles // 2):
        at = slice(128 * j, 128 * j + 128)
        base_out[:, at] = vol[:, at] - factor * adjoint[:, at]
        scale_out[0:1, at] = jnp.full((1, 128), limit, jnp.float32)
        scale_out[1:2, at] = jnp.full((1, 128), factor, jnp.float32)

    used = count[0]
    per = slots // CHUNKS
    for g in range(slots // GROUP):
        if GROUP * g % per == 0:
            copies[GROUP * g // per].wait()
        n = GROUP * g
        rows = jnp.concatenate(
            [
                jnp.where(top, table[ray[n + 2 * i]], table[ray[n + 2 * i + 1]])
                for i in range(GROUP // 2)
            ],
            axis=0,
        )
        back = lax.dot_general(
            rows.astype(jnp.bfloat16),
            tiles[n:n + GROUP].reshape(GROUP * TV, TR),
            (((1,), (1,)), ((), ())),
            preferred_element_type=jnp.float32,
        )
        for i in range(GROUP):
            at = jnp.where(n + i < used, voxel[n + i], voxel_tiles)
            k = i // 2
            accs[i][at] += back[8 * k:8 * k + 8, 128 * k:128 * k + 128]
    for j in range(voxel_tiles // 2):
        at = slice(128 * j, 128 * j + 128)
        even = [acc0[2 * j + k] + acc2[2 * j + k] for k in range(2)]
        odd = [acc1[2 * j + k] + acc3[2 * j + k] for k in range(2)]
        turned = pltpu.roll(jnp.where(top, even[1], odd[0]), TV, axis=1)
        both = jnp.where(top == low, jnp.where(top, even[0], odd[1]), turned)
        grad = (both + pltpu.roll(both, 4, axis=0))[0:4]
        grad_out[:, at] = grad


def update_kernel(
    grad, grad_other, from_next, from_previous, base, edge, first, dual, scales,
    new_volume, new_split, new_dual,
):
    slab, slabs = lax.axis_index("slab"), lax.axis_size("slab")
    row, lane = iotas((8, 128))
    short = lax.broadcasted_iota(jnp.int32, (4, 128), 0)
    row_mask, col_mask = plane_masks(lane)
    inner = jnp.logical_or(row < 3, slab < slabs - 1)
    for j in range(dual.shape[2] // 128):
        at = slice(128 * j, 128 * j + 128)
        limit, factor = scales[0:1, at], scales[1:2, at]
        above = jnp.where(slab == slabs - 1, 0.0, factor * (from_next[1:2, at] - edge[:, at]))
        below = jnp.where(slab == 0, 0.0, factor * (first[:, at] - from_previous[0:1, at]))
        own = base[:, at] - TAU * (grad[:, at] + grad_other[:, at])
        own += jnp.where(short == 0, -below, jnp.where(short == 3, above, 0.0))
        ahead = from_next[0:1, at] - above
        field = jnp.where(row < 4, jnp.concatenate([own] * 2, axis=0), ahead)
        new_volume[:, at] = own
        steps = (
            jnp.where(inner, pltpu.roll(field, 7, axis=0) - field, 0.0),
            jnp.where(row_mask, pltpu.roll(field, 120, axis=1) - field, 0.0),
            jnp.where(col_mask, pltpu.roll(field, 127, axis=1) - field, 0.0),
        )
        for k in range(3):
            mixed = steps[k][0:4] + dual[k, :, at]
            clipped = jnp.clip(mixed, -limit, limit)
            new_dual[k, :, at] = clipped
            new_split[k, :, at] = mixed - clipped


def vmem():
    return pl.BlockSpec(memory_space=pltpu.VMEM)


def smem():
    return pl.BlockSpec(memory_space=pltpu.SMEM)


def hbm():
    return pl.BlockSpec(memory_space=pltpu.HBM)


def params():
    return pltpu.CompilerParams(vmem_limit_bytes=VMEM_LIMIT)


def shards(
    volume, split_var, dual_var, sinogram, proj_tiles, ray_index, voxel_index, tile_count, rho
):
    f32, bf16 = jnp.float32, jnp.bfloat16
    slices, width = volume.shape
    slots = ray_index.shape[0]
    owned = sinogram.shape[0]
    group = lax.axis_size(("tile", "rep"))
    reps = lax.axis_size("rep")
    slabs = lax.axis_size("slab")
    rays = owned * group
    voxel_tiles = width // TV
    volume_here, dual_here = volume, dual_var
    volume, split_var, dual_var, sinogram, proj_tiles, ray_index, voxel_index = (
        pltpu.with_memory_space_constraint(x, pltpu.HBM)
        for x in (
            volume, split_var, dual_var, sinogram, proj_tiles, ray_index, voxel_index
        )
    )

    partial, adjoint, edge, first = pl.pallas_call(
        forward_kernel,
        out_shape=(
            jax.ShapeDtypeStruct((rays * slices, TR), bf16),
            jax.ShapeDtypeStruct((slices, width), f32),
            jax.ShapeDtypeStruct((1, width), f32),
            jax.ShapeDtypeStruct((1, width), f32),
        ),
        in_specs=[smem()] + [hbm()] * 7,
        out_specs=(vmem(),) * 4,
        scratch_shapes=[
            pltpu.SMEM((slots,), jnp.int32),
            pltpu.SMEM((slots,), jnp.int32),
            pltpu.VMEM((slices, width), f32),
            pltpu.VMEM((3, slices, width), f32),
            pltpu.VMEM((3, slices, width), f32),
            pltpu.VMEM(sinogram.shape, f32),
            pltpu.VMEM(proj_tiles.shape, bf16),
            pltpu.VMEM((8, width), f32),
            pltpu.VMEM((voxel_tiles, 8, 128), f32),
        ]
        + [pltpu.VMEM((rays + 1, 8, 128), f32)] * 4
        + [pltpu.SemaphoreType.DMA((6,)), pltpu.SemaphoreType.DMA((CHUNKS,))],
        compiler_params=params(),
        name="forward",
    )(
        tile_count, ray_index, voxel_index, volume, split_var, dual_var, sinogram, proj_tiles
    )

    swap = [(i, i ^ 1) for i in range(reps)]
    moved = lax.ppermute(partial, "rep", swap)
    total = (partial.astype(f32) + moved.astype(f32)).astype(bf16)
    step = reps
    while step < group:
        pairs = [(i, i ^ step if i % reps == reps - 1 else i) for i in range(group)]
        moved = lax.ppermute(total, ("tile", "rep"), pairs)
        total = (total.astype(f32) + moved.astype(f32)).astype(bf16)
        step *= 2
    shared = lax.ppermute(total, "rep", swap)

    grad, base, scales = pl.pallas_call(
        backward_kernel,
        out_shape=(
            jax.ShapeDtypeStruct((slices, width), f32),
            jax.ShapeDtypeStruct((slices, width), f32),
            jax.ShapeDtypeStruct((2, width), f32),
        ),
        in_specs=[smem()] * 2 + [hbm()] * 3 + [vmem()] * 4,
        out_specs=(vmem(), vmem(), vmem()),
        scratch_shapes=[
            pltpu.SMEM((slots,), jnp.int32),
            pltpu.SMEM((slots,), jnp.int32),
            pltpu.VMEM(proj_tiles.shape, bf16),
            pltpu.VMEM((rays, 8, 128), f32),
        ]
        + [pltpu.VMEM((voxel_tiles + 1, 8, 128), f32)] * 4
        + [pltpu.SemaphoreType.DMA((2,)), pltpu.SemaphoreType.DMA((CHUNKS,))],
        compiler_params=params(),
        name="backward",
    )(
        tile_count, rho, ray_index, voxel_index, proj_tiles,
        total, shared, volume_here, adjoint,
    )
    grad_other = lax.ppermute(grad, "rep", swap)
    ahead = jnp.concatenate([base[0:1] - TAU * (grad[0:1] + grad_other[0:1]), first], axis=0)
    behind = jnp.concatenate([edge, edge], axis=0)
    if slabs == 2:
        halo = jnp.where(lax.axis_index("slab") == 0, behind, ahead)
        from_next = from_previous = lax.ppermute(halo, "slab", [(0, 1), (1, 0)])
    else:
        from_next = lax.ppermute(ahead, "slab", [(i, i - 1) for i in range(1, slabs)])
        from_previous = lax.ppermute(behind, "slab", [(i - 1, i) for i in range(1, slabs)])

    return pl.pallas_call(
        update_kernel,
        out_shape=(
            jax.ShapeDtypeStruct((slices, width), f32),
            jax.ShapeDtypeStruct((3, slices, width), f32),
            jax.ShapeDtypeStruct((3, slices, width), f32),
        ),
        in_specs=[vmem()] * 9,
        out_specs=(vmem(), vmem(), vmem()),
        compiler_params=params(),
        name="update",
    )(grad, grad_other, from_next, from_previous, base, edge, first, dual_here, scales)


def solution(mesh):
    return jax.shard_map(
        shards,
        mesh=mesh,
        in_specs=(
            P(("parts", "slab"), "tile"),
            P(None, ("parts", "slab"), "tile"),
            P(None, ("parts", "slab"), "tile"),
            P(("tile", "rep"), ("parts", "slab"), None),
            P(("tile", "rep"), None, None),
            P(("tile", "rep")),
            P(("tile", "rep")),
            P(("tile", "rep")),
            P(),
        ),
        out_specs=(
            P(("parts", "slab"), "tile"),
            P(None, ("parts", "slab"), "tile"),
            P(None, ("parts", "slab"), "tile"),
        ),
        check_vma=False,
    )
```

```python
import jax
import jax.numpy as jnp
from jax import lax
from jax.experimental import pallas as pl
from jax.experimental.pallas import tpu as pltpu
from jax.sharding import PartitionSpec as P

TV = 64
TR = 128
TAU = 0.5
GROUP = 4
CHUNKS = 8
VMEM_LIMIT = 16 * 1024 * 1024


def iotas(shape):
    row = lax.broadcasted_iota(jnp.int32, shape, 0)
    lane = lax.broadcasted_iota(jnp.int32, shape, 1)
    return row, lane


def start_tiles(proj_hbm, tiles, sems):
    per = proj_hbm.shape[0] // CHUNKS
    copies = []
    for c in range(CHUNKS):
        part = pl.ds(c * per, per)
        copy = pltpu.make_async_copy(proj_hbm.at[part], tiles.at[part], sems.at[c])
        copy.start()
        copies.append(copy)
    return copies


def plane_masks(lane):
    return (lane % TV) // 8 < 7, lane % 8 < 7


def rows8(start):
    return pl.ds(pl.multiple_of(start, 8), 8)


def add_rows(accs, starts, values):
    held = [acc[rows8(start), :] for acc, start in zip(accs, starts)]
    for acc, start, old, value in zip(accs, starts, held, values):
        acc[rows8(start), :] = old + value


def forward_kernel(
    count, ray_hbm, voxel_hbm, vol_hbm, split_hbm, dual_hbm, sino_hbm, proj_hbm,
    partial_out, adjoint_out, edge_out, first_out, index_out, tiles,
    ray, voxel, index, vol, split, dual, sino, double, table, acc0, acc1, acc2, acc3,
    sems, tile_sems,
):
    slots = proj_hbm.shape[0]
    lines = ray.shape[0]
    rays = acc0.shape[0] // 8 - 1
    voxel_tiles = table.shape[0] // 8
    owned = sino.shape[0]
    width = vol.shape[1]
    loads = [
        pltpu.make_async_copy(source, target, sems.at[i])
        for i, (source, target) in enumerate(
            [
                (vol_hbm, vol), (voxel_hbm, voxel), (ray_hbm, ray), (sino_hbm, sino),
                (split_hbm, split), (dual_hbm, dual),
            ]
        )
    ]
    for load in loads:
        load.start()
    copies = start_tiles(proj_hbm, tiles, tile_sems)
    accs = (acc0, acc1, acc2, acc3)
    for acc in accs:
        acc[...] = jnp.zeros_like(acc)
    row, lane = iotas((8, 128))
    low, top = lane < TV, row < 4

    loads[0].wait()
    field = vol[...]
    double[0:4, :] = field
    double[4:8, :] = field
    for j in range(width // 128):
        x = double[:, 128 * j:128 * j + 128].astype(jnp.bfloat16).astype(jnp.float32)
        turned = pltpu.roll(x, TV, axis=1)
        zero = jnp.zeros_like(x)
        first = jnp.where(jnp.logical_and(top, low), x, zero)
        second = jnp.where(jnp.logical_and(top, low), turned, zero)
        other = jnp.logical_not(jnp.logical_or(top, low))
        table[16 * j:16 * j + 8, :] = jnp.where(other, turned, first)
        table[16 * j + 8:16 * j + 16, :] = jnp.where(other, x, second)

    loads[1].wait()
    loads[2].wait()
    line, place = iotas((lines, 128))
    live = 128 * line + place < count[0]
    rays8, voxels8 = ray[...] * 8, voxel[...] * 8
    index_out[0:lines, :] = voxels8
    index_out[lines:2 * lines, :] = jnp.where(live, rays8, rays * 8)
    index_out[2 * lines:3 * lines, :] = rays8
    index_out[3 * lines:4 * lines, :] = jnp.where(live, voxels8, voxel_tiles * 8)
    to_scalar = pltpu.make_async_copy(index_out, index, sems.at[6])
    to_scalar.start()

    for load in loads[3:]:
        load.wait()
    mine = (lax.axis_index("tile") * lax.axis_size("rep") + lax.axis_index("rep")) * owned
    for r in range(owned):
        acc0[pl.ds(pl.multiple_of((mine + r) * 8, 8), 4), :] = -sino[r]
    row_mask, col_mask = plane_masks(lane)
    for j in range(width // 128):
        at = slice(128 * j, 128 * j + 128)
        x = double[:, at]
        gap = [
            jnp.concatenate([dual[k, :, at] - split[k, :, at]] * 2, axis=0) for k in range(3)
        ]
        depth = jnp.where(row < 3, pltpu.roll(x, 7, axis=0) - x + gap[0], 0.0)
        across = jnp.where(row_mask, pltpu.roll(x, 120, axis=1) - x + gap[1], 0.0)
        along = jnp.where(col_mask, pltpu.roll(x, 127, axis=1) - x + gap[2], 0.0)
        adjoint = pltpu.roll(depth, 1, axis=0) - depth
        adjoint += jnp.where((lane % TV) >= 8, pltpu.roll(across, 8, axis=1), 0.0) - across
        adjoint += jnp.where(lane % 8 >= 1, pltpu.roll(along, 1, axis=1), 0.0) - along
        adjoint_out[:, at] = adjoint[0:4]
        edge_out[:, at] = (x - gap[0])[3:4]
        first_out[:, at] = x[0:1]

    to_scalar.wait()
    per = slots // CHUNKS
    for g in range(slots // GROUP):
        if GROUP * g % per == 0:
            copies[GROUP * g // per].wait()
        n = GROUP * g
        at = [divmod(n + i, 128) for i in range(GROUP)]
        picked = [table[rows8(index[line, place]), :] for line, place in at]
        pairs = [jnp.where(top, picked[2 * i], picked[2 * i + 1]) for i in range(2)]
        zero = jnp.zeros_like(pairs[0])
        left = jnp.concatenate([pairs[0], zero], axis=0).astype(jnp.bfloat16)
        right = jnp.concatenate([zero, pairs[1]], axis=0).astype(jnp.bfloat16)
        sums = jnp.dot(
            jnp.concatenate([left, right], axis=1),
            tiles[n:n + GROUP].reshape(GROUP * TV, TR),
            preferred_element_type=jnp.float32,
        )
        add_rows(
            accs,
            [index[lines + line, place] for line, place in at],
            [sums[0:8], sums[0:8], sums[8:16], sums[8:16]],
        )
    for q in range(rays // 4):
        halves = []
        for r in (4 * q, 4 * q + 2):
            at = [slice(8 * (r + k), 8 * (r + k) + 8) for k in range(2)]
            even = [acc0[at[k], :] + acc2[at[k], :] for k in range(2)]
            odd = [acc1[at[k], :] + acc3[at[k], :] for k in range(2)]
            halves.append(
                jnp.where(top, even[0], odd[1])
                + pltpu.roll(jnp.where(top, even[1], odd[0]), 4, axis=0)
            )
        partial_out[16 * q:16 * q + 16, :] = jnp.concatenate(halves, axis=0).astype(jnp.bfloat16)


def backward_kernel(
    rho, indices, tiles, part, moved, vol, adjoint,
    grad_out, base_out, scale_out,
    index, table, acc0, acc1, acc2, acc3, sem,
):
    slots = tiles.shape[0]
    lines = indices.shape[0] // 4
    rays = table.shape[0] // 8
    voxel_tiles = acc0.shape[0] // 8 - 1
    to_scalar = pltpu.make_async_copy(indices, index, sem)
    to_scalar.start()
    accs = (acc0, acc1, acc2, acc3)
    for acc in accs:
        acc[...] = jnp.zeros_like(acc)
    row, lane = iotas((8, 128))
    low, top = lane < TV, row < 4
    for q in range(rays // 4):
        at = slice(16 * q, 16 * q + 16)
        total = part[at, :].astype(jnp.float32) + moved[at, :].astype(jnp.float32)
        for k in range(2):
            x = total[8 * k:8 * k + 8]
            turned = pltpu.roll(x, 4, axis=0)
            r = 8 * (4 * q + 2 * k)
            table[r:r + 8, :] = jnp.where(top, x, turned)
            table[r + 8:r + 16, :] = jnp.where(top, turned, x)

    factor = TAU * rho[0]
    limit = 1.0 / rho[0]
    for j in range(voxel_tiles // 2):
        at = slice(128 * j, 128 * j + 128)
        base_out[:, at] = vol[:, at] - factor * adjoint[:, at]
        scale_out[0:1, at] = jnp.full((1, 128), limit, jnp.float32)
        scale_out[1:2, at] = jnp.full((1, 128), factor, jnp.float32)

    to_scalar.wait()
    for g in range(slots // GROUP):
        n = GROUP * g
        at = [divmod(n + i, 128) for i in range(GROUP)]
        picked = [table[rows8(index[2 * lines + line, place]), :] for line, place in at]
        rows = jnp.concatenate(
            [jnp.where(top, picked[2 * i], picked[2 * i + 1]) for i in range(2)], axis=0
        )
        back = lax.dot_general(
            rows.astype(jnp.bfloat16),
            tiles[n:n + GROUP].reshape(GROUP * TV, TR),
            (((1,), (1,)), ((), ())),
            preferred_element_type=jnp.float32,
        )
        add_rows(
            accs,
            [index[3 * lines + line, place] for line, place in at],
            [back[8 * k:8 * k + 8, 128 * k:128 * k + 128] for k in (0, 0, 1, 1)],
        )
    for j in range(voxel_tiles // 2):
        at = [slice(16 * j + 8 * k, 16 * j + 8 * k + 8) for k in range(2)]
        even = [acc0[at[k], :] + acc2[at[k], :] for k in range(2)]
        odd = [acc1[at[k], :] + acc3[at[k], :] for k in range(2)]
        turned = pltpu.roll(jnp.where(top, even[1], odd[0]), TV, axis=1)
        both = jnp.where(top == low, jnp.where(top, even[0], odd[1]), turned)
        grad_out[:, 128 * j:128 * j + 128] = (both + pltpu.roll(both, 4, axis=0))[0:4]


def update_kernel(
    grad, grad_other, from_next, from_previous, base, edge, first, dual, scales,
    new_volume, new_split, new_dual,
):
    slab, slabs = lax.axis_index("slab"), lax.axis_size("slab")
    row, lane = iotas((8, 128))
    short = lax.broadcasted_iota(jnp.int32, (4, 128), 0)
    row_mask, col_mask = plane_masks(lane)
    inner = jnp.logical_or(row < 3, slab < slabs - 1)
    for j in range(dual.shape[2] // 128):
        at = slice(128 * j, 128 * j + 128)
        limit, factor = scales[0:1, at], scales[1:2, at]
        above = jnp.where(slab == slabs - 1, 0.0, factor * (from_next[1:2, at] - edge[:, at]))
        below = jnp.where(slab == 0, 0.0, factor * (first[:, at] - from_previous[0:1, at]))
        own = base[:, at] - TAU * (grad[:, at] + grad_other[:, at])
        own += jnp.where(short == 0, -below, jnp.where(short == 3, above, 0.0))
        ahead = from_next[0:1, at] - above
        field = jnp.where(row < 4, jnp.concatenate([own] * 2, axis=0), ahead)
        new_volume[:, at] = own
        steps = (
            jnp.where(inner, pltpu.roll(field, 7, axis=0) - field, 0.0),
            jnp.where(row_mask, pltpu.roll(field, 120, axis=1) - field, 0.0),
            jnp.where(col_mask, pltpu.roll(field, 127, axis=1) - field, 0.0),
        )
        for k in range(3):
            mixed = steps[k][0:4] + dual[k, :, at]
            clipped = jnp.clip(mixed, -limit, limit)
            new_dual[k, :, at] = clipped
            new_split[k, :, at] = mixed - clipped


def vmem():
    return pl.BlockSpec(memory_space=pltpu.VMEM)


def smem():
    return pl.BlockSpec(memory_space=pltpu.SMEM)


def hbm():
    return pl.BlockSpec(memory_space=pltpu.HBM)


def params():
    return pltpu.CompilerParams(vmem_limit_bytes=VMEM_LIMIT)


def shards(
    volume, split_var, dual_var, sinogram, proj_tiles, ray_index, voxel_index, tile_count, rho
):
    f32, bf16 = jnp.float32, jnp.bfloat16
    slices, width = volume.shape
    slots = ray_index.shape[0]
    owned = sinogram.shape[0]
    group = lax.axis_size(("tile", "rep"))
    reps = lax.axis_size("rep")
    slabs = lax.axis_size("slab")
    rays = owned * group
    voxel_tiles = width // TV
    volume_here, dual_here = volume, dual_var
    lines = slots // 128
    ray_index, voxel_index = ray_index.reshape(lines, 128), voxel_index.reshape(lines, 128)
    volume, split_var, dual_var, sinogram, proj_tiles, ray_index, voxel_index = (
        pltpu.with_memory_space_constraint(x, pltpu.HBM)
        for x in (
            volume, split_var, dual_var, sinogram, proj_tiles, ray_index, voxel_index
        )
    )

    partial, adjoint, edge, first, indices, tiles = pl.pallas_call(
        forward_kernel,
        out_shape=(
            jax.ShapeDtypeStruct((rays * slices, TR), bf16),
            jax.ShapeDtypeStruct((slices, width), f32),
            jax.ShapeDtypeStruct((1, width), f32),
            jax.ShapeDtypeStruct((1, width), f32),
            jax.ShapeDtypeStruct((4 * lines, 128), jnp.int32),
            jax.ShapeDtypeStruct(proj_tiles.shape, bf16),
        ),
        in_specs=[smem()] + [hbm()] * 7,
        out_specs=(vmem(),) * 6,
        scratch_shapes=[
            pltpu.VMEM((lines, 128), jnp.int32),
            pltpu.VMEM((lines, 128), jnp.int32),
            pltpu.SMEM((4 * lines, 128), jnp.int32),
            pltpu.VMEM((slices, width), f32),
            pltpu.VMEM((3, slices, width), f32),
            pltpu.VMEM((3, slices, width), f32),
            pltpu.VMEM(sinogram.shape, f32),
            pltpu.VMEM((8, width), f32),
            pltpu.VMEM((voxel_tiles * 8, 128), f32),
        ]
        + [pltpu.VMEM((rays * 8 + 8, 128), f32)] * 4
        + [pltpu.SemaphoreType.DMA((7,)), pltpu.SemaphoreType.DMA((CHUNKS,))],
        compiler_params=params(),
        name="forward",
    )(tile_count, ray_index, voxel_index, volume, split_var, dual_var, sinogram, proj_tiles)

    swap = [(i, i ^ 1) for i in range(reps)]
    step = 1
    while True:
        moved = lax.ppermute(
            partial, ("tile", "rep"), [(i, i ^ step) for i in range(group)]
        )
        step *= 2
        if step == group:
            break
        partial = (partial.astype(f32) + moved.astype(f32)).astype(bf16)

    grad, base, scales = pl.pallas_call(
        backward_kernel,
        out_shape=(
            jax.ShapeDtypeStruct((slices, width), f32),
            jax.ShapeDtypeStruct((slices, width), f32),
            jax.ShapeDtypeStruct((2, width), f32),
        ),
        in_specs=[smem()] + [vmem()] * 6,
        out_specs=(vmem(), vmem(), vmem()),
        scratch_shapes=[
            pltpu.SMEM((4 * lines, 128), jnp.int32),
            pltpu.VMEM((rays * 8, 128), f32),
        ]
        + [pltpu.VMEM((voxel_tiles * 8 + 8, 128), f32)] * 4
        + [pltpu.SemaphoreType.DMA],
        compiler_params=params(),
        name="backward",
    )(rho, indices, tiles, partial, moved, volume_here, adjoint)
    grad_other = lax.ppermute(grad, "rep", swap)
    ahead = jnp.concatenate([base[0:1] - TAU * (grad[0:1] + grad_other[0:1]), first], axis=0)
    behind = jnp.concatenate([edge, edge], axis=0)
    if slabs == 2:
        halo = jnp.where(lax.axis_index("slab") == 0, behind, ahead)
        from_next = from_previous = lax.ppermute(halo, "slab", [(0, 1), (1, 0)])
    else:
        from_next = lax.ppermute(ahead, "slab", [(i, i - 1) for i in range(1, slabs)])
        from_previous = lax.ppermute(behind, "slab", [(i - 1, i) for i in range(1, slabs)])

    return pl.pallas_call(
        update_kernel,
        out_shape=(
            jax.ShapeDtypeStruct((slices, width), f32),
            jax.ShapeDtypeStruct((3, slices, width), f32),
            jax.ShapeDtypeStruct((3, slices, width), f32),
        ),
        in_specs=[vmem()] * 9,
        out_specs=(vmem(), vmem(), vmem()),
        compiler_params=params(),
        name="update",
    )(grad, grad_other, from_next, from_previous, base, edge, first, dual_here, scales)


def solution(mesh):
    return jax.shard_map(
        shards,
        mesh=mesh,
        in_specs=(
            P(("parts", "slab"), "tile"),
            P(None, ("parts", "slab"), "tile"),
            P(None, ("parts", "slab"), "tile"),
            P(("tile", "rep"), ("parts", "slab"), None),
            P(("tile", "rep"), None, None),
            P(("tile", "rep")),
            P(("tile", "rep")),
            P(("tile", "rep")),
            P(),
        ),
        out_specs=(
            P(("parts", "slab"), "tile"),
            P(None, ("parts", "slab"), "tile"),
            P(None, ("parts", "slab"), "tile"),
        ),
        check_vma=False,
    )
```

```python
import jax
import jax.numpy as jnp
from jax import lax
from jax.experimental import pallas as pl
from jax.experimental.pallas import tpu as pltpu
from jax.sharding import PartitionSpec as P

TV = 64
TR = 128
TAU = 0.5
GROUP = 4
CHUNKS = 8
VMEM_LIMIT = 16 * 1024 * 1024


def iotas(shape):
    row = lax.broadcasted_iota(jnp.int32, shape, 0)
    lane = lax.broadcasted_iota(jnp.int32, shape, 1)
    return row, lane


def start_tiles(proj_hbm, tiles, sems):
    per = proj_hbm.shape[0] // CHUNKS
    copies = []
    for c in range(CHUNKS):
        part = pl.ds(c * per, per)
        copy = pltpu.make_async_copy(proj_hbm.at[part], tiles.at[part], sems.at[c])
        copy.start()
        copies.append(copy)
    return copies


def plane_masks(lane):
    return (lane % TV) // 8 < 7, lane % 8 < 7


def rows8(start):
    return pl.ds(pl.multiple_of(start, 8), 8)


def add_rows(accs, starts, values):
    held = [acc[rows8(start), :] for acc, start in zip(accs, starts)]
    for acc, start, old, value in zip(accs, starts, held, values):
        acc[rows8(start), :] = old + value


def forward_kernel(
    count, ray_hbm, voxel_hbm, vol_hbm, sino_hbm, proj_hbm,
    partial_out, index_out, tiles,
    ray, voxel, index, vol, sino, double, table, acc0, acc1, acc2, acc3,
    sems, tile_sems,
):
    slots = proj_hbm.shape[0]
    lines = ray.shape[0]
    rays = acc0.shape[0] // 8 - 1
    voxel_tiles = table.shape[0] // 8
    owned = sino.shape[0]
    width = vol.shape[1]
    loads = [
        pltpu.make_async_copy(source, target, sems.at[i])
        for i, (source, target) in enumerate(
            [(vol_hbm, vol), (voxel_hbm, voxel), (ray_hbm, ray), (sino_hbm, sino)]
        )
    ]
    for load in loads:
        load.start()
    copies = start_tiles(proj_hbm, tiles, tile_sems)
    accs = (acc0, acc1, acc2, acc3)
    for acc in accs:
        acc[...] = jnp.zeros_like(acc)
    row, lane = iotas((8, 128))
    low, top = lane < TV, row < 4

    loads[0].wait()
    field = vol[...]
    double[0:4, :] = field
    double[4:8, :] = field
    for j in range(width // 128):
        x = double[:, 128 * j:128 * j + 128].astype(jnp.bfloat16).astype(jnp.float32)
        turned = pltpu.roll(x, TV, axis=1)
        zero = jnp.zeros_like(x)
        first = jnp.where(jnp.logical_and(top, low), x, zero)
        second = jnp.where(jnp.logical_and(top, low), turned, zero)
        other = jnp.logical_not(jnp.logical_or(top, low))
        table[16 * j:16 * j + 8, :] = jnp.where(other, turned, first)
        table[16 * j + 8:16 * j + 16, :] = jnp.where(other, x, second)

    loads[1].wait()
    loads[2].wait()
    line, place = iotas((lines, 128))
    live = 128 * line + place < count[0]
    rays8, voxels8 = ray[...] * 8, voxel[...] * 8
    index_out[0:lines, :] = voxels8
    index_out[lines:2 * lines, :] = jnp.where(live, rays8, rays * 8)
    index_out[2 * lines:3 * lines, :] = rays8
    index_out[3 * lines:4 * lines, :] = jnp.where(live, voxels8, voxel_tiles * 8)
    to_scalar = pltpu.make_async_copy(index_out, index, sems.at[4])
    to_scalar.start()

    loads[3].wait()
    mine = (lax.axis_index("tile") * lax.axis_size("rep") + lax.axis_index("rep")) * owned
    for r in range(owned):
        acc0[pl.ds(pl.multiple_of((mine + r) * 8, 8), 4), :] = -sino[r]
    to_scalar.wait()
    per = slots // CHUNKS
    for g in range(slots // GROUP):
        if GROUP * g % per == 0:
            copies[GROUP * g // per].wait()
        n = GROUP * g
        at = [divmod(n + i, 128) for i in range(GROUP)]
        picked = [table[rows8(index[line, place]), :] for line, place in at]
        pairs = [jnp.where(top, picked[2 * i], picked[2 * i + 1]) for i in range(2)]
        zero = jnp.zeros_like(pairs[0])
        left = jnp.concatenate([pairs[0], zero], axis=0).astype(jnp.bfloat16)
        right = jnp.concatenate([zero, pairs[1]], axis=0).astype(jnp.bfloat16)
        sums = jnp.dot(
            jnp.concatenate([left, right], axis=1),
            tiles[n:n + GROUP].reshape(GROUP * TV, TR),
            preferred_element_type=jnp.float32,
        )
        add_rows(
            accs,
            [index[lines + line, place] for line, place in at],
            [sums[0:8], sums[0:8], sums[8:16], sums[8:16]],
        )
    for q in range(rays // 4):
        halves = []
        for r in (4 * q, 4 * q + 2):
            at = [slice(8 * (r + k), 8 * (r + k) + 8) for k in range(2)]
            even = [acc0[at[k], :] + acc2[at[k], :] for k in range(2)]
            odd = [acc1[at[k], :] + acc3[at[k], :] for k in range(2)]
            halves.append(
                jnp.where(top, even[0], odd[1])
                + pltpu.roll(jnp.where(top, even[1], odd[0]), 4, axis=0)
            )
        partial_out[16 * q:16 * q + 16, :] = jnp.concatenate(halves, axis=0).astype(jnp.bfloat16)


def local_kernel(rho, vol, split, dual, base_out, edge_out, first_out, scale_out):
    factor = TAU * rho[0]
    limit = 1.0 / rho[0]
    row, lane = iotas((8, 128))
    row_mask, col_mask = plane_masks(lane)
    for j in range(vol.shape[1] // 128):
        at = slice(128 * j, 128 * j + 128)
        field = vol[:, at]
        x = jnp.concatenate([field] * 2, axis=0)
        gap = [
            jnp.concatenate([dual[k, :, at] - split[k, :, at]] * 2, axis=0) for k in range(3)
        ]
        depth = jnp.where(row < 3, pltpu.roll(x, 7, axis=0) - x + gap[0], 0.0)
        across = jnp.where(row_mask, pltpu.roll(x, 120, axis=1) - x + gap[1], 0.0)
        along = jnp.where(col_mask, pltpu.roll(x, 127, axis=1) - x + gap[2], 0.0)
        adjoint = pltpu.roll(depth, 1, axis=0) - depth
        adjoint += jnp.where((lane % TV) >= 8, pltpu.roll(across, 8, axis=1), 0.0) - across
        adjoint += jnp.where(lane % 8 >= 1, pltpu.roll(along, 1, axis=1), 0.0) - along
        base_out[:, at] = (x - factor * adjoint)[0:4]
        edge_out[:, at] = (x - gap[0])[3:4]
        first_out[:, at] = field[0:1]
        scale_out[0:1, at] = jnp.full((1, 128), limit, jnp.float32)
        scale_out[1:2, at] = jnp.full((1, 128), factor, jnp.float32)


def backward_kernel(
    indices, tiles, part, moved, grad_out,
    index, table, acc0, acc1, acc2, acc3, sem,
):
    slots = tiles.shape[0]
    lines = indices.shape[0] // 4
    rays = table.shape[0] // 8
    voxel_tiles = acc0.shape[0] // 8 - 1
    to_scalar = pltpu.make_async_copy(indices, index, sem)
    to_scalar.start()
    accs = (acc0, acc1, acc2, acc3)
    for acc in accs:
        acc[...] = jnp.zeros_like(acc)
    row, lane = iotas((8, 128))
    low, top = lane < TV, row < 4
    for q in range(rays // 4):
        at = slice(16 * q, 16 * q + 16)
        total = part[at, :].astype(jnp.float32) + moved[at, :].astype(jnp.float32)
        for k in range(2):
            x = total[8 * k:8 * k + 8]
            turned = pltpu.roll(x, 4, axis=0)
            r = 8 * (4 * q + 2 * k)
            table[r:r + 8, :] = jnp.where(top, x, turned)
            table[r + 8:r + 16, :] = jnp.where(top, turned, x)

    to_scalar.wait()
    for g in range(slots // GROUP):
        n = GROUP * g
        at = [divmod(n + i, 128) for i in range(GROUP)]
        picked = [table[rows8(index[2 * lines + line, place]), :] for line, place in at]
        rows = jnp.concatenate(
            [jnp.where(top, picked[2 * i], picked[2 * i + 1]) for i in range(2)], axis=0
        )
        back = lax.dot_general(
            rows.astype(jnp.bfloat16),
            tiles[n:n + GROUP].reshape(GROUP * TV, TR),
            (((1,), (1,)), ((), ())),
            preferred_element_type=jnp.float32,
        )
        add_rows(
            accs,
            [index[3 * lines + line, place] for line, place in at],
            [back[8 * k:8 * k + 8, 128 * k:128 * k + 128] for k in (0, 0, 1, 1)],
        )
    for j in range(voxel_tiles // 2):
        at = [slice(16 * j + 8 * k, 16 * j + 8 * k + 8) for k in range(2)]
        even = [acc0[at[k], :] + acc2[at[k], :] for k in range(2)]
        odd = [acc1[at[k], :] + acc3[at[k], :] for k in range(2)]
        turned = pltpu.roll(jnp.where(top, even[1], odd[0]), TV, axis=1)
        both = jnp.where(top == low, jnp.where(top, even[0], odd[1]), turned)
        grad_out[:, 128 * j:128 * j + 128] = (both + pltpu.roll(both, 4, axis=0))[0:4]


def update_kernel(
    grad, grad_other, from_next, from_previous, base, edge, first, dual, scales,
    new_volume, new_split, new_dual,
):
    slab, slabs = lax.axis_index("slab"), lax.axis_size("slab")
    row, lane = iotas((8, 128))
    short = lax.broadcasted_iota(jnp.int32, (4, 128), 0)
    row_mask, col_mask = plane_masks(lane)
    inner = jnp.logical_or(row < 3, slab < slabs - 1)
    for j in range(dual.shape[2] // 128):
        at = slice(128 * j, 128 * j + 128)
        limit, factor = scales[0:1, at], scales[1:2, at]
        above = jnp.where(slab == slabs - 1, 0.0, factor * (from_next[1:2, at] - edge[:, at]))
        below = jnp.where(slab == 0, 0.0, factor * (first[:, at] - from_previous[0:1, at]))
        own = base[:, at] - TAU * (grad[:, at] + grad_other[:, at])
        own += jnp.where(short == 0, -below, jnp.where(short == 3, above, 0.0))
        ahead = from_next[0:1, at] - above
        field = jnp.where(row < 4, jnp.concatenate([own] * 2, axis=0), ahead)
        new_volume[:, at] = own
        steps = (
            jnp.where(inner, pltpu.roll(field, 7, axis=0) - field, 0.0),
            jnp.where(row_mask, pltpu.roll(field, 120, axis=1) - field, 0.0),
            jnp.where(col_mask, pltpu.roll(field, 127, axis=1) - field, 0.0),
        )
        for k in range(3):
            mixed = steps[k][0:4] + dual[k, :, at]
            clipped = jnp.clip(mixed, -limit, limit)
            new_dual[k, :, at] = clipped
            new_split[k, :, at] = mixed - clipped


def vmem():
    return pl.BlockSpec(memory_space=pltpu.VMEM)


def smem():
    return pl.BlockSpec(memory_space=pltpu.SMEM)


def hbm():
    return pl.BlockSpec(memory_space=pltpu.HBM)


def params():
    return pltpu.CompilerParams(vmem_limit_bytes=VMEM_LIMIT)


def shards(
    volume, split_var, dual_var, sinogram, proj_tiles, ray_index, voxel_index, tile_count, rho
):
    f32, bf16 = jnp.float32, jnp.bfloat16
    slices, width = volume.shape
    slots = ray_index.shape[0]
    owned = sinogram.shape[0]
    group = lax.axis_size(("tile", "rep"))
    reps = lax.axis_size("rep")
    slabs = lax.axis_size("slab")
    rays = owned * group
    voxel_tiles = width // TV
    lines = slots // 128
    ray_index, voxel_index = ray_index.reshape(lines, 128), voxel_index.reshape(lines, 128)
    sources = [
        pltpu.with_memory_space_constraint(x, pltpu.HBM)
        for x in (ray_index, voxel_index, volume, sinogram, proj_tiles)
    ]

    partial, indices, tiles = pl.pallas_call(
        forward_kernel,
        out_shape=(
            jax.ShapeDtypeStruct((rays * slices, TR), bf16),
            jax.ShapeDtypeStruct((4 * lines, 128), jnp.int32),
            jax.ShapeDtypeStruct(proj_tiles.shape, bf16),
        ),
        in_specs=[smem()] + [hbm()] * 5,
        out_specs=(vmem(),) * 3,
        scratch_shapes=[
            pltpu.VMEM((lines, 128), jnp.int32),
            pltpu.VMEM((lines, 128), jnp.int32),
            pltpu.SMEM((4 * lines, 128), jnp.int32),
            pltpu.VMEM((slices, width), f32),
            pltpu.VMEM(sinogram.shape, f32),
            pltpu.VMEM((8, width), f32),
            pltpu.VMEM((voxel_tiles * 8, 128), f32),
        ]
        + [pltpu.VMEM((rays * 8 + 8, 128), f32)] * 4
        + [pltpu.SemaphoreType.DMA((5,)), pltpu.SemaphoreType.DMA((CHUNKS,))],
        compiler_params=params(),
        name="forward",
    )(tile_count, *sources)

    base, edge, first, scales = pl.pallas_call(
        local_kernel,
        out_shape=(
            jax.ShapeDtypeStruct((slices, width), f32),
            jax.ShapeDtypeStruct((1, width), f32),
            jax.ShapeDtypeStruct((1, width), f32),
            jax.ShapeDtypeStruct((2, width), f32),
        ),
        in_specs=[smem()] + [vmem()] * 3,
        out_specs=(vmem(),) * 4,
        compiler_params=params(),
        name="local",
    )(rho, volume, split_var, dual_var)

    swap = [(i, i ^ 1) for i in range(reps)]
    moved = lax.ppermute(partial, "rep", swap)
    step = reps
    while step < group:
        partial = (partial.astype(f32) + moved.astype(f32)).astype(bf16)
        moved = lax.ppermute(
            partial, ("tile", "rep"), [(i, i ^ (step + 1)) for i in range(group)]
        )
        step *= 2
    moved, base, edge, first, scales = lax.optimization_barrier(
        (moved, base, edge, first, scales)
    )

    grad = pl.pallas_call(
        backward_kernel,
        out_shape=jax.ShapeDtypeStruct((slices, width), f32),
        in_specs=[vmem()] * 4,
        out_specs=vmem(),
        scratch_shapes=[
            pltpu.SMEM((4 * lines, 128), jnp.int32),
            pltpu.VMEM((rays * 8, 128), f32),
        ]
        + [pltpu.VMEM((voxel_tiles * 8 + 8, 128), f32)] * 4
        + [pltpu.SemaphoreType.DMA],
        compiler_params=params(),
        name="backward",
    )(indices, tiles, partial, moved)
    grad_other = lax.ppermute(grad, "rep", swap)
    ahead = jnp.concatenate([base[0:1] - TAU * (grad[0:1] + grad_other[0:1]), first], axis=0)
    behind = jnp.concatenate([edge, edge], axis=0)
    if slabs == 2:
        halo = jnp.where(lax.axis_index("slab") == 0, behind, ahead)
        from_next = from_previous = lax.ppermute(
            halo, ("slab", "rep"), [(i, i ^ 3) for i in range(2 * reps)]
        )
    else:
        from_next = lax.ppermute(ahead, "slab", [(i, i - 1) for i in range(1, slabs)])
        from_previous = lax.ppermute(behind, "slab", [(i - 1, i) for i in range(1, slabs)])

    return pl.pallas_call(
        update_kernel,
        out_shape=(
            jax.ShapeDtypeStruct((slices, width), f32),
            jax.ShapeDtypeStruct((3, slices, width), f32),
            jax.ShapeDtypeStruct((3, slices, width), f32),
        ),
        in_specs=[vmem()] * 9,
        out_specs=(vmem(), vmem(), vmem()),
        compiler_params=params(),
        name="update",
    )(grad, grad_other, from_next, from_previous, base, edge, first, dual_var, scales)


def solution(mesh):
    return jax.shard_map(
        shards,
        mesh=mesh,
        in_specs=(
            P(("parts", "slab"), "tile"),
            P(None, ("parts", "slab"), "tile"),
            P(None, ("parts", "slab"), "tile"),
            P(("tile", "rep"), ("parts", "slab"), None),
            P(("tile", "rep"), None, None),
            P(("tile", "rep")),
            P(("tile", "rep")),
            P(("tile", "rep")),
            P(),
        ),
        out_specs=(
            P(("parts", "slab"), "tile"),
            P(None, ("parts", "slab"), "tile"),
            P(None, ("parts", "slab"), "tile"),
        ),
        check_vma=False,
    )
```

```python
import jax
import jax.numpy as jnp
from jax import lax
from jax.experimental import pallas as pl
from jax.experimental.pallas import tpu as pltpu
from jax.sharding import PartitionSpec as P

TV = 64
TR = 128
TAU = 0.5
GROUP = 4
CHUNKS = 2
VMEM_LIMIT = 16 * 1024 * 1024


def iotas(shape):
    row = lax.broadcasted_iota(jnp.int32, shape, 0)
    lane = lax.broadcasted_iota(jnp.int32, shape, 1)
    return row, lane


def start_tiles(proj_hbm, tiles, sems):
    per = proj_hbm.shape[0] // CHUNKS
    copies = []
    for c in range(CHUNKS):
        part = pl.ds(c * per, per)
        copy = pltpu.make_async_copy(proj_hbm.at[part], tiles.at[part], sems.at[c])
        copy.start()
        copies.append(copy)
    return copies


def plane_masks(lane):
    return (lane % TV) // 8 < 7, lane % 8 < 7


def rows8(start):
    return pl.ds(pl.multiple_of(start, 8), 8)


def add_rows(accs, starts, values):
    held = [acc[rows8(start), :] for acc, start in zip(accs, starts)]
    for acc, start, old, value in zip(accs, starts, held, values):
        acc[rows8(start), :] = old + value


def forward_kernel(
    count, ray_hbm, voxel_hbm, vol_hbm, sino_hbm, proj_hbm,
    partial_out, index_out, tiles,
    ray, voxel, index, vol, sino, double, table, acc0, acc1, acc2, acc3,
    sems, tile_sems,
):
    slots = proj_hbm.shape[0]
    lines = ray.shape[0]
    rays = acc0.shape[0] // 8 - 1
    voxel_tiles = table.shape[0] // 8
    owned = sino.shape[0]
    width = vol.shape[1]
    loads = [
        pltpu.make_async_copy(source, target, sems.at[i])
        for i, (source, target) in enumerate(
            [(voxel_hbm, voxel), (ray_hbm, ray), (vol_hbm, vol), (sino_hbm, sino)]
        )
    ]
    for load in loads:
        load.start()
    copies = start_tiles(proj_hbm, tiles, tile_sems)
    accs = (acc0, acc1, acc2, acc3)
    for acc in accs:
        acc[...] = jnp.zeros_like(acc)
    row, lane = iotas((8, 128))
    low, top = lane < TV, row < 4

    loads[0].wait()
    loads[1].wait()
    line, place = iotas((lines, 128))
    live = 128 * line + place < count[0]
    rays8, voxels8 = ray[...] * 8, voxel[...] * 8
    index_out[0:lines, :] = voxels8
    index_out[lines:2 * lines, :] = jnp.where(live, rays8, rays * 8)
    index_out[2 * lines:3 * lines, :] = rays8
    index_out[3 * lines:4 * lines, :] = jnp.where(live, voxels8, voxel_tiles * 8)
    to_scalar = pltpu.make_async_copy(index_out, index, sems.at[4])
    to_scalar.start()

    loads[2].wait()
    field = vol[...]
    double[0:4, :] = field
    double[4:8, :] = field
    for j in range(width // 128):
        x = double[:, 128 * j:128 * j + 128].astype(jnp.bfloat16).astype(jnp.float32)
        turned = pltpu.roll(x, TV, axis=1)
        zero = jnp.zeros_like(x)
        first = jnp.where(jnp.logical_and(top, low), x, zero)
        second = jnp.where(jnp.logical_and(top, low), turned, zero)
        other = jnp.logical_not(jnp.logical_or(top, low))
        table[16 * j:16 * j + 8, :] = jnp.where(other, turned, first)
        table[16 * j + 8:16 * j + 16, :] = jnp.where(other, x, second)

    loads[3].wait()
    mine = (lax.axis_index("tile") * lax.axis_size("rep") + lax.axis_index("rep")) * owned
    for r in range(owned):
        acc0[pl.ds(pl.multiple_of((mine + r) * 8, 8), 4), :] = -sino[r]
    to_scalar.wait()
    per = slots // CHUNKS
    for g in range(slots // GROUP):
        if GROUP * g % per == 0:
            copies[GROUP * g // per].wait()
        n = GROUP * g
        at = [divmod(n + i, 128) for i in range(GROUP)]
        picked = [table[rows8(index[line, place]), :] for line, place in at]
        pairs = [jnp.where(top, picked[2 * i], picked[2 * i + 1]) for i in range(2)]
        zero = jnp.zeros_like(pairs[0])
        left = jnp.concatenate([pairs[0], zero], axis=0).astype(jnp.bfloat16)
        right = jnp.concatenate([zero, pairs[1]], axis=0).astype(jnp.bfloat16)
        sums = jnp.dot(
            jnp.concatenate([left, right], axis=1),
            tiles[n:n + GROUP].reshape(GROUP * TV, TR),
            preferred_element_type=jnp.float32,
        )
        add_rows(
            accs,
            [index[lines + line, place] for line, place in at],
            [sums[0:8], sums[0:8], sums[8:16], sums[8:16]],
        )
    for q in range(rays // 4):
        halves = []
        for r in (4 * q, 4 * q + 2):
            at = [slice(8 * (r + k), 8 * (r + k) + 8) for k in range(2)]
            even = [acc0[at[k], :] + acc2[at[k], :] for k in range(2)]
            odd = [acc1[at[k], :] + acc3[at[k], :] for k in range(2)]
            halves.append(
                jnp.where(top, even[0], odd[1])
                + pltpu.roll(jnp.where(top, even[1], odd[0]), 4, axis=0)
            )
        partial_out[16 * q:16 * q + 16, :] = jnp.concatenate(halves, axis=0).astype(jnp.bfloat16)


def local_kernel(rho, vol, split, dual, base_out, edge_out, first_out, scale_out):
    factor = TAU * rho[0]
    limit = 1.0 / rho[0]
    row, lane = iotas((8, 128))
    row_mask, col_mask = plane_masks(lane)
    for j in range(vol.shape[1] // 128):
        at = slice(128 * j, 128 * j + 128)
        field = vol[:, at]
        x = jnp.concatenate([field] * 2, axis=0)
        gap = [
            jnp.concatenate([dual[k, :, at] - split[k, :, at]] * 2, axis=0) for k in range(3)
        ]
        depth = jnp.where(row < 3, pltpu.roll(x, 7, axis=0) - x + gap[0], 0.0)
        across = jnp.where(row_mask, pltpu.roll(x, 120, axis=1) - x + gap[1], 0.0)
        along = jnp.where(col_mask, pltpu.roll(x, 127, axis=1) - x + gap[2], 0.0)
        adjoint = pltpu.roll(depth, 1, axis=0) - depth
        adjoint += jnp.where((lane % TV) >= 8, pltpu.roll(across, 8, axis=1), 0.0) - across
        adjoint += jnp.where(lane % 8 >= 1, pltpu.roll(along, 1, axis=1), 0.0) - along
        base_out[:, at] = (x - factor * adjoint)[0:4]
        edge_out[:, at] = (x - gap[0])[3:4]
        first_out[:, at] = field[0:1]
        scale_out[0:1, at] = jnp.full((1, 128), limit, jnp.float32)
        scale_out[1:2, at] = jnp.full((1, 128), factor, jnp.float32)


def backward_kernel(
    indices, tiles, part, moved, grad_out,
    index, table, acc0, acc1, acc2, acc3, sem,
):
    slots = tiles.shape[0]
    lines = indices.shape[0] // 4
    rays = table.shape[0] // 8
    voxel_tiles = acc0.shape[0] // 8 - 1
    to_scalar = pltpu.make_async_copy(indices, index, sem)
    to_scalar.start()
    accs = (acc0, acc1, acc2, acc3)
    for acc in accs:
        acc[...] = jnp.zeros_like(acc)
    row, lane = iotas((8, 128))
    low, top = lane < TV, row < 4
    for q in range(rays // 4):
        at = slice(16 * q, 16 * q + 16)
        total = part[at, :].astype(jnp.float32) + moved[at, :].astype(jnp.float32)
        for k in range(2):
            x = total[8 * k:8 * k + 8]
            turned = pltpu.roll(x, 4, axis=0)
            r = 8 * (4 * q + 2 * k)
            table[r:r + 8, :] = jnp.where(top, x, turned)
            table[r + 8:r + 16, :] = jnp.where(top, turned, x)

    to_scalar.wait()
    for g in range(slots // GROUP):
        n = GROUP * g
        at = [divmod(n + i, 128) for i in range(GROUP)]
        picked = [table[rows8(index[2 * lines + line, place]), :] for line, place in at]
        rows = jnp.concatenate(
            [jnp.where(top, picked[2 * i], picked[2 * i + 1]) for i in range(2)], axis=0
        )
        back = lax.dot_general(
            rows.astype(jnp.bfloat16),
            tiles[n:n + GROUP].reshape(GROUP * TV, TR),
            (((1,), (1,)), ((), ())),
            preferred_element_type=jnp.float32,
        )
        add_rows(
            accs,
            [index[3 * lines + line, place] for line, place in at],
            [back[8 * k:8 * k + 8, 128 * k:128 * k + 128] for k in (0, 0, 1, 1)],
        )
    for j in range(voxel_tiles // 2):
        at = [slice(16 * j + 8 * k, 16 * j + 8 * k + 8) for k in range(2)]
        even = [acc0[at[k], :] + acc2[at[k], :] for k in range(2)]
        odd = [acc1[at[k], :] + acc3[at[k], :] for k in range(2)]
        turned = pltpu.roll(jnp.where(top, even[1], odd[0]), TV, axis=1)
        both = jnp.where(top == low, jnp.where(top, even[0], odd[1]), turned)
        grad_out[:, 128 * j:128 * j + 128] = (both + pltpu.roll(both, 4, axis=0))[0:4]


def update_kernel(
    grad, grad_other, from_next, from_previous, base, edge, first, dual, scales,
    new_volume, new_split, new_dual,
):
    slab, slabs = lax.axis_index("slab"), lax.axis_size("slab")
    row, lane = iotas((8, 128))
    short = lax.broadcasted_iota(jnp.int32, (4, 128), 0)
    row_mask, col_mask = plane_masks(lane)
    inner = jnp.logical_or(row < 3, slab < slabs - 1)
    for j in range(dual.shape[2] // 128):
        at = slice(128 * j, 128 * j + 128)
        limit, factor = scales[0:1, at], scales[1:2, at]
        above = jnp.where(slab == slabs - 1, 0.0, factor * (from_next[1:2, at] - edge[:, at]))
        below = jnp.where(slab == 0, 0.0, factor * (first[:, at] - from_previous[0:1, at]))
        own = base[:, at] - TAU * (grad[:, at] + grad_other[:, at])
        own += jnp.where(short == 0, -below, jnp.where(short == 3, above, 0.0))
        ahead = from_next[0:1, at] - above
        field = jnp.where(row < 4, jnp.concatenate([own] * 2, axis=0), ahead)
        new_volume[:, at] = own
        steps = (
            jnp.where(inner, pltpu.roll(field, 7, axis=0) - field, 0.0),
            jnp.where(row_mask, pltpu.roll(field, 120, axis=1) - field, 0.0),
            jnp.where(col_mask, pltpu.roll(field, 127, axis=1) - field, 0.0),
        )
        for k in range(3):
            mixed = steps[k][0:4] + dual[k, :, at]
            clipped = jnp.clip(mixed, -limit, limit)
            new_dual[k, :, at] = clipped
            new_split[k, :, at] = mixed - clipped


def vmem():
    return pl.BlockSpec(memory_space=pltpu.VMEM)


def smem():
    return pl.BlockSpec(memory_space=pltpu.SMEM)


def hbm():
    return pl.BlockSpec(memory_space=pltpu.HBM)


def params():
    return pltpu.CompilerParams(vmem_limit_bytes=VMEM_LIMIT)


def shards(
    volume, split_var, dual_var, sinogram, proj_tiles, ray_index, voxel_index, tile_count, rho
):
    f32, bf16 = jnp.float32, jnp.bfloat16
    slices, width = volume.shape
    slots = ray_index.shape[0]
    owned = sinogram.shape[0]
    group = lax.axis_size(("tile", "rep"))
    reps = lax.axis_size("rep")
    slabs = lax.axis_size("slab")
    rays = owned * group
    voxel_tiles = width // TV
    lines = slots // 128
    ray_index, voxel_index = ray_index.reshape(lines, 128), voxel_index.reshape(lines, 128)
    sources = [
        pltpu.with_memory_space_constraint(x, pltpu.HBM)
        for x in (ray_index, voxel_index, volume, sinogram, proj_tiles)
    ]

    partial, indices, tiles = pl.pallas_call(
        forward_kernel,
        out_shape=(
            jax.ShapeDtypeStruct((rays * slices, TR), bf16),
            jax.ShapeDtypeStruct((4 * lines, 128), jnp.int32),
            jax.ShapeDtypeStruct(proj_tiles.shape, bf16),
        ),
        in_specs=[smem()] + [hbm()] * 5,
        out_specs=(vmem(),) * 3,
        scratch_shapes=[
            pltpu.VMEM((lines, 128), jnp.int32),
            pltpu.VMEM((lines, 128), jnp.int32),
            pltpu.SMEM((4 * lines, 128), jnp.int32),
            pltpu.VMEM((slices, width), f32),
            pltpu.VMEM(sinogram.shape, f32),
            pltpu.VMEM((8, width), f32),
            pltpu.VMEM((voxel_tiles * 8, 128), f32),
        ]
        + [pltpu.VMEM((rays * 8 + 8, 128), f32)] * 4
        + [pltpu.SemaphoreType.DMA((5,)), pltpu.SemaphoreType.DMA((CHUNKS,))],
        compiler_params=params(),
        name="forward",
    )(tile_count, *sources)

    base, edge, first, scales = pl.pallas_call(
        local_kernel,
        out_shape=(
            jax.ShapeDtypeStruct((slices, width), f32),
            jax.ShapeDtypeStruct((1, width), f32),
            jax.ShapeDtypeStruct((1, width), f32),
            jax.ShapeDtypeStruct((2, width), f32),
        ),
        in_specs=[smem()] + [vmem()] * 3,
        out_specs=(vmem(),) * 4,
        compiler_params=params(),
        name="local",
    )(rho, volume, split_var, dual_var)

    swap = [(i, i ^ 1) for i in range(reps)]
    moved = lax.ppermute(partial, "rep", swap)
    step = reps
    while step < group:
        partial = (partial.astype(f32) + moved.astype(f32)).astype(bf16)
        moved = lax.ppermute(
            partial, ("tile", "rep"), [(i, i ^ (step + 1)) for i in range(group)]
        )
        step *= 2
    moved, base, edge, first, scales = lax.optimization_barrier(
        (moved, base, edge, first, scales)
    )

    grad = pl.pallas_call(
        backward_kernel,
        out_shape=jax.ShapeDtypeStruct((slices, width), f32),
        in_specs=[vmem()] * 4,
        out_specs=vmem(),
        scratch_shapes=[
            pltpu.SMEM((4 * lines, 128), jnp.int32),
            pltpu.VMEM((rays * 8, 128), f32),
        ]
        + [pltpu.VMEM((voxel_tiles * 8 + 8, 128), f32)] * 4
        + [pltpu.SemaphoreType.DMA],
        compiler_params=params(),
        name="backward",
    )(indices, tiles, partial, moved)
    grad_other = lax.ppermute(grad, "rep", swap)
    ahead = jnp.concatenate([base[0:1] - TAU * (grad[0:1] + grad_other[0:1]), first], axis=0)
    behind = jnp.concatenate([edge, edge], axis=0)
    if slabs == 2:
        halo = jnp.where(lax.axis_index("slab") == 0, behind, ahead)
        from_next = from_previous = lax.ppermute(
            halo, ("slab", "rep"), [(i, i ^ 3) for i in range(2 * reps)]
        )
    else:
        from_next = lax.ppermute(ahead, "slab", [(i, i - 1) for i in range(1, slabs)])
        from_previous = lax.ppermute(behind, "slab", [(i - 1, i) for i in range(1, slabs)])

    return pl.pallas_call(
        update_kernel,
        out_shape=(
            jax.ShapeDtypeStruct((slices, width), f32),
            jax.ShapeDtypeStruct((3, slices, width), f32),
            jax.ShapeDtypeStruct((3, slices, width), f32),
        ),
        in_specs=[vmem()] * 9,
        out_specs=(vmem(), vmem(), vmem()),
        compiler_params=params(),
        name="update",
    )(grad, grad_other, from_next, from_previous, base, edge, first, dual_var, scales)


def solution(mesh):
    return jax.shard_map(
        shards,
        mesh=mesh,
        in_specs=(
            P(("parts", "slab"), "tile"),
            P(None, ("parts", "slab"), "tile"),
            P(None, ("parts", "slab"), "tile"),
            P(("tile", "rep"), ("parts", "slab"), None),
            P(("tile", "rep"), None, None),
            P(("tile", "rep")),
            P(("tile", "rep")),
            P(("tile", "rep")),
            P(),
        ),
        out_specs=(
            P(("parts", "slab"), "tile"),
            P(None, ("parts", "slab"), "tile"),
            P(None, ("parts", "slab"), "tile"),
        ),
        check_vma=False,
    )
```

```python
import jax
import jax.numpy as jnp
from jax import lax
from jax.experimental import pallas as pl
from jax.experimental.pallas import tpu as pltpu
from jax.sharding import PartitionSpec as P

TV = 64
TR = 128
TAU = 0.5
GROUP = 4
CHUNKS = 8
WAITS = 2
VMEM_LIMIT = 16 * 1024 * 1024


def iotas(shape):
    row = lax.broadcasted_iota(jnp.int32, shape, 0)
    lane = lax.broadcasted_iota(jnp.int32, shape, 1)
    return row, lane


def start_tiles(proj_hbm, tiles, sems):
    per = proj_hbm.shape[0] // CHUNKS
    copies = []
    for c in range(CHUNKS):
        part = pl.ds(c * per, per)
        copy = pltpu.make_async_copy(proj_hbm.at[part], tiles.at[part], sems.at[c])
        copy.start()
        copies.append(copy)
    return copies


def plane_masks(lane):
    return (lane % TV) // 8 < 7, lane % 8 < 7


def rows8(start):
    return pl.ds(pl.multiple_of(start, 8), 8)


def add_rows(accs, starts, values):
    held = [acc[rows8(start), :] for acc, start in zip(accs, starts)]
    for acc, start, old, value in zip(accs, starts, held, values):
        acc[rows8(start), :] = old + value


def forward_kernel(
    count, ray_hbm, voxel_hbm, vol_hbm, sino_hbm, proj_hbm,
    partial_out, index_out, tiles,
    ray, voxel, index, vol, sino, double, table, acc0, acc1, acc2, acc3,
    sems, tile_sems,
):
    slots = proj_hbm.shape[0]
    lines = ray.shape[0]
    rays = acc0.shape[0] // 8 - 1
    voxel_tiles = table.shape[0] // 8
    owned = sino.shape[0]
    width = vol.shape[1]
    loads = [
        pltpu.make_async_copy(source, target, sems.at[i])
        for i, (source, target) in enumerate(
            [(voxel_hbm, voxel), (ray_hbm, ray), (vol_hbm, vol), (sino_hbm, sino)]
        )
    ]
    for load in loads:
        load.start()
    copies = start_tiles(proj_hbm, tiles, tile_sems)
    accs = (acc0, acc1, acc2, acc3)
    for acc in accs:
        acc[...] = jnp.zeros_like(acc)
    row, lane = iotas((8, 128))
    low, top = lane < TV, row < 4

    loads[0].wait()
    loads[1].wait()
    line, place = iotas((lines, 128))
    live = 128 * line + place < count[0]
    rays8, voxels8 = ray[...] * 8, voxel[...] * 8
    index_out[0:lines, :] = voxels8
    index_out[lines:2 * lines, :] = jnp.where(live, rays8, rays * 8)
    index_out[2 * lines:3 * lines, :] = rays8
    index_out[3 * lines:4 * lines, :] = jnp.where(live, voxels8, voxel_tiles * 8)
    to_scalar = pltpu.make_async_copy(index_out, index, sems.at[4])
    to_scalar.start()

    loads[2].wait()
    field = vol[...]
    double[0:4, :] = field
    double[4:8, :] = field
    for j in range(width // 128):
        x = double[:, 128 * j:128 * j + 128].astype(jnp.bfloat16).astype(jnp.float32)
        turned = pltpu.roll(x, TV, axis=1)
        zero = jnp.zeros_like(x)
        first = jnp.where(jnp.logical_and(top, low), x, zero)
        second = jnp.where(jnp.logical_and(top, low), turned, zero)
        other = jnp.logical_not(jnp.logical_or(top, low))
        table[16 * j:16 * j + 8, :] = jnp.where(other, turned, first)
        table[16 * j + 8:16 * j + 16, :] = jnp.where(other, x, second)

    loads[3].wait()
    mine = (lax.axis_index("tile") * lax.axis_size("rep") + lax.axis_index("rep")) * owned
    for r in range(owned):
        acc0[pl.ds(pl.multiple_of((mine + r) * 8, 8), 4), :] = -sino[r]
    to_scalar.wait()
    per = slots // WAITS
    for g in range(slots // GROUP):
        if GROUP * g % per == 0:
            part = GROUP * g // per * CHUNKS // WAITS
            for copy in copies[part:part + CHUNKS // WAITS]:
                copy.wait()
        n = GROUP * g
        at = [divmod(n + i, 128) for i in range(GROUP)]
        picked = [table[rows8(index[line, place]), :] for line, place in at]
        pairs = [jnp.where(top, picked[2 * i], picked[2 * i + 1]) for i in range(2)]
        zero = jnp.zeros_like(pairs[0])
        left = jnp.concatenate([pairs[0], zero], axis=0).astype(jnp.bfloat16)
        right = jnp.concatenate([zero, pairs[1]], axis=0).astype(jnp.bfloat16)
        sums = jnp.dot(
            jnp.concatenate([left, right], axis=1),
            tiles[n:n + GROUP].reshape(GROUP * TV, TR),
            preferred_element_type=jnp.float32,
        )
        add_rows(
            accs,
            [index[lines + line, place] for line, place in at],
            [sums[0:8], sums[0:8], sums[8:16], sums[8:16]],
        )
    for q in range(rays // 4):
        halves = []
        for r in (4 * q, 4 * q + 2):
            at = [slice(8 * (r + k), 8 * (r + k) + 8) for k in range(2)]
            even = [acc0[at[k], :] + acc2[at[k], :] for k in range(2)]
            odd = [acc1[at[k], :] + acc3[at[k], :] for k in range(2)]
            halves.append(
                jnp.where(top, even[0], odd[1])
                + pltpu.roll(jnp.where(top, even[1], odd[0]), 4, axis=0)
            )
        partial_out[16 * q:16 * q + 16, :] = jnp.concatenate(halves, axis=0).astype(jnp.bfloat16)


def local_kernel(rho, vol, split, dual, base_out, edge_out, first_out, scale_out):
    factor = TAU * rho[0]
    limit = 1.0 / rho[0]
    row, lane = iotas((8, 128))
    row_mask, col_mask = plane_masks(lane)
    for j in range(vol.shape[1] // 128):
        at = slice(128 * j, 128 * j + 128)
        field = vol[:, at]
        x = jnp.concatenate([field] * 2, axis=0)
        gap = [
            jnp.concatenate([dual[k, :, at] - split[k, :, at]] * 2, axis=0) for k in range(3)
        ]
        depth = jnp.where(row < 3, pltpu.roll(x, 7, axis=0) - x + gap[0], 0.0)
        across = jnp.where(row_mask, pltpu.roll(x, 120, axis=1) - x + gap[1], 0.0)
        along = jnp.where(col_mask, pltpu.roll(x, 127, axis=1) - x + gap[2], 0.0)
        adjoint = pltpu.roll(depth, 1, axis=0) - depth
        adjoint += jnp.where((lane % TV) >= 8, pltpu.roll(across, 8, axis=1), 0.0) - across
        adjoint += jnp.where(lane % 8 >= 1, pltpu.roll(along, 1, axis=1), 0.0) - along
        base_out[:, at] = (x - factor * adjoint)[0:4]
        edge_out[:, at] = (x - gap[0])[3:4]
        first_out[:, at] = field[0:1]
        scale_out[0:1, at] = jnp.full((1, 128), limit, jnp.float32)
        scale_out[1:2, at] = jnp.full((1, 128), factor, jnp.float32)


def backward_kernel(
    indices, tiles, part, moved, grad_out,
    index, table, acc0, acc1, acc2, acc3, sem,
):
    slots = tiles.shape[0]
    lines = indices.shape[0] // 4
    rays = table.shape[0] // 8
    voxel_tiles = acc0.shape[0] // 8 - 1
    to_scalar = pltpu.make_async_copy(indices, index, sem)
    to_scalar.start()
    accs = (acc0, acc1, acc2, acc3)
    for acc in accs:
        acc[...] = jnp.zeros_like(acc)
    row, lane = iotas((8, 128))
    low, top = lane < TV, row < 4
    for q in range(rays // 4):
        at = slice(16 * q, 16 * q + 16)
        total = part[at, :].astype(jnp.float32) + moved[at, :].astype(jnp.float32)
        for k in range(2):
            x = total[8 * k:8 * k + 8]
            turned = pltpu.roll(x, 4, axis=0)
            r = 8 * (4 * q + 2 * k)
            table[r:r + 8, :] = jnp.where(top, x, turned)
            table[r + 8:r + 16, :] = jnp.where(top, turned, x)

    to_scalar.wait()
    for g in range(slots // GROUP):
        n = GROUP * g
        at = [divmod(n + i, 128) for i in range(GROUP)]
        picked = [table[rows8(index[2 * lines + line, place]), :] for line, place in at]
        pairs = [jnp.where(top, picked[2 * i], picked[2 * i + 1]) for i in range(2)]
        zero = jnp.zeros_like(pairs[0])
        left = jnp.concatenate([pairs[0], zero], axis=0).astype(jnp.bfloat16)
        right = jnp.concatenate([zero, pairs[1]], axis=0).astype(jnp.bfloat16)
        back = lax.dot_general(
            jnp.concatenate([left, right], axis=1),
            jnp.concatenate(
                [tiles[n + 2 * i:n + 2 * i + 2].reshape(2 * TV, TR) for i in range(2)], axis=1
            ),
            (((1,), (1,)), ((), ())),
            preferred_element_type=jnp.float32,
        )
        add_rows(
            accs,
            [index[3 * lines + line, place] for line, place in at],
            [back[0:8], back[0:8], back[8:16], back[8:16]],
        )
    for j in range(voxel_tiles // 2):
        at = [slice(16 * j + 8 * k, 16 * j + 8 * k + 8) for k in range(2)]
        even = [acc0[at[k], :] + acc2[at[k], :] for k in range(2)]
        odd = [acc1[at[k], :] + acc3[at[k], :] for k in range(2)]
        turned = pltpu.roll(jnp.where(top, even[1], odd[0]), TV, axis=1)
        both = jnp.where(top == low, jnp.where(top, even[0], odd[1]), turned)
        grad_out[:, 128 * j:128 * j + 128] = (both + pltpu.roll(both, 4, axis=0))[0:4]


def update_kernel(
    grad, grad_other, from_next, from_previous, base, edge, first, dual, scales,
    new_volume, new_split, new_dual,
):
    slab, slabs = lax.axis_index("slab"), lax.axis_size("slab")
    row, lane = iotas((8, 128))
    short = lax.broadcasted_iota(jnp.int32, (4, 128), 0)
    row_mask, col_mask = plane_masks(lane)
    inner = jnp.logical_or(row < 3, slab < slabs - 1)
    for j in range(dual.shape[2] // 128):
        at = slice(128 * j, 128 * j + 128)
        limit, factor = scales[0:1, at], scales[1:2, at]
        above = jnp.where(slab == slabs - 1, 0.0, factor * (from_next[1:2, at] - edge[:, at]))
        below = jnp.where(slab == 0, 0.0, factor * (first[:, at] - from_previous[0:1, at]))
        own = base[:, at] - TAU * (grad[:, at] + grad_other[:, at])
        own += jnp.where(short == 0, -below, jnp.where(short == 3, above, 0.0))
        ahead = from_next[0:1, at] - above
        field = jnp.where(row < 4, jnp.concatenate([own] * 2, axis=0), ahead)
        new_volume[:, at] = own
        steps = (
            jnp.where(inner, pltpu.roll(field, 7, axis=0) - field, 0.0),
            jnp.where(row_mask, pltpu.roll(field, 120, axis=1) - field, 0.0),
            jnp.where(col_mask, pltpu.roll(field, 127, axis=1) - field, 0.0),
        )
        for k in range(3):
            mixed = steps[k][0:4] + dual[k, :, at]
            clipped = jnp.clip(mixed, -limit, limit)
            new_dual[k, :, at] = clipped
            new_split[k, :, at] = mixed - clipped


def vmem():
    return pl.BlockSpec(memory_space=pltpu.VMEM)


def smem():
    return pl.BlockSpec(memory_space=pltpu.SMEM)


def hbm():
    return pl.BlockSpec(memory_space=pltpu.HBM)


def params():
    return pltpu.CompilerParams(vmem_limit_bytes=VMEM_LIMIT)


def shards(
    volume, split_var, dual_var, sinogram, proj_tiles, ray_index, voxel_index, tile_count, rho
):
    f32, bf16 = jnp.float32, jnp.bfloat16
    slices, width = volume.shape
    slots = ray_index.shape[0]
    owned = sinogram.shape[0]
    group = lax.axis_size(("tile", "rep"))
    reps = lax.axis_size("rep")
    slabs = lax.axis_size("slab")
    rays = owned * group
    voxel_tiles = width // TV
    lines = slots // 128
    ray_index, voxel_index = ray_index.reshape(lines, 128), voxel_index.reshape(lines, 128)
    sources = [
        pltpu.with_memory_space_constraint(x, pltpu.HBM)
        for x in (ray_index, voxel_index, volume, sinogram, proj_tiles)
    ]

    partial, indices, tiles = pl.pallas_call(
        forward_kernel,
        out_shape=(
            jax.ShapeDtypeStruct((rays * slices, TR), bf16),
            jax.ShapeDtypeStruct((4 * lines, 128), jnp.int32),
            jax.ShapeDtypeStruct(proj_tiles.shape, bf16),
        ),
        in_specs=[smem()] + [hbm()] * 5,
        out_specs=(vmem(),) * 3,
        scratch_shapes=[
            pltpu.VMEM((lines, 128), jnp.int32),
            pltpu.VMEM((lines, 128), jnp.int32),
            pltpu.SMEM((4 * lines, 128), jnp.int32),
            pltpu.VMEM((slices, width), f32),
            pltpu.VMEM(sinogram.shape, f32),
            pltpu.VMEM((8, width), f32),
            pltpu.VMEM((voxel_tiles * 8, 128), f32),
        ]
        + [pltpu.VMEM((rays * 8 + 8, 128), f32)] * 4
        + [pltpu.SemaphoreType.DMA((5,)), pltpu.SemaphoreType.DMA((CHUNKS,))],
        compiler_params=params(),
        name="forward",
    )(tile_count, *sources)

    base, edge, first, scales = pl.pallas_call(
        local_kernel,
        out_shape=(
            jax.ShapeDtypeStruct((slices, width), f32),
            jax.ShapeDtypeStruct((1, width), f32),
            jax.ShapeDtypeStruct((1, width), f32),
            jax.ShapeDtypeStruct((2, width), f32),
        ),
        in_specs=[smem()] + [vmem()] * 3,
        out_specs=(vmem(),) * 4,
        compiler_params=params(),
        name="local",
    )(rho, volume, split_var, dual_var)

    swap = [(i, i ^ 1) for i in range(reps)]
    moved = lax.ppermute(partial, "rep", swap)
    step = reps
    while step < group:
        partial = (partial.astype(f32) + moved.astype(f32)).astype(bf16)
        moved = lax.ppermute(
            partial, ("tile", "rep"), [(i, i ^ (step + 1)) for i in range(group)]
        )
        step *= 2
    moved, base, edge, first, scales = lax.optimization_barrier(
        (moved, base, edge, first, scales)
    )

    grad = pl.pallas_call(
        backward_kernel,
        out_shape=jax.ShapeDtypeStruct((slices, width), f32),
        in_specs=[vmem()] * 4,
        out_specs=vmem(),
        scratch_shapes=[
            pltpu.SMEM((4 * lines, 128), jnp.int32),
            pltpu.VMEM((rays * 8, 128), f32),
        ]
        + [pltpu.VMEM((voxel_tiles * 8 + 8, 128), f32)] * 4
        + [pltpu.SemaphoreType.DMA],
        compiler_params=params(),
        name="backward",
    )(indices, tiles, partial, moved)
    grad_other = lax.ppermute(grad, "rep", swap)
    ahead = jnp.concatenate([base[0:1] - TAU * (grad[0:1] + grad_other[0:1]), first], axis=0)
    behind = jnp.concatenate([edge, edge], axis=0)
    if slabs == 2:
        halo = jnp.where(lax.axis_index("slab") == 0, behind, ahead)
        from_next = from_previous = lax.ppermute(
            halo, ("slab", "rep"), [(i, i ^ 3) for i in range(2 * reps)]
        )
    else:
        from_next = lax.ppermute(ahead, "slab", [(i, i - 1) for i in range(1, slabs)])
        from_previous = lax.ppermute(behind, "slab", [(i - 1, i) for i in range(1, slabs)])

    return pl.pallas_call(
        update_kernel,
        out_shape=(
            jax.ShapeDtypeStruct((slices, width), f32),
            jax.ShapeDtypeStruct((3, slices, width), f32),
            jax.ShapeDtypeStruct((3, slices, width), f32),
        ),
        in_specs=[vmem()] * 9,
        out_specs=(vmem(), vmem(), vmem()),
        compiler_params=params(),
        name="update",
    )(grad, grad_other, from_next, from_previous, base, edge, first, dual_var, scales)


def solution(mesh):
    return jax.shard_map(
        shards,
        mesh=mesh,
        in_specs=(
            P(("parts", "slab"), "tile"),
            P(None, ("parts", "slab"), "tile"),
            P(None, ("parts", "slab"), "tile"),
            P(("tile", "rep"), ("parts", "slab"), None),
            P(("tile", "rep"), None, None),
            P(("tile", "rep")),
            P(("tile", "rep")),
            P(("tile", "rep")),
            P(),
        ),
        out_specs=(
            P(("parts", "slab"), "tile"),
            P(None, ("parts", "slab"), "tile"),
            P(None, ("parts", "slab"), "tile"),
        ),
        check_vma=False,
    )
```

```python
import jax
import jax.numpy as jnp
from jax import lax
from jax.experimental import pallas as pl
from jax.experimental.pallas import tpu as pltpu
from jax.sharding import PartitionSpec as P

TV = 64
TR = 128
TAU = 0.5
GROUP = 4
CHUNKS = 2
BATCH = 2
VMEM_LIMIT = 16 * 1024 * 1024


def iotas(shape):
    row = lax.broadcasted_iota(jnp.int32, shape, 0)
    lane = lax.broadcasted_iota(jnp.int32, shape, 1)
    return row, lane


def start_tiles(proj_hbm, tiles, sems):
    per = proj_hbm.shape[0] // CHUNKS
    copies = []
    for c in range(CHUNKS):
        part = pl.ds(c * per, per)
        copy = pltpu.make_async_copy(proj_hbm.at[part], tiles.at[part], sems.at[c])
        copy.start()
        copies.append(copy)
    return copies


def plane_masks(lane):
    return (lane % TV) // 8 < 7, lane % 8 < 7


def rows8(start):
    return pl.ds(pl.multiple_of(start, 8), 8)


def add_rows(accs, starts, values):
    held = [acc[rows8(start), :] for acc, start in zip(accs, starts)]
    for acc, start, old, value in zip(accs, starts, held, values):
        acc[rows8(start), :] = old + value


def sum_of(accs, at):
    total = accs[0][at, :]
    for acc in accs[1:]:
        total += acc[at, :]
    return total


def forward_kernel(
    count, ray_hbm, voxel_hbm, vol_hbm, sino_hbm, proj_hbm,
    partial_out, index_out, tiles,
    ray, voxel, index, vol, sino, double, table, *rest,
):
    accs, (sems, tile_sems) = rest[:-2], rest[-2:]
    acc0 = accs[0]
    slots = proj_hbm.shape[0]
    lines = ray.shape[0]
    rays = acc0.shape[0] // 8 - 1
    voxel_tiles = table.shape[0] // 8
    owned = sino.shape[0]
    width = vol.shape[1]
    loads = [
        pltpu.make_async_copy(source, target, sems.at[i])
        for i, (source, target) in enumerate(
            [(voxel_hbm, voxel), (ray_hbm, ray), (vol_hbm, vol), (sino_hbm, sino)]
        )
    ]
    for load in loads:
        load.start()
    copies = start_tiles(proj_hbm, tiles, tile_sems)
    for acc in accs:
        acc[...] = jnp.zeros_like(acc)
    row, lane = iotas((8, 128))
    low, top = lane < TV, row < 4

    loads[0].wait()
    loads[1].wait()
    line, place = iotas((lines, 128))
    live = 128 * line + place < count[0]
    rays8, voxels8 = ray[...] * 8, voxel[...] * 8
    index_out[0:lines, :] = voxels8
    index_out[lines:2 * lines, :] = jnp.where(live, rays8, rays * 8)
    index_out[2 * lines:3 * lines, :] = rays8
    index_out[3 * lines:4 * lines, :] = jnp.where(live, voxels8, voxel_tiles * 8)
    to_scalar = pltpu.make_async_copy(index_out, index, sems.at[4])
    to_scalar.start()

    loads[2].wait()
    field = vol[...]
    double[0:4, :] = field
    double[4:8, :] = field
    for j in range(width // 128):
        x = double[:, 128 * j:128 * j + 128].astype(jnp.bfloat16).astype(jnp.float32)
        turned = pltpu.roll(x, TV, axis=1)
        zero = jnp.zeros_like(x)
        first = jnp.where(jnp.logical_and(top, low), x, zero)
        second = jnp.where(jnp.logical_and(top, low), turned, zero)
        other = jnp.logical_not(jnp.logical_or(top, low))
        table[16 * j:16 * j + 8, :] = jnp.where(other, turned, first)
        table[16 * j + 8:16 * j + 16, :] = jnp.where(other, x, second)

    loads[3].wait()
    mine = (lax.axis_index("tile") * lax.axis_size("rep") + lax.axis_index("rep")) * owned
    for r in range(owned):
        acc0[pl.ds(pl.multiple_of((mine + r) * 8, 8), 4), :] = -sino[r]
    to_scalar.wait()
    per = slots // CHUNKS
    for first in range(0, slots, GROUP * BATCH):
        if first % per == 0:
            copies[first // per].wait()
        starts, values = [], []
        for n in range(first, first + GROUP * BATCH, GROUP):
            at = [divmod(n + i, 128) for i in range(GROUP)]
            picked = [table[rows8(index[line, place]), :] for line, place in at]
            pairs = [jnp.where(top, picked[2 * i], picked[2 * i + 1]) for i in range(2)]
            zero = jnp.zeros_like(pairs[0])
            left = jnp.concatenate([pairs[0], zero], axis=0).astype(jnp.bfloat16)
            right = jnp.concatenate([zero, pairs[1]], axis=0).astype(jnp.bfloat16)
            sums = jnp.dot(
                jnp.concatenate([left, right], axis=1),
                tiles[n:n + GROUP].reshape(GROUP * TV, TR),
                preferred_element_type=jnp.float32,
            )
            starts += [index[lines + line, place] for line, place in at]
            values += [sums[0:8], sums[0:8], sums[8:16], sums[8:16]]
        add_rows(accs, starts, values)
    for q in range(rays // 4):
        halves = []
        for r in (4 * q, 4 * q + 2):
            at = [slice(8 * (r + k), 8 * (r + k) + 8) for k in range(2)]
            even = [sum_of(accs[0::2], at[k]) for k in range(2)]
            odd = [sum_of(accs[1::2], at[k]) for k in range(2)]
            halves.append(
                jnp.where(top, even[0], odd[1])
                + pltpu.roll(jnp.where(top, even[1], odd[0]), 4, axis=0)
            )
        partial_out[16 * q:16 * q + 16, :] = jnp.concatenate(halves, axis=0).astype(jnp.bfloat16)


def local_kernel(rho, vol, split, dual, base_out, edge_out, first_out, scale_out):
    factor = TAU * rho[0]
    limit = 1.0 / rho[0]
    row, lane = iotas((8, 128))
    row_mask, col_mask = plane_masks(lane)
    for j in range(vol.shape[1] // 128):
        at = slice(128 * j, 128 * j + 128)
        field = vol[:, at]
        x = jnp.concatenate([field] * 2, axis=0)
        gap = [
            jnp.concatenate([dual[k, :, at] - split[k, :, at]] * 2, axis=0) for k in range(3)
        ]
        depth = jnp.where(row < 3, pltpu.roll(x, 7, axis=0) - x + gap[0], 0.0)
        across = jnp.where(row_mask, pltpu.roll(x, 120, axis=1) - x + gap[1], 0.0)
        along = jnp.where(col_mask, pltpu.roll(x, 127, axis=1) - x + gap[2], 0.0)
        adjoint = pltpu.roll(depth, 1, axis=0) - depth
        adjoint += jnp.where((lane % TV) >= 8, pltpu.roll(across, 8, axis=1), 0.0) - across
        adjoint += jnp.where(lane % 8 >= 1, pltpu.roll(along, 1, axis=1), 0.0) - along
        base_out[:, at] = (x - factor * adjoint)[0:4]
        edge_out[:, at] = (x - gap[0])[3:4]
        first_out[:, at] = field[0:1]
        scale_out[0:1, at] = jnp.full((1, 128), limit, jnp.float32)
        scale_out[1:2, at] = jnp.full((1, 128), factor, jnp.float32)


def backward_kernel(
    indices, tiles, part, moved, grad_out,
    index, table, *rest,
):
    accs, sem = rest[:-1], rest[-1]
    acc0 = accs[0]
    slots = tiles.shape[0]
    lines = indices.shape[0] // 4
    rays = table.shape[0] // 8
    voxel_tiles = acc0.shape[0] // 8 - 1
    to_scalar = pltpu.make_async_copy(indices, index, sem)
    to_scalar.start()
    for acc in accs:
        acc[...] = jnp.zeros_like(acc)
    row, lane = iotas((8, 128))
    low, top = lane < TV, row < 4
    for q in range(rays // 4):
        at = slice(16 * q, 16 * q + 16)
        total = part[at, :].astype(jnp.float32) + moved[at, :].astype(jnp.float32)
        for k in range(2):
            x = total[8 * k:8 * k + 8]
            turned = pltpu.roll(x, 4, axis=0)
            r = 8 * (4 * q + 2 * k)
            table[r:r + 8, :] = jnp.where(top, x, turned)
            table[r + 8:r + 16, :] = jnp.where(top, turned, x)

    to_scalar.wait()
    for first in range(0, slots, GROUP * BATCH):
        starts, values = [], []
        for n in range(first, first + GROUP * BATCH, GROUP):
            at = [divmod(n + i, 128) for i in range(GROUP)]
            picked = [table[rows8(index[2 * lines + line, place]), :] for line, place in at]
            rows = jnp.concatenate(
                [jnp.where(top, picked[2 * i], picked[2 * i + 1]) for i in range(2)], axis=0
            )
            back = lax.dot_general(
                rows.astype(jnp.bfloat16),
                tiles[n:n + GROUP].reshape(GROUP * TV, TR),
                (((1,), (1,)), ((), ())),
                preferred_element_type=jnp.float32,
            )
            starts += [index[3 * lines + line, place] for line, place in at]
            values += [back[8 * k:8 * k + 8, 128 * k:128 * k + 128] for k in (0, 0, 1, 1)]
        add_rows(accs, starts, values)
    for j in range(voxel_tiles // 2):
        at = [slice(16 * j + 8 * k, 16 * j + 8 * k + 8) for k in range(2)]
        even = [sum_of(accs[0::2], at[k]) for k in range(2)]
        odd = [sum_of(accs[1::2], at[k]) for k in range(2)]
        turned = pltpu.roll(jnp.where(top, even[1], odd[0]), TV, axis=1)
        both = jnp.where(top == low, jnp.where(top, even[0], odd[1]), turned)
        grad_out[:, 128 * j:128 * j + 128] = (both + pltpu.roll(both, 4, axis=0))[0:4]


def update_kernel(
    grad, grad_other, from_next, from_previous, base, edge, first, dual, scales,
    new_volume, new_split, new_dual,
):
    slab, slabs = lax.axis_index("slab"), lax.axis_size("slab")
    row, lane = iotas((8, 128))
    short = lax.broadcasted_iota(jnp.int32, (4, 128), 0)
    row_mask, col_mask = plane_masks(lane)
    inner = jnp.logical_or(row < 3, slab < slabs - 1)
    for j in range(dual.shape[2] // 128):
        at = slice(128 * j, 128 * j + 128)
        limit, factor = scales[0:1, at], scales[1:2, at]
        above = jnp.where(slab == slabs - 1, 0.0, factor * (from_next[1:2, at] - edge[:, at]))
        below = jnp.where(slab == 0, 0.0, factor * (first[:, at] - from_previous[0:1, at]))
        own = base[:, at] - TAU * (grad[:, at] + grad_other[:, at])
        own += jnp.where(short == 0, -below, jnp.where(short == 3, above, 0.0))
        ahead = from_next[0:1, at] - above
        field = jnp.where(row < 4, jnp.concatenate([own] * 2, axis=0), ahead)
        new_volume[:, at] = own
        steps = (
            jnp.where(inner, pltpu.roll(field, 7, axis=0) - field, 0.0),
            jnp.where(row_mask, pltpu.roll(field, 120, axis=1) - field, 0.0),
            jnp.where(col_mask, pltpu.roll(field, 127, axis=1) - field, 0.0),
        )
        for k in range(3):
            mixed = steps[k][0:4] + dual[k, :, at]
            clipped = jnp.clip(mixed, -limit, limit)
            new_dual[k, :, at] = clipped
            new_split[k, :, at] = mixed - clipped


def vmem():
    return pl.BlockSpec(memory_space=pltpu.VMEM)


def smem():
    return pl.BlockSpec(memory_space=pltpu.SMEM)


def hbm():
    return pl.BlockSpec(memory_space=pltpu.HBM)


def params():
    return pltpu.CompilerParams(vmem_limit_bytes=VMEM_LIMIT)


def shards(
    volume, split_var, dual_var, sinogram, proj_tiles, ray_index, voxel_index, tile_count, rho
):
    f32, bf16 = jnp.float32, jnp.bfloat16
    slices, width = volume.shape
    slots = ray_index.shape[0]
    owned = sinogram.shape[0]
    group = lax.axis_size(("tile", "rep"))
    reps = lax.axis_size("rep")
    slabs = lax.axis_size("slab")
    rays = owned * group
    voxel_tiles = width // TV
    lines = slots // 128
    ray_index, voxel_index = ray_index.reshape(lines, 128), voxel_index.reshape(lines, 128)
    sources = [
        pltpu.with_memory_space_constraint(x, pltpu.HBM)
        for x in (ray_index, voxel_index, volume, sinogram, proj_tiles)
    ]

    partial, indices, tiles = pl.pallas_call(
        forward_kernel,
        out_shape=(
            jax.ShapeDtypeStruct((rays * slices, TR), bf16),
            jax.ShapeDtypeStruct((4 * lines, 128), jnp.int32),
            jax.ShapeDtypeStruct(proj_tiles.shape, bf16),
        ),
        in_specs=[smem()] + [hbm()] * 5,
        out_specs=(vmem(),) * 3,
        scratch_shapes=[
            pltpu.VMEM((lines, 128), jnp.int32),
            pltpu.VMEM((lines, 128), jnp.int32),
            pltpu.SMEM((4 * lines, 128), jnp.int32),
            pltpu.VMEM((slices, width), f32),
            pltpu.VMEM(sinogram.shape, f32),
            pltpu.VMEM((8, width), f32),
            pltpu.VMEM((voxel_tiles * 8, 128), f32),
        ]
        + [pltpu.VMEM((rays * 8 + 8, 128), f32)] * (GROUP * BATCH)
        + [pltpu.SemaphoreType.DMA((5,)), pltpu.SemaphoreType.DMA((CHUNKS,))],
        compiler_params=params(),
        name="forward",
    )(tile_count, *sources)

    base, edge, first, scales = pl.pallas_call(
        local_kernel,
        out_shape=(
            jax.ShapeDtypeStruct((slices, width), f32),
            jax.ShapeDtypeStruct((1, width), f32),
            jax.ShapeDtypeStruct((1, width), f32),
            jax.ShapeDtypeStruct((2, width), f32),
        ),
        in_specs=[smem()] + [vmem()] * 3,
        out_specs=(vmem(),) * 4,
        compiler_params=params(),
        name="local",
    )(rho, volume, split_var, dual_var)

    swap = [(i, i ^ 1) for i in range(reps)]
    moved = lax.ppermute(partial, "rep", swap)
    step = reps
    while step < group:
        partial = (partial.astype(f32) + moved.astype(f32)).astype(bf16)
        moved = lax.ppermute(
            partial, ("tile", "rep"), [(i, i ^ (step + 1)) for i in range(group)]
        )
        step *= 2
    moved, base, edge, first, scales = lax.optimization_barrier(
        (moved, base, edge, first, scales)
    )

    grad = pl.pallas_call(
        backward_kernel,
        out_shape=jax.ShapeDtypeStruct((slices, width), f32),
        in_specs=[vmem()] * 4,
        out_specs=vmem(),
        scratch_shapes=[
            pltpu.SMEM((4 * lines, 128), jnp.int32),
            pltpu.VMEM((rays * 8, 128), f32),
        ]
        + [pltpu.VMEM((voxel_tiles * 8 + 8, 128), f32)] * (GROUP * BATCH)
        + [pltpu.SemaphoreType.DMA],
        compiler_params=params(),
        name="backward",
    )(indices, tiles, partial, moved)
    grad_other = lax.ppermute(grad, "rep", swap)
    ahead = jnp.concatenate([base[0:1] - TAU * (grad[0:1] + grad_other[0:1]), first], axis=0)
    behind = jnp.concatenate([edge, edge], axis=0)
    if slabs == 2:
        halo = jnp.where(lax.axis_index("slab") == 0, behind, ahead)
        from_next = from_previous = lax.ppermute(
            halo, ("slab", "rep"), [(i, i ^ 3) for i in range(2 * reps)]
        )
    else:
        from_next = lax.ppermute(ahead, "slab", [(i, i - 1) for i in range(1, slabs)])
        from_previous = lax.ppermute(behind, "slab", [(i - 1, i) for i in range(1, slabs)])

    return pl.pallas_call(
        update_kernel,
        out_shape=(
            jax.ShapeDtypeStruct((slices, width), f32),
            jax.ShapeDtypeStruct((3, slices, width), f32),
            jax.ShapeDtypeStruct((3, slices, width), f32),
        ),
        in_specs=[vmem()] * 9,
        out_specs=(vmem(), vmem(), vmem()),
        compiler_params=params(),
        name="update",
    )(grad, grad_other, from_next, from_previous, base, edge, first, dual_var, scales)


def solution(mesh):
    return jax.shard_map(
        shards,
        mesh=mesh,
        in_specs=(
            P(("parts", "slab"), "tile"),
            P(None, ("parts", "slab"), "tile"),
            P(None, ("parts", "slab"), "tile"),
            P(("tile", "rep"), ("parts", "slab"), None),
            P(("tile", "rep"), None, None),
            P(("tile", "rep")),
            P(("tile", "rep")),
            P(("tile", "rep")),
            P(),
        ),
        out_specs=(
            P(("parts", "slab"), "tile"),
            P(None, ("parts", "slab"), "tile"),
            P(None, ("parts", "slab"), "tile"),
        ),
        check_vma=False,
    )
```

```python
import jax
import jax.numpy as jnp
from jax import lax
from jax.experimental import pallas as pl
from jax.experimental.pallas import tpu as pltpu
from jax.sharding import PartitionSpec as P

TV = 64
TR = 128
TAU = 0.5
GROUP = 4
CHUNKS = 2
VMEM_LIMIT = 16 * 1024 * 1024


def iotas(shape):
    row = lax.broadcasted_iota(jnp.int32, shape, 0)
    lane = lax.broadcasted_iota(jnp.int32, shape, 1)
    return row, lane


def start_tiles(proj_hbm, tiles, sems):
    per = proj_hbm.shape[0] // CHUNKS
    copies = []
    for c in range(CHUNKS):
        part = pl.ds(c * per, per)
        copy = pltpu.make_async_copy(proj_hbm.at[part], tiles.at[part], sems.at[c])
        copy.start()
        copies.append(copy)
    return copies


def plane_masks(lane):
    return (lane % TV) // 8 < 7, lane % 8 < 7


def rows8(start):
    return pl.ds(pl.multiple_of(start, 8), 8)


def add_rows(accs, starts, values):
    held = [acc[rows8(start), :] for acc, start in zip(accs, starts)]
    for acc, start, old, value in zip(accs, starts, held, values):
        acc[rows8(start), :] = old + value


def forward_kernel(
    count, ray_hbm, voxel_hbm, vol_hbm, sino_hbm, proj_hbm,
    partial_out, index_out, tiles,
    ray, voxel, index, vol, sino, double, table, acc0, acc1, acc2, acc3,
    sems, tile_sems,
):
    slots = proj_hbm.shape[0]
    lines = ray.shape[0]
    rays = acc0.shape[0] // 8 - 1
    voxel_tiles = table.shape[0] // 8
    owned = sino.shape[0]
    width = vol.shape[1]
    loads = [
        pltpu.make_async_copy(source, target, sems.at[i])
        for i, (source, target) in enumerate(
            [(voxel_hbm, voxel), (ray_hbm, ray), (vol_hbm, vol), (sino_hbm, sino)]
        )
    ]
    for load in loads:
        load.start()
    copies = start_tiles(proj_hbm, tiles, tile_sems)
    accs = (acc0, acc1, acc2, acc3)
    for acc in accs:
        acc[...] = jnp.zeros_like(acc)
    row, lane = iotas((8, 128))
    low, top = lane < TV, row < 4

    loads[0].wait()
    loads[1].wait()
    line, place = iotas((lines, 128))
    live = 128 * line + place < count[0]
    rays8, voxels8 = ray[...] * 8, voxel[...] * 8
    index_out[0:lines, :] = voxels8
    index_out[lines:2 * lines, :] = jnp.where(live, rays8, rays * 8)
    index_out[2 * lines:3 * lines, :] = rays8
    index_out[3 * lines:4 * lines, :] = jnp.where(live, voxels8, voxel_tiles * 8)
    to_scalar = pltpu.make_async_copy(index_out, index, sems.at[4])
    to_scalar.start()

    loads[2].wait()
    field = vol[...]
    double[0:4, :] = field
    double[4:8, :] = field
    for j in range(width // 128):
        x = double[:, 128 * j:128 * j + 128].astype(jnp.bfloat16).astype(jnp.float32)
        turned = pltpu.roll(x, TV, axis=1)
        zero = jnp.zeros_like(x)
        first = jnp.where(jnp.logical_and(top, low), x, zero)
        second = jnp.where(jnp.logical_and(top, low), turned, zero)
        other = jnp.logical_not(jnp.logical_or(top, low))
        table[16 * j:16 * j + 8, :] = jnp.where(other, turned, first)
        table[16 * j + 8:16 * j + 16, :] = jnp.where(other, x, second)

    loads[3].wait()
    mine = (lax.axis_index("tile") * lax.axis_size("rep") + lax.axis_index("rep")) * owned
    for r in range(owned):
        acc0[pl.ds(pl.multiple_of((mine + r) * 8, 8), 4), :] = -sino[r]
    to_scalar.wait()
    per = slots // CHUNKS
    for g in range(slots // GROUP):
        if GROUP * g % per == 0:
            copies[GROUP * g // per].wait()
        n = GROUP * g
        at = [divmod(n + i, 128) for i in range(GROUP)]
        picked = [table[rows8(index[line, place]), :] for line, place in at]
        pairs = [jnp.where(top, picked[2 * i], picked[2 * i + 1]) for i in range(2)]
        zero = jnp.zeros_like(pairs[0])
        left = jnp.concatenate([pairs[0], zero], axis=0).astype(jnp.bfloat16)
        right = jnp.concatenate([zero, pairs[1]], axis=0).astype(jnp.bfloat16)
        sums = jnp.dot(
            jnp.concatenate([left, right], axis=1),
            tiles[n:n + GROUP].reshape(GROUP * TV, TR),
            preferred_element_type=jnp.float32,
        )
        add_rows(
            accs,
            [index[lines + line, place] for line, place in at],
            [sums[0:8], sums[0:8], sums[8:16], sums[8:16]],
        )
    for q in range(rays // 4):
        halves = []
        for r in (4 * q, 4 * q + 2):
            at = [slice(8 * (r + k), 8 * (r + k) + 8) for k in range(2)]
            even = [acc0[at[k], :] + acc2[at[k], :] for k in range(2)]
            odd = [acc1[at[k], :] + acc3[at[k], :] for k in range(2)]
            halves.append(
                jnp.where(top, even[0], odd[1])
                + pltpu.roll(jnp.where(top, even[1], odd[0]), 4, axis=0)
            )
        partial_out[16 * q:16 * q + 16, :] = jnp.concatenate(halves, axis=0).astype(jnp.bfloat16)


def edges_kernel(vol, split, dual, edge_out, first_out, halo_out):
    start = lax.axis_index("slab") == 0
    for j in range(vol.shape[1] // 128):
        at = slice(128 * j, 128 * j + 128)
        edge = vol[3:4, at] - dual[0, 3:4, at] + split[0, 3:4, at]
        first = vol[0:1, at]
        edge_out[:, at] = edge
        first_out[:, at] = first
        halo_out[:, at] = jnp.broadcast_to(jnp.where(start, edge, first), (4, 128))


def local_kernel(rho, vol, split, dual, edge, from_next, from_previous, base_out):
    slab, slabs = lax.axis_index("slab"), lax.axis_size("slab")
    factor = TAU * rho[0]
    row, lane = iotas((8, 128))
    row_mask, col_mask = plane_masks(lane)
    for j in range(vol.shape[1] // 128):
        at = slice(128 * j, 128 * j + 128)
        x = jnp.concatenate([vol[:, at]] * 2, axis=0)
        gap = [
            jnp.concatenate([dual[k, :, at] - split[k, :, at]] * 2, axis=0) for k in range(3)
        ]
        above = jnp.where(slab == slabs - 1, 0.0, from_next[0:1, at] - edge[:, at])
        below = jnp.where(slab == 0, 0.0, x[0:1] - from_previous[0:1, at])
        depth = jnp.where(row < 3, pltpu.roll(x, 7, axis=0) - x + gap[0], above)
        across = jnp.where(row_mask, pltpu.roll(x, 120, axis=1) - x + gap[1], 0.0)
        along = jnp.where(col_mask, pltpu.roll(x, 127, axis=1) - x + gap[2], 0.0)
        adjoint = jnp.where(row == 0, below, pltpu.roll(depth, 1, axis=0)) - depth
        adjoint += jnp.where((lane % TV) >= 8, pltpu.roll(across, 8, axis=1), 0.0) - across
        adjoint += jnp.where(lane % 8 >= 1, pltpu.roll(along, 1, axis=1), 0.0) - along
        base_out[:, at] = (x - factor * adjoint)[0:4]


def backward_kernel(
    indices, tiles, part, moved, grad_out,
    index, table, acc0, acc1, acc2, acc3, sem,
):
    slots = tiles.shape[0]
    lines = indices.shape[0] // 4
    rays = table.shape[0] // 8
    voxel_tiles = acc0.shape[0] // 8 - 1
    to_scalar = pltpu.make_async_copy(indices, index, sem)
    to_scalar.start()
    accs = (acc0, acc1, acc2, acc3)
    for acc in accs:
        acc[...] = jnp.zeros_like(acc)
    row, lane = iotas((8, 128))
    low, top = lane < TV, row < 4
    for q in range(rays // 4):
        at = slice(16 * q, 16 * q + 16)
        total = part[at, :].astype(jnp.float32) + moved[at, :].astype(jnp.float32)
        for k in range(2):
            x = total[8 * k:8 * k + 8]
            turned = pltpu.roll(x, 4, axis=0)
            r = 8 * (4 * q + 2 * k)
            table[r:r + 8, :] = jnp.where(top, x, turned)
            table[r + 8:r + 16, :] = jnp.where(top, turned, x)

    to_scalar.wait()
    for g in range(slots // GROUP):
        n = GROUP * g
        at = [divmod(n + i, 128) for i in range(GROUP)]
        picked = [table[rows8(index[2 * lines + line, place]), :] for line, place in at]
        rows = jnp.concatenate(
            [jnp.where(top, picked[2 * i], picked[2 * i + 1]) for i in range(2)], axis=0
        )
        back = lax.dot_general(
            rows.astype(jnp.bfloat16),
            tiles[n:n + GROUP].reshape(GROUP * TV, TR),
            (((1,), (1,)), ((), ())),
            preferred_element_type=jnp.float32,
        )
        add_rows(
            accs,
            [index[3 * lines + line, place] for line, place in at],
            [back[8 * k:8 * k + 8, 128 * k:128 * k + 128] for k in (0, 0, 1, 1)],
        )
    for j in range(voxel_tiles // 2):
        at = [slice(16 * j + 8 * k, 16 * j + 8 * k + 8) for k in range(2)]
        even = [acc0[at[k], :] + acc2[at[k], :] for k in range(2)]
        odd = [acc1[at[k], :] + acc3[at[k], :] for k in range(2)]
        turned = pltpu.roll(jnp.where(top, even[1], odd[0]), TV, axis=1)
        both = jnp.where(top == low, jnp.where(top, even[0], odd[1]), turned)
        grad_out[:, 128 * j:128 * j + 128] = (both + pltpu.roll(both, 4, axis=0))[0:4]


def plane_kernel(
    grad, grad_other, base, dual, limits,
    new_volume, field_out, split_hbm, dual_hbm,
    split, clipped, sems,
):
    row, lane = iotas((4, 128))
    row_mask, col_mask = plane_masks(lane)
    for j in range(dual.shape[2] // 128):
        at = slice(128 * j, 128 * j + 128)
        limit = limits[:, at]
        field = base[:, at] - TAU * (grad[:, at] + grad_other[:, at])
        new_volume[:, at] = field
        field_out[:, at] = field
        x = jnp.concatenate([field] * 2, axis=0)
        steps = (
            jnp.where(row_mask, pltpu.roll(x, 120, axis=1)[0:4] - field, 0.0),
            jnp.where(col_mask, pltpu.roll(x, 127, axis=1)[0:4] - field, 0.0),
        )
        for k in range(2):
            mixed = steps[k] + dual[k + 1, :, at]
            bounded = jnp.clip(mixed, -limit, limit)
            clipped[k, :, at] = bounded
            split[k, :, at] = mixed - bounded
    copies = [
        pltpu.make_async_copy(split, split_hbm.at[pl.ds(1, 2)], sems.at[0]),
        pltpu.make_async_copy(clipped, dual_hbm.at[pl.ds(1, 2)], sems.at[1]),
    ]
    for copy in copies:
        copy.start()
    for copy in copies:
        copy.wait()


def depth_kernel(
    field_in, ahead, dual, limits, split_in, dual_in,
    split_hbm, dual_hbm,
    split, clipped, sems,
):
    del split_in, dual_in
    last = lax.axis_index("slab") == lax.axis_size("slab") - 1
    row, lane = iotas((8, 128))
    inner = jnp.logical_or(row < 3, jnp.logical_not(last))
    for j in range(dual.shape[2] // 128):
        at = slice(128 * j, 128 * j + 128)
        limit = limits[:, at]
        x = jnp.concatenate([field_in[:, at]] * 2, axis=0)
        following = jnp.where(row < 3, pltpu.roll(x, 7, axis=0), ahead[:, at])
        mixed = jnp.where(inner, following - x, 0.0)[0:4] + dual[0, :, at]
        bounded = jnp.clip(mixed, -limit, limit)
        clipped[:, at] = bounded
        split[:, at] = mixed - bounded
    copies = [
        pltpu.make_async_copy(split, split_hbm.at[0], sems.at[0]),
        pltpu.make_async_copy(clipped, dual_hbm.at[0], sems.at[1]),
    ]
    for copy in copies:
        copy.start()
    for copy in copies:
        copy.wait()


def vmem():
    return pl.BlockSpec(memory_space=pltpu.VMEM)


def smem():
    return pl.BlockSpec(memory_space=pltpu.SMEM)


def hbm():
    return pl.BlockSpec(memory_space=pltpu.HBM)


def params():
    return pltpu.CompilerParams(vmem_limit_bytes=VMEM_LIMIT)


def shards(
    volume, split_var, dual_var, sinogram, proj_tiles, ray_index, voxel_index, tile_count, rho
):
    f32, bf16 = jnp.float32, jnp.bfloat16
    slices, width = volume.shape
    slots = ray_index.shape[0]
    owned = sinogram.shape[0]
    group = lax.axis_size(("tile", "rep"))
    reps = lax.axis_size("rep")
    slabs = lax.axis_size("slab")
    rays = owned * group
    voxel_tiles = width // TV
    lines = slots // 128
    ray_index, voxel_index = ray_index.reshape(lines, 128), voxel_index.reshape(lines, 128)
    sources = [
        pltpu.with_memory_space_constraint(x, pltpu.HBM)
        for x in (ray_index, voxel_index, volume, sinogram, proj_tiles)
    ]

    partial, indices, tiles = pl.pallas_call(
        forward_kernel,
        out_shape=(
            jax.ShapeDtypeStruct((rays * slices, TR), bf16),
            jax.ShapeDtypeStruct((4 * lines, 128), jnp.int32),
            jax.ShapeDtypeStruct(proj_tiles.shape, bf16),
        ),
        in_specs=[smem()] + [hbm()] * 5,
        out_specs=(vmem(),) * 3,
        scratch_shapes=[
            pltpu.VMEM((lines, 128), jnp.int32),
            pltpu.VMEM((lines, 128), jnp.int32),
            pltpu.SMEM((4 * lines, 128), jnp.int32),
            pltpu.VMEM((slices, width), f32),
            pltpu.VMEM(sinogram.shape, f32),
            pltpu.VMEM((8, width), f32),
            pltpu.VMEM((voxel_tiles * 8, 128), f32),
        ]
        + [pltpu.VMEM((rays * 8 + 8, 128), f32)] * 4
        + [pltpu.SemaphoreType.DMA((5,)), pltpu.SemaphoreType.DMA((CHUNKS,))],
        compiler_params=params(),
        name="forward",
    )(tile_count, *sources)

    row = jax.ShapeDtypeStruct((1, width), f32)
    edge, first, halo = pl.pallas_call(
        edges_kernel,
        out_shape=(row, row, jax.ShapeDtypeStruct((4, width), f32)),
        in_specs=[vmem()] * 3,
        out_specs=(vmem(),) * 3,
        compiler_params=params(),
        name="edges",
    )(volume, split_var, dual_var)
    across = [(i, i ^ 3) for i in range(2 * reps)]
    down = [(i, i - 1) for i in range(1, slabs)]
    if slabs == 2:
        from_next = from_previous = lax.ppermute(halo, ("slab", "rep"), across)
    else:
        from_next = lax.ppermute(first, "slab", down)
        from_previous = lax.ppermute(edge, "slab", [(i - 1, i) for i in range(1, slabs)])
    swap = [(i, i ^ 1) for i in range(reps)]
    moved = lax.ppermute(partial, "rep", swap)
    step = reps
    while step < group:
        partial = (partial.astype(f32) + moved.astype(f32)).astype(bf16)
        moved = lax.ppermute(
            partial, ("tile", "rep"), [(i, i ^ (step + 1)) for i in range(group)]
        )
        step *= 2
    limits = jnp.broadcast_to((1.0 / rho)[:, None], (1, width))
    moved, from_next, from_previous, limits = lax.optimization_barrier(
        (moved, from_next, from_previous, limits)
    )

    base = pl.pallas_call(
        local_kernel,
        out_shape=jax.ShapeDtypeStruct((slices, width), f32),
        in_specs=[smem()] + [vmem()] * 6,
        out_specs=vmem(),
        compiler_params=params(),
        name="local",
    )(rho, volume, split_var, dual_var, edge, from_next, from_previous)

    grad = pl.pallas_call(
        backward_kernel,
        out_shape=jax.ShapeDtypeStruct((slices, width), f32),
        in_specs=[vmem()] * 4,
        out_specs=vmem(),
        scratch_shapes=[
            pltpu.SMEM((4 * lines, 128), jnp.int32),
            pltpu.VMEM((rays * 8, 128), f32),
        ]
        + [pltpu.VMEM((voxel_tiles * 8 + 8, 128), f32)] * 4
        + [pltpu.SemaphoreType.DMA],
        compiler_params=params(),
        name="backward",
    )(indices, tiles, partial, moved)
    grad_other = lax.ppermute(grad, "rep", swap)
    ahead = base[0:1] - TAU * (grad[0:1] + grad_other[0:1])
    if slabs == 2:
        ahead = lax.ppermute(ahead, ("slab", "rep"), across)
    else:
        ahead = lax.ppermute(ahead, "slab", down)

    whole = jax.ShapeDtypeStruct((slices, width), f32)
    triple = jax.ShapeDtypeStruct((3, slices, width), f32)
    new_volume, field, new_split, new_dual = pl.pallas_call(
        plane_kernel,
        out_shape=(whole, whole, triple, triple),
        in_specs=[vmem()] * 5,
        out_specs=(vmem(), vmem(), hbm(), hbm()),
        scratch_shapes=[pltpu.VMEM((2, slices, width), f32)] * 2
        + [pltpu.SemaphoreType.DMA((2,))],
        compiler_params=params(),
        name="plane",
    )(grad, grad_other, base, dual_var, limits)
    new_split, new_dual = pl.pallas_call(
        depth_kernel,
        out_shape=(triple, triple),
        in_specs=[vmem()] * 4 + [hbm()] * 2,
        out_specs=(hbm(), hbm()),
        scratch_shapes=[pltpu.VMEM((slices, width), f32)] * 2
        + [pltpu.SemaphoreType.DMA((2,))],
        input_output_aliases={4: 0, 5: 1},
        compiler_params=params(),
        name="depth",
    )(field, ahead, dual_var, limits, new_split, new_dual)
    return new_volume, new_split, new_dual


def solution(mesh):
    return jax.shard_map(
        shards,
        mesh=mesh,
        in_specs=(
            P(("parts", "slab"), "tile"),
            P(None, ("parts", "slab"), "tile"),
            P(None, ("parts", "slab"), "tile"),
            P(("tile", "rep"), ("parts", "slab"), None),
            P(("tile", "rep"), None, None),
            P(("tile", "rep")),
            P(("tile", "rep")),
            P(("tile", "rep")),
            P(),
        ),
        out_specs=(
            P(("parts", "slab"), "tile"),
            P(None, ("parts", "slab"), "tile"),
            P(None, ("parts", "slab"), "tile"),
        ),
        check_vma=False,
    )
```

```python
import jax
import jax.numpy as jnp
from jax import lax
from jax.experimental import pallas as pl
from jax.experimental.pallas import tpu as pltpu
from jax.sharding import PartitionSpec as P

TV = 64
TR = 128
TAU = 0.5
GROUP = 4
CHUNKS = 2
VMEM_LIMIT = 16 * 1024 * 1024


def iotas(shape):
    row = lax.broadcasted_iota(jnp.int32, shape, 0)
    lane = lax.broadcasted_iota(jnp.int32, shape, 1)
    return row, lane


def start_tiles(proj_hbm, tiles, sems):
    per = proj_hbm.shape[0] // CHUNKS
    copies = []
    for c in range(CHUNKS):
        part = pl.ds(c * per, per)
        copy = pltpu.make_async_copy(proj_hbm.at[part], tiles.at[part], sems.at[c])
        copy.start()
        copies.append(copy)
    return copies


def plane_masks(lane):
    return (lane % TV) // 8 < 7, lane % 8 < 7


def rows8(start):
    return pl.ds(pl.multiple_of(start, 8), 8)


def add_rows(accs, starts, values):
    held = [acc[rows8(start), :] for acc, start in zip(accs, starts)]
    for acc, start, old, value in zip(accs, starts, held, values):
        acc[rows8(start), :] = old + value


def forward_kernel(
    count, ray_hbm, voxel_hbm, vol_hbm, sino_hbm, proj_hbm,
    partial_out, index_out, tiles,
    ray, voxel, index, vol, sino, double, table, acc0, acc1, acc2, acc3,
    sems, tile_sems,
):
    slots = proj_hbm.shape[0]
    lines = ray.shape[0]
    rays = acc0.shape[0] // 8 - 1
    voxel_tiles = table.shape[0] // 8
    owned = sino.shape[0]
    width = vol.shape[1]
    loads = [
        pltpu.make_async_copy(source, target, sems.at[i])
        for i, (source, target) in enumerate(
            [(voxel_hbm, voxel), (ray_hbm, ray), (vol_hbm, vol), (sino_hbm, sino)]
        )
    ]
    for load in loads:
        load.start()
    copies = start_tiles(proj_hbm, tiles, tile_sems)
    accs = (acc0, acc1, acc2, acc3)
    for acc in accs:
        acc[...] = jnp.zeros_like(acc)
    row, lane = iotas((8, 128))
    low, top = lane < TV, row < 4

    loads[0].wait()
    loads[1].wait()
    line, place = iotas((lines, 128))
    live = 128 * line + place < count[0]
    rays8, voxels8 = ray[...] * 8, voxel[...] * 8
    index_out[0:lines, :] = voxels8
    index_out[lines:2 * lines, :] = jnp.where(live, rays8, rays * 8)
    index_out[2 * lines:3 * lines, :] = rays8
    index_out[3 * lines:4 * lines, :] = jnp.where(live, voxels8, voxel_tiles * 8)
    to_scalar = pltpu.make_async_copy(index_out, index, sems.at[4])
    to_scalar.start()

    loads[2].wait()
    field = vol[...]
    double[0:4, :] = field
    double[4:8, :] = field
    for j in range(width // 128):
        x = double[:, 128 * j:128 * j + 128].astype(jnp.bfloat16).astype(jnp.float32)
        turned = pltpu.roll(x, TV, axis=1)
        zero = jnp.zeros_like(x)
        first = jnp.where(jnp.logical_and(top, low), x, zero)
        second = jnp.where(jnp.logical_and(top, low), turned, zero)
        other = jnp.logical_not(jnp.logical_or(top, low))
        table[16 * j:16 * j + 8, :] = jnp.where(other, turned, first)
        table[16 * j + 8:16 * j + 16, :] = jnp.where(other, x, second)

    loads[3].wait()
    mine = (lax.axis_index("tile") * lax.axis_size("rep") + lax.axis_index("rep")) * owned
    for r in range(owned):
        acc0[pl.ds(pl.multiple_of((mine + r) * 8, 8), 4), :] = -sino[r]
    to_scalar.wait()
    per = slots // CHUNKS
    for g in range(slots // GROUP):
        if GROUP * g % per == 0:
            copies[GROUP * g // per].wait()
        n = GROUP * g
        at = [divmod(n + i, 128) for i in range(GROUP)]
        picked = [table[rows8(index[line, place]), :] for line, place in at]
        pairs = [jnp.where(top, picked[2 * i], picked[2 * i + 1]) for i in range(2)]
        zero = jnp.zeros_like(pairs[0])
        left = jnp.concatenate([pairs[0], zero], axis=0).astype(jnp.bfloat16)
        right = jnp.concatenate([zero, pairs[1]], axis=0).astype(jnp.bfloat16)
        sums = jnp.dot(
            jnp.concatenate([left, right], axis=1),
            tiles[n:n + GROUP].reshape(GROUP * TV, TR),
            preferred_element_type=jnp.float32,
        )
        add_rows(
            accs,
            [index[lines + line, place] for line, place in at],
            [sums[0:8], sums[0:8], sums[8:16], sums[8:16]],
        )
    for q in range(rays // 4):
        halves = []
        for r in (4 * q, 4 * q + 2):
            at = [slice(8 * (r + k), 8 * (r + k) + 8) for k in range(2)]
            even = [acc0[at[k], :] + acc2[at[k], :] for k in range(2)]
            odd = [acc1[at[k], :] + acc3[at[k], :] for k in range(2)]
            halves.append(
                jnp.where(top, even[0], odd[1])
                + pltpu.roll(jnp.where(top, even[1], odd[0]), 4, axis=0)
            )
        partial_out[16 * q:16 * q + 16, :] = jnp.concatenate(halves, axis=0).astype(jnp.bfloat16)


def edges_kernel(vol, split, dual, edge_out, halo_out):
    start = lax.axis_index("slab") == 0
    for j in range(vol.shape[1] // 128):
        at = slice(128 * j, 128 * j + 128)
        edge = vol[3:4, at] - dual[0, 3:4, at] + split[0, 3:4, at]
        edge_out[:, at] = edge
        halo_out[:, at] = jnp.broadcast_to(jnp.where(start, edge, vol[0:1, at]), (4, 128))


def local_kernel(rho, vol, split, dual, edge, from_next, from_previous, base_out):
    slab, slabs = lax.axis_index("slab"), lax.axis_size("slab")
    factor = TAU * rho[0]
    row, lane = iotas((8, 128))
    row_mask, col_mask = plane_masks(lane)
    for j in range(vol.shape[1] // 128):
        at = slice(128 * j, 128 * j + 128)
        x = jnp.concatenate([vol[:, at]] * 2, axis=0)
        gap = [
            jnp.concatenate([dual[k, :, at] - split[k, :, at]] * 2, axis=0) for k in range(3)
        ]
        above = jnp.where(slab == slabs - 1, 0.0, from_next[0:1, at] - edge[:, at])
        below = jnp.where(slab == 0, 0.0, x[0:1] - from_previous[0:1, at])
        depth = jnp.where(row < 3, pltpu.roll(x, 7, axis=0) - x + gap[0], above)
        across = jnp.where(row_mask, pltpu.roll(x, 120, axis=1) - x + gap[1], 0.0)
        along = jnp.where(col_mask, pltpu.roll(x, 127, axis=1) - x + gap[2], 0.0)
        adjoint = jnp.where(row == 0, below, pltpu.roll(depth, 1, axis=0)) - depth
        adjoint += jnp.where((lane % TV) >= 8, pltpu.roll(across, 8, axis=1), 0.0) - across
        adjoint += jnp.where(lane % 8 >= 1, pltpu.roll(along, 1, axis=1), 0.0) - along
        base_out[:, at] = (x - factor * adjoint)[0:4]


def backward_kernel(
    indices, tiles, part, moved, grad_out,
    index, table, acc0, acc1, acc2, acc3, sem,
):
    slots = tiles.shape[0]
    lines = indices.shape[0] // 4
    rays = table.shape[0] // 8
    voxel_tiles = acc0.shape[0] // 8 - 1
    to_scalar = pltpu.make_async_copy(indices, index, sem)
    to_scalar.start()
    accs = (acc0, acc1, acc2, acc3)
    for acc in accs:
        acc[...] = jnp.zeros_like(acc)
    row, lane = iotas((8, 128))
    low, top = lane < TV, row < 4
    for q in range(rays // 4):
        at = slice(16 * q, 16 * q + 16)
        total = part[at, :].astype(jnp.float32) + moved[at, :].astype(jnp.float32)
        for k in range(2):
            x = total[8 * k:8 * k + 8]
            turned = pltpu.roll(x, 4, axis=0)
            r = 8 * (4 * q + 2 * k)
            table[r:r + 8, :] = jnp.where(top, x, turned)
            table[r + 8:r + 16, :] = jnp.where(top, turned, x)

    to_scalar.wait()
    for g in range(slots // GROUP):
        n = GROUP * g
        at = [divmod(n + i, 128) for i in range(GROUP)]
        picked = [table[rows8(index[2 * lines + line, place]), :] for line, place in at]
        rows = jnp.concatenate(
            [jnp.where(top, picked[2 * i], picked[2 * i + 1]) for i in range(2)], axis=0
        )
        back = lax.dot_general(
            rows.astype(jnp.bfloat16),
            tiles[n:n + GROUP].reshape(GROUP * TV, TR),
            (((1,), (1,)), ((), ())),
            preferred_element_type=jnp.float32,
        )
        add_rows(
            accs,
            [index[3 * lines + line, place] for line, place in at],
            [back[8 * k:8 * k + 8, 128 * k:128 * k + 128] for k in (0, 0, 1, 1)],
        )
    for j in range(voxel_tiles // 2):
        at = [slice(16 * j + 8 * k, 16 * j + 8 * k + 8) for k in range(2)]
        even = [acc0[at[k], :] + acc2[at[k], :] for k in range(2)]
        odd = [acc1[at[k], :] + acc3[at[k], :] for k in range(2)]
        turned = pltpu.roll(jnp.where(top, even[1], odd[0]), TV, axis=1)
        both = jnp.where(top == low, jnp.where(top, even[0], odd[1]), turned)
        grad_out[:, 128 * j:128 * j + 128] = (both + pltpu.roll(both, 4, axis=0))[0:4]


def update_kernel(
    grad, grad_other, ahead, base, dual, limits,
    new_volume, new_split, new_dual,
):
    last = lax.axis_index("slab") == lax.axis_size("slab") - 1
    row, lane = iotas((8, 128))
    row_mask, col_mask = plane_masks(lane)
    inner = jnp.logical_or(row < 3, jnp.logical_not(last))
    for j in range(dual.shape[2] // 128):
        at = slice(128 * j, 128 * j + 128)
        limit = limits[:, at]
        own = base[:, at] - TAU * (grad[:, at] + grad_other[:, at])
        field = jnp.where(row < 4, jnp.concatenate([own] * 2, axis=0), ahead[:, at])
        new_volume[:, at] = own
        steps = (
            jnp.where(inner, pltpu.roll(field, 7, axis=0) - field, 0.0),
            jnp.where(row_mask, pltpu.roll(field, 120, axis=1) - field, 0.0),
            jnp.where(col_mask, pltpu.roll(field, 127, axis=1) - field, 0.0),
        )
        for k in range(3):
            mixed = steps[k][0:4] + dual[k, :, at]
            clipped = jnp.clip(mixed, -limit, limit)
            new_dual[k, :, at] = clipped
            new_split[k, :, at] = mixed - clipped


def vmem():
    return pl.BlockSpec(memory_space=pltpu.VMEM)


def smem():
    return pl.BlockSpec(memory_space=pltpu.SMEM)


def hbm():
    return pl.BlockSpec(memory_space=pltpu.HBM)


def params():
    return pltpu.CompilerParams(vmem_limit_bytes=VMEM_LIMIT)


def shards(
    volume, split_var, dual_var, sinogram, proj_tiles, ray_index, voxel_index, tile_count, rho
):
    f32, bf16 = jnp.float32, jnp.bfloat16
    slices, width = volume.shape
    slots = ray_index.shape[0]
    owned = sinogram.shape[0]
    group = lax.axis_size(("tile", "rep"))
    reps = lax.axis_size("rep")
    slabs = lax.axis_size("slab")
    rays = owned * group
    voxel_tiles = width // TV
    lines = slots // 128
    ray_index, voxel_index = ray_index.reshape(lines, 128), voxel_index.reshape(lines, 128)
    sources = [
        pltpu.with_memory_space_constraint(x, pltpu.HBM)
        for x in (ray_index, voxel_index, volume, sinogram, proj_tiles)
    ]

    partial, indices, tiles = pl.pallas_call(
        forward_kernel,
        out_shape=(
            jax.ShapeDtypeStruct((rays * slices, TR), bf16),
            jax.ShapeDtypeStruct((4 * lines, 128), jnp.int32),
            jax.ShapeDtypeStruct(proj_tiles.shape, bf16),
        ),
        in_specs=[smem()] + [hbm()] * 5,
        out_specs=(vmem(),) * 3,
        scratch_shapes=[
            pltpu.VMEM((lines, 128), jnp.int32),
            pltpu.VMEM((lines, 128), jnp.int32),
            pltpu.SMEM((4 * lines, 128), jnp.int32),
            pltpu.VMEM((slices, width), f32),
            pltpu.VMEM(sinogram.shape, f32),
            pltpu.VMEM((8, width), f32),
            pltpu.VMEM((voxel_tiles * 8, 128), f32),
        ]
        + [pltpu.VMEM((rays * 8 + 8, 128), f32)] * 4
        + [pltpu.SemaphoreType.DMA((5,)), pltpu.SemaphoreType.DMA((CHUNKS,))],
        compiler_params=params(),
        name="forward",
    )(tile_count, *sources)

    row = jax.ShapeDtypeStruct((1, width), f32)
    edge, halo = pl.pallas_call(
        edges_kernel,
        out_shape=(row, jax.ShapeDtypeStruct((4, width), f32)),
        in_specs=[vmem()] * 3,
        out_specs=(vmem(),) * 2,
        compiler_params=params(),
        name="edges",
    )(volume, split_var, dual_var)
    across = [(i, i ^ 3) for i in range(2 * reps)]
    down = [(i, i - 1) for i in range(1, slabs)]
    if slabs == 2:
        from_next = from_previous = lax.ppermute(halo, ("slab", "rep"), across)
    else:
        from_next = lax.ppermute(volume[0:1], "slab", down)
        from_previous = lax.ppermute(edge, "slab", [(i - 1, i) for i in range(1, slabs)])
    swap = [(i, i ^ 1) for i in range(reps)]
    moved = lax.ppermute(partial, "rep", swap)
    step = reps
    while step < group:
        partial = (partial.astype(f32) + moved.astype(f32)).astype(bf16)
        moved = lax.ppermute(
            partial, ("tile", "rep"), [(i, i ^ (step + 1)) for i in range(group)]
        )
        step *= 2
    limits = jnp.broadcast_to((1.0 / rho)[:, None], (1, width))
    moved, from_next, from_previous, limits = lax.optimization_barrier(
        (moved, from_next, from_previous, limits)
    )

    base = pl.pallas_call(
        local_kernel,
        out_shape=jax.ShapeDtypeStruct((slices, width), f32),
        in_specs=[smem()] + [vmem()] * 6,
        out_specs=vmem(),
        compiler_params=params(),
        name="local",
    )(rho, volume, split_var, dual_var, edge, from_next, from_previous)

    grad = pl.pallas_call(
        backward_kernel,
        out_shape=jax.ShapeDtypeStruct((slices, width), f32),
        in_specs=[vmem()] * 4,
        out_specs=vmem(),
        scratch_shapes=[
            pltpu.SMEM((4 * lines, 128), jnp.int32),
            pltpu.VMEM((rays * 8, 128), f32),
        ]
        + [pltpu.VMEM((voxel_tiles * 8 + 8, 128), f32)] * 4
        + [pltpu.SemaphoreType.DMA],
        compiler_params=params(),
        name="backward",
    )(indices, tiles, partial, moved)
    grad_other = lax.ppermute(grad, "rep", swap)
    ahead = base[0:1] - TAU * (grad[0:1] + grad_other[0:1])
    if slabs == 2:
        ahead = lax.ppermute(ahead, ("slab", "rep"), across)
    else:
        ahead = lax.ppermute(ahead, "slab", down)

    triple = jax.ShapeDtypeStruct((3, slices, width), f32)
    return pl.pallas_call(
        update_kernel,
        out_shape=(jax.ShapeDtypeStruct((slices, width), f32), triple, triple),
        in_specs=[vmem()] * 6,
        out_specs=(vmem(),) * 3,
        compiler_params=params(),
        name="update",
    )(grad, grad_other, ahead, base, dual_var, limits)


def solution(mesh):
    return jax.shard_map(
        shards,
        mesh=mesh,
        in_specs=(
            P(("parts", "slab"), "tile"),
            P(None, ("parts", "slab"), "tile"),
            P(None, ("parts", "slab"), "tile"),
            P(("tile", "rep"), ("parts", "slab"), None),
            P(("tile", "rep"), None, None),
            P(("tile", "rep")),
            P(("tile", "rep")),
            P(("tile", "rep")),
            P(),
        ),
        out_specs=(
            P(("parts", "slab"), "tile"),
            P(None, ("parts", "slab"), "tile"),
            P(None, ("parts", "slab"), "tile"),
        ),
        check_vma=False,
    )
```

```python
import jax
import jax.numpy as jnp
from jax import lax
from jax.experimental import pallas as pl
from jax.experimental.pallas import tpu as pltpu
from jax.sharding import PartitionSpec as P

TV = 64
TR = 128
TAU = 0.5
GROUP = 4
CHUNKS = 2
VMEM_LIMIT = 16 * 1024 * 1024


def iotas(shape):
    row = lax.broadcasted_iota(jnp.int32, shape, 0)
    lane = lax.broadcasted_iota(jnp.int32, shape, 1)
    return row, lane


def start_tiles(proj_hbm, tiles, sems):
    per = proj_hbm.shape[0] // CHUNKS
    copies = []
    for c in range(CHUNKS):
        part = pl.ds(c * per, per)
        copy = pltpu.make_async_copy(proj_hbm.at[part], tiles.at[part], sems.at[c])
        copy.start()
        copies.append(copy)
    return copies


def plane_masks(lane):
    return (lane % TV) // 8 < 7, lane % 8 < 7


def rows8(start):
    return pl.ds(pl.multiple_of(start, 8), 8)


def add_rows(accs, starts, values):
    held = [acc[rows8(start), :] for acc, start in zip(accs, starts)]
    for acc, start, old, value in zip(accs, starts, held, values):
        acc[rows8(start), :] = old + value


def forward_kernel(
    count, ray_hbm, voxel_hbm, vol_hbm, sino_hbm, proj_hbm,
    partial_out, index_out, tiles,
    ray, voxel, index, vol, sino, double, table, acc0, acc1, acc2, acc3,
    sems, tile_sems,
):
    slots = proj_hbm.shape[0]
    lines = ray.shape[0]
    rays = acc0.shape[0] // 8 - 1
    voxel_tiles = table.shape[0] // 8
    owned = sino.shape[0]
    width = vol.shape[1]
    loads = [
        pltpu.make_async_copy(source, target, sems.at[i])
        for i, (source, target) in enumerate(
            [(voxel_hbm, voxel), (ray_hbm, ray), (vol_hbm, vol), (sino_hbm, sino)]
        )
    ]
    copies = start_tiles(proj_hbm, tiles, tile_sems)
    for load in loads:
        load.start()
    accs = (acc0, acc1, acc2, acc3)
    for acc in accs:
        acc[...] = jnp.zeros_like(acc)
    row, lane = iotas((8, 128))
    low, top = lane < TV, row < 4

    loads[0].wait()
    loads[1].wait()
    line, place = iotas((lines, 128))
    live = 128 * line + place < count[0]
    rays8, voxels8 = ray[...] * 8, voxel[...] * 8
    index_out[0:lines, :] = voxels8
    index_out[lines:2 * lines, :] = jnp.where(live, rays8, rays * 8)
    index_out[2 * lines:3 * lines, :] = rays8
    index_out[3 * lines:4 * lines, :] = jnp.where(live, voxels8, voxel_tiles * 8)
    to_scalar = pltpu.make_async_copy(index_out, index, sems.at[4])
    to_scalar.start()

    loads[2].wait()
    field = vol[...]
    double[0:4, :] = field
    double[4:8, :] = field
    for j in range(width // 128):
        x = double[:, 128 * j:128 * j + 128].astype(jnp.bfloat16).astype(jnp.float32)
        turned = pltpu.roll(x, TV, axis=1)
        zero = jnp.zeros_like(x)
        first = jnp.where(jnp.logical_and(top, low), x, zero)
        second = jnp.where(jnp.logical_and(top, low), turned, zero)
        other = jnp.logical_not(jnp.logical_or(top, low))
        table[16 * j:16 * j + 8, :] = jnp.where(other, turned, first)
        table[16 * j + 8:16 * j + 16, :] = jnp.where(other, x, second)

    loads[3].wait()
    mine = (lax.axis_index("tile") * lax.axis_size("rep") + lax.axis_index("rep")) * owned
    for r in range(owned):
        acc0[pl.ds(pl.multiple_of((mine + r) * 8, 8), 4), :] = -sino[r]
    to_scalar.wait()
    per = slots // CHUNKS
    for g in range(slots // GROUP):
        if GROUP * g % per == 0:
            copies[GROUP * g // per].wait()
        n = GROUP * g
        at = [divmod(n + i, 128) for i in range(GROUP)]
        picked = [table[rows8(index[line, place]), :] for line, place in at]
        pairs = [jnp.where(top, picked[2 * i], picked[2 * i + 1]) for i in range(2)]
        zero = jnp.zeros_like(pairs[0])
        left = jnp.concatenate([pairs[0], zero], axis=0).astype(jnp.bfloat16)
        right = jnp.concatenate([zero, pairs[1]], axis=0).astype(jnp.bfloat16)
        sums = jnp.dot(
            jnp.concatenate([left, right], axis=1),
            tiles[n:n + GROUP].reshape(GROUP * TV, TR),
            preferred_element_type=jnp.float32,
        )
        add_rows(
            accs,
            [index[lines + line, place] for line, place in at],
            [sums[0:8], sums[0:8], sums[8:16], sums[8:16]],
        )
    for q in range(rays // 4):
        halves = []
        for r in (4 * q, 4 * q + 2):
            at = [slice(8 * (r + k), 8 * (r + k) + 8) for k in range(2)]
            even = [acc0[at[k], :] + acc2[at[k], :] for k in range(2)]
            odd = [acc1[at[k], :] + acc3[at[k], :] for k in range(2)]
            halves.append(
                jnp.where(top, even[0], odd[1])
                + pltpu.roll(jnp.where(top, even[1], odd[0]), 4, axis=0)
            )
        partial_out[16 * q:16 * q + 16, :] = jnp.concatenate(halves, axis=0).astype(jnp.bfloat16)


def edges_kernel(vol, split, dual, edge_out, halo_out):
    start = lax.axis_index("slab") == 0
    for j in range(vol.shape[1] // 128):
        at = slice(128 * j, 128 * j + 128)
        edge = vol[3:4, at] - dual[0, 3:4, at] + split[0, 3:4, at]
        edge_out[:, at] = edge
        halo_out[:, at] = jnp.broadcast_to(jnp.where(start, edge, vol[0:1, at]), (4, 128))


def local_kernel(rho, vol, split, dual, edge, from_next, from_previous, base_out):
    slab, slabs = lax.axis_index("slab"), lax.axis_size("slab")
    factor = TAU * rho[0]
    row, lane = iotas((8, 128))
    row_mask, col_mask = plane_masks(lane)
    for j in range(vol.shape[1] // 128):
        at = slice(128 * j, 128 * j + 128)
        x = jnp.concatenate([vol[:, at]] * 2, axis=0)
        gap = [
            jnp.concatenate([dual[k, :, at] - split[k, :, at]] * 2, axis=0) for k in range(3)
        ]
        above = jnp.where(slab == slabs - 1, 0.0, from_next[0:1, at] - edge[:, at])
        below = jnp.where(slab == 0, 0.0, x[0:1] - from_previous[0:1, at])
        depth = jnp.where(row < 3, pltpu.roll(x, 7, axis=0) - x + gap[0], above)
        across = jnp.where(row_mask, pltpu.roll(x, 120, axis=1) - x + gap[1], 0.0)
        along = jnp.where(col_mask, pltpu.roll(x, 127, axis=1) - x + gap[2], 0.0)
        adjoint = jnp.where(row == 0, below, pltpu.roll(depth, 1, axis=0)) - depth
        adjoint += jnp.where((lane % TV) >= 8, pltpu.roll(across, 8, axis=1), 0.0) - across
        adjoint += jnp.where(lane % 8 >= 1, pltpu.roll(along, 1, axis=1), 0.0) - along
        base_out[:, at] = (x - factor * adjoint)[0:4]


def backward_kernel(
    indices, tiles, part, moved, grad_out,
    index, table, acc0, acc1, sem,
):
    slots = tiles.shape[0]
    lines = indices.shape[0] // 4
    rays = table.shape[0] // 8
    voxel_tiles = acc0.shape[0] // 8 - 1
    to_scalar = pltpu.make_async_copy(indices, index, sem)
    to_scalar.start()
    accs = (acc0, acc1)
    for acc in accs:
        acc[...] = jnp.zeros_like(acc)
    row, lane = iotas((8, 128))
    low, top = lane < TV, row < 4
    for q in range(rays // 4):
        at = slice(16 * q, 16 * q + 16)
        total = part[at, :].astype(jnp.float32) + moved[at, :].astype(jnp.float32)
        for k in range(2):
            x = total[8 * k:8 * k + 8]
            turned = pltpu.roll(x, 4, axis=0)
            r = 8 * (4 * q + 2 * k)
            table[r:r + 8, :] = jnp.where(top, x, turned)
            table[r + 8:r + 16, :] = jnp.where(top, turned, x)

    to_scalar.wait()
    for g in range(slots // GROUP):
        n = GROUP * g
        at = [divmod(n + i, 128) for i in range(GROUP)]
        picked = [table[rows8(index[2 * lines + line, place]), :] for line, place in at]
        rows = jnp.concatenate(
            [jnp.where(top, picked[2 * i], picked[2 * i + 1]) for i in range(2)], axis=0
        )
        back = lax.dot_general(
            rows.astype(jnp.bfloat16),
            tiles[n:n + GROUP].reshape(GROUP * TV, TR),
            (((1,), (1,)), ((), ())),
            preferred_element_type=jnp.float32,
        )
        for k in range(2):
            value = back[8 * k:8 * k + 8, 128 * k:128 * k + 128]
            starts = [index[3 * lines + line, place] for line, place in at[2 * k:2 * k + 2]]
            add_rows(accs, starts, [value, value])
    for j in range(voxel_tiles // 2):
        at = [slice(16 * j + 8 * k, 16 * j + 8 * k + 8) for k in range(2)]
        even = [acc0[at[k], :] for k in range(2)]
        odd = [acc1[at[k], :] for k in range(2)]
        turned = pltpu.roll(jnp.where(top, even[1], odd[0]), TV, axis=1)
        both = jnp.where(top == low, jnp.where(top, even[0], odd[1]), turned)
        grad_out[:, 128 * j:128 * j + 128] = (both + pltpu.roll(both, 4, axis=0))[0:4]


def update_kernel(
    grad, grad_other, ahead, base, dual, limits,
    new_volume, new_split, new_dual,
):
    last = lax.axis_index("slab") == lax.axis_size("slab") - 1
    row, lane = iotas((8, 128))
    row_mask, col_mask = plane_masks(lane)
    inner = jnp.logical_or(row < 3, jnp.logical_not(last))
    for j in range(dual.shape[2] // 128):
        at = slice(128 * j, 128 * j + 128)
        limit = limits[:, at]
        own = base[:, at] - TAU * (grad[:, at] + grad_other[:, at])
        field = jnp.where(row < 4, jnp.concatenate([own] * 2, axis=0), ahead[:, at])
        new_volume[:, at] = own
        steps = (
            jnp.where(inner, pltpu.roll(field, 7, axis=0) - field, 0.0),
            jnp.where(row_mask, pltpu.roll(field, 120, axis=1) - field, 0.0),
            jnp.where(col_mask, pltpu.roll(field, 127, axis=1) - field, 0.0),
        )
        for k in range(3):
            mixed = steps[k][0:4] + dual[k, :, at]
            clipped = jnp.clip(mixed, -limit, limit)
            new_dual[k, :, at] = clipped
            new_split[k, :, at] = mixed - clipped


def vmem():
    return pl.BlockSpec(memory_space=pltpu.VMEM)


def smem():
    return pl.BlockSpec(memory_space=pltpu.SMEM)


def hbm():
    return pl.BlockSpec(memory_space=pltpu.HBM)


def params():
    return pltpu.CompilerParams(vmem_limit_bytes=VMEM_LIMIT)


def shards(
    volume, split_var, dual_var, sinogram, proj_tiles, ray_index, voxel_index, tile_count, rho
):
    f32, bf16 = jnp.float32, jnp.bfloat16
    slices, width = volume.shape
    slots = ray_index.shape[0]
    owned = sinogram.shape[0]
    group = lax.axis_size(("tile", "rep"))
    reps = lax.axis_size("rep")
    slabs = lax.axis_size("slab")
    rays = owned * group
    voxel_tiles = width // TV
    lines = slots // 128
    ray_index, voxel_index = ray_index.reshape(lines, 128), voxel_index.reshape(lines, 128)
    sources = [
        pltpu.with_memory_space_constraint(x, pltpu.HBM)
        for x in (ray_index, voxel_index, volume, sinogram, proj_tiles)
    ]

    partial, indices, tiles = pl.pallas_call(
        forward_kernel,
        out_shape=(
            jax.ShapeDtypeStruct((rays * slices, TR), bf16),
            jax.ShapeDtypeStruct((4 * lines, 128), jnp.int32),
            jax.ShapeDtypeStruct(proj_tiles.shape, bf16),
        ),
        in_specs=[smem()] + [hbm()] * 5,
        out_specs=(vmem(),) * 3,
        scratch_shapes=[
            pltpu.VMEM((lines, 128), jnp.int32),
            pltpu.VMEM((lines, 128), jnp.int32),
            pltpu.SMEM((4 * lines, 128), jnp.int32),
            pltpu.VMEM((slices, width), f32),
            pltpu.VMEM(sinogram.shape, f32),
            pltpu.VMEM((8, width), f32),
            pltpu.VMEM((voxel_tiles * 8, 128), f32),
        ]
        + [pltpu.VMEM((rays * 8 + 8, 128), f32)] * 4
        + [pltpu.SemaphoreType.DMA((5,)), pltpu.SemaphoreType.DMA((CHUNKS,))],
        compiler_params=params(),
        name="forward",
    )(tile_count, *sources)

    row = jax.ShapeDtypeStruct((1, width), f32)
    edge, halo = pl.pallas_call(
        edges_kernel,
        out_shape=(row, jax.ShapeDtypeStruct((4, width), f32)),
        in_specs=[vmem()] * 3,
        out_specs=(vmem(),) * 2,
        compiler_params=params(),
        name="edges",
    )(volume, split_var, dual_var)
    across = [(i, i ^ 3) for i in range(2 * reps)]
    down = [(i, i - 1) for i in range(1, slabs)]
    if slabs == 2:
        from_next = from_previous = lax.ppermute(halo, ("slab", "rep"), across)
    else:
        from_next = lax.ppermute(volume[0:1], "slab", down)
        from_previous = lax.ppermute(edge, "slab", [(i - 1, i) for i in range(1, slabs)])
    swap = [(i, i ^ 1) for i in range(reps)]
    moved = lax.ppermute(partial, "rep", swap)
    step = reps
    while step < group:
        partial = (partial.astype(f32) + moved.astype(f32)).astype(bf16)
        moved = lax.ppermute(
            partial, ("tile", "rep"), [(i, i ^ (step + 1)) for i in range(group)]
        )
        step *= 2
    limits = jnp.broadcast_to((1.0 / rho)[:, None], (1, width))
    moved, from_next, from_previous, limits = lax.optimization_barrier(
        (moved, from_next, from_previous, limits)
    )

    base = pl.pallas_call(
        local_kernel,
        out_shape=jax.ShapeDtypeStruct((slices, width), f32),
        in_specs=[smem()] + [vmem()] * 6,
        out_specs=vmem(),
        compiler_params=params(),
        name="local",
    )(rho, volume, split_var, dual_var, edge, from_next, from_previous)

    grad = pl.pallas_call(
        backward_kernel,
        out_shape=jax.ShapeDtypeStruct((slices, width), f32),
        in_specs=[vmem()] * 4,
        out_specs=vmem(),
        scratch_shapes=[
            pltpu.SMEM((4 * lines, 128), jnp.int32),
            pltpu.VMEM((rays * 8, 128), f32),
        ]
        + [pltpu.VMEM((voxel_tiles * 8 + 8, 128), f32)] * 2
        + [pltpu.SemaphoreType.DMA],
        compiler_params=params(),
        name="backward",
    )(indices, tiles, partial, moved)
    grad_other = lax.ppermute(grad, "rep", swap)
    ahead = base[0:1] - TAU * (grad[0:1] + grad_other[0:1])
    if slabs == 2:
        ahead = lax.ppermute(ahead, ("slab", "rep"), across)
    else:
        ahead = lax.ppermute(ahead, "slab", down)

    triple = jax.ShapeDtypeStruct((3, slices, width), f32)
    return pl.pallas_call(
        update_kernel,
        out_shape=(jax.ShapeDtypeStruct((slices, width), f32), triple, triple),
        in_specs=[vmem()] * 6,
        out_specs=(vmem(),) * 3,
        compiler_params=params(),
        name="update",
    )(grad, grad_other, ahead, base, dual_var, limits)


def solution(mesh):
    return jax.shard_map(
        shards,
        mesh=mesh,
        in_specs=(
            P(("parts", "slab"), "tile"),
            P(None, ("parts", "slab"), "tile"),
            P(None, ("parts", "slab"), "tile"),
            P(("tile", "rep"), ("parts", "slab"), None),
            P(("tile", "rep"), None, None),
            P(("tile", "rep")),
            P(("tile", "rep")),
            P(("tile", "rep")),
            P(),
        ),
        out_specs=(
            P(("parts", "slab"), "tile"),
            P(None, ("parts", "slab"), "tile"),
            P(None, ("parts", "slab"), "tile"),
        ),
        check_vma=False,
    )
```

```python
import jax
import jax.numpy as jnp
from jax import lax
from jax.experimental import pallas as pl
from jax.experimental.pallas import tpu as pltpu
from jax.sharding import PartitionSpec as P

TV = 64
TR = 128
TAU = 0.5
GROUP = 4
CHUNKS = 2
VMEM_LIMIT = 16 * 1024 * 1024


def iotas(shape):
    row = lax.broadcasted_iota(jnp.int32, shape, 0)
    lane = lax.broadcasted_iota(jnp.int32, shape, 1)
    return row, lane


def start_tiles(proj_hbm, tiles, sems):
    per = proj_hbm.shape[0] // CHUNKS
    copies = []
    for c in range(CHUNKS):
        part = pl.ds(c * per, per)
        copy = pltpu.make_async_copy(proj_hbm.at[part], tiles.at[part], sems.at[c])
        copy.start()
        copies.append(copy)
    return copies


def plane_masks(lane):
    return (lane % TV) // 8 < 7, lane % 8 < 7


def rows8(start):
    return pl.ds(pl.multiple_of(start, 8), 8)


def add_rows(accs, starts, values):
    held = [acc[rows8(start), :] for acc, start in zip(accs, starts)]
    for acc, start, old, value in zip(accs, starts, held, values):
        acc[rows8(start), :] = old + value


def forward_kernel(
    count, ray_hbm, voxel_hbm, vol_hbm, sino_hbm, proj_hbm,
    partial_out, index_out, tiles,
    ray, voxel, index, vol, sino, double, table, acc0, acc1, acc2, acc3,
    sems, tile_sems,
):
    slots = proj_hbm.shape[0]
    lines = ray.shape[0]
    rays = acc0.shape[0] // 8 - 1
    voxel_tiles = table.shape[0] // 8
    owned = sino.shape[0]
    width = vol.shape[1]
    loads = [
        pltpu.make_async_copy(source, target, sems.at[i])
        for i, (source, target) in enumerate(
            [(voxel_hbm, voxel), (ray_hbm, ray), (vol_hbm, vol), (sino_hbm, sino)]
        )
    ]
    for load in loads:
        load.start()
    copies = start_tiles(proj_hbm, tiles, tile_sems)
    accs = (acc0, acc1, acc2, acc3)
    for acc in accs:
        acc[...] = jnp.zeros_like(acc)
    row, lane = iotas((8, 128))
    low, top = lane < TV, row < 4

    loads[0].wait()
    loads[1].wait()
    line, place = iotas((lines, 128))
    live = 128 * line + place < count[0]
    rays8, voxels8 = ray[...] * 8, voxel[...] * 8
    index_out[0:lines, :] = voxels8
    index_out[lines:2 * lines, :] = jnp.where(live, rays8, rays * 8)
    index_out[2 * lines:3 * lines, :] = rays8
    index_out[3 * lines:4 * lines, :] = jnp.where(live, voxels8, voxel_tiles * 8)
    to_scalar = pltpu.make_async_copy(index_out, index, sems.at[4])
    to_scalar.start()

    loads[2].wait()
    field = vol[...]
    double[0:4, :] = field
    double[4:8, :] = field
    for j in range(width // 128):
        x = double[:, 128 * j:128 * j + 128].astype(jnp.bfloat16).astype(jnp.float32)
        turned = pltpu.roll(x, TV, axis=1)
        zero = jnp.zeros_like(x)
        first = jnp.where(jnp.logical_and(top, low), x, zero)
        second = jnp.where(jnp.logical_and(top, low), turned, zero)
        other = jnp.logical_not(jnp.logical_or(top, low))
        table[16 * j:16 * j + 8, :] = jnp.where(other, turned, first)
        table[16 * j + 8:16 * j + 16, :] = jnp.where(other, x, second)

    loads[3].wait()
    mine = (lax.axis_index("tile") * lax.axis_size("rep") + lax.axis_index("rep")) * owned
    for r in range(owned):
        acc0[pl.ds(pl.multiple_of((mine + r) * 8, 8), 4), :] = -sino[r]
    to_scalar.wait()
    per = slots // CHUNKS
    for g in range(slots // GROUP):
        if GROUP * g % per == 0:
            copies[GROUP * g // per].wait()
        n = GROUP * g
        at = [divmod(n + i, 128) for i in range(GROUP)]
        picked = [table[rows8(index[line, place]), :] for line, place in at]
        pairs = [jnp.where(top, picked[2 * i], picked[2 * i + 1]) for i in range(2)]
        zero = jnp.zeros_like(pairs[0])
        left = jnp.concatenate([pairs[0], zero], axis=0).astype(jnp.bfloat16)
        right = jnp.concatenate([zero, pairs[1]], axis=0).astype(jnp.bfloat16)
        sums = jnp.dot(
            jnp.concatenate([left, right], axis=1),
            tiles[n:n + GROUP].reshape(GROUP * TV, TR),
            preferred_element_type=jnp.float32,
        )
        add_rows(
            accs,
            [index[lines + line, place] for line, place in at],
            [sums[0:8], sums[0:8], sums[8:16], sums[8:16]],
        )
    for q in range(rays // 4):
        halves = []
        for r in (4 * q, 4 * q + 2):
            at = [slice(8 * (r + k), 8 * (r + k) + 8) for k in range(2)]
            even = [acc0[at[k], :] + acc2[at[k], :] for k in range(2)]
            odd = [acc1[at[k], :] + acc3[at[k], :] for k in range(2)]
            halves.append(
                jnp.where(top, even[0], odd[1])
                + pltpu.roll(jnp.where(top, even[1], odd[0]), 4, axis=0)
            )
        partial_out[16 * q:16 * q + 16, :] = jnp.concatenate(halves, axis=0).astype(jnp.bfloat16)


def edges_kernel(vol, split, dual, edge_out, halo_out):
    start = lax.axis_index("slab") == 0
    for j in range(vol.shape[1] // 128):
        at = slice(128 * j, 128 * j + 128)
        edge = vol[3:4, at] - dual[0, 3:4, at] + split[0, 3:4, at]
        edge_out[:, at] = edge
        halo_out[:, at] = jnp.broadcast_to(jnp.where(start, edge, vol[0:1, at]), (4, 128))


def local_kernel(rho, vol, split, dual, edge, from_next, from_previous, base_out):
    slab, slabs = lax.axis_index("slab"), lax.axis_size("slab")
    factor = TAU * rho[0]
    row, lane = iotas((8, 128))
    row_mask, col_mask = plane_masks(lane)
    for j in range(vol.shape[1] // 128):
        at = slice(128 * j, 128 * j + 128)
        x = jnp.concatenate([vol[:, at]] * 2, axis=0)
        gap = [
            jnp.concatenate([dual[k, :, at] - split[k, :, at]] * 2, axis=0) for k in range(3)
        ]
        above = jnp.where(slab == slabs - 1, 0.0, from_next[0:1, at] - edge[:, at])
        below = jnp.where(slab == 0, 0.0, x[0:1] - from_previous[0:1, at])
        depth = jnp.where(row < 3, pltpu.roll(x, 7, axis=0) - x + gap[0], above)
        across = jnp.where(row_mask, pltpu.roll(x, 120, axis=1) - x + gap[1], 0.0)
        along = jnp.where(col_mask, pltpu.roll(x, 127, axis=1) - x + gap[2], 0.0)
        adjoint = jnp.where(row == 0, below, pltpu.roll(depth, 1, axis=0)) - depth
        adjoint += jnp.where((lane % TV) >= 8, pltpu.roll(across, 8, axis=1), 0.0) - across
        adjoint += jnp.where(lane % 8 >= 1, pltpu.roll(along, 1, axis=1), 0.0) - along
        base_out[:, at] = (x - factor * adjoint)[0:4]


def backward_kernel(
    indices, tiles, part, moved, base, grad_out, row_out,
    index, table, acc0, acc1, acc2, acc3, sem,
):
    slots = tiles.shape[0]
    lines = indices.shape[0] // 4
    rays = table.shape[0] // 8
    voxel_tiles = acc0.shape[0] // 8 - 1
    to_scalar = pltpu.make_async_copy(indices, index, sem)
    to_scalar.start()
    accs = (acc0, acc1, acc2, acc3)
    for acc in accs:
        acc[...] = jnp.zeros_like(acc)
    row, lane = iotas((8, 128))
    low, top = lane < TV, row < 4
    for q in range(rays // 4):
        at = slice(16 * q, 16 * q + 16)
        total = part[at, :].astype(jnp.float32) + moved[at, :].astype(jnp.float32)
        for k in range(2):
            x = total[8 * k:8 * k + 8]
            turned = pltpu.roll(x, 4, axis=0)
            r = 8 * (4 * q + 2 * k)
            table[r:r + 8, :] = jnp.where(top, x, turned)
            table[r + 8:r + 16, :] = jnp.where(top, turned, x)

    to_scalar.wait()
    for g in range(slots // GROUP):
        n = GROUP * g
        at = [divmod(n + i, 128) for i in range(GROUP)]
        picked = [table[rows8(index[2 * lines + line, place]), :] for line, place in at]
        rows = jnp.concatenate(
            [jnp.where(top, picked[2 * i], picked[2 * i + 1]) for i in range(2)], axis=0
        )
        back = lax.dot_general(
            rows.astype(jnp.bfloat16),
            tiles[n:n + GROUP].reshape(GROUP * TV, TR),
            (((1,), (1,)), ((), ())),
            preferred_element_type=jnp.float32,
        )
        add_rows(
            accs,
            [index[3 * lines + line, place] for line, place in at],
            [back[8 * k:8 * k + 8, 128 * k:128 * k + 128] for k in (0, 0, 1, 1)],
        )
    for j in range(voxel_tiles // 2):
        at = [slice(16 * j + 8 * k, 16 * j + 8 * k + 8) for k in range(2)]
        even = [acc0[at[k], :] + acc2[at[k], :] for k in range(2)]
        odd = [acc1[at[k], :] + acc3[at[k], :] for k in range(2)]
        turned = pltpu.roll(jnp.where(top, even[1], odd[0]), TV, axis=1)
        both = jnp.where(top == low, jnp.where(top, even[0], odd[1]), turned)
        grad = (both + pltpu.roll(both, 4, axis=0))[0:4]
        lanes = slice(128 * j, 128 * j + 128)
        grad_out[:, lanes] = grad
        row_out[:, lanes] = 0.5 * base[0:1, lanes] - TAU * grad[0:1]


def update_kernel(
    grad, grad_other, piece, piece_other, base, dual, limits,
    new_volume, new_split, new_dual,
):
    last = lax.axis_index("slab") == lax.axis_size("slab") - 1
    row, lane = iotas((8, 128))
    row_mask, col_mask = plane_masks(lane)
    inner = jnp.logical_or(row < 3, jnp.logical_not(last))
    for j in range(dual.shape[2] // 128):
        at = slice(128 * j, 128 * j + 128)
        limit = limits[:, at]
        own = base[:, at] - TAU * (grad[:, at] + grad_other[:, at])
        ahead = piece[:, at] + piece_other[:, at]
        field = jnp.where(row < 4, jnp.concatenate([own] * 2, axis=0), ahead)
        new_volume[:, at] = own
        steps = (
            jnp.where(inner, pltpu.roll(field, 7, axis=0) - field, 0.0),
            jnp.where(row_mask, pltpu.roll(field, 120, axis=1) - field, 0.0),
            jnp.where(col_mask, pltpu.roll(field, 127, axis=1) - field, 0.0),
        )
        for k in range(3):
            mixed = steps[k][0:4] + dual[k, :, at]
            clipped = jnp.clip(mixed, -limit, limit)
            new_dual[k, :, at] = clipped
            new_split[k, :, at] = mixed - clipped


def vmem():
    return pl.BlockSpec(memory_space=pltpu.VMEM)


def smem():
    return pl.BlockSpec(memory_space=pltpu.SMEM)


def hbm():
    return pl.BlockSpec(memory_space=pltpu.HBM)


def params():
    return pltpu.CompilerParams(vmem_limit_bytes=VMEM_LIMIT)


def shards(
    volume, split_var, dual_var, sinogram, proj_tiles, ray_index, voxel_index, tile_count, rho
):
    f32, bf16 = jnp.float32, jnp.bfloat16
    slices, width = volume.shape
    slots = ray_index.shape[0]
    owned = sinogram.shape[0]
    group = lax.axis_size(("tile", "rep"))
    reps = lax.axis_size("rep")
    slabs = lax.axis_size("slab")
    rays = owned * group
    voxel_tiles = width // TV
    lines = slots // 128
    ray_index, voxel_index = ray_index.reshape(lines, 128), voxel_index.reshape(lines, 128)
    sources = [
        pltpu.with_memory_space_constraint(x, pltpu.HBM)
        for x in (ray_index, voxel_index, volume, sinogram, proj_tiles)
    ]

    partial, indices, tiles = pl.pallas_call(
        forward_kernel,
        out_shape=(
            jax.ShapeDtypeStruct((rays * slices, TR), bf16),
            jax.ShapeDtypeStruct((4 * lines, 128), jnp.int32),
            jax.ShapeDtypeStruct(proj_tiles.shape, bf16),
        ),
        in_specs=[smem()] + [hbm()] * 5,
        out_specs=(vmem(),) * 3,
        scratch_shapes=[
            pltpu.VMEM((lines, 128), jnp.int32),
            pltpu.VMEM((lines, 128), jnp.int32),
            pltpu.SMEM((4 * lines, 128), jnp.int32),
            pltpu.VMEM((slices, width), f32),
            pltpu.VMEM(sinogram.shape, f32),
            pltpu.VMEM((8, width), f32),
            pltpu.VMEM((voxel_tiles * 8, 128), f32),
        ]
        + [pltpu.VMEM((rays * 8 + 8, 128), f32)] * 4
        + [pltpu.SemaphoreType.DMA((5,)), pltpu.SemaphoreType.DMA((CHUNKS,))],
        compiler_params=params(),
        name="forward",
    )(tile_count, *sources)

    row = jax.ShapeDtypeStruct((1, width), f32)
    edge, halo = pl.pallas_call(
        edges_kernel,
        out_shape=(row, jax.ShapeDtypeStruct((4, width), f32)),
        in_specs=[vmem()] * 3,
        out_specs=(vmem(),) * 2,
        compiler_params=params(),
        name="edges",
    )(volume, split_var, dual_var)
    across = [(i, i ^ 3) for i in range(2 * reps)]
    down = [(i, i - 1) for i in range(1, slabs)]
    if slabs == 2:
        from_next = from_previous = lax.ppermute(halo, ("slab", "rep"), across)
    else:
        from_next = lax.ppermute(volume[0:1], "slab", down)
        from_previous = lax.ppermute(edge, "slab", [(i - 1, i) for i in range(1, slabs)])
    swap = [(i, i ^ 1) for i in range(reps)]
    moved = lax.ppermute(partial, "rep", swap)
    step = reps
    while step < group:
        partial = (partial.astype(f32) + moved.astype(f32)).astype(bf16)
        moved = lax.ppermute(
            partial, ("tile", "rep"), [(i, i ^ (step + 1)) for i in range(group)]
        )
        step *= 2
    base = pl.pallas_call(
        local_kernel,
        out_shape=jax.ShapeDtypeStruct((slices, width), f32),
        in_specs=[smem()] + [vmem()] * 6,
        out_specs=vmem(),
        compiler_params=params(),
        name="local",
    )(rho, volume, split_var, dual_var, edge, from_next, from_previous)

    limits = jnp.broadcast_to((1.0 / rho)[:, None], (1, width))
    moved, base, limits = lax.optimization_barrier((moved, base, limits))

    grad, piece = pl.pallas_call(
        backward_kernel,
        out_shape=(jax.ShapeDtypeStruct((slices, width), f32), row),
        in_specs=[vmem()] * 5,
        out_specs=(vmem(), vmem()),
        scratch_shapes=[
            pltpu.SMEM((4 * lines, 128), jnp.int32),
            pltpu.VMEM((rays * 8, 128), f32),
        ]
        + [pltpu.VMEM((voxel_tiles * 8 + 8, 128), f32)] * 4
        + [pltpu.SemaphoreType.DMA],
        compiler_params=params(),
        name="backward",
    )(indices, tiles, partial, moved, base)
    if slabs == 2:
        piece = lax.ppermute(piece, ("slab", "rep"), across)
    else:
        piece = lax.ppermute(piece, "slab", down)
    grad_other = lax.ppermute(grad, "rep", swap)
    piece_other = lax.ppermute(piece, "rep", swap)

    triple = jax.ShapeDtypeStruct((3, slices, width), f32)
    return pl.pallas_call(
        update_kernel,
        out_shape=(jax.ShapeDtypeStruct((slices, width), f32), triple, triple),
        in_specs=[vmem()] * 7,
        out_specs=(vmem(),) * 3,
        compiler_params=params(),
        name="update",
    )(grad, grad_other, piece, piece_other, base, dual_var, limits)


def solution(mesh):
    return jax.shard_map(
        shards,
        mesh=mesh,
        in_specs=(
            P(("parts", "slab"), "tile"),
            P(None, ("parts", "slab"), "tile"),
            P(None, ("parts", "slab"), "tile"),
            P(("tile", "rep"), ("parts", "slab"), None),
            P(("tile", "rep"), None, None),
            P(("tile", "rep")),
            P(("tile", "rep")),
            P(("tile", "rep")),
            P(),
        ),
        out_specs=(
            P(("parts", "slab"), "tile"),
            P(None, ("parts", "slab"), "tile"),
            P(None, ("parts", "slab"), "tile"),
        ),
        check_vma=False,
    )
```

```python
import jax
import jax.numpy as jnp
from jax import lax
from jax.experimental import pallas as pl
from jax.experimental.pallas import tpu as pltpu
from jax.sharding import PartitionSpec as P

TV = 64
TR = 128
TAU = 0.5
GROUP = 4
CHUNKS = 2
VMEM_LIMIT = 16 * 1024 * 1024


def iotas(shape):
    row = lax.broadcasted_iota(jnp.int32, shape, 0)
    lane = lax.broadcasted_iota(jnp.int32, shape, 1)
    return row, lane


def start_tiles(proj_hbm, tiles, sems):
    per = proj_hbm.shape[0] // CHUNKS
    copies = []
    for c in range(CHUNKS):
        part = pl.ds(c * per, per)
        copy = pltpu.make_async_copy(proj_hbm.at[part], tiles.at[part], sems.at[c])
        copy.start()
        copies.append(copy)
    return copies


def plane_masks(lane):
    return (lane % TV) // 8 < 7, lane % 8 < 7


def rows8(start):
    return pl.ds(pl.multiple_of(start, 8), 8)


def add_rows(accs, starts, values):
    held = [acc[rows8(start), :] for acc, start in zip(accs, starts)]
    for acc, start, old, value in zip(accs, starts, held, values):
        acc[rows8(start), :] = old + value


def forward_kernel(
    count, ray_hbm, voxel_hbm, vol_hbm, sino_hbm, proj_hbm,
    partial_out, index_out, tiles,
    ray, voxel, index, vol, sino, double, table, acc0, acc1, acc2, acc3,
    sems, tile_sems,
):
    slots = proj_hbm.shape[0]
    lines = ray.shape[0]
    rays = acc0.shape[0] // 8 - 1
    voxel_tiles = table.shape[0] // 8
    owned = sino.shape[0]
    width = vol.shape[1]
    loads = [
        pltpu.make_async_copy(source, target, sems.at[i])
        for i, (source, target) in enumerate(
            [(voxel_hbm, voxel), (ray_hbm, ray), (vol_hbm, vol), (sino_hbm, sino)]
        )
    ]
    for load in loads:
        load.start()
    copies = start_tiles(proj_hbm, tiles, tile_sems)
    accs = (acc0, acc1, acc2, acc3)
    for acc in accs:
        acc[...] = jnp.zeros_like(acc)
    row, lane = iotas((8, 128))
    low, top = lane < TV, row < 4

    loads[0].wait()
    loads[1].wait()
    line, place = iotas((lines, 128))
    live = 128 * line + place < count[0]
    rays8, voxels8 = ray[...] * 8, voxel[...] * 8
    index_out[0:lines, :] = voxels8
    index_out[lines:2 * lines, :] = jnp.where(live, rays8, rays * 8)
    index_out[2 * lines:3 * lines, :] = rays8
    index_out[3 * lines:4 * lines, :] = jnp.where(live, voxels8, voxel_tiles * 8)
    to_scalar = pltpu.make_async_copy(index_out, index, sems.at[4])
    to_scalar.start()

    loads[2].wait()
    field = vol[...]
    double[0:4, :] = field
    double[4:8, :] = field
    for j in range(width // 128):
        x = double[:, 128 * j:128 * j + 128].astype(jnp.bfloat16).astype(jnp.float32)
        turned = pltpu.roll(x, TV, axis=1)
        zero = jnp.zeros_like(x)
        first = jnp.where(jnp.logical_and(top, low), x, zero)
        second = jnp.where(jnp.logical_and(top, low), turned, zero)
        other = jnp.logical_not(jnp.logical_or(top, low))
        table[16 * j:16 * j + 8, :] = jnp.where(other, turned, first)
        table[16 * j + 8:16 * j + 16, :] = jnp.where(other, x, second)

    loads[3].wait()
    mine = (lax.axis_index("tile") * lax.axis_size("rep") + lax.axis_index("rep")) * owned
    for r in range(owned):
        acc0[pl.ds(pl.multiple_of((mine + r) * 8, 8), 4), :] = -sino[r]
    to_scalar.wait()
    per = slots // CHUNKS
    for first in range(0, slots, 2 * GROUP):
        if first % per == 0:
            copies[first // per].wait()
        rows = []
        for n in (first, first + GROUP):
            picked = [
                table[rows8(index[(n + i) // 128, (n + i) % 128]), :] for i in range(GROUP)
            ]
            pairs = [jnp.where(top, picked[2 * i], picked[2 * i + 1]) for i in range(2)]
            zero = jnp.zeros_like(pairs[0])
            left = jnp.concatenate([pairs[0], zero], axis=0).astype(jnp.bfloat16)
            right = jnp.concatenate([zero, pairs[1]], axis=0).astype(jnp.bfloat16)
            rows.append(jnp.concatenate([left, right], axis=1))
        sums = jnp.dot(
            jnp.concatenate(rows, axis=0),
            jnp.concatenate(
                [
                    tiles[n:n + GROUP].reshape(GROUP * TV, TR)
                    for n in (first, first + GROUP)
                ],
                axis=1,
            ),
            preferred_element_type=jnp.float32,
        )
        for part, n in enumerate((first, first + GROUP)):
            mine = sums[16 * part:16 * part + 16, TR * part:TR * part + TR]
            add_rows(
                accs,
                [index[lines + (n + i) // 128, (n + i) % 128] for i in range(GROUP)],
                [mine[0:8], mine[0:8], mine[8:16], mine[8:16]],
            )
    for q in range(rays // 4):
        halves = []
        for r in (4 * q, 4 * q + 2):
            at = [slice(8 * (r + k), 8 * (r + k) + 8) for k in range(2)]
            even = [acc0[at[k], :] + acc2[at[k], :] for k in range(2)]
            odd = [acc1[at[k], :] + acc3[at[k], :] for k in range(2)]
            halves.append(
                jnp.where(top, even[0], odd[1])
                + pltpu.roll(jnp.where(top, even[1], odd[0]), 4, axis=0)
            )
        partial_out[16 * q:16 * q + 16, :] = jnp.concatenate(halves, axis=0).astype(jnp.bfloat16)


def edges_kernel(vol, split, dual, edge_out, halo_out):
    start = lax.axis_index("slab") == 0
    for j in range(vol.shape[1] // 128):
        at = slice(128 * j, 128 * j + 128)
        edge = vol[3:4, at] - dual[0, 3:4, at] + split[0, 3:4, at]
        edge_out[:, at] = edge
        halo_out[:, at] = jnp.broadcast_to(jnp.where(start, edge, vol[0:1, at]), (4, 128))


def local_kernel(rho, vol, split, dual, edge, from_next, from_previous, base_out):
    slab, slabs = lax.axis_index("slab"), lax.axis_size("slab")
    factor = TAU * rho[0]
    row, lane = iotas((8, 128))
    row_mask, col_mask = plane_masks(lane)
    for j in range(vol.shape[1] // 128):
        at = slice(128 * j, 128 * j + 128)
        x = jnp.concatenate([vol[:, at]] * 2, axis=0)
        gap = [
            jnp.concatenate([dual[k, :, at] - split[k, :, at]] * 2, axis=0) for k in range(3)
        ]
        above = jnp.where(slab == slabs - 1, 0.0, from_next[0:1, at] - edge[:, at])
        below = jnp.where(slab == 0, 0.0, x[0:1] - from_previous[0:1, at])
        depth = jnp.where(row < 3, pltpu.roll(x, 7, axis=0) - x + gap[0], above)
        across = jnp.where(row_mask, pltpu.roll(x, 120, axis=1) - x + gap[1], 0.0)
        along = jnp.where(col_mask, pltpu.roll(x, 127, axis=1) - x + gap[2], 0.0)
        adjoint = jnp.where(row == 0, below, pltpu.roll(depth, 1, axis=0)) - depth
        adjoint += jnp.where((lane % TV) >= 8, pltpu.roll(across, 8, axis=1), 0.0) - across
        adjoint += jnp.where(lane % 8 >= 1, pltpu.roll(along, 1, axis=1), 0.0) - along
        base_out[:, at] = (x - factor * adjoint)[0:4]


def backward_kernel(
    indices, tiles, part, moved, grad_out,
    index, table, acc0, acc1, acc2, acc3, sem,
):
    slots = tiles.shape[0]
    lines = indices.shape[0] // 4
    rays = table.shape[0] // 8
    voxel_tiles = acc0.shape[0] // 8 - 1
    to_scalar = pltpu.make_async_copy(indices, index, sem)
    to_scalar.start()
    accs = (acc0, acc1, acc2, acc3)
    for acc in accs:
        acc[...] = jnp.zeros_like(acc)
    row, lane = iotas((8, 128))
    low, top = lane < TV, row < 4
    for q in range(rays // 4):
        at = slice(16 * q, 16 * q + 16)
        total = part[at, :].astype(jnp.float32) + moved[at, :].astype(jnp.float32)
        for k in range(2):
            x = total[8 * k:8 * k + 8]
            turned = pltpu.roll(x, 4, axis=0)
            r = 8 * (4 * q + 2 * k)
            table[r:r + 8, :] = jnp.where(top, x, turned)
            table[r + 8:r + 16, :] = jnp.where(top, turned, x)

    to_scalar.wait()
    for first in range(0, slots, 2 * GROUP):
        rows = []
        for n in (first, first + GROUP):
            picked = [
                table[rows8(index[2 * lines + (n + i) // 128, (n + i) % 128]), :]
                for i in range(GROUP)
            ]
            pairs = [jnp.where(top, picked[2 * i], picked[2 * i + 1]) for i in range(2)]
            rows.append(jnp.concatenate(pairs, axis=0).astype(jnp.bfloat16))
        zero = jnp.zeros_like(rows[0])
        back = lax.dot_general(
            jnp.concatenate(
                [
                    jnp.concatenate([rows[0], zero], axis=1),
                    jnp.concatenate([zero, rows[1]], axis=1),
                ],
                axis=0,
            ),
            jnp.concatenate(
                [
                    tiles[n:n + GROUP].reshape(GROUP * TV, TR)
                    for n in (first, first + GROUP)
                ],
                axis=1,
            ),
            (((1,), (1,)), ((), ())),
            preferred_element_type=jnp.float32,
        )
        for part, n in enumerate((first, first + GROUP)):
            mine = back[16 * part:16 * part + 16]
            add_rows(
                accs,
                [index[3 * lines + (n + i) // 128, (n + i) % 128] for i in range(GROUP)],
                [mine[8 * k:8 * k + 8, 128 * k:128 * k + 128] for k in (0, 0, 1, 1)],
            )
    for j in range(voxel_tiles // 2):
        at = [slice(16 * j + 8 * k, 16 * j + 8 * k + 8) for k in range(2)]
        even = [acc0[at[k], :] + acc2[at[k], :] for k in range(2)]
        odd = [acc1[at[k], :] + acc3[at[k], :] for k in range(2)]
        turned = pltpu.roll(jnp.where(top, even[1], odd[0]), TV, axis=1)
        both = jnp.where(top == low, jnp.where(top, even[0], odd[1]), turned)
        grad_out[:, 128 * j:128 * j + 128] = (both + pltpu.roll(both, 4, axis=0))[0:4]


def update_kernel(
    grad, grad_other, ahead, base, dual, limits,
    new_volume, new_split, new_dual,
):
    last = lax.axis_index("slab") == lax.axis_size("slab") - 1
    row, lane = iotas((8, 128))
    row_mask, col_mask = plane_masks(lane)
    inner = jnp.logical_or(row < 3, jnp.logical_not(last))
    for j in range(dual.shape[2] // 128):
        at = slice(128 * j, 128 * j + 128)
        limit = limits[:, at]
        own = base[:, at] - TAU * (grad[:, at] + grad_other[:, at])
        field = jnp.where(row < 4, jnp.concatenate([own] * 2, axis=0), ahead[:, at])
        new_volume[:, at] = own
        steps = (
            jnp.where(inner, pltpu.roll(field, 7, axis=0) - field, 0.0),
            jnp.where(row_mask, pltpu.roll(field, 120, axis=1) - field, 0.0),
            jnp.where(col_mask, pltpu.roll(field, 127, axis=1) - field, 0.0),
        )
        for k in range(3):
            mixed = steps[k][0:4] + dual[k, :, at]
            clipped = jnp.clip(mixed, -limit, limit)
            new_dual[k, :, at] = clipped
            new_split[k, :, at] = mixed - clipped


def vmem():
    return pl.BlockSpec(memory_space=pltpu.VMEM)


def smem():
    return pl.BlockSpec(memory_space=pltpu.SMEM)


def hbm():
    return pl.BlockSpec(memory_space=pltpu.HBM)


def params():
    return pltpu.CompilerParams(vmem_limit_bytes=VMEM_LIMIT)


def shards(
    volume, split_var, dual_var, sinogram, proj_tiles, ray_index, voxel_index, tile_count, rho
):
    f32, bf16 = jnp.float32, jnp.bfloat16
    slices, width = volume.shape
    slots = ray_index.shape[0]
    owned = sinogram.shape[0]
    group = lax.axis_size(("tile", "rep"))
    reps = lax.axis_size("rep")
    slabs = lax.axis_size("slab")
    rays = owned * group
    voxel_tiles = width // TV
    lines = slots // 128
    ray_index, voxel_index = ray_index.reshape(lines, 128), voxel_index.reshape(lines, 128)
    sources = [
        pltpu.with_memory_space_constraint(x, pltpu.HBM)
        for x in (ray_index, voxel_index, volume, sinogram, proj_tiles)
    ]

    partial, indices, tiles = pl.pallas_call(
        forward_kernel,
        out_shape=(
            jax.ShapeDtypeStruct((rays * slices, TR), bf16),
            jax.ShapeDtypeStruct((4 * lines, 128), jnp.int32),
            jax.ShapeDtypeStruct(proj_tiles.shape, bf16),
        ),
        in_specs=[smem()] + [hbm()] * 5,
        out_specs=(vmem(),) * 3,
        scratch_shapes=[
            pltpu.VMEM((lines, 128), jnp.int32),
            pltpu.VMEM((lines, 128), jnp.int32),
            pltpu.SMEM((4 * lines, 128), jnp.int32),
            pltpu.VMEM((slices, width), f32),
            pltpu.VMEM(sinogram.shape, f32),
            pltpu.VMEM((8, width), f32),
            pltpu.VMEM((voxel_tiles * 8, 128), f32),
        ]
        + [pltpu.VMEM((rays * 8 + 8, 128), f32)] * 4
        + [pltpu.SemaphoreType.DMA((5,)), pltpu.SemaphoreType.DMA((CHUNKS,))],
        compiler_params=params(),
        name="forward",
    )(tile_count, *sources)

    row = jax.ShapeDtypeStruct((1, width), f32)
    edge, halo = pl.pallas_call(
        edges_kernel,
        out_shape=(row, jax.ShapeDtypeStruct((4, width), f32)),
        in_specs=[vmem()] * 3,
        out_specs=(vmem(),) * 2,
        compiler_params=params(),
        name="edges",
    )(volume, split_var, dual_var)
    across = [(i, i ^ 3) for i in range(2 * reps)]
    down = [(i, i - 1) for i in range(1, slabs)]
    if slabs == 2:
        from_next = from_previous = lax.ppermute(halo, ("slab", "rep"), across)
    else:
        from_next = lax.ppermute(volume[0:1], "slab", down)
        from_previous = lax.ppermute(edge, "slab", [(i - 1, i) for i in range(1, slabs)])
    swap = [(i, i ^ 1) for i in range(reps)]
    moved = lax.ppermute(partial, "rep", swap)
    step = reps
    while step < group:
        partial = (partial.astype(f32) + moved.astype(f32)).astype(bf16)
        moved = lax.ppermute(
            partial, ("tile", "rep"), [(i, i ^ (step + 1)) for i in range(group)]
        )
        step *= 2
    limits = jnp.broadcast_to((1.0 / rho)[:, None], (1, width))
    moved, from_next, from_previous, limits = lax.optimization_barrier(
        (moved, from_next, from_previous, limits)
    )

    base = pl.pallas_call(
        local_kernel,
        out_shape=jax.ShapeDtypeStruct((slices, width), f32),
        in_specs=[smem()] + [vmem()] * 6,
        out_specs=vmem(),
        compiler_params=params(),
        name="local",
    )(rho, volume, split_var, dual_var, edge, from_next, from_previous)

    grad = pl.pallas_call(
        backward_kernel,
        out_shape=jax.ShapeDtypeStruct((slices, width), f32),
        in_specs=[vmem()] * 4,
        out_specs=vmem(),
        scratch_shapes=[
            pltpu.SMEM((4 * lines, 128), jnp.int32),
            pltpu.VMEM((rays * 8, 128), f32),
        ]
        + [pltpu.VMEM((voxel_tiles * 8 + 8, 128), f32)] * 4
        + [pltpu.SemaphoreType.DMA],
        compiler_params=params(),
        name="backward",
    )(indices, tiles, partial, moved)
    grad_other = lax.ppermute(grad, "rep", swap)
    ahead = base[0:1] - TAU * (grad[0:1] + grad_other[0:1])
    if slabs == 2:
        ahead = lax.ppermute(ahead, ("slab", "rep"), across)
    else:
        ahead = lax.ppermute(ahead, "slab", down)

    triple = jax.ShapeDtypeStruct((3, slices, width), f32)
    return pl.pallas_call(
        update_kernel,
        out_shape=(jax.ShapeDtypeStruct((slices, width), f32), triple, triple),
        in_specs=[vmem()] * 6,
        out_specs=(vmem(),) * 3,
        compiler_params=params(),
        name="update",
    )(grad, grad_other, ahead, base, dual_var, limits)


def solution(mesh):
    return jax.shard_map(
        shards,
        mesh=mesh,
        in_specs=(
            P(("parts", "slab"), "tile"),
            P(None, ("parts", "slab"), "tile"),
            P(None, ("parts", "slab"), "tile"),
            P(("tile", "rep"), ("parts", "slab"), None),
            P(("tile", "rep"), None, None),
            P(("tile", "rep")),
            P(("tile", "rep")),
            P(("tile", "rep")),
            P(),
        ),
        out_specs=(
            P(("parts", "slab"), "tile"),
            P(None, ("parts", "slab"), "tile"),
            P(None, ("parts", "slab"), "tile"),
        ),
        check_vma=False,
    )
```

```python
import functools

import jax
import jax.numpy as jnp
from jax import lax
from jax.experimental import pallas as pl
from jax.experimental.pallas import tpu as pltpu
from jax.sharding import PartitionSpec as P

TV = 64
TR = 128
TAU = 0.5
GROUP = 4
CUTS = (0, 2, 5, 8)
VMEM_LIMIT = 16 * 1024 * 1024


def iotas(shape):
    row = lax.broadcasted_iota(jnp.int32, shape, 0)
    lane = lax.broadcasted_iota(jnp.int32, shape, 1)
    return row, lane


def start_tiles(proj_hbm, tiles, sems):
    eighth = proj_hbm.shape[0] // CUTS[-1]
    copies = {}
    for c, (low, high) in enumerate(zip(CUTS, CUTS[1:])):
        part = pl.ds(low * eighth, (high - low) * eighth)
        copy = pltpu.make_async_copy(proj_hbm.at[part], tiles.at[part], sems.at[c])
        copy.start()
        copies[low * eighth] = copy
    return copies


def plane_masks(lane):
    return (lane % TV) // 8 < 7, lane % 8 < 7


def rows8(start):
    return pl.ds(pl.multiple_of(start, 8), 8)


def add_rows(accs, starts, values):
    held = [acc[rows8(start), :] for acc, start in zip(accs, starts)]
    for acc, start, old, value in zip(accs, starts, held, values):
        acc[rows8(start), :] = old + value


def forward_kernel(
    count, ray_hbm, voxel_hbm, vol_hbm, sino_hbm, proj_hbm,
    partial_out, index_out, tiles,
    ray, voxel, vol, sino, double, table, acc0, acc1, acc2, acc3,
    sems, tile_sems,
):
    slots = proj_hbm.shape[0]
    lines = ray.shape[0]
    rays = acc0.shape[0] // 8 - 1
    owned = sino.shape[0]
    width = vol.shape[1]
    pairs = [
        (voxel_hbm, voxel), (ray_hbm, ray), (vol_hbm, vol), (sino_hbm, sino),
        (voxel_hbm, index_out.at[pl.ds(0, lines)]), (ray_hbm, index_out.at[pl.ds(lines, lines)]),
    ]
    loads = [
        pltpu.make_async_copy(source, target, sems.at[i]) for i, (source, target) in enumerate(pairs)
    ]
    for load in loads[:3]:
        load.start()
    copies = start_tiles(proj_hbm, tiles, tile_sems)
    for load in loads[3:]:
        load.start()
    accs = (acc0, acc1, acc2, acc3)
    for acc in accs:
        acc[...] = jnp.zeros_like(acc)
    row, lane = iotas((8, 128))
    low, top = lane < TV, row < 4

    loads[2].wait()
    field = vol[...]
    double[0:4, :] = field
    double[4:8, :] = field
    for j in range(width // 128):
        x = double[:, 128 * j:128 * j + 128].astype(jnp.bfloat16).astype(jnp.float32)
        turned = pltpu.roll(x, TV, axis=1)
        zero = jnp.zeros_like(x)
        first = jnp.where(jnp.logical_and(top, low), x, zero)
        second = jnp.where(jnp.logical_and(top, low), turned, zero)
        other = jnp.logical_not(jnp.logical_or(top, low))
        table[16 * j:16 * j + 8, :] = jnp.where(other, turned, first)
        table[16 * j + 8:16 * j + 16, :] = jnp.where(other, x, second)

    loads[3].wait()
    mine = (lax.axis_index("tile") * lax.axis_size("rep") + lax.axis_index("rep")) * owned
    for r in range(owned):
        acc0[pl.ds(pl.multiple_of((mine + r) * 8, 8), 4), :] = -sino[r]
    loads[0].wait()
    loads[1].wait()
    used = count[0]
    for n in range(0, slots, GROUP):
        if n in copies:
            copies[n].wait()
        at = [divmod(n + i, 128) for i in range(GROUP)]
        picked = [table[rows8(voxel[line, place] * 8), :] for line, place in at]
        pairs = [jnp.where(top, picked[2 * i], picked[2 * i + 1]) for i in range(2)]
        zero = jnp.zeros_like(pairs[0])
        left = jnp.concatenate([pairs[0], zero], axis=0).astype(jnp.bfloat16)
        right = jnp.concatenate([zero, pairs[1]], axis=0).astype(jnp.bfloat16)
        sums = jnp.dot(
            jnp.concatenate([left, right], axis=1),
            tiles[n:n + GROUP].reshape(GROUP * TV, TR),
            preferred_element_type=jnp.float32,
        )
        add_rows(
            accs,
            [
                jnp.where(n + i < used, ray[line, place], rays) * 8
                for i, (line, place) in enumerate(at)
            ],
            [sums[0:8], sums[0:8], sums[8:16], sums[8:16]],
        )
    loads[4].wait()
    loads[5].wait()
    for q in range(rays // 4):
        halves = []
        for r in (4 * q, 4 * q + 2):
            at = [slice(8 * (r + k), 8 * (r + k) + 8) for k in range(2)]
            even = [acc0[at[k], :] + acc2[at[k], :] for k in range(2)]
            odd = [acc1[at[k], :] + acc3[at[k], :] for k in range(2)]
            halves.append(
                jnp.where(top, even[0], odd[1])
                + pltpu.roll(jnp.where(top, even[1], odd[0]), 4, axis=0)
            )
        partial_out[16 * q:16 * q + 16, :] = jnp.concatenate(halves, axis=0).astype(jnp.bfloat16)


def local_kernel(rho, vol, split, dual, base_out, edge_out, first_out, scale_out):
    factor = TAU * rho[0]
    limit = 1.0 / rho[0]
    row, lane = iotas((8, 128))
    row_mask, col_mask = plane_masks(lane)
    for j in range(vol.shape[1] // 128):
        at = slice(128 * j, 128 * j + 128)
        field = vol[:, at]
        x = jnp.concatenate([field] * 2, axis=0)
        gap = [
            jnp.concatenate([dual[k, :, at] - split[k, :, at]] * 2, axis=0) for k in range(3)
        ]
        depth = jnp.where(row < 3, pltpu.roll(x, 7, axis=0) - x + gap[0], 0.0)
        across = jnp.where(row_mask, pltpu.roll(x, 120, axis=1) - x + gap[1], 0.0)
        along = jnp.where(col_mask, pltpu.roll(x, 127, axis=1) - x + gap[2], 0.0)
        adjoint = pltpu.roll(depth, 1, axis=0) - depth
        adjoint += jnp.where((lane % TV) >= 8, pltpu.roll(across, 8, axis=1), 0.0) - across
        adjoint += jnp.where(lane % 8 >= 1, pltpu.roll(along, 1, axis=1), 0.0) - along
        base_out[:, at] = (x - factor * adjoint)[0:4]
        edge_out[:, at] = (x - gap[0])[3:4]
        first_out[:, at] = field[0:1]
        scale_out[0:1, at] = jnp.full((1, 128), limit, jnp.float32)
        scale_out[1:2, at] = jnp.full((1, 128), factor, jnp.float32)


def backward_kernel(columns, count, indices, tiles, *refs):
    parts, (grad_out, index, table, acc0, acc1, acc2, acc3, sem) = refs[:columns], refs[columns:]
    slots = tiles.shape[0]
    lines = indices.shape[0] // 2
    rays = table.shape[0] // 8
    voxel_tiles = acc0.shape[0] // 8 - 1
    to_scalar = pltpu.make_async_copy(indices, index, sem)
    to_scalar.start()
    accs = (acc0, acc1, acc2, acc3)
    for acc in accs:
        acc[...] = jnp.zeros_like(acc)
    row, lane = iotas((8, 128))
    low, top = lane < TV, row < 4
    for q in range(rays // 4):
        at = slice(16 * q, 16 * q + 16)
        total = parts[0][at, :].astype(jnp.float32)
        for part in parts[1:]:
            total += part[at, :].astype(jnp.float32)
        for k in range(2):
            x = total[8 * k:8 * k + 8]
            turned = pltpu.roll(x, 4, axis=0)
            r = 8 * (4 * q + 2 * k)
            table[r:r + 8, :] = jnp.where(top, x, turned)
            table[r + 8:r + 16, :] = jnp.where(top, turned, x)

    to_scalar.wait()
    used = count[0]
    for n in range(0, slots, GROUP):
        at = [divmod(n + i, 128) for i in range(GROUP)]
        picked = [table[rows8(index[lines + line, place] * 8), :] for line, place in at]
        rows = jnp.concatenate(
            [jnp.where(top, picked[2 * i], picked[2 * i + 1]) for i in range(2)], axis=0
        )
        back = lax.dot_general(
            rows.astype(jnp.bfloat16),
            tiles[n:n + GROUP].reshape(GROUP * TV, TR),
            (((1,), (1,)), ((), ())),
            preferred_element_type=jnp.float32,
        )
        add_rows(
            accs,
            [
                jnp.where(n + i < used, index[line, place], voxel_tiles) * 8
                for i, (line, place) in enumerate(at)
            ],
            [back[8 * k:8 * k + 8, 128 * k:128 * k + 128] for k in (0, 0, 1, 1)],
        )
    for j in range(voxel_tiles // 2):
        at = [slice(16 * j + 8 * k, 16 * j + 8 * k + 8) for k in range(2)]
        even = [acc0[at[k], :] + acc2[at[k], :] for k in range(2)]
        odd = [acc1[at[k], :] + acc3[at[k], :] for k in range(2)]
        turned = pltpu.roll(jnp.where(top, even[1], odd[0]), TV, axis=1)
        both = jnp.where(top == low, jnp.where(top, even[0], odd[1]), turned)
        grad_out[:, 128 * j:128 * j + 128] = (both + pltpu.roll(both, 4, axis=0))[0:4]


def update_kernel(
    grad, grad_other, from_next, from_previous, base, edge, first, dual, scales,
    new_volume, new_split, new_dual,
):
    slab, slabs = lax.axis_index("slab"), lax.axis_size("slab")
    row, lane = iotas((8, 128))
    short = lax.broadcasted_iota(jnp.int32, (4, 128), 0)
    row_mask, col_mask = plane_masks(lane)
    inner = jnp.logical_or(row < 3, slab < slabs - 1)
    for j in range(dual.shape[2] // 128):
        at = slice(128 * j, 128 * j + 128)
        limit, factor = scales[0:1, at], scales[1:2, at]
        above = jnp.where(slab == slabs - 1, 0.0, factor * (from_next[1:2, at] - edge[:, at]))
        below = jnp.where(slab == 0, 0.0, factor * (first[:, at] - from_previous[0:1, at]))
        own = base[:, at] - TAU * (grad[:, at] + grad_other[:, at])
        own += jnp.where(short == 0, -below, jnp.where(short == 3, above, 0.0))
        ahead = from_next[0:1, at] - above
        field = jnp.where(row < 4, jnp.concatenate([own] * 2, axis=0), ahead)
        new_volume[:, at] = own
        steps = (
            jnp.where(inner, pltpu.roll(field, 7, axis=0) - field, 0.0),
            jnp.where(row_mask, pltpu.roll(field, 120, axis=1) - field, 0.0),
            jnp.where(col_mask, pltpu.roll(field, 127, axis=1) - field, 0.0),
        )
        for k in range(3):
            mixed = steps[k][0:4] + dual[k, :, at]
            clipped = jnp.clip(mixed, -limit, limit)
            new_dual[k, :, at] = clipped
            new_split[k, :, at] = mixed - clipped


def vmem():
    return pl.BlockSpec(memory_space=pltpu.VMEM)


def smem():
    return pl.BlockSpec(memory_space=pltpu.SMEM)


def hbm():
    return pl.BlockSpec(memory_space=pltpu.HBM)


def params():
    return pltpu.CompilerParams(vmem_limit_bytes=VMEM_LIMIT)


def shards(
    volume, split_var, dual_var, sinogram, proj_tiles, ray_index, voxel_index, tile_count, rho
):
    f32, bf16 = jnp.float32, jnp.bfloat16
    slices, width = volume.shape
    slots = ray_index.shape[0]
    owned = sinogram.shape[0]
    group = lax.axis_size(("tile", "rep"))
    reps = lax.axis_size("rep")
    slabs = lax.axis_size("slab")
    rays = owned * group
    voxel_tiles = width // TV
    lines = slots // 128
    ray_index, voxel_index = ray_index.reshape(lines, 128), voxel_index.reshape(lines, 128)
    sources = [
        pltpu.with_memory_space_constraint(x, pltpu.HBM)
        for x in (ray_index, voxel_index, volume, sinogram, proj_tiles)
    ]

    partial, indices, tiles = pl.pallas_call(
        forward_kernel,
        out_shape=(
            jax.ShapeDtypeStruct((rays * slices, TR), bf16),
            jax.ShapeDtypeStruct((2 * lines, 128), jnp.int32),
            jax.ShapeDtypeStruct(proj_tiles.shape, bf16),
        ),
        in_specs=[smem()] + [hbm()] * 5,
        out_specs=(vmem(),) * 3,
        scratch_shapes=[
            pltpu.SMEM((lines, 128), jnp.int32),
            pltpu.SMEM((lines, 128), jnp.int32),
            pltpu.VMEM((slices, width), f32),
            pltpu.VMEM(sinogram.shape, f32),
            pltpu.VMEM((8, width), f32),
            pltpu.VMEM((voxel_tiles * 8, 128), f32),
        ]
        + [pltpu.VMEM((rays * 8 + 8, 128), f32)] * 4
        + [pltpu.SemaphoreType.DMA((6,)), pltpu.SemaphoreType.DMA((len(CUTS) - 1,))],
        compiler_params=params(),
        name="forward",
    )(tile_count, *sources)

    base, edge, first, scales = pl.pallas_call(
        local_kernel,
        out_shape=(
            jax.ShapeDtypeStruct((slices, width), f32),
            jax.ShapeDtypeStruct((1, width), f32),
            jax.ShapeDtypeStruct((1, width), f32),
            jax.ShapeDtypeStruct((2, width), f32),
        ),
        in_specs=[smem()] + [vmem()] * 3,
        out_specs=(vmem(),) * 4,
        compiler_params=params(),
        name="local",
    )(rho, volume, split_var, dual_var)

    swap = [(i, i ^ 1) for i in range(reps)]
    moved = lax.ppermute(partial, "rep", swap)
    chip = (partial.astype(f32) + moved.astype(f32)).astype(bf16)
    columns = group // reps
    steps = [*range(1, columns)]
    steps[:2] = steps[1::-1]
    parts = [chip] + [
        lax.ppermute(
            chip, ("tile", "rep"), [(i, i ^ (reps * step + 1)) for i in range(group)]
        )
        for step in steps
    ]
    parts[-1], base, edge, first, scales = lax.optimization_barrier(
        (parts[-1], base, edge, first, scales)
    )

    grad = pl.pallas_call(
        functools.partial(backward_kernel, columns),
        out_shape=jax.ShapeDtypeStruct((slices, width), f32),
        in_specs=[smem()] + [vmem()] * (2 + columns),
        out_specs=vmem(),
        scratch_shapes=[
            pltpu.SMEM((2 * lines, 128), jnp.int32),
            pltpu.VMEM((rays * 8, 128), f32),
        ]
        + [pltpu.VMEM((voxel_tiles * 8 + 8, 128), f32)] * 4
        + [pltpu.SemaphoreType.DMA],
        compiler_params=params(),
        name="backward",
    )(tile_count, indices, tiles, *parts)
    grad_other = lax.ppermute(grad, "rep", swap)
    ahead = jnp.concatenate([base[0:1] - TAU * (grad[0:1] + grad_other[0:1]), first], axis=0)
    behind = jnp.concatenate([edge, edge], axis=0)
    if slabs == 2:
        halo = jnp.where(lax.axis_index("slab") == 0, behind, ahead)
        from_next = from_previous = lax.ppermute(
            halo, ("slab", "rep"), [(i, i ^ 3) for i in range(2 * reps)]
        )
    else:
        from_next = lax.ppermute(ahead, "slab", [(i, i - 1) for i in range(1, slabs)])
        from_previous = lax.ppermute(behind, "slab", [(i - 1, i) for i in range(1, slabs)])

    return pl.pallas_call(
        update_kernel,
        out_shape=(
            jax.ShapeDtypeStruct((slices, width), f32),
            jax.ShapeDtypeStruct((3, slices, width), f32),
            jax.ShapeDtypeStruct((3, slices, width), f32),
        ),
        in_specs=[vmem()] * 9,
        out_specs=(vmem(), vmem(), vmem()),
        compiler_params=params(),
        name="update",
    )(grad, grad_other, from_next, from_previous, base, edge, first, dual_var, scales)


def solution(mesh):
    return jax.shard_map(
        shards,
        mesh=mesh,
        in_specs=(
            P(("parts", "slab"), "tile"),
            P(None, ("parts", "slab"), "tile"),
            P(None, ("parts", "slab"), "tile"),
            P(("tile", "rep"), ("parts", "slab"), None),
            P(("tile", "rep"), None, None),
            P(("tile", "rep")),
            P(("tile", "rep")),
            P(("tile", "rep")),
            P(),
        ),
        out_specs=(
            P(("parts", "slab"), "tile"),
            P(None, ("parts", "slab"), "tile"),
            P(None, ("parts", "slab"), "tile"),
        ),
        check_vma=False,
    )
```

```python
import jax
import jax.numpy as jnp
from jax import lax
from jax.experimental import pallas as pl
from jax.experimental.pallas import tpu as pltpu
from jax.sharding import PartitionSpec as P

TV = 64
TR = 128
TAU = 0.5
GROUP = 4
CUTS = (0, 2, 5, 8)
VMEM_LIMIT = 16 * 1024 * 1024


def iotas(shape):
    row = lax.broadcasted_iota(jnp.int32, shape, 0)
    lane = lax.broadcasted_iota(jnp.int32, shape, 1)
    return row, lane


def start_tiles(proj_hbm, tiles, sems):
    eighth = proj_hbm.shape[0] // CUTS[-1]
    copies = {}
    for c, (low, high) in enumerate(zip(CUTS, CUTS[1:])):
        part = pl.ds(low * eighth, (high - low) * eighth)
        copy = pltpu.make_async_copy(proj_hbm.at[part], tiles.at[part], sems.at[c])
        copy.start()
        copies[low * eighth] = copy
    return copies


def plane_masks(lane):
    return (lane % TV) // 8 < 7, lane % 8 < 7


def rows8(start):
    return pl.ds(pl.multiple_of(start, 8), 8)


def add_rows(accs, starts, values):
    held = [acc[rows8(start), :] for acc, start in zip(accs, starts)]
    for acc, start, old, value in zip(accs, starts, held, values):
        acc[rows8(start), :] = old + value


def forward_kernel(
    count, ray_hbm, voxel_hbm, vol_hbm, sino_hbm, proj_hbm,
    partial_out, index_out, tiles,
    ray, voxel, vol, sino, double, table, acc0, acc1, acc2, acc3,
    sems, tile_sems,
):
    slots = proj_hbm.shape[0]
    lines = ray.shape[0]
    rays = acc0.shape[0] // 8 - 1
    owned = sino.shape[0]
    width = vol.shape[1]
    pairs = [
        (voxel_hbm, voxel), (ray_hbm, ray), (vol_hbm, vol), (sino_hbm, sino),
        (voxel_hbm, index_out.at[pl.ds(0, lines)]), (ray_hbm, index_out.at[pl.ds(lines, lines)]),
    ]
    loads = [
        pltpu.make_async_copy(source, target, sems.at[i]) for i, (source, target) in enumerate(pairs)
    ]
    for load in loads[:3]:
        load.start()
    copies = start_tiles(proj_hbm, tiles, tile_sems)
    for load in loads[3:]:
        load.start()
    accs = (acc0, acc1, acc2, acc3)
    for acc in accs:
        acc[...] = jnp.zeros_like(acc)
    row, lane = iotas((8, 128))
    low, top = lane < TV, row < 4

    loads[2].wait()
    field = vol[...]
    double[0:4, :] = field
    double[4:8, :] = field
    for j in range(width // 128):
        x = double[:, 128 * j:128 * j + 128].astype(jnp.bfloat16).astype(jnp.float32)
        turned = pltpu.roll(x, TV, axis=1)
        zero = jnp.zeros_like(x)
        first = jnp.where(jnp.logical_and(top, low), x, zero)
        second = jnp.where(jnp.logical_and(top, low), turned, zero)
        other = jnp.logical_not(jnp.logical_or(top, low))
        table[16 * j:16 * j + 8, :] = jnp.where(other, turned, first)
        table[16 * j + 8:16 * j + 16, :] = jnp.where(other, x, second)

    loads[3].wait()
    mine = (lax.axis_index("tile") * lax.axis_size("rep") + lax.axis_index("rep")) * owned
    for r in range(owned):
        acc0[pl.ds(pl.multiple_of((mine + r) * 8, 8), 4), :] = -sino[r]
    loads[0].wait()
    loads[1].wait()
    used = count[0]
    for n in range(0, slots, GROUP):
        if n in copies:
            copies[n].wait()
        at = [divmod(n + i, 128) for i in range(GROUP)]
        picked = [table[rows8(voxel[line, place] * 8), :] for line, place in at]
        pairs = [jnp.where(top, picked[2 * i], picked[2 * i + 1]) for i in range(2)]
        zero = jnp.zeros_like(pairs[0])
        left = jnp.concatenate([pairs[0], zero], axis=0).astype(jnp.bfloat16)
        right = jnp.concatenate([zero, pairs[1]], axis=0).astype(jnp.bfloat16)
        sums = jnp.dot(
            jnp.concatenate([left, right], axis=1),
            tiles[n:n + GROUP].reshape(GROUP * TV, TR),
            preferred_element_type=jnp.float32,
        )
        add_rows(
            accs,
            [
                jnp.where(n + i < used, ray[line, place], rays) * 8
                for i, (line, place) in enumerate(at)
            ],
            [sums[0:8], sums[0:8], sums[8:16], sums[8:16]],
        )
    loads[4].wait()
    loads[5].wait()
    for q in range(rays // 4):
        halves = []
        for r in (4 * q, 4 * q + 2):
            at = [slice(8 * (r + k), 8 * (r + k) + 8) for k in range(2)]
            even = [acc0[at[k], :] + acc2[at[k], :] for k in range(2)]
            odd = [acc1[at[k], :] + acc3[at[k], :] for k in range(2)]
            halves.append(
                jnp.where(top, even[0], odd[1])
                + pltpu.roll(jnp.where(top, even[1], odd[0]), 4, axis=0)
            )
        partial_out[16 * q:16 * q + 16, :] = jnp.concatenate(halves, axis=0).astype(jnp.bfloat16)


def edges_kernel(vol, split, dual, edge_out, halo_out):
    start = lax.axis_index("slab") == 0
    for j in range(vol.shape[1] // 128):
        at = slice(128 * j, 128 * j + 128)
        edge = vol[3:4, at] - dual[0, 3:4, at] + split[0, 3:4, at]
        edge_out[:, at] = edge
        halo_out[:, at] = jnp.broadcast_to(jnp.where(start, edge, vol[0:1, at]), (4, 128))


def local_kernel(rho, vol, split, dual, edge, from_next, from_previous, base_out):
    slab, slabs = lax.axis_index("slab"), lax.axis_size("slab")
    factor = TAU * rho[0]
    row, lane = iotas((8, 128))
    row_mask, col_mask = plane_masks(lane)
    for j in range(vol.shape[1] // 128):
        at = slice(128 * j, 128 * j + 128)
        x = jnp.concatenate([vol[:, at]] * 2, axis=0)
        gap = [
            jnp.concatenate([dual[k, :, at] - split[k, :, at]] * 2, axis=0) for k in range(3)
        ]
        above = jnp.where(slab == slabs - 1, 0.0, from_next[0:1, at] - edge[:, at])
        below = jnp.where(slab == 0, 0.0, x[0:1] - from_previous[0:1, at])
        depth = jnp.where(row < 3, pltpu.roll(x, 7, axis=0) - x + gap[0], above)
        across = jnp.where(row_mask, pltpu.roll(x, 120, axis=1) - x + gap[1], 0.0)
        along = jnp.where(col_mask, pltpu.roll(x, 127, axis=1) - x + gap[2], 0.0)
        adjoint = jnp.where(row == 0, below, pltpu.roll(depth, 1, axis=0)) - depth
        adjoint += jnp.where((lane % TV) >= 8, pltpu.roll(across, 8, axis=1), 0.0) - across
        adjoint += jnp.where(lane % 8 >= 1, pltpu.roll(along, 1, axis=1), 0.0) - along
        base_out[:, at] = (x - factor * adjoint)[0:4]


def backward_kernel(
    count, indices, tiles, part, moved, grad_out,
    index, table, acc0, acc1, acc2, acc3, sem,
):
    slots = tiles.shape[0]
    lines = indices.shape[0] // 2
    rays = table.shape[0] // 8
    voxel_tiles = acc0.shape[0] // 8 - 1
    to_scalar = pltpu.make_async_copy(indices, index, sem)
    to_scalar.start()
    accs = (acc0, acc1, acc2, acc3)
    for acc in accs:
        acc[...] = jnp.zeros_like(acc)
    row, lane = iotas((8, 128))
    low, top = lane < TV, row < 4
    for q in range(rays // 4):
        at = slice(16 * q, 16 * q + 16)
        total = part[at, :].astype(jnp.float32) + moved[at, :].astype(jnp.float32)
        for k in range(2):
            x = total[8 * k:8 * k + 8]
            turned = pltpu.roll(x, 4, axis=0)
            r = 8 * (4 * q + 2 * k)
            table[r:r + 8, :] = jnp.where(top, x, turned)
            table[r + 8:r + 16, :] = jnp.where(top, turned, x)

    to_scalar.wait()
    used = count[0]
    for n in range(0, slots, GROUP):
        at = [divmod(n + i, 128) for i in range(GROUP)]
        picked = [table[rows8(index[lines + line, place] * 8), :] for line, place in at]
        rows = jnp.concatenate(
            [jnp.where(top, picked[2 * i], picked[2 * i + 1]) for i in range(2)], axis=0
        )
        back = lax.dot_general(
            rows.astype(jnp.bfloat16),
            tiles[n:n + GROUP].reshape(GROUP * TV, TR),
            (((1,), (1,)), ((), ())),
            preferred_element_type=jnp.float32,
        )
        add_rows(
            accs,
            [
                jnp.where(n + i < used, index[line, place], voxel_tiles) * 8
                for i, (line, place) in enumerate(at)
            ],
            [back[8 * k:8 * k + 8, 128 * k:128 * k + 128] for k in (0, 0, 1, 1)],
        )
    for j in range(voxel_tiles // 2):
        at = [slice(16 * j + 8 * k, 16 * j + 8 * k + 8) for k in range(2)]
        even = [acc0[at[k], :] + acc2[at[k], :] for k in range(2)]
        odd = [acc1[at[k], :] + acc3[at[k], :] for k in range(2)]
        turned = pltpu.roll(jnp.where(top, even[1], odd[0]), TV, axis=1)
        both = jnp.where(top == low, jnp.where(top, even[0], odd[1]), turned)
        grad_out[:, 128 * j:128 * j + 128] = (both + pltpu.roll(both, 4, axis=0))[0:4]


def plane_kernel(
    grad, grad_other, base, dual, limits,
    field_out, volume_hbm, split_hbm, dual_hbm,
    split, clipped, sems,
):
    row, lane = iotas((4, 128))
    row_mask, col_mask = plane_masks(lane)
    for j in range(dual.shape[2] // 128):
        at = slice(128 * j, 128 * j + 128)
        limit = limits[:, at]
        field = base[:, at] - TAU * (grad[:, at] + grad_other[:, at])
        field_out[:, at] = field
        x = jnp.concatenate([field] * 2, axis=0)
        steps = (
            jnp.where(row_mask, pltpu.roll(x, 120, axis=1)[0:4] - field, 0.0),
            jnp.where(col_mask, pltpu.roll(x, 127, axis=1)[0:4] - field, 0.0),
        )
        for k in range(2):
            mixed = steps[k] + dual[k + 1, :, at]
            bounded = jnp.clip(mixed, -limit, limit)
            clipped[k, :, at] = bounded
            split[k, :, at] = mixed - bounded
    copies = [
        pltpu.make_async_copy(split, split_hbm.at[pl.ds(1, 2)], sems.at[0]),
        pltpu.make_async_copy(clipped, dual_hbm.at[pl.ds(1, 2)], sems.at[1]),
        pltpu.make_async_copy(field_out, volume_hbm, sems.at[2]),
    ]
    for copy in copies:
        copy.start()
    for copy in copies:
        copy.wait()


def depth_kernel(
    field_in, ahead, dual, limits, split_in, dual_in,
    split_hbm, dual_hbm,
    split, clipped, sems,
):
    del split_in, dual_in
    last = lax.axis_index("slab") == lax.axis_size("slab") - 1
    row, lane = iotas((8, 128))
    inner = jnp.logical_or(row < 3, jnp.logical_not(last))
    for j in range(dual.shape[2] // 128):
        at = slice(128 * j, 128 * j + 128)
        limit = limits[:, at]
        x = jnp.concatenate([field_in[:, at]] * 2, axis=0)
        following = jnp.where(row < 3, pltpu.roll(x, 7, axis=0), ahead[:, at])
        mixed = jnp.where(inner, following - x, 0.0)[0:4] + dual[0, :, at]
        bounded = jnp.clip(mixed, -limit, limit)
        clipped[:, at] = bounded
        split[:, at] = mixed - bounded
    copies = [
        pltpu.make_async_copy(split, split_hbm.at[0], sems.at[0]),
        pltpu.make_async_copy(clipped, dual_hbm.at[0], sems.at[1]),
    ]
    for copy in copies:
        copy.start()
    for copy in copies:
        copy.wait()


def vmem():
    return pl.BlockSpec(memory_space=pltpu.VMEM)


def smem():
    return pl.BlockSpec(memory_space=pltpu.SMEM)


def hbm():
    return pl.BlockSpec(memory_space=pltpu.HBM)


def params():
    return pltpu.CompilerParams(vmem_limit_bytes=VMEM_LIMIT)


def shards(
    volume, split_var, dual_var, sinogram, proj_tiles, ray_index, voxel_index, tile_count, rho
):
    f32, bf16 = jnp.float32, jnp.bfloat16
    slices, width = volume.shape
    slots = ray_index.shape[0]
    owned = sinogram.shape[0]
    group = lax.axis_size(("tile", "rep"))
    reps = lax.axis_size("rep")
    slabs = lax.axis_size("slab")
    rays = owned * group
    voxel_tiles = width // TV
    lines = slots // 128
    ray_index, voxel_index = ray_index.reshape(lines, 128), voxel_index.reshape(lines, 128)
    sources = [
        pltpu.with_memory_space_constraint(x, pltpu.HBM)
        for x in (ray_index, voxel_index, volume, sinogram, proj_tiles)
    ]

    partial, indices, tiles = pl.pallas_call(
        forward_kernel,
        out_shape=(
            jax.ShapeDtypeStruct((rays * slices, TR), bf16),
            jax.ShapeDtypeStruct((2 * lines, 128), jnp.int32),
            jax.ShapeDtypeStruct(proj_tiles.shape, bf16),
        ),
        in_specs=[smem()] + [hbm()] * 5,
        out_specs=(vmem(),) * 3,
        scratch_shapes=[
            pltpu.SMEM((lines, 128), jnp.int32),
            pltpu.SMEM((lines, 128), jnp.int32),
            pltpu.VMEM((slices, width), f32),
            pltpu.VMEM(sinogram.shape, f32),
            pltpu.VMEM((8, width), f32),
            pltpu.VMEM((voxel_tiles * 8, 128), f32),
        ]
        + [pltpu.VMEM((rays * 8 + 8, 128), f32)] * 4
        + [pltpu.SemaphoreType.DMA((6,)), pltpu.SemaphoreType.DMA((len(CUTS) - 1,))],
        compiler_params=params(),
        name="forward",
    )(tile_count, *sources)

    row = jax.ShapeDtypeStruct((1, width), f32)
    edge, halo = pl.pallas_call(
        edges_kernel,
        out_shape=(row, jax.ShapeDtypeStruct((4, width), f32)),
        in_specs=[vmem()] * 3,
        out_specs=(vmem(),) * 2,
        compiler_params=params(),
        name="edges",
    )(volume, split_var, dual_var)
    across = [(i, i ^ 3) for i in range(2 * reps)]
    down = [(i, i - 1) for i in range(1, slabs)]
    if slabs == 2:
        from_next = from_previous = lax.ppermute(halo, ("slab", "rep"), across)
    else:
        from_next = lax.ppermute(volume[0:1], "slab", down)
        from_previous = lax.ppermute(edge, "slab", [(i - 1, i) for i in range(1, slabs)])
    swap = [(i, i ^ 1) for i in range(reps)]
    moved = lax.ppermute(partial, "rep", swap)
    step = reps
    while step < group:
        partial = (partial.astype(f32) + moved.astype(f32)).astype(bf16)
        moved = lax.ppermute(
            partial, ("tile", "rep"), [(i, i ^ (step + 1)) for i in range(group)]
        )
        step *= 2
    limits = jnp.broadcast_to((1.0 / rho)[:, None], (1, width))
    moved, from_next, from_previous, limits = lax.optimization_barrier(
        (moved, from_next, from_previous, limits)
    )

    base = pl.pallas_call(
        local_kernel,
        out_shape=jax.ShapeDtypeStruct((slices, width), f32),
        in_specs=[smem()] + [vmem()] * 6,
        out_specs=vmem(),
        compiler_params=params(),
        name="local",
    )(rho, volume, split_var, dual_var, edge, from_next, from_previous)

    grad = pl.pallas_call(
        backward_kernel,
        out_shape=jax.ShapeDtypeStruct((slices, width), f32),
        in_specs=[smem()] + [vmem()] * 4,
        out_specs=vmem(),
        scratch_shapes=[
            pltpu.SMEM((2 * lines, 128), jnp.int32),
            pltpu.VMEM((rays * 8, 128), f32),
        ]
        + [pltpu.VMEM((voxel_tiles * 8 + 8, 128), f32)] * 4
        + [pltpu.SemaphoreType.DMA],
        compiler_params=params(),
        name="backward",
    )(tile_count, indices, tiles, partial, moved)
    grad_other = lax.ppermute(grad, "rep", swap)
    ahead = base[0:1] - TAU * (grad[0:1] + grad_other[0:1])
    if slabs == 2:
        ahead = lax.ppermute(ahead, ("slab", "rep"), across)
    else:
        ahead = lax.ppermute(ahead, "slab", down)

    whole = jax.ShapeDtypeStruct((slices, width), f32)
    triple = jax.ShapeDtypeStruct((3, slices, width), f32)
    field, new_volume, new_split, new_dual = pl.pallas_call(
        plane_kernel,
        out_shape=(whole, whole, triple, triple),
        in_specs=[vmem()] * 5,
        out_specs=(vmem(), hbm(), hbm(), hbm()),
        scratch_shapes=[pltpu.VMEM((2, slices, width), f32)] * 2
        + [pltpu.SemaphoreType.DMA((3,))],
        compiler_params=params(),
        name="plane",
    )(grad, grad_other, base, dual_var, limits)
    new_split, new_dual = pl.pallas_call(
        depth_kernel,
        out_shape=(triple, triple),
        in_specs=[vmem()] * 4 + [hbm()] * 2,
        out_specs=(hbm(), hbm()),
        scratch_shapes=[pltpu.VMEM((slices, width), f32)] * 2
        + [pltpu.SemaphoreType.DMA((2,))],
        input_output_aliases={4: 0, 5: 1},
        compiler_params=params(),
        name="depth",
    )(field, ahead, dual_var, limits, new_split, new_dual)
    return new_volume, new_split, new_dual


def solution(mesh):
    return jax.shard_map(
        shards,
        mesh=mesh,
        in_specs=(
            P(("parts", "slab"), "tile"),
            P(None, ("parts", "slab"), "tile"),
            P(None, ("parts", "slab"), "tile"),
            P(("tile", "rep"), ("parts", "slab"), None),
            P(("tile", "rep"), None, None),
            P(("tile", "rep")),
            P(("tile", "rep")),
            P(("tile", "rep")),
            P(),
        ),
        out_specs=(
            P(("parts", "slab"), "tile"),
            P(None, ("parts", "slab"), "tile"),
            P(None, ("parts", "slab"), "tile"),
        ),
        check_vma=False,
    )
```

```python
import jax
import jax.numpy as jnp
from jax import lax
from jax.experimental import pallas as pl
from jax.experimental.pallas import tpu as pltpu
from jax.sharding import PartitionSpec as P

TV = 64
TR = 128
TAU = 0.5
GROUP = 4
CUTS = (0, 2, 5, 8)
VMEM_LIMIT = 16 * 1024 * 1024


def iotas(shape):
    row = lax.broadcasted_iota(jnp.int32, shape, 0)
    lane = lax.broadcasted_iota(jnp.int32, shape, 1)
    return row, lane


def start_tiles(proj_hbm, tiles, sems):
    eighth = proj_hbm.shape[0] // CUTS[-1]
    copies = {}
    for c, (low, high) in enumerate(zip(CUTS, CUTS[1:])):
        part = pl.ds(low * eighth, (high - low) * eighth)
        copy = pltpu.make_async_copy(proj_hbm.at[part], tiles.at[part], sems.at[c])
        copy.start()
        copies[low * eighth] = copy
    return copies


def plane_masks(lane):
    return (lane % TV) // 8 < 7, lane % 8 < 7


def rows8(start):
    return pl.ds(pl.multiple_of(start, 8), 8)


def add_rows(accs, starts, values):
    held = [acc[rows8(start), :] for acc, start in zip(accs, starts)]
    for acc, start, old, value in zip(accs, starts, held, values):
        acc[rows8(start), :] = old + value


def forward_kernel(
    count, ray_hbm, voxel_hbm, vol_hbm, sino_hbm, proj_hbm,
    partial_out, tiles,
    ray, voxel, vol, sino, double, table, acc0, acc1, acc2, acc3,
    sems, tile_sems,
):
    slots = proj_hbm.shape[0]
    rays = acc0.shape[0] // 8 - 1
    owned = sino.shape[0]
    width = vol.shape[1]
    pairs = [(voxel_hbm, voxel), (ray_hbm, ray), (vol_hbm, vol), (sino_hbm, sino)]
    loads = [
        pltpu.make_async_copy(source, target, sems.at[i]) for i, (source, target) in enumerate(pairs)
    ]
    for load in loads[:3]:
        load.start()
    copies = start_tiles(proj_hbm, tiles, tile_sems)
    for load in loads[3:]:
        load.start()
    accs = (acc0, acc1, acc2, acc3)
    for acc in accs:
        acc[...] = jnp.zeros_like(acc)
    row, lane = iotas((8, 128))
    low, top = lane < TV, row < 4

    loads[2].wait()
    field = vol[...]
    double[0:4, :] = field
    double[4:8, :] = field
    for j in range(width // 128):
        x = double[:, 128 * j:128 * j + 128].astype(jnp.bfloat16).astype(jnp.float32)
        turned = pltpu.roll(x, TV, axis=1)
        zero = jnp.zeros_like(x)
        first = jnp.where(jnp.logical_and(top, low), x, zero)
        second = jnp.where(jnp.logical_and(top, low), turned, zero)
        other = jnp.logical_not(jnp.logical_or(top, low))
        table[16 * j:16 * j + 8, :] = jnp.where(other, turned, first)
        table[16 * j + 8:16 * j + 16, :] = jnp.where(other, x, second)

    loads[3].wait()
    mine = (lax.axis_index("tile") * lax.axis_size("rep") + lax.axis_index("rep")) * owned
    for r in range(owned):
        acc0[pl.ds(pl.multiple_of((mine + r) * 8, 8), 4), :] = -sino[r]
    loads[0].wait()
    loads[1].wait()
    used = count[0]
    for n in range(0, slots, GROUP):
        if n in copies:
            copies[n].wait()
        at = [divmod(n + i, 128) for i in range(GROUP)]
        picked = [table[rows8(voxel[line, place] * 8), :] for line, place in at]
        pairs = [jnp.where(top, picked[2 * i], picked[2 * i + 1]) for i in range(2)]
        zero = jnp.zeros_like(pairs[0])
        left = jnp.concatenate([pairs[0], zero], axis=0).astype(jnp.bfloat16)
        right = jnp.concatenate([zero, pairs[1]], axis=0).astype(jnp.bfloat16)
        sums = jnp.dot(
            jnp.concatenate([left, right], axis=1),
            tiles[n:n + GROUP].reshape(GROUP * TV, TR),
            preferred_element_type=jnp.float32,
        )
        add_rows(
            accs,
            [
                jnp.where(n + i < used, ray[line, place], rays) * 8
                for i, (line, place) in enumerate(at)
            ],
            [sums[0:8], sums[0:8], sums[8:16], sums[8:16]],
        )
    for q in range(rays // 4):
        halves = []
        for r in (4 * q, 4 * q + 2):
            at = [slice(8 * (r + k), 8 * (r + k) + 8) for k in range(2)]
            even = [acc0[at[k], :] + acc2[at[k], :] for k in range(2)]
            odd = [acc1[at[k], :] + acc3[at[k], :] for k in range(2)]
            halves.append(
                jnp.where(top, even[0], odd[1])
                + pltpu.roll(jnp.where(top, even[1], odd[0]), 4, axis=0)
            )
        partial_out[16 * q:16 * q + 16, :] = jnp.concatenate(halves, axis=0).astype(jnp.bfloat16)


def edges_kernel(vol, split, dual, edge_out, halo_out):
    start = lax.axis_index("slab") == 0
    for j in range(vol.shape[1] // 128):
        at = slice(128 * j, 128 * j + 128)
        edge = vol[3:4, at] - dual[0, 3:4, at] + split[0, 3:4, at]
        edge_out[:, at] = edge
        halo_out[:, at] = jnp.broadcast_to(jnp.where(start, edge, vol[0:1, at]), (4, 128))


def local_kernel(rho, vol, split, dual, edge, from_next, from_previous, base_out):
    slab, slabs = lax.axis_index("slab"), lax.axis_size("slab")
    factor = TAU * rho[0]
    row, lane = iotas((8, 128))
    row_mask, col_mask = plane_masks(lane)
    for j in range(vol.shape[1] // 128):
        at = slice(128 * j, 128 * j + 128)
        x = jnp.concatenate([vol[:, at]] * 2, axis=0)
        gap = [
            jnp.concatenate([dual[k, :, at] - split[k, :, at]] * 2, axis=0) for k in range(3)
        ]
        above = jnp.where(slab == slabs - 1, 0.0, from_next[0:1, at] - edge[:, at])
        below = jnp.where(slab == 0, 0.0, x[0:1] - from_previous[0:1, at])
        depth = jnp.where(row < 3, pltpu.roll(x, 7, axis=0) - x + gap[0], above)
        across = jnp.where(row_mask, pltpu.roll(x, 120, axis=1) - x + gap[1], 0.0)
        along = jnp.where(col_mask, pltpu.roll(x, 127, axis=1) - x + gap[2], 0.0)
        adjoint = jnp.where(row == 0, below, pltpu.roll(depth, 1, axis=0)) - depth
        adjoint += jnp.where((lane % TV) >= 8, pltpu.roll(across, 8, axis=1), 0.0) - across
        adjoint += jnp.where(lane % 8 >= 1, pltpu.roll(along, 1, axis=1), 0.0) - along
        base_out[:, at] = (x - factor * adjoint)[0:4]


def backward_kernel(
    count, voxel_in, ray_in, tiles, part, moved, grad_out,
    voxel, ray, table, acc0, acc1, acc2, acc3, sems,
):
    slots = tiles.shape[0]
    rays = table.shape[0] // 8
    voxel_tiles = acc0.shape[0] // 8 - 1
    loads = [
        pltpu.make_async_copy(ray_in, ray, sems.at[0]),
        pltpu.make_async_copy(voxel_in, voxel, sems.at[1]),
    ]
    for load in loads:
        load.start()
    accs = (acc0, acc1, acc2, acc3)
    for acc in accs:
        acc[...] = jnp.zeros_like(acc)
    row, lane = iotas((8, 128))
    low, top = lane < TV, row < 4
    for q in range(rays // 4):
        at = slice(16 * q, 16 * q + 16)
        total = part[at, :].astype(jnp.float32) + moved[at, :].astype(jnp.float32)
        for k in range(2):
            x = total[8 * k:8 * k + 8]
            turned = pltpu.roll(x, 4, axis=0)
            r = 8 * (4 * q + 2 * k)
            table[r:r + 8, :] = jnp.where(top, x, turned)
            table[r + 8:r + 16, :] = jnp.where(top, turned, x)

    for load in loads:
        load.wait()
    used = count[0]
    for n in range(0, slots, GROUP):
        at = [divmod(n + i, 128) for i in range(GROUP)]
        picked = [table[rows8(ray[line, place] * 8), :] for line, place in at]
        rows = jnp.concatenate(
            [jnp.where(top, picked[2 * i], picked[2 * i + 1]) for i in range(2)], axis=0
        )
        back = lax.dot_general(
            rows.astype(jnp.bfloat16),
            tiles[n:n + GROUP].reshape(GROUP * TV, TR),
            (((1,), (1,)), ((), ())),
            preferred_element_type=jnp.float32,
        )
        add_rows(
            accs,
            [
                jnp.where(n + i < used, voxel[line, place], voxel_tiles) * 8
                for i, (line, place) in enumerate(at)
            ],
            [back[8 * k:8 * k + 8, 128 * k:128 * k + 128] for k in (0, 0, 1, 1)],
        )
    for j in range(voxel_tiles // 2):
        at = [slice(16 * j + 8 * k, 16 * j + 8 * k + 8) for k in range(2)]
        even = [acc0[at[k], :] + acc2[at[k], :] for k in range(2)]
        odd = [acc1[at[k], :] + acc3[at[k], :] for k in range(2)]
        turned = pltpu.roll(jnp.where(top, even[1], odd[0]), TV, axis=1)
        both = jnp.where(top == low, jnp.where(top, even[0], odd[1]), turned)
        grad_out[:, 128 * j:128 * j + 128] = (both + pltpu.roll(both, 4, axis=0))[0:4]


def plane_kernel(
    grad, grad_other, base, dual, limits,
    field_out, volume_hbm, split_hbm, dual_hbm,
    split, clipped, sems,
):
    row, lane = iotas((4, 128))
    row_mask, col_mask = plane_masks(lane)
    for j in range(dual.shape[2] // 128):
        at = slice(128 * j, 128 * j + 128)
        limit = limits[:, at]
        field = base[:, at] - TAU * (grad[:, at] + grad_other[:, at])
        field_out[:, at] = field
        x = jnp.concatenate([field] * 2, axis=0)
        steps = (
            jnp.where(row_mask, pltpu.roll(x, 120, axis=1)[0:4] - field, 0.0),
            jnp.where(col_mask, pltpu.roll(x, 127, axis=1)[0:4] - field, 0.0),
        )
        for k in range(2):
            mixed = steps[k] + dual[k + 1, :, at]
            bounded = jnp.clip(mixed, -limit, limit)
            clipped[k, :, at] = bounded
            split[k, :, at] = mixed - bounded
    copies = [
        pltpu.make_async_copy(split, split_hbm.at[pl.ds(1, 2)], sems.at[0]),
        pltpu.make_async_copy(clipped, dual_hbm.at[pl.ds(1, 2)], sems.at[1]),
        pltpu.make_async_copy(field_out, volume_hbm, sems.at[2]),
    ]
    for copy in copies:
        copy.start()
    for copy in copies:
        copy.wait()


def depth_kernel(
    field_in, ahead, dual, limits, split_in, dual_in,
    split_hbm, dual_hbm,
    split, clipped, sems,
):
    del split_in, dual_in
    last = lax.axis_index("slab") == lax.axis_size("slab") - 1
    row, lane = iotas((8, 128))
    inner = jnp.logical_or(row < 3, jnp.logical_not(last))
    for j in range(dual.shape[2] // 128):
        at = slice(128 * j, 128 * j + 128)
        limit = limits[:, at]
        x = jnp.concatenate([field_in[:, at]] * 2, axis=0)
        following = jnp.where(row < 3, pltpu.roll(x, 7, axis=0), ahead[:, at])
        mixed = jnp.where(inner, following - x, 0.0)[0:4] + dual[0, :, at]
        bounded = jnp.clip(mixed, -limit, limit)
        clipped[:, at] = bounded
        split[:, at] = mixed - bounded
    copies = [
        pltpu.make_async_copy(split, split_hbm.at[0], sems.at[0]),
        pltpu.make_async_copy(clipped, dual_hbm.at[0], sems.at[1]),
    ]
    for copy in copies:
        copy.start()
    for copy in copies:
        copy.wait()


def vmem():
    return pl.BlockSpec(memory_space=pltpu.VMEM)


def smem():
    return pl.BlockSpec(memory_space=pltpu.SMEM)


def hbm():
    return pl.BlockSpec(memory_space=pltpu.HBM)


def params():
    return pltpu.CompilerParams(vmem_limit_bytes=VMEM_LIMIT)


def shards(
    volume, split_var, dual_var, sinogram, proj_tiles, ray_index, voxel_index, tile_count, rho
):
    f32, bf16 = jnp.float32, jnp.bfloat16
    slices, width = volume.shape
    slots = ray_index.shape[0]
    owned = sinogram.shape[0]
    group = lax.axis_size(("tile", "rep"))
    reps = lax.axis_size("rep")
    slabs = lax.axis_size("slab")
    rays = owned * group
    voxel_tiles = width // TV
    lines = slots // 128
    ray_index, voxel_index = ray_index.reshape(lines, 128), voxel_index.reshape(lines, 128)
    sources = [
        pltpu.with_memory_space_constraint(x, pltpu.HBM)
        for x in (ray_index, voxel_index, volume, sinogram, proj_tiles)
    ]

    partial, tiles = pl.pallas_call(
        forward_kernel,
        out_shape=(
            jax.ShapeDtypeStruct((rays * slices, TR), bf16),
            jax.ShapeDtypeStruct(proj_tiles.shape, bf16),
        ),
        in_specs=[smem()] + [hbm()] * 5,
        out_specs=(vmem(),) * 2,
        scratch_shapes=[
            pltpu.SMEM((lines, 128), jnp.int32),
            pltpu.SMEM((lines, 128), jnp.int32),
            pltpu.VMEM((slices, width), f32),
            pltpu.VMEM(sinogram.shape, f32),
            pltpu.VMEM((8, width), f32),
            pltpu.VMEM((voxel_tiles * 8, 128), f32),
        ]
        + [pltpu.VMEM((rays * 8 + 8, 128), f32)] * 4
        + [pltpu.SemaphoreType.DMA((4,)), pltpu.SemaphoreType.DMA((len(CUTS) - 1,))],
        compiler_params=params(),
        name="forward",
    )(tile_count, *sources)

    row = jax.ShapeDtypeStruct((1, width), f32)
    edge, halo = pl.pallas_call(
        edges_kernel,
        out_shape=(row, jax.ShapeDtypeStruct((4, width), f32)),
        in_specs=[vmem()] * 3,
        out_specs=(vmem(),) * 2,
        compiler_params=params(),
        name="edges",
    )(volume, split_var, dual_var)
    across = [(i, i ^ 3) for i in range(2 * reps)]
    down = [(i, i - 1) for i in range(1, slabs)]
    if slabs == 2:
        from_next = from_previous = lax.ppermute(halo, ("slab", "rep"), across)
    else:
        from_next = lax.ppermute(volume[0:1], "slab", down)
        from_previous = lax.ppermute(edge, "slab", [(i - 1, i) for i in range(1, slabs)])
    swap = [(i, i ^ 1) for i in range(reps)]
    moved = lax.ppermute(partial, "rep", swap)
    step = reps
    while step < group:
        partial = (partial.astype(f32) + moved.astype(f32)).astype(bf16)
        moved = lax.ppermute(
            partial, ("tile", "rep"), [(i, i ^ (step + 1)) for i in range(group)]
        )
        step *= 2
    limits = jnp.broadcast_to((1.0 / rho)[:, None], (1, width))
    moved, from_next, from_previous, limits = lax.optimization_barrier(
        (moved, from_next, from_previous, limits)
    )

    base = pl.pallas_call(
        local_kernel,
        out_shape=jax.ShapeDtypeStruct((slices, width), f32),
        in_specs=[smem()] + [vmem()] * 6,
        out_specs=vmem(),
        compiler_params=params(),
        name="local",
    )(rho, volume, split_var, dual_var, edge, from_next, from_previous)

    grad = pl.pallas_call(
        backward_kernel,
        out_shape=jax.ShapeDtypeStruct((slices, width), f32),
        in_specs=[smem()] + [vmem()] * 5,
        out_specs=vmem(),
        scratch_shapes=[
            pltpu.SMEM((lines, 128), jnp.int32),
            pltpu.SMEM((lines, 128), jnp.int32),
            pltpu.VMEM((rays * 8, 128), f32),
        ]
        + [pltpu.VMEM((voxel_tiles * 8 + 8, 128), f32)] * 4
        + [pltpu.SemaphoreType.DMA((2,))],
        compiler_params=params(),
        name="backward",
    )(tile_count, voxel_index, ray_index, tiles, partial, moved)
    grad_other = lax.ppermute(grad, "rep", swap)
    ahead = base[0:1] - TAU * (grad[0:1] + grad_other[0:1])
    if slabs == 2:
        ahead = lax.ppermute(ahead, ("slab", "rep"), across)
    else:
        ahead = lax.ppermute(ahead, "slab", down)

    whole = jax.ShapeDtypeStruct((slices, width), f32)
    triple = jax.ShapeDtypeStruct((3, slices, width), f32)
    field, new_volume, new_split, new_dual = pl.pallas_call(
        plane_kernel,
        out_shape=(whole, whole, triple, triple),
        in_specs=[vmem()] * 5,
        out_specs=(vmem(), hbm(), hbm(), hbm()),
        scratch_shapes=[pltpu.VMEM((2, slices, width), f32)] * 2
        + [pltpu.SemaphoreType.DMA((3,))],
        compiler_params=params(),
        name="plane",
    )(grad, grad_other, base, dual_var, limits)
    new_split, new_dual = pl.pallas_call(
        depth_kernel,
        out_shape=(triple, triple),
        in_specs=[vmem()] * 4 + [hbm()] * 2,
        out_specs=(hbm(), hbm()),
        scratch_shapes=[pltpu.VMEM((slices, width), f32)] * 2
        + [pltpu.SemaphoreType.DMA((2,))],
        input_output_aliases={4: 0, 5: 1},
        compiler_params=params(),
        name="depth",
    )(field, ahead, dual_var, limits, new_split, new_dual)
    return new_volume, new_split, new_dual


def solution(mesh):
    return jax.shard_map(
        shards,
        mesh=mesh,
        in_specs=(
            P(("parts", "slab"), "tile"),
            P(None, ("parts", "slab"), "tile"),
            P(None, ("parts", "slab"), "tile"),
            P(("tile", "rep"), ("parts", "slab"), None),
            P(("tile", "rep"), None, None),
            P(("tile", "rep")),
            P(("tile", "rep")),
            P(("tile", "rep")),
            P(),
        ),
        out_specs=(
            P(("parts", "slab"), "tile"),
            P(None, ("parts", "slab"), "tile"),
            P(None, ("parts", "slab"), "tile"),
        ),
        check_vma=False,
    )
```

```python
import jax
import jax.numpy as jnp
from jax import lax
from jax.experimental import pallas as pl
from jax.experimental.pallas import tpu as pltpu
from jax.sharding import PartitionSpec as P

TV = 64
TR = 128
TAU = 0.5
GROUP = 4
CUTS = (0, 2, 5, 8)
VMEM_LIMIT = 16 * 1024 * 1024


def iotas(shape):
    row = lax.broadcasted_iota(jnp.int32, shape, 0)
    lane = lax.broadcasted_iota(jnp.int32, shape, 1)
    return row, lane


def start_tiles(proj_hbm, tiles, sems):
    eighth = proj_hbm.shape[0] // CUTS[-1]
    copies = {}
    for c, (low, high) in enumerate(zip(CUTS, CUTS[1:])):
        part = pl.ds(low * eighth, (high - low) * eighth)
        copy = pltpu.make_async_copy(proj_hbm.at[part], tiles.at[part], sems.at[c])
        copy.start()
        copies[low * eighth] = copy
    return copies


def plane_masks(lane):
    return (lane % TV) // 8 < 7, lane % 8 < 7


def rows8(start):
    return pl.ds(pl.multiple_of(start, 8), 8)


def add_rows(accs, starts, values):
    held = [acc[rows8(start), :] for acc, start in zip(accs, starts)]
    for acc, start, old, value in zip(accs, starts, held, values):
        acc[rows8(start), :] = old + value


def forward_kernel(
    count, ray_hbm, voxel_hbm, vol_hbm, sino_hbm, proj_hbm,
    partial_out, index_out, tiles,
    ray, voxel, vol, sino, double, table, acc0, acc1, acc2, acc3,
    sems, tile_sems,
):
    slots = proj_hbm.shape[0]
    lines = ray.shape[0]
    rays = acc0.shape[0] // 8 - 1
    owned = sino.shape[0]
    width = vol.shape[1]
    pairs = [
        (voxel_hbm, voxel), (ray_hbm, ray), (vol_hbm, vol), (sino_hbm, sino),
        (voxel_hbm, index_out.at[pl.ds(0, lines)]), (ray_hbm, index_out.at[pl.ds(lines, lines)]),
    ]
    loads = [
        pltpu.make_async_copy(source, target, sems.at[i]) for i, (source, target) in enumerate(pairs)
    ]
    for load in loads[:3]:
        load.start()
    copies = start_tiles(proj_hbm, tiles, tile_sems)
    for load in loads[3:]:
        load.start()
    accs = (acc0, acc1, acc2, acc3)
    for acc in accs:
        acc[...] = jnp.zeros_like(acc)
    row, lane = iotas((8, 128))
    low, top = lane < TV, row < 4

    loads[2].wait()
    field = vol[...]
    double[0:4, :] = field
    double[4:8, :] = field
    for j in range(width // 128):
        x = double[:, 128 * j:128 * j + 128].astype(jnp.bfloat16).astype(jnp.float32)
        turned = pltpu.roll(x, TV, axis=1)
        zero = jnp.zeros_like(x)
        first = jnp.where(jnp.logical_and(top, low), x, zero)
        second = jnp.where(jnp.logical_and(top, low), turned, zero)
        other = jnp.logical_not(jnp.logical_or(top, low))
        table[16 * j:16 * j + 8, :] = jnp.where(other, turned, first)
        table[16 * j + 8:16 * j + 16, :] = jnp.where(other, x, second)

    loads[3].wait()
    mine = (lax.axis_index("tile") * lax.axis_size("rep") + lax.axis_index("rep")) * owned
    for r in range(owned):
        acc0[pl.ds(pl.multiple_of((mine + r) * 8, 8), 4), :] = -sino[r]
    loads[0].wait()
    loads[1].wait()
    used = count[0]
    for n in range(0, slots, GROUP):
        if n in copies:
            copies[n].wait()
        at = [divmod(n + i, 128) for i in range(GROUP)]
        picked = [table[rows8(voxel[line, place] * 8), :] for line, place in at]
        pairs = [jnp.where(top, picked[2 * i], picked[2 * i + 1]) for i in range(2)]
        zero = jnp.zeros_like(pairs[0])
        left = jnp.concatenate([pairs[0], zero], axis=0).astype(jnp.bfloat16)
        right = jnp.concatenate([zero, pairs[1]], axis=0).astype(jnp.bfloat16)
        sums = jnp.dot(
            jnp.concatenate([left, right], axis=1),
            tiles[n:n + GROUP].reshape(GROUP * TV, TR),
            preferred_element_type=jnp.float32,
        )
        add_rows(
            accs,
            [
                jnp.where(n + i < used, ray[line, place], rays) * 8
                for i, (line, place) in enumerate(at)
            ],
            [sums[0:8], sums[0:8], sums[8:16], sums[8:16]],
        )
    loads[4].wait()
    loads[5].wait()
    for q in range(rays // 4):
        halves = []
        for r in (4 * q, 4 * q + 2):
            at = [slice(8 * (r + k), 8 * (r + k) + 8) for k in range(2)]
            even = [acc0[at[k], :] + acc2[at[k], :] for k in range(2)]
            odd = [acc1[at[k], :] + acc3[at[k], :] for k in range(2)]
            halves.append(
                jnp.where(top, even[0], odd[1])
                + pltpu.roll(jnp.where(top, even[1], odd[0]), 4, axis=0)
            )
        partial_out[16 * q:16 * q + 16, :] = jnp.concatenate(halves, axis=0).astype(jnp.bfloat16)


def edges_kernel(
    vol_hbm, split_hbm, dual_hbm, edge_out, halo_out, vol, split, dual, sems
):
    loads = [
        pltpu.make_async_copy(source, target, sems.at[i])
        for i, (source, target) in enumerate([(vol_hbm, vol), (split_hbm, split), (dual_hbm, dual)])
    ]
    for load in loads:
        load.start()
    for load in loads:
        load.wait()
    start = lax.axis_index("slab") == 0
    for j in range(vol.shape[1] // 128):
        at = slice(128 * j, 128 * j + 128)
        edge = vol[3:4, at] - dual[0, 3:4, at] + split[0, 3:4, at]
        edge_out[:, at] = edge
        halo_out[:, at] = jnp.broadcast_to(jnp.where(start, edge, vol[0:1, at]), (4, 128))


def local_kernel(rho, vol, split, dual, edge, from_next, from_previous, base_out):
    slab, slabs = lax.axis_index("slab"), lax.axis_size("slab")
    factor = TAU * rho[0]
    row, lane = iotas((8, 128))
    row_mask, col_mask = plane_masks(lane)
    for j in range(vol.shape[1] // 128):
        at = slice(128 * j, 128 * j + 128)
        x = jnp.concatenate([vol[:, at]] * 2, axis=0)
        gap = [
            jnp.concatenate([dual[k, :, at] - split[k, :, at]] * 2, axis=0) for k in range(3)
        ]
        above = jnp.where(slab == slabs - 1, 0.0, from_next[0:1, at] - edge[:, at])
        below = jnp.where(slab == 0, 0.0, x[0:1] - from_previous[0:1, at])
        depth = jnp.where(row < 3, pltpu.roll(x, 7, axis=0) - x + gap[0], above)
        across = jnp.where(row_mask, pltpu.roll(x, 120, axis=1) - x + gap[1], 0.0)
        along = jnp.where(col_mask, pltpu.roll(x, 127, axis=1) - x + gap[2], 0.0)
        adjoint = jnp.where(row == 0, below, pltpu.roll(depth, 1, axis=0)) - depth
        adjoint += jnp.where((lane % TV) >= 8, pltpu.roll(across, 8, axis=1), 0.0) - across
        adjoint += jnp.where(lane % 8 >= 1, pltpu.roll(along, 1, axis=1), 0.0) - along
        base_out[:, at] = (x - factor * adjoint)[0:4]


def backward_kernel(
    count, indices, tiles, part, moved, grad_out,
    index, table, acc0, acc1, acc2, acc3, sem,
):
    slots = tiles.shape[0]
    lines = indices.shape[0] // 2
    rays = table.shape[0] // 8
    voxel_tiles = acc0.shape[0] // 8 - 1
    to_scalar = pltpu.make_async_copy(indices, index, sem)
    to_scalar.start()
    accs = (acc0, acc1, acc2, acc3)
    for acc in accs:
        acc[...] = jnp.zeros_like(acc)
    row, lane = iotas((8, 128))
    low, top = lane < TV, row < 4
    for q in range(rays // 4):
        at = slice(16 * q, 16 * q + 16)
        total = part[at, :].astype(jnp.float32) + moved[at, :].astype(jnp.float32)
        for k in range(2):
            x = total[8 * k:8 * k + 8]
            turned = pltpu.roll(x, 4, axis=0)
            r = 8 * (4 * q + 2 * k)
            table[r:r + 8, :] = jnp.where(top, x, turned)
            table[r + 8:r + 16, :] = jnp.where(top, turned, x)

    to_scalar.wait()
    used = count[0]
    for n in range(0, slots, GROUP):
        at = [divmod(n + i, 128) for i in range(GROUP)]
        picked = [table[rows8(index[lines + line, place] * 8), :] for line, place in at]
        rows = jnp.concatenate(
            [jnp.where(top, picked[2 * i], picked[2 * i + 1]) for i in range(2)], axis=0
        )
        back = lax.dot_general(
            rows.astype(jnp.bfloat16),
            tiles[n:n + GROUP].reshape(GROUP * TV, TR),
            (((1,), (1,)), ((), ())),
            preferred_element_type=jnp.float32,
        )
        add_rows(
            accs,
            [
                jnp.where(n + i < used, index[line, place], voxel_tiles) * 8
                for i, (line, place) in enumerate(at)
            ],
            [back[8 * k:8 * k + 8, 128 * k:128 * k + 128] for k in (0, 0, 1, 1)],
        )
    for j in range(voxel_tiles // 2):
        at = [slice(16 * j + 8 * k, 16 * j + 8 * k + 8) for k in range(2)]
        even = [acc0[at[k], :] + acc2[at[k], :] for k in range(2)]
        odd = [acc1[at[k], :] + acc3[at[k], :] for k in range(2)]
        turned = pltpu.roll(jnp.where(top, even[1], odd[0]), TV, axis=1)
        both = jnp.where(top == low, jnp.where(top, even[0], odd[1]), turned)
        grad_out[:, 128 * j:128 * j + 128] = (both + pltpu.roll(both, 4, axis=0))[0:4]


def plane_kernel(
    grad, grad_other, base, dual, limits,
    field_out, volume_hbm, split_hbm, dual_hbm,
    split, clipped, sems,
):
    row, lane = iotas((4, 128))
    row_mask, col_mask = plane_masks(lane)
    for j in range(dual.shape[2] // 128):
        at = slice(128 * j, 128 * j + 128)
        limit = limits[:, at]
        field = base[:, at] - TAU * (grad[:, at] + grad_other[:, at])
        field_out[:, at] = field
        x = jnp.concatenate([field] * 2, axis=0)
        steps = (
            jnp.where(row_mask, pltpu.roll(x, 120, axis=1)[0:4] - field, 0.0),
            jnp.where(col_mask, pltpu.roll(x, 127, axis=1)[0:4] - field, 0.0),
        )
        for k in range(2):
            mixed = steps[k] + dual[k + 1, :, at]
            bounded = jnp.clip(mixed, -limit, limit)
            clipped[k, :, at] = bounded
            split[k, :, at] = mixed - bounded
    copies = [
        pltpu.make_async_copy(split, split_hbm.at[pl.ds(1, 2)], sems.at[0]),
        pltpu.make_async_copy(clipped, dual_hbm.at[pl.ds(1, 2)], sems.at[1]),
        pltpu.make_async_copy(field_out, volume_hbm, sems.at[2]),
    ]
    for copy in copies:
        copy.start()
    for copy in copies:
        copy.wait()


def depth_kernel(
    field_in, ahead, dual, limits, split_in, dual_in,
    split_hbm, dual_hbm,
    split, clipped, sems,
):
    del split_in, dual_in
    last = lax.axis_index("slab") == lax.axis_size("slab") - 1
    row, lane = iotas((8, 128))
    inner = jnp.logical_or(row < 3, jnp.logical_not(last))
    for j in range(dual.shape[2] // 128):
        at = slice(128 * j, 128 * j + 128)
        limit = limits[:, at]
        x = jnp.concatenate([field_in[:, at]] * 2, axis=0)
        following = jnp.where(row < 3, pltpu.roll(x, 7, axis=0), ahead[:, at])
        mixed = jnp.where(inner, following - x, 0.0)[0:4] + dual[0, :, at]
        bounded = jnp.clip(mixed, -limit, limit)
        clipped[:, at] = bounded
        split[:, at] = mixed - bounded
    copies = [
        pltpu.make_async_copy(split, split_hbm.at[0], sems.at[0]),
        pltpu.make_async_copy(clipped, dual_hbm.at[0], sems.at[1]),
    ]
    for copy in copies:
        copy.start()
    for copy in copies:
        copy.wait()


def vmem():
    return pl.BlockSpec(memory_space=pltpu.VMEM)


def smem():
    return pl.BlockSpec(memory_space=pltpu.SMEM)


def hbm():
    return pl.BlockSpec(memory_space=pltpu.HBM)


def params():
    return pltpu.CompilerParams(vmem_limit_bytes=VMEM_LIMIT)


def shards(
    volume, split_var, dual_var, sinogram, proj_tiles, ray_index, voxel_index, tile_count, rho
):
    f32, bf16 = jnp.float32, jnp.bfloat16
    slices, width = volume.shape
    slots = ray_index.shape[0]
    owned = sinogram.shape[0]
    group = lax.axis_size(("tile", "rep"))
    reps = lax.axis_size("rep")
    slabs = lax.axis_size("slab")
    rays = owned * group
    voxel_tiles = width // TV
    lines = slots // 128
    ray_index, voxel_index = ray_index.reshape(lines, 128), voxel_index.reshape(lines, 128)
    sources = [
        pltpu.with_memory_space_constraint(x, pltpu.HBM)
        for x in (ray_index, voxel_index, volume, sinogram, proj_tiles)
    ]

    partial, indices, tiles = pl.pallas_call(
        forward_kernel,
        out_shape=(
            jax.ShapeDtypeStruct((rays * slices, TR), bf16),
            jax.ShapeDtypeStruct((2 * lines, 128), jnp.int32),
            jax.ShapeDtypeStruct(proj_tiles.shape, bf16),
        ),
        in_specs=[smem()] + [hbm()] * 5,
        out_specs=(vmem(),) * 3,
        scratch_shapes=[
            pltpu.SMEM((lines, 128), jnp.int32),
            pltpu.SMEM((lines, 128), jnp.int32),
            pltpu.VMEM((slices, width), f32),
            pltpu.VMEM(sinogram.shape, f32),
            pltpu.VMEM((8, width), f32),
            pltpu.VMEM((voxel_tiles * 8, 128), f32),
        ]
        + [pltpu.VMEM((rays * 8 + 8, 128), f32)] * 4
        + [pltpu.SemaphoreType.DMA((6,)), pltpu.SemaphoreType.DMA((len(CUTS) - 1,))],
        compiler_params=params(),
        name="forward",
    )(tile_count, *sources)

    row = jax.ShapeDtypeStruct((1, width), f32)
    whole = jax.ShapeDtypeStruct((slices, width), f32)
    triple = jax.ShapeDtypeStruct((3, slices, width), f32)
    wide = [pltpu.with_memory_space_constraint(x, pltpu.HBM) for x in (split_var, dual_var)]
    edge, halo, vol_near, split_near, dual_near = pl.pallas_call(
        edges_kernel,
        out_shape=(row, whole, whole, triple, triple),
        in_specs=[hbm()] * 3,
        out_specs=(vmem(),) * 5,
        scratch_shapes=[pltpu.SemaphoreType.DMA((3,))],
        compiler_params=params(),
        name="edges",
    )(sources[2], *wide)
    swap = [(i, i ^ 1) for i in range(reps)]
    moved = lax.ppermute(partial, "rep", swap)
    moved, halo = lax.optimization_barrier((moved, halo))
    across = [(i, i ^ 3) for i in range(2 * reps)]
    down = [(i, i - 1) for i in range(1, slabs)]
    if slabs == 2:
        from_next = from_previous = lax.ppermute(halo, ("slab", "rep"), across)
    else:
        from_next = lax.ppermute(volume[0:1], "slab", down)
        from_previous = lax.ppermute(edge, "slab", [(i - 1, i) for i in range(1, slabs)])
    step = reps
    while step < group:
        partial = (partial.astype(f32) + moved.astype(f32)).astype(bf16)
        moved = lax.ppermute(
            partial, ("tile", "rep"), [(i, i ^ (step + 1)) for i in range(group)]
        )
        step *= 2
    limits = jnp.broadcast_to((1.0 / rho)[:, None], (1, width))
    moved, from_next, from_previous, limits = lax.optimization_barrier(
        (moved, from_next, from_previous, limits)
    )

    base = pl.pallas_call(
        local_kernel,
        out_shape=jax.ShapeDtypeStruct((slices, width), f32),
        in_specs=[smem()] + [vmem()] * 6,
        out_specs=vmem(),
        compiler_params=params(),
        name="local",
    )(rho, vol_near, split_near, dual_near, edge, from_next, from_previous)

    grad = pl.pallas_call(
        backward_kernel,
        out_shape=jax.ShapeDtypeStruct((slices, width), f32),
        in_specs=[smem()] + [vmem()] * 4,
        out_specs=vmem(),
        scratch_shapes=[
            pltpu.SMEM((2 * lines, 128), jnp.int32),
            pltpu.VMEM((rays * 8, 128), f32),
        ]
        + [pltpu.VMEM((voxel_tiles * 8 + 8, 128), f32)] * 4
        + [pltpu.SemaphoreType.DMA],
        compiler_params=params(),
        name="backward",
    )(tile_count, indices, tiles, partial, moved)
    grad_other = lax.ppermute(grad, "rep", swap)
    ahead = base[0:1] - TAU * (grad[0:1] + grad_other[0:1])
    if slabs == 2:
        ahead = lax.ppermute(ahead, ("slab", "rep"), across)
    else:
        ahead = lax.ppermute(ahead, "slab", down)

    field, new_volume, new_split, new_dual = pl.pallas_call(
        plane_kernel,
        out_shape=(whole, whole, triple, triple),
        in_specs=[vmem()] * 5,
        out_specs=(vmem(), hbm(), hbm(), hbm()),
        scratch_shapes=[pltpu.VMEM((2, slices, width), f32)] * 2
        + [pltpu.SemaphoreType.DMA((3,))],
        compiler_params=params(),
        name="plane",
    )(grad, grad_other, base, dual_near, limits)
    new_split, new_dual = pl.pallas_call(
        depth_kernel,
        out_shape=(triple, triple),
        in_specs=[vmem()] * 4 + [hbm()] * 2,
        out_specs=(hbm(), hbm()),
        scratch_shapes=[pltpu.VMEM((slices, width), f32)] * 2
        + [pltpu.SemaphoreType.DMA((2,))],
        input_output_aliases={4: 0, 5: 1},
        compiler_params=params(),
        name="depth",
    )(field, ahead, dual_near, limits, new_split, new_dual)
    return new_volume, new_split, new_dual


def solution(mesh):
    return jax.shard_map(
        shards,
        mesh=mesh,
        in_specs=(
            P(("parts", "slab"), "tile"),
            P(None, ("parts", "slab"), "tile"),
            P(None, ("parts", "slab"), "tile"),
            P(("tile", "rep"), ("parts", "slab"), None),
            P(("tile", "rep"), None, None),
            P(("tile", "rep")),
            P(("tile", "rep")),
            P(("tile", "rep")),
            P(),
        ),
        out_specs=(
            P(("parts", "slab"), "tile"),
            P(None, ("parts", "slab"), "tile"),
            P(None, ("parts", "slab"), "tile"),
        ),
        check_vma=False,
    )
```

```python
import jax
import jax.numpy as jnp
from jax import lax
from jax.experimental import pallas as pl
from jax.experimental.pallas import tpu as pltpu
from jax.sharding import PartitionSpec as P

TV = 64
TR = 128
TAU = 0.5
GROUP = 4
CUTS = (0, 2, 5, 8)
VMEM_LIMIT = 16 * 1024 * 1024


def iotas(shape):
    row = lax.broadcasted_iota(jnp.int32, shape, 0)
    lane = lax.broadcasted_iota(jnp.int32, shape, 1)
    return row, lane


def tile_copies(proj_hbm, tiles, sems):
    eighth = proj_hbm.shape[0] // CUTS[-1]
    copies = {}
    for c, (low, high) in enumerate(zip(CUTS, CUTS[1:])):
        part = pl.ds(low * eighth, (high - low) * eighth)
        copies[low * eighth] = pltpu.make_async_copy(
            proj_hbm.at[part], tiles.at[part], sems.at[c]
        )
    return copies


def plane_masks(lane):
    return (lane % TV) // 8 < 7, lane % 8 < 7


def rows8(start):
    return pl.ds(pl.multiple_of(start, 8), 8)


def add_rows(accs, starts, values):
    held = [acc[rows8(start), :] for acc, start in zip(accs, starts)]
    for acc, start, old, value in zip(accs, starts, held, values):
        acc[rows8(start), :] = old + value


def forward_kernel(
    count, ray_hbm, voxel_hbm, vol_hbm, sino_hbm, proj_hbm,
    partial_out, index_out, tiles,
    ray, voxel, vol, sino, double, table, acc0, acc1, acc2, acc3,
    sems, tile_sems,
):
    slots = proj_hbm.shape[0]
    lines = ray.shape[0]
    rays = acc0.shape[0] // 8 - 1
    owned = sino.shape[0]
    width = vol.shape[1]
    pairs = [
        (voxel_hbm, voxel), (ray_hbm, ray), (vol_hbm, vol), (sino_hbm, sino),
        (voxel_hbm, index_out.at[pl.ds(0, lines)]), (ray_hbm, index_out.at[pl.ds(lines, lines)]),
    ]
    loads = [
        pltpu.make_async_copy(source, target, sems.at[i]) for i, (source, target) in enumerate(pairs)
    ]
    copies = tile_copies(proj_hbm, tiles, tile_sems)
    loads[2].start()
    loads[0].start()
    copies[0].start()
    loads[1].start()
    for n in copies:
        if n > 0:
            copies[n].start()
    for load in loads[3:]:
        load.start()
    accs = (acc0, acc1, acc2, acc3)
    for acc in accs:
        acc[...] = jnp.zeros_like(acc)
    row, lane = iotas((8, 128))
    low, top = lane < TV, row < 4

    loads[2].wait()
    field = vol[...]
    double[0:4, :] = field
    double[4:8, :] = field
    for j in range(width // 128):
        x = double[:, 128 * j:128 * j + 128].astype(jnp.bfloat16).astype(jnp.float32)
        turned = pltpu.roll(x, TV, axis=1)
        zero = jnp.zeros_like(x)
        first = jnp.where(jnp.logical_and(top, low), x, zero)
        second = jnp.where(jnp.logical_and(top, low), turned, zero)
        other = jnp.logical_not(jnp.logical_or(top, low))
        table[16 * j:16 * j + 8, :] = jnp.where(other, turned, first)
        table[16 * j + 8:16 * j + 16, :] = jnp.where(other, x, second)

    loads[0].wait()
    loads[1].wait()
    used = count[0]
    for n in range(0, slots, GROUP):
        if n in copies:
            copies[n].wait()
        at = [divmod(n + i, 128) for i in range(GROUP)]
        picked = [table[rows8(voxel[line, place] * 8), :] for line, place in at]
        pairs = [jnp.where(top, picked[2 * i], picked[2 * i + 1]) for i in range(2)]
        zero = jnp.zeros_like(pairs[0])
        left = jnp.concatenate([pairs[0], zero], axis=0).astype(jnp.bfloat16)
        right = jnp.concatenate([zero, pairs[1]], axis=0).astype(jnp.bfloat16)
        sums = jnp.dot(
            jnp.concatenate([left, right], axis=1),
            tiles[n:n + GROUP].reshape(GROUP * TV, TR),
            preferred_element_type=jnp.float32,
        )
        add_rows(
            accs,
            [
                jnp.where(n + i < used, ray[line, place], rays) * 8
                for i, (line, place) in enumerate(at)
            ],
            [sums[0:8], sums[0:8], sums[8:16], sums[8:16]],
        )
    loads[3].wait()
    mine = (lax.axis_index("tile") * lax.axis_size("rep") + lax.axis_index("rep")) * owned
    for r in range(owned):
        at = pl.ds(pl.multiple_of((mine + r) * 8, 8), 4)
        acc0[at, :] = acc0[at, :] - sino[r]
    loads[4].wait()
    loads[5].wait()
    for q in range(rays // 4):
        halves = []
        for r in (4 * q, 4 * q + 2):
            at = [slice(8 * (r + k), 8 * (r + k) + 8) for k in range(2)]
            even = [acc0[at[k], :] + acc2[at[k], :] for k in range(2)]
            odd = [acc1[at[k], :] + acc3[at[k], :] for k in range(2)]
            halves.append(
                jnp.where(top, even[0], odd[1])
                + pltpu.roll(jnp.where(top, even[1], odd[0]), 4, axis=0)
            )
        partial_out[16 * q:16 * q + 16, :] = jnp.concatenate(halves, axis=0).astype(jnp.bfloat16)


def edges_kernel(vol, split, dual, edge_out, halo_out):
    start = lax.axis_index("slab") == 0
    for j in range(vol.shape[1] // 128):
        at = slice(128 * j, 128 * j + 128)
        edge = vol[3:4, at] - dual[0, 3:4, at] + split[0, 3:4, at]
        edge_out[:, at] = edge
        halo_out[:, at] = jnp.broadcast_to(jnp.where(start, edge, vol[0:1, at]), (4, 128))


def local_kernel(rho, vol, split, dual, edge, from_next, from_previous, base_out):
    slab, slabs = lax.axis_index("slab"), lax.axis_size("slab")
    factor = TAU * rho[0]
    row, lane = iotas((8, 128))
    row_mask, col_mask = plane_masks(lane)
    for j in range(vol.shape[1] // 128):
        at = slice(128 * j, 128 * j + 128)
        x = jnp.concatenate([vol[:, at]] * 2, axis=0)
        gap = [
            jnp.concatenate([dual[k, :, at] - split[k, :, at]] * 2, axis=0) for k in range(3)
        ]
        above = jnp.where(slab == slabs - 1, 0.0, from_next[0:1, at] - edge[:, at])
        below = jnp.where(slab == 0, 0.0, x[0:1] - from_previous[0:1, at])
        depth = jnp.where(row < 3, pltpu.roll(x, 7, axis=0) - x + gap[0], above)
        across = jnp.where(row_mask, pltpu.roll(x, 120, axis=1) - x + gap[1], 0.0)
        along = jnp.where(col_mask, pltpu.roll(x, 127, axis=1) - x + gap[2], 0.0)
        adjoint = jnp.where(row == 0, below, pltpu.roll(depth, 1, axis=0)) - depth
        adjoint += jnp.where((lane % TV) >= 8, pltpu.roll(across, 8, axis=1), 0.0) - across
        adjoint += jnp.where(lane % 8 >= 1, pltpu.roll(along, 1, axis=1), 0.0) - along
        base_out[:, at] = (x - factor * adjoint)[0:4]


def backward_kernel(
    count, indices, tiles, part, moved, grad_out,
    index, table, acc0, acc1, acc2, acc3, sem,
):
    slots = tiles.shape[0]
    lines = indices.shape[0] // 2
    rays = table.shape[0] // 8
    voxel_tiles = acc0.shape[0] // 8 - 1
    to_scalar = pltpu.make_async_copy(indices, index, sem)
    to_scalar.start()
    accs = (acc0, acc1, acc2, acc3)
    for acc in accs:
        acc[...] = jnp.zeros_like(acc)
    row, lane = iotas((8, 128))
    low, top = lane < TV, row < 4
    for q in range(rays // 4):
        at = slice(16 * q, 16 * q + 16)
        total = part[at, :].astype(jnp.float32) + moved[at, :].astype(jnp.float32)
        for k in range(2):
            x = total[8 * k:8 * k + 8]
            turned = pltpu.roll(x, 4, axis=0)
            r = 8 * (4 * q + 2 * k)
            table[r:r + 8, :] = jnp.where(top, x, turned)
            table[r + 8:r + 16, :] = jnp.where(top, turned, x)

    to_scalar.wait()
    used = count[0]
    for n in range(0, slots, GROUP):
        at = [divmod(n + i, 128) for i in range(GROUP)]
        picked = [table[rows8(index[lines + line, place] * 8), :] for line, place in at]
        rows = jnp.concatenate(
            [jnp.where(top, picked[2 * i], picked[2 * i + 1]) for i in range(2)], axis=0
        )
        back = lax.dot_general(
            rows.astype(jnp.bfloat16),
            tiles[n:n + GROUP].reshape(GROUP * TV, TR),
            (((1,), (1,)), ((), ())),
            preferred_element_type=jnp.float32,
        )
        add_rows(
            accs,
            [
                jnp.where(n + i < used, index[line, place], voxel_tiles) * 8
                for i, (line, place) in enumerate(at)
            ],
            [back[8 * k:8 * k + 8, 128 * k:128 * k + 128] for k in (0, 0, 1, 1)],
        )
    for j in range(voxel_tiles // 2):
        at = [slice(16 * j + 8 * k, 16 * j + 8 * k + 8) for k in range(2)]
        even = [acc0[at[k], :] + acc2[at[k], :] for k in range(2)]
        odd = [acc1[at[k], :] + acc3[at[k], :] for k in range(2)]
        turned = pltpu.roll(jnp.where(top, even[1], odd[0]), TV, axis=1)
        both = jnp.where(top == low, jnp.where(top, even[0], odd[1]), turned)
        grad_out[:, 128 * j:128 * j + 128] = (both + pltpu.roll(both, 4, axis=0))[0:4]


def plane_kernel(
    grad, grad_other, base, dual, limits,
    field_out, volume_hbm, split_hbm, dual_hbm,
    split, clipped, sems,
):
    row, lane = iotas((4, 128))
    row_mask, col_mask = plane_masks(lane)
    for j in range(dual.shape[2] // 128):
        at = slice(128 * j, 128 * j + 128)
        limit = limits[:, at]
        field = base[:, at] - TAU * (grad[:, at] + grad_other[:, at])
        field_out[:, at] = field
        x = jnp.concatenate([field] * 2, axis=0)
        steps = (
            jnp.where(row_mask, pltpu.roll(x, 120, axis=1)[0:4] - field, 0.0),
            jnp.where(col_mask, pltpu.roll(x, 127, axis=1)[0:4] - field, 0.0),
        )
        for k in range(2):
            mixed = steps[k] + dual[k + 1, :, at]
            bounded = jnp.clip(mixed, -limit, limit)
            clipped[k, :, at] = bounded
            split[k, :, at] = mixed - bounded
    copies = [
        pltpu.make_async_copy(split, split_hbm.at[pl.ds(1, 2)], sems.at[0]),
        pltpu.make_async_copy(clipped, dual_hbm.at[pl.ds(1, 2)], sems.at[1]),
        pltpu.make_async_copy(field_out, volume_hbm, sems.at[2]),
    ]
    for copy in copies:
        copy.start()
    for copy in copies:
        copy.wait()


def depth_kernel(
    field_in, ahead, dual, limits, split_in, dual_in,
    split_hbm, dual_hbm,
    split, clipped, sems,
):
    del split_in, dual_in
    last = lax.axis_index("slab") == lax.axis_size("slab") - 1
    row, lane = iotas((8, 128))
    inner = jnp.logical_or(row < 3, jnp.logical_not(last))
    for j in range(dual.shape[2] // 128):
        at = slice(128 * j, 128 * j + 128)
        limit = limits[:, at]
        x = jnp.concatenate([field_in[:, at]] * 2, axis=0)
        following = jnp.where(row < 3, pltpu.roll(x, 7, axis=0), ahead[:, at])
        mixed = jnp.where(inner, following - x, 0.0)[0:4] + dual[0, :, at]
        bounded = jnp.clip(mixed, -limit, limit)
        clipped[:, at] = bounded
        split[:, at] = mixed - bounded
    copies = [
        pltpu.make_async_copy(split, split_hbm.at[0], sems.at[0]),
        pltpu.make_async_copy(clipped, dual_hbm.at[0], sems.at[1]),
    ]
    for copy in copies:
        copy.start()
    for copy in copies:
        copy.wait()


def vmem():
    return pl.BlockSpec(memory_space=pltpu.VMEM)


def smem():
    return pl.BlockSpec(memory_space=pltpu.SMEM)


def hbm():
    return pl.BlockSpec(memory_space=pltpu.HBM)


def params():
    return pltpu.CompilerParams(vmem_limit_bytes=VMEM_LIMIT)


def shards(
    volume, split_var, dual_var, sinogram, proj_tiles, ray_index, voxel_index, tile_count, rho
):
    f32, bf16 = jnp.float32, jnp.bfloat16
    slices, width = volume.shape
    slots = ray_index.shape[0]
    owned = sinogram.shape[0]
    group = lax.axis_size(("tile", "rep"))
    reps = lax.axis_size("rep")
    slabs = lax.axis_size("slab")
    rays = owned * group
    voxel_tiles = width // TV
    lines = slots // 128
    ray_index, voxel_index = ray_index.reshape(lines, 128), voxel_index.reshape(lines, 128)
    sources = [
        pltpu.with_memory_space_constraint(x, pltpu.HBM)
        for x in (ray_index, voxel_index, volume, sinogram, proj_tiles)
    ]

    partial, indices, tiles = pl.pallas_call(
        forward_kernel,
        out_shape=(
            jax.ShapeDtypeStruct((rays * slices, TR), bf16),
            jax.ShapeDtypeStruct((2 * lines, 128), jnp.int32),
            jax.ShapeDtypeStruct(proj_tiles.shape, bf16),
        ),
        in_specs=[smem()] + [hbm()] * 5,
        out_specs=(vmem(),) * 3,
        scratch_shapes=[
            pltpu.SMEM((lines, 128), jnp.int32),
            pltpu.SMEM((lines, 128), jnp.int32),
            pltpu.VMEM((slices, width), f32),
            pltpu.VMEM(sinogram.shape, f32),
            pltpu.VMEM((8, width), f32),
            pltpu.VMEM((voxel_tiles * 8, 128), f32),
        ]
        + [pltpu.VMEM((rays * 8 + 8, 128), f32)] * 4
        + [pltpu.SemaphoreType.DMA((6,)), pltpu.SemaphoreType.DMA((len(CUTS) - 1,))],
        compiler_params=params(),
        name="forward",
    )(tile_count, *sources)

    row = jax.ShapeDtypeStruct((1, width), f32)
    edge, halo = pl.pallas_call(
        edges_kernel,
        out_shape=(row, jax.ShapeDtypeStruct((4, width), f32)),
        in_specs=[vmem()] * 3,
        out_specs=(vmem(),) * 2,
        compiler_params=params(),
        name="edges",
    )(volume, split_var, dual_var)
    across = [(i, i ^ 3) for i in range(2 * reps)]
    down = [(i, i - 1) for i in range(1, slabs)]
    if slabs == 2:
        from_next = from_previous = lax.ppermute(halo, ("slab", "rep"), across)
    else:
        from_next = lax.ppermute(volume[0:1], "slab", down)
        from_previous = lax.ppermute(edge, "slab", [(i - 1, i) for i in range(1, slabs)])
    swap = [(i, i ^ 1) for i in range(reps)]
    moved = lax.ppermute(partial, "rep", swap)
    step = reps
    while step < group:
        partial = (partial.astype(f32) + moved.astype(f32)).astype(bf16)
        moved = lax.ppermute(
            partial, ("tile", "rep"), [(i, i ^ (step + 1)) for i in range(group)]
        )
        step *= 2
    limits = jnp.broadcast_to((1.0 / rho)[:, None], (1, width))
    moved, from_next, from_previous, limits = lax.optimization_barrier(
        (moved, from_next, from_previous, limits)
    )

    base = pl.pallas_call(
        local_kernel,
        out_shape=jax.ShapeDtypeStruct((slices, width), f32),
        in_specs=[smem()] + [vmem()] * 6,
        out_specs=vmem(),
        compiler_params=params(),
        name="local",
    )(rho, volume, split_var, dual_var, edge, from_next, from_previous)

    grad = pl.pallas_call(
        backward_kernel,
        out_shape=jax.ShapeDtypeStruct((slices, width), f32),
        in_specs=[smem()] + [vmem()] * 4,
        out_specs=vmem(),
        scratch_shapes=[
            pltpu.SMEM((2 * lines, 128), jnp.int32),
            pltpu.VMEM((rays * 8, 128), f32),
        ]
        + [pltpu.VMEM((voxel_tiles * 8 + 8, 128), f32)] * 4
        + [pltpu.SemaphoreType.DMA],
        compiler_params=params(),
        name="backward",
    )(tile_count, indices, tiles, partial, moved)
    grad_other = lax.ppermute(grad, "rep", swap)
    ahead = base[0:1] - TAU * (grad[0:1] + grad_other[0:1])
    if slabs == 2:
        ahead = lax.ppermute(ahead, ("slab", "rep"), across)
    else:
        ahead = lax.ppermute(ahead, "slab", down)

    whole = jax.ShapeDtypeStruct((slices, width), f32)
    triple = jax.ShapeDtypeStruct((3, slices, width), f32)
    field, new_volume, new_split, new_dual = pl.pallas_call(
        plane_kernel,
        out_shape=(whole, whole, triple, triple),
        in_specs=[vmem()] * 5,
        out_specs=(vmem(), hbm(), hbm(), hbm()),
        scratch_shapes=[pltpu.VMEM((2, slices, width), f32)] * 2
        + [pltpu.SemaphoreType.DMA((3,))],
        compiler_params=params(),
        name="plane",
    )(grad, grad_other, base, dual_var, limits)
    new_split, new_dual = pl.pallas_call(
        depth_kernel,
        out_shape=(triple, triple),
        in_specs=[vmem()] * 4 + [hbm()] * 2,
        out_specs=(hbm(), hbm()),
        scratch_shapes=[pltpu.VMEM((slices, width), f32)] * 2
        + [pltpu.SemaphoreType.DMA((2,))],
        input_output_aliases={4: 0, 5: 1},
        compiler_params=params(),
        name="depth",
    )(field, ahead, dual_var, limits, new_split, new_dual)
    return new_volume, new_split, new_dual


def solution(mesh):
    return jax.shard_map(
        shards,
        mesh=mesh,
        in_specs=(
            P(("parts", "slab"), "tile"),
            P(None, ("parts", "slab"), "tile"),
            P(None, ("parts", "slab"), "tile"),
            P(("tile", "rep"), ("parts", "slab"), None),
            P(("tile", "rep"), None, None),
            P(("tile", "rep")),
            P(("tile", "rep")),
            P(("tile", "rep")),
            P(),
        ),
        out_specs=(
            P(("parts", "slab"), "tile"),
            P(None, ("parts", "slab"), "tile"),
            P(None, ("parts", "slab"), "tile"),
        ),
        check_vma=False,
    )
```

```python
import jax
import jax.numpy as jnp
from jax import lax
from jax.experimental import pallas as pl
from jax.experimental.pallas import tpu as pltpu
from jax.sharding import PartitionSpec as P

TV = 64
TR = 128
TAU = 0.5
GROUP = 4
CUTS = (0, 2, 5, 8)
VMEM_LIMIT = 16 * 1024 * 1024


def iotas(shape):
    row = lax.broadcasted_iota(jnp.int32, shape, 0)
    lane = lax.broadcasted_iota(jnp.int32, shape, 1)
    return row, lane


def tile_copies(proj_hbm, tiles, sems):
    eighth = proj_hbm.shape[0] // CUTS[-1]
    copies = {}
    for c, (low, high) in enumerate(zip(CUTS, CUTS[1:])):
        part = pl.ds(low * eighth, (high - low) * eighth)
        copies[low * eighth] = pltpu.make_async_copy(
            proj_hbm.at[part], tiles.at[part], sems.at[c]
        )
    return copies


def plane_masks(lane):
    return (lane % TV) // 8 < 7, lane % 8 < 7


def rows8(start):
    return pl.ds(pl.multiple_of(start, 8), 8)


def add_rows(accs, starts, values):
    held = [acc[rows8(start), :] for acc, start in zip(accs, starts)]
    for acc, start, old, value in zip(accs, starts, held, values):
        acc[rows8(start), :] = old + value


def forward_kernel(
    count, ray_hbm, voxel_hbm, vol_hbm, sino_hbm, proj_hbm,
    partial_out, index_out, tiles,
    ray, voxel, vol, sino, double, table, acc0, acc1, acc2, acc3,
    sems, tile_sems,
):
    slots = proj_hbm.shape[0]
    lines = ray.shape[0]
    rays = acc0.shape[0] // 8 - 1
    owned = sino.shape[0]
    width = vol.shape[1]
    pairs = [
        (voxel_hbm, voxel), (ray_hbm, ray), (vol_hbm, vol), (sino_hbm, sino),
        (voxel_hbm, index_out.at[pl.ds(0, lines)]), (ray_hbm, index_out.at[pl.ds(lines, lines)]),
    ]
    loads = [
        pltpu.make_async_copy(source, target, sems.at[i]) for i, (source, target) in enumerate(pairs)
    ]
    copies = tile_copies(proj_hbm, tiles, tile_sems)
    loads[2].start()
    loads[0].start()
    copies[0].start()
    loads[1].start()
    for n in copies:
        if n > 0:
            copies[n].start()
    for load in loads[3:]:
        load.start()
    accs = (acc0, acc1, acc2, acc3)
    for acc in accs:
        acc[...] = jnp.zeros_like(acc)
    row, lane = iotas((8, 128))
    low, top = lane < TV, row < 4

    loads[2].wait()
    field = vol[...]
    double[0:4, :] = field
    double[4:8, :] = field
    for j in range(width // 128):
        x = double[:, 128 * j:128 * j + 128].astype(jnp.bfloat16).astype(jnp.float32)
        turned = pltpu.roll(x, TV, axis=1)
        zero = jnp.zeros_like(x)
        first = jnp.where(jnp.logical_and(top, low), x, zero)
        second = jnp.where(jnp.logical_and(top, low), turned, zero)
        other = jnp.logical_not(jnp.logical_or(top, low))
        table[16 * j:16 * j + 8, :] = jnp.where(other, turned, first)
        table[16 * j + 8:16 * j + 16, :] = jnp.where(other, x, second)

    loads[0].wait()
    loads[1].wait()
    used = count[0]
    for n in range(0, slots, GROUP):
        if n in copies:
            copies[n].wait()
        at = [divmod(n + i, 128) for i in range(GROUP)]
        picked = [table[rows8(voxel[line, place] * 8), :] for line, place in at]
        pairs = [jnp.where(top, picked[2 * i], picked[2 * i + 1]) for i in range(2)]
        zero = jnp.zeros_like(pairs[0])
        left = jnp.concatenate([pairs[0], zero], axis=0).astype(jnp.bfloat16)
        right = jnp.concatenate([zero, pairs[1]], axis=0).astype(jnp.bfloat16)
        sums = jnp.dot(
            jnp.concatenate([left, right], axis=1),
            tiles[n:n + GROUP].reshape(GROUP * TV, TR),
            preferred_element_type=jnp.float32,
        )
        add_rows(
            accs,
            [
                jnp.where(n + i < used, ray[line, place], rays) * 8
                for i, (line, place) in enumerate(at)
            ],
            [sums[0:8], sums[0:8], sums[8:16], sums[8:16]],
        )
    loads[3].wait()
    mine = (lax.axis_index("tile") * lax.axis_size("rep") + lax.axis_index("rep")) * owned
    for r in range(owned):
        at = pl.ds(pl.multiple_of((mine + r) * 8, 8), 4)
        acc0[at, :] = acc0[at, :] - sino[r]
    loads[4].wait()
    loads[5].wait()
    for q in range(rays // 4):
        halves = []
        for r in (4 * q, 4 * q + 2):
            at = [slice(8 * (r + k), 8 * (r + k) + 8) for k in range(2)]
            even = [acc0[at[k], :] + acc2[at[k], :] for k in range(2)]
            odd = [acc1[at[k], :] + acc3[at[k], :] for k in range(2)]
            halves.append(
                jnp.where(top, even[0], odd[1])
                + pltpu.roll(jnp.where(top, even[1], odd[0]), 4, axis=0)
            )
        partial_out[16 * q:16 * q + 16, :] = jnp.concatenate(halves, axis=0).astype(jnp.bfloat16)


def edges_kernel(vol, split, dual, edge_out, halo_out):
    start = lax.axis_index("slab") == 0
    for j in range(vol.shape[1] // 128):
        at = slice(128 * j, 128 * j + 128)
        edge = vol[3:4, at] - dual[0, 3:4, at] + split[0, 3:4, at]
        edge_out[:, at] = edge
        halo_out[:, at] = jnp.broadcast_to(jnp.where(start, edge, vol[0:1, at]), (4, 128))


def local_kernel(rho, vol, split, dual, edge, from_next, from_previous, base_out):
    slab, slabs = lax.axis_index("slab"), lax.axis_size("slab")
    factor = TAU * rho[0]
    row, lane = iotas((8, 128))
    row_mask, col_mask = plane_masks(lane)
    for j in range(vol.shape[1] // 128):
        at = slice(128 * j, 128 * j + 128)
        x = jnp.concatenate([vol[:, at]] * 2, axis=0)
        gap = [
            jnp.concatenate([dual[k, :, at] - split[k, :, at]] * 2, axis=0) for k in range(3)
        ]
        above = jnp.where(slab == slabs - 1, 0.0, from_next[0:1, at] - edge[:, at])
        below = jnp.where(slab == 0, 0.0, x[0:1] - from_previous[0:1, at])
        depth = jnp.where(row < 3, pltpu.roll(x, 7, axis=0) - x + gap[0], above)
        across = jnp.where(row_mask, pltpu.roll(x, 120, axis=1) - x + gap[1], 0.0)
        along = jnp.where(col_mask, pltpu.roll(x, 127, axis=1) - x + gap[2], 0.0)
        adjoint = jnp.where(row == 0, below, pltpu.roll(depth, 1, axis=0)) - depth
        adjoint += jnp.where((lane % TV) >= 8, pltpu.roll(across, 8, axis=1), 0.0) - across
        adjoint += jnp.where(lane % 8 >= 1, pltpu.roll(along, 1, axis=1), 0.0) - along
        base_out[:, at] = (x - factor * adjoint)[0:4]


def backward_kernel(
    count, indices, tiles, part, moved, grad_out,
    index, table, acc0, acc1, acc2, acc3, sem,
):
    slots = tiles.shape[0]
    lines = indices.shape[0] // 2
    rays = table.shape[0] // 8
    voxel_tiles = acc0.shape[0] // 8 - 1
    to_scalar = pltpu.make_async_copy(indices, index, sem)
    to_scalar.start()
    accs = (acc0, acc1, acc2, acc3)
    for acc in accs:
        acc[...] = jnp.zeros_like(acc)
    row, lane = iotas((8, 128))
    low, top = lane < TV, row < 4
    for q in range(rays // 4):
        at = slice(16 * q, 16 * q + 16)
        total = part[at, :].astype(jnp.float32) + moved[at, :].astype(jnp.float32)
        for k in range(2):
            x = total[8 * k:8 * k + 8]
            turned = pltpu.roll(x, 4, axis=0)
            r = 8 * (4 * q + 2 * k)
            table[r:r + 8, :] = jnp.where(top, x, turned)
            table[r + 8:r + 16, :] = jnp.where(top, turned, x)

    to_scalar.wait()
    used = count[0]
    for n in range(0, slots, GROUP):
        at = [divmod(n + i, 128) for i in range(GROUP)]
        picked = [table[rows8(index[lines + line, place] * 8), :] for line, place in at]
        rows = jnp.concatenate(
            [jnp.where(top, picked[2 * i], picked[2 * i + 1]) for i in range(2)], axis=0
        )
        back = lax.dot_general(
            rows.astype(jnp.bfloat16),
            tiles[n:n + GROUP].reshape(GROUP * TV, TR),
            (((1,), (1,)), ((), ())),
            preferred_element_type=jnp.float32,
        )
        add_rows(
            accs,
            [
                jnp.where(n + i < used, index[line, place], voxel_tiles) * 8
                for i, (line, place) in enumerate(at)
            ],
            [back[8 * k:8 * k + 8, 128 * k:128 * k + 128] for k in (0, 0, 1, 1)],
        )
    for j in range(voxel_tiles // 2):
        at = [slice(16 * j + 8 * k, 16 * j + 8 * k + 8) for k in range(2)]
        even = [acc0[at[k], :] + acc2[at[k], :] for k in range(2)]
        odd = [acc1[at[k], :] + acc3[at[k], :] for k in range(2)]
        turned = pltpu.roll(jnp.where(top, even[1], odd[0]), TV, axis=1)
        both = jnp.where(top == low, jnp.where(top, even[0], odd[1]), turned)
        grad_out[:, 128 * j:128 * j + 128] = (both + pltpu.roll(both, 4, axis=0))[0:4]


def plane_kernel(
    grad, grad_other, base, dual, limits,
    field_out, volume_hbm, split_hbm, dual_hbm,
    split, clipped, sems,
):
    row, lane = iotas((4, 128))
    row_mask, col_mask = plane_masks(lane)
    for j in range(dual.shape[2] // 128):
        at = slice(128 * j, 128 * j + 128)
        limit = limits[:, at]
        field = base[:, at] - TAU * (grad[:, at] + grad_other[:, at])
        field_out[:, at] = field
        x = jnp.concatenate([field] * 2, axis=0)
        steps = (
            jnp.where(row_mask, pltpu.roll(x, 120, axis=1)[0:4] - field, 0.0),
            jnp.where(col_mask, pltpu.roll(x, 127, axis=1)[0:4] - field, 0.0),
        )
        for k in range(2):
            mixed = steps[k] + dual[k + 1, :, at]
            bounded = jnp.clip(mixed, -limit, limit)
            clipped[k, :, at] = bounded
            split[k, :, at] = mixed - bounded
    copies = [
        pltpu.make_async_copy(split, split_hbm.at[pl.ds(1, 2)], sems.at[0]),
        pltpu.make_async_copy(clipped, dual_hbm.at[pl.ds(1, 2)], sems.at[1]),
        pltpu.make_async_copy(field_out, volume_hbm, sems.at[2]),
    ]
    for copy in copies:
        copy.start()
    for copy in copies:
        copy.wait()


def depth_kernel(
    field_in, ahead, dual, limits, split_in, dual_in,
    split_hbm, dual_hbm,
    split, clipped, sems,
):
    del split_in, dual_in
    last = lax.axis_index("slab") == lax.axis_size("slab") - 1
    row, lane = iotas((8, 128))
    inner = jnp.logical_or(row < 3, jnp.logical_not(last))
    for j in range(dual.shape[2] // 128):
        at = slice(128 * j, 128 * j + 128)
        limit = limits[:, at]
        x = jnp.concatenate([field_in[:, at]] * 2, axis=0)
        following = jnp.where(row < 3, pltpu.roll(x, 7, axis=0), ahead[:, at])
        mixed = jnp.where(inner, following - x, 0.0)[0:4] + dual[0, :, at]
        bounded = jnp.clip(mixed, -limit, limit)
        clipped[:, at] = bounded
        split[:, at] = mixed - bounded
    copies = [
        pltpu.make_async_copy(split, split_hbm.at[0], sems.at[0]),
        pltpu.make_async_copy(clipped, dual_hbm.at[0], sems.at[1]),
    ]
    for copy in copies:
        copy.start()
    for copy in copies:
        copy.wait()


def vmem():
    return pl.BlockSpec(memory_space=pltpu.VMEM)


def smem():
    return pl.BlockSpec(memory_space=pltpu.SMEM)


def hbm():
    return pl.BlockSpec(memory_space=pltpu.HBM)


def params():
    return pltpu.CompilerParams(vmem_limit_bytes=VMEM_LIMIT)


def shards(
    volume, split_var, dual_var, sinogram, proj_tiles, ray_index, voxel_index, tile_count, rho
):
    f32, bf16 = jnp.float32, jnp.bfloat16
    slices, width = volume.shape
    slots = ray_index.shape[0]
    owned = sinogram.shape[0]
    group = lax.axis_size(("tile", "rep"))
    reps = lax.axis_size("rep")
    slabs = lax.axis_size("slab")
    rays = owned * group
    voxel_tiles = width // TV
    lines = slots // 128
    ray_index, voxel_index = ray_index.reshape(lines, 128), voxel_index.reshape(lines, 128)
    sources = [
        pltpu.with_memory_space_constraint(x, pltpu.HBM)
        for x in (ray_index, voxel_index, volume, sinogram, proj_tiles)
    ]

    partial, indices, tiles = pl.pallas_call(
        forward_kernel,
        out_shape=(
            jax.ShapeDtypeStruct((rays * slices, TR), bf16),
            jax.ShapeDtypeStruct((2 * lines, 128), jnp.int32),
            jax.ShapeDtypeStruct(proj_tiles.shape, bf16),
        ),
        in_specs=[smem()] + [hbm()] * 5,
        out_specs=(vmem(),) * 3,
        scratch_shapes=[
            pltpu.SMEM((lines, 128), jnp.int32),
            pltpu.SMEM((lines, 128), jnp.int32),
            pltpu.VMEM((slices, width), f32),
            pltpu.VMEM(sinogram.shape, f32),
            pltpu.VMEM((8, width), f32),
            pltpu.VMEM((voxel_tiles * 8, 128), f32),
        ]
        + [pltpu.VMEM((rays * 8 + 8, 128), f32)] * 4
        + [pltpu.SemaphoreType.DMA((6,)), pltpu.SemaphoreType.DMA((len(CUTS) - 1,))],
        compiler_params=params(),
        name="forward",
    )(tile_count, *sources)

    row = jax.ShapeDtypeStruct((1, width), f32)
    edge, halo = pl.pallas_call(
        edges_kernel,
        out_shape=(row, jax.ShapeDtypeStruct((4, width), f32)),
        in_specs=[vmem()] * 3,
        out_specs=(vmem(),) * 2,
        compiler_params=params(),
        name="edges",
    )(volume, split_var, dual_var)
    across = [(i, i ^ 3) for i in range(2 * reps)]
    down = [(i, i - 1) for i in range(1, slabs)]
    if slabs == 2:
        from_next = from_previous = lax.ppermute(halo, ("slab", "rep"), across)
    else:
        from_next = lax.ppermute(volume[0:1], "slab", down)
        from_previous = lax.ppermute(edge, "slab", [(i - 1, i) for i in range(1, slabs)])
    swap = [(i, i ^ 1) for i in range(reps)]
    moved = lax.ppermute(partial, "rep", swap)
    step = group // 2
    while step >= reps:
        partial = (partial.astype(f32) + moved.astype(f32)).astype(bf16)
        moved = lax.ppermute(
            partial, ("tile", "rep"), [(i, i ^ (step + 1)) for i in range(group)]
        )
        step //= 2
    limits = jnp.broadcast_to((1.0 / rho)[:, None], (1, width))
    moved, from_next, from_previous, limits = lax.optimization_barrier(
        (moved, from_next, from_previous, limits)
    )

    base = pl.pallas_call(
        local_kernel,
        out_shape=jax.ShapeDtypeStruct((slices, width), f32),
        in_specs=[smem()] + [vmem()] * 6,
        out_specs=vmem(),
        compiler_params=params(),
        name="local",
    )(rho, volume, split_var, dual_var, edge, from_next, from_previous)

    grad = pl.pallas_call(
        backward_kernel,
        out_shape=jax.ShapeDtypeStruct((slices, width), f32),
        in_specs=[smem()] + [vmem()] * 4,
        out_specs=vmem(),
        scratch_shapes=[
            pltpu.SMEM((2 * lines, 128), jnp.int32),
            pltpu.VMEM((rays * 8, 128), f32),
        ]
        + [pltpu.VMEM((voxel_tiles * 8 + 8, 128), f32)] * 4
        + [pltpu.SemaphoreType.DMA],
        compiler_params=params(),
        name="backward",
    )(tile_count, indices, tiles, partial, moved)
    grad_other = lax.ppermute(grad, "rep", swap)
    ahead = base[0:1] - TAU * (grad[0:1] + grad_other[0:1])
    if slabs == 2:
        ahead = lax.ppermute(ahead, ("slab", "rep"), across)
    else:
        ahead = lax.ppermute(ahead, "slab", down)

    whole = jax.ShapeDtypeStruct((slices, width), f32)
    triple = jax.ShapeDtypeStruct((3, slices, width), f32)
    field, new_volume, new_split, new_dual = pl.pallas_call(
        plane_kernel,
        out_shape=(whole, whole, triple, triple),
        in_specs=[vmem()] * 5,
        out_specs=(vmem(), hbm(), hbm(), hbm()),
        scratch_shapes=[pltpu.VMEM((2, slices, width), f32)] * 2
        + [pltpu.SemaphoreType.DMA((3,))],
        compiler_params=params(),
        name="plane",
    )(grad, grad_other, base, dual_var, limits)
    new_split, new_dual = pl.pallas_call(
        depth_kernel,
        out_shape=(triple, triple),
        in_specs=[vmem()] * 4 + [hbm()] * 2,
        out_specs=(hbm(), hbm()),
        scratch_shapes=[pltpu.VMEM((slices, width), f32)] * 2
        + [pltpu.SemaphoreType.DMA((2,))],
        input_output_aliases={4: 0, 5: 1},
        compiler_params=params(),
        name="depth",
    )(field, ahead, dual_var, limits, new_split, new_dual)
    return new_volume, new_split, new_dual


def solution(mesh):
    return jax.shard_map(
        shards,
        mesh=mesh,
        in_specs=(
            P(("parts", "slab"), "tile"),
            P(None, ("parts", "slab"), "tile"),
            P(None, ("parts", "slab"), "tile"),
            P(("tile", "rep"), ("parts", "slab"), None),
            P(("tile", "rep"), None, None),
            P(("tile", "rep")),
            P(("tile", "rep")),
            P(("tile", "rep")),
            P(),
        ),
        out_specs=(
            P(("parts", "slab"), "tile"),
            P(None, ("parts", "slab"), "tile"),
            P(None, ("parts", "slab"), "tile"),
        ),
        check_vma=False,
    )
```

```python
import functools

import jax
import jax.numpy as jnp
from jax import lax
from jax.experimental import pallas as pl
from jax.experimental.pallas import tpu as pltpu
from jax.sharding import PartitionSpec as P

TV = 64
TR = 128
TAU = 0.5
GROUP = 4
CUTS = (0, 2, 5, 8)
VMEM_LIMIT = 16 * 1024 * 1024


def iotas(shape):
    row = lax.broadcasted_iota(jnp.int32, shape, 0)
    lane = lax.broadcasted_iota(jnp.int32, shape, 1)
    return row, lane


def tile_copies(proj_hbm, tiles, sems):
    eighth = proj_hbm.shape[0] // CUTS[-1]
    copies = {}
    for c, (low, high) in enumerate(zip(CUTS, CUTS[1:])):
        part = pl.ds(low * eighth, (high - low) * eighth)
        copies[low * eighth] = pltpu.make_async_copy(
            proj_hbm.at[part], tiles.at[part], sems.at[c]
        )
    return copies


def plane_masks(lane):
    return (lane % TV) // 8 < 7, lane % 8 < 7


def rows8(start):
    return pl.ds(pl.multiple_of(start, 8), 8)


def add_rows(accs, starts, values):
    held = [acc[rows8(start), :] for acc, start in zip(accs, starts)]
    for acc, start, old, value in zip(accs, starts, held, values):
        acc[rows8(start), :] = old + value


def forward_kernel(
    count, ray_hbm, voxel_hbm, vol_hbm, sino_hbm, proj_hbm,
    partial_out, index_out, tiles,
    ray, voxel, vol, sino, double, table, acc0, acc1, acc2, acc3,
    sems, tile_sems,
):
    slots = proj_hbm.shape[0]
    lines = ray.shape[0]
    rays = acc0.shape[0] // 8 - 1
    owned = sino.shape[0]
    width = vol.shape[1]
    pairs = [
        (voxel_hbm, voxel), (ray_hbm, ray), (vol_hbm, vol), (sino_hbm, sino),
        (voxel_hbm, index_out.at[pl.ds(0, lines)]), (ray_hbm, index_out.at[pl.ds(lines, lines)]),
    ]
    loads = [
        pltpu.make_async_copy(source, target, sems.at[i]) for i, (source, target) in enumerate(pairs)
    ]
    copies = tile_copies(proj_hbm, tiles, tile_sems)
    loads[2].start()
    loads[0].start()
    copies[0].start()
    loads[1].start()
    used = count[0]
    for n in copies:
        if n > 0:
            pl.when(used > n)(copies[n].start)
    for load in loads[3:]:
        load.start()
    accs = (acc0, acc1, acc2, acc3)
    for acc in accs:
        acc[...] = jnp.zeros_like(acc)
    row, lane = iotas((8, 128))
    low, top = lane < TV, row < 4

    loads[2].wait()
    field = vol[...]
    double[0:4, :] = field
    double[4:8, :] = field
    for j in range(width // 128):
        x = double[:, 128 * j:128 * j + 128].astype(jnp.bfloat16).astype(jnp.float32)
        turned = pltpu.roll(x, TV, axis=1)
        zero = jnp.zeros_like(x)
        first = jnp.where(jnp.logical_and(top, low), x, zero)
        second = jnp.where(jnp.logical_and(top, low), turned, zero)
        other = jnp.logical_not(jnp.logical_or(top, low))
        table[16 * j:16 * j + 8, :] = jnp.where(other, turned, first)
        table[16 * j + 8:16 * j + 16, :] = jnp.where(other, x, second)

    loads[0].wait()
    loads[1].wait()

    def add_part(low, high):
        copies[low].wait()
        for n in range(low, high, GROUP):
            at = [divmod(n + i, 128) for i in range(GROUP)]
            picked = [table[rows8(voxel[line, place] * 8), :] for line, place in at]
            pairs = [jnp.where(top, picked[2 * i], picked[2 * i + 1]) for i in range(2)]
            zero = jnp.zeros_like(pairs[0])
            left = jnp.concatenate([pairs[0], zero], axis=0).astype(jnp.bfloat16)
            right = jnp.concatenate([zero, pairs[1]], axis=0).astype(jnp.bfloat16)
            sums = jnp.dot(
                jnp.concatenate([left, right], axis=1),
                tiles[n:n + GROUP].reshape(GROUP * TV, TR),
                preferred_element_type=jnp.float32,
            )
            add_rows(
                accs,
                [
                    jnp.where(n + i < used, ray[line, place], rays) * 8
                    for i, (line, place) in enumerate(at)
                ],
                [sums[0:8], sums[0:8], sums[8:16], sums[8:16]],
            )

    lows = [*copies, slots]
    add_part(0, lows[1])
    for low, high in zip(lows[1:], lows[2:]):
        pl.when(used > low)(functools.partial(add_part, low, high))

    loads[3].wait()
    mine = (lax.axis_index("tile") * lax.axis_size("rep") + lax.axis_index("rep")) * owned
    for r in range(owned):
        at = pl.ds(pl.multiple_of((mine + r) * 8, 8), 4)
        acc0[at, :] = acc0[at, :] - sino[r]
    loads[4].wait()
    loads[5].wait()
    for q in range(rays // 4):
        halves = []
        for r in (4 * q, 4 * q + 2):
            at = [slice(8 * (r + k), 8 * (r + k) + 8) for k in range(2)]
            even = [acc0[at[k], :] + acc2[at[k], :] for k in range(2)]
            odd = [acc1[at[k], :] + acc3[at[k], :] for k in range(2)]
            halves.append(
                jnp.where(top, even[0], odd[1])
                + pltpu.roll(jnp.where(top, even[1], odd[0]), 4, axis=0)
            )
        partial_out[16 * q:16 * q + 16, :] = jnp.concatenate(halves, axis=0).astype(jnp.bfloat16)


def edges_kernel(vol, split, dual, edge_out, halo_out):
    start = lax.axis_index("slab") == 0
    for j in range(vol.shape[1] // 128):
        at = slice(128 * j, 128 * j + 128)
        edge = vol[3:4, at] - dual[0, 3:4, at] + split[0, 3:4, at]
        edge_out[:, at] = edge
        halo_out[:, at] = jnp.broadcast_to(jnp.where(start, edge, vol[0:1, at]), (4, 128))


def local_kernel(rho, vol, split, dual, edge, from_next, from_previous, base_out):
    slab, slabs = lax.axis_index("slab"), lax.axis_size("slab")
    factor = TAU * rho[0]
    row, lane = iotas((8, 128))
    row_mask, col_mask = plane_masks(lane)
    for j in range(vol.shape[1] // 128):
        at = slice(128 * j, 128 * j + 128)
        x = jnp.concatenate([vol[:, at]] * 2, axis=0)
        gap = [
            jnp.concatenate([dual[k, :, at] - split[k, :, at]] * 2, axis=0) for k in range(3)
        ]
        above = jnp.where(slab == slabs - 1, 0.0, from_next[0:1, at] - edge[:, at])
        below = jnp.where(slab == 0, 0.0, x[0:1] - from_previous[0:1, at])
        depth = jnp.where(row < 3, pltpu.roll(x, 7, axis=0) - x + gap[0], above)
        across = jnp.where(row_mask, pltpu.roll(x, 120, axis=1) - x + gap[1], 0.0)
        along = jnp.where(col_mask, pltpu.roll(x, 127, axis=1) - x + gap[2], 0.0)
        adjoint = jnp.where(row == 0, below, pltpu.roll(depth, 1, axis=0)) - depth
        adjoint += jnp.where((lane % TV) >= 8, pltpu.roll(across, 8, axis=1), 0.0) - across
        adjoint += jnp.where(lane % 8 >= 1, pltpu.roll(along, 1, axis=1), 0.0) - along
        base_out[:, at] = (x - factor * adjoint)[0:4]


def backward_kernel(
    count, indices, tiles, part, moved, grad_out,
    index, table, acc0, acc1, acc2, acc3, sem,
):
    slots = tiles.shape[0]
    lines = indices.shape[0] // 2
    rays = table.shape[0] // 8
    voxel_tiles = acc0.shape[0] // 8 - 1
    to_scalar = pltpu.make_async_copy(indices, index, sem)
    to_scalar.start()
    accs = (acc0, acc1, acc2, acc3)
    for acc in accs:
        acc[...] = jnp.zeros_like(acc)
    row, lane = iotas((8, 128))
    low, top = lane < TV, row < 4
    for q in range(rays // 4):
        at = slice(16 * q, 16 * q + 16)
        total = part[at, :].astype(jnp.float32) + moved[at, :].astype(jnp.float32)
        for k in range(2):
            x = total[8 * k:8 * k + 8]
            turned = pltpu.roll(x, 4, axis=0)
            r = 8 * (4 * q + 2 * k)
            table[r:r + 8, :] = jnp.where(top, x, turned)
            table[r + 8:r + 16, :] = jnp.where(top, turned, x)

    to_scalar.wait()
    used = count[0]
    for n in range(0, slots, GROUP):
        at = [divmod(n + i, 128) for i in range(GROUP)]
        picked = [table[rows8(index[lines + line, place] * 8), :] for line, place in at]
        rows = jnp.concatenate(
            [jnp.where(top, picked[2 * i], picked[2 * i + 1]) for i in range(2)], axis=0
        )
        back = lax.dot_general(
            rows.astype(jnp.bfloat16),
            tiles[n:n + GROUP].reshape(GROUP * TV, TR),
            (((1,), (1,)), ((), ())),
            preferred_element_type=jnp.float32,
        )
        add_rows(
            accs,
            [
                jnp.where(n + i < used, index[line, place], voxel_tiles) * 8
                for i, (line, place) in enumerate(at)
            ],
            [back[8 * k:8 * k + 8, 128 * k:128 * k + 128] for k in (0, 0, 1, 1)],
        )
    for j in range(voxel_tiles // 2):
        at = [slice(16 * j + 8 * k, 16 * j + 8 * k + 8) for k in range(2)]
        even = [acc0[at[k], :] + acc2[at[k], :] for k in range(2)]
        odd = [acc1[at[k], :] + acc3[at[k], :] for k in range(2)]
        turned = pltpu.roll(jnp.where(top, even[1], odd[0]), TV, axis=1)
        both = jnp.where(top == low, jnp.where(top, even[0], odd[1]), turned)
        grad_out[:, 128 * j:128 * j + 128] = (both + pltpu.roll(both, 4, axis=0))[0:4]


def plane_kernel(
    grad, grad_other, base, dual, limits,
    field_out, volume_hbm, split_hbm, dual_hbm,
    split, clipped, sems,
):
    row, lane = iotas((4, 128))
    row_mask, col_mask = plane_masks(lane)
    for j in range(dual.shape[2] // 128):
        at = slice(128 * j, 128 * j + 128)
        limit = limits[:, at]
        field = base[:, at] - TAU * (grad[:, at] + grad_other[:, at])
        field_out[:, at] = field
        x = jnp.concatenate([field] * 2, axis=0)
        steps = (
            jnp.where(row_mask, pltpu.roll(x, 120, axis=1)[0:4] - field, 0.0),
            jnp.where(col_mask, pltpu.roll(x, 127, axis=1)[0:4] - field, 0.0),
        )
        for k in range(2):
            mixed = steps[k] + dual[k + 1, :, at]
            bounded = jnp.clip(mixed, -limit, limit)
            clipped[k, :, at] = bounded
            split[k, :, at] = mixed - bounded
    copies = [
        pltpu.make_async_copy(split, split_hbm.at[pl.ds(1, 2)], sems.at[0]),
        pltpu.make_async_copy(clipped, dual_hbm.at[pl.ds(1, 2)], sems.at[1]),
        pltpu.make_async_copy(field_out, volume_hbm, sems.at[2]),
    ]
    for copy in copies:
        copy.start()
    for copy in copies:
        copy.wait()


def depth_kernel(
    field_in, ahead, dual, limits, split_in, dual_in,
    split_hbm, dual_hbm,
    split, clipped, sems,
):
    del split_in, dual_in
    last = lax.axis_index("slab") == lax.axis_size("slab") - 1
    row, lane = iotas((8, 128))
    inner = jnp.logical_or(row < 3, jnp.logical_not(last))
    for j in range(dual.shape[2] // 128):
        at = slice(128 * j, 128 * j + 128)
        limit = limits[:, at]
        x = jnp.concatenate([field_in[:, at]] * 2, axis=0)
        following = jnp.where(row < 3, pltpu.roll(x, 7, axis=0), ahead[:, at])
        mixed = jnp.where(inner, following - x, 0.0)[0:4] + dual[0, :, at]
        bounded = jnp.clip(mixed, -limit, limit)
        clipped[:, at] = bounded
        split[:, at] = mixed - bounded
    copies = [
        pltpu.make_async_copy(split, split_hbm.at[0], sems.at[0]),
        pltpu.make_async_copy(clipped, dual_hbm.at[0], sems.at[1]),
    ]
    for copy in copies:
        copy.start()
    for copy in copies:
        copy.wait()


def vmem():
    return pl.BlockSpec(memory_space=pltpu.VMEM)


def smem():
    return pl.BlockSpec(memory_space=pltpu.SMEM)


def hbm():
    return pl.BlockSpec(memory_space=pltpu.HBM)


def params():
    return pltpu.CompilerParams(vmem_limit_bytes=VMEM_LIMIT)


def shards(
    volume, split_var, dual_var, sinogram, proj_tiles, ray_index, voxel_index, tile_count, rho
):
    f32, bf16 = jnp.float32, jnp.bfloat16
    slices, width = volume.shape
    slots = ray_index.shape[0]
    owned = sinogram.shape[0]
    group = lax.axis_size(("tile", "rep"))
    reps = lax.axis_size("rep")
    slabs = lax.axis_size("slab")
    rays = owned * group
    voxel_tiles = width // TV
    lines = slots // 128
    ray_index, voxel_index = ray_index.reshape(lines, 128), voxel_index.reshape(lines, 128)
    sources = [
        pltpu.with_memory_space_constraint(x, pltpu.HBM)
        for x in (ray_index, voxel_index, volume, sinogram, proj_tiles)
    ]

    partial, indices, tiles = pl.pallas_call(
        forward_kernel,
        out_shape=(
            jax.ShapeDtypeStruct((rays * slices, TR), bf16),
            jax.ShapeDtypeStruct((2 * lines, 128), jnp.int32),
            jax.ShapeDtypeStruct(proj_tiles.shape, bf16),
        ),
        in_specs=[smem()] + [hbm()] * 5,
        out_specs=(vmem(),) * 3,
        scratch_shapes=[
            pltpu.SMEM((lines, 128), jnp.int32),
            pltpu.SMEM((lines, 128), jnp.int32),
            pltpu.VMEM((slices, width), f32),
            pltpu.VMEM(sinogram.shape, f32),
            pltpu.VMEM((8, width), f32),
            pltpu.VMEM((voxel_tiles * 8, 128), f32),
        ]
        + [pltpu.VMEM((rays * 8 + 8, 128), f32)] * 4
        + [pltpu.SemaphoreType.DMA((6,)), pltpu.SemaphoreType.DMA((len(CUTS) - 1,))],
        compiler_params=params(),
        name="forward",
    )(tile_count, *sources)

    row = jax.ShapeDtypeStruct((1, width), f32)
    edge, halo = pl.pallas_call(
        edges_kernel,
        out_shape=(row, jax.ShapeDtypeStruct((4, width), f32)),
        in_specs=[vmem()] * 3,
        out_specs=(vmem(),) * 2,
        compiler_params=params(),
        name="edges",
    )(volume, split_var, dual_var)
    across = [(i, i ^ 3) for i in range(2 * reps)]
    down = [(i, i - 1) for i in range(1, slabs)]
    if slabs == 2:
        from_next = from_previous = lax.ppermute(halo, ("slab", "rep"), across)
    else:
        from_next = lax.ppermute(volume[0:1], "slab", down)
        from_previous = lax.ppermute(edge, "slab", [(i - 1, i) for i in range(1, slabs)])
    swap = [(i, i ^ 1) for i in range(reps)]
    moved = lax.ppermute(partial, "rep", swap)
    step = reps
    while step < group:
        partial = (partial.astype(f32) + moved.astype(f32)).astype(bf16)
        moved = lax.ppermute(
            partial, ("tile", "rep"), [(i, i ^ (step + 1)) for i in range(group)]
        )
        step *= 2
    limits = jnp.broadcast_to((1.0 / rho)[:, None], (1, width))
    moved, from_next, from_previous, limits = lax.optimization_barrier(
        (moved, from_next, from_previous, limits)
    )

    base = pl.pallas_call(
        local_kernel,
        out_shape=jax.ShapeDtypeStruct((slices, width), f32),
        in_specs=[smem()] + [vmem()] * 6,
        out_specs=vmem(),
        compiler_params=params(),
        name="local",
    )(rho, volume, split_var, dual_var, edge, from_next, from_previous)

    grad = pl.pallas_call(
        backward_kernel,
        out_shape=jax.ShapeDtypeStruct((slices, width), f32),
        in_specs=[smem()] + [vmem()] * 4,
        out_specs=vmem(),
        scratch_shapes=[
            pltpu.SMEM((2 * lines, 128), jnp.int32),
            pltpu.VMEM((rays * 8, 128), f32),
        ]
        + [pltpu.VMEM((voxel_tiles * 8 + 8, 128), f32)] * 4
        + [pltpu.SemaphoreType.DMA],
        compiler_params=params(),
        name="backward",
    )(tile_count, indices, tiles, partial, moved)
    grad_other = lax.ppermute(grad, "rep", swap)
    ahead = base[0:1] - TAU * (grad[0:1] + grad_other[0:1])
    if slabs == 2:
        ahead = lax.ppermute(ahead, ("slab", "rep"), across)
    else:
        ahead = lax.ppermute(ahead, "slab", down)

    whole = jax.ShapeDtypeStruct((slices, width), f32)
    triple = jax.ShapeDtypeStruct((3, slices, width), f32)
    field, new_volume, new_split, new_dual = pl.pallas_call(
        plane_kernel,
        out_shape=(whole, whole, triple, triple),
        in_specs=[vmem()] * 5,
        out_specs=(vmem(), hbm(), hbm(), hbm()),
        scratch_shapes=[pltpu.VMEM((2, slices, width), f32)] * 2
        + [pltpu.SemaphoreType.DMA((3,))],
        compiler_params=params(),
        name="plane",
    )(grad, grad_other, base, dual_var, limits)
    new_split, new_dual = pl.pallas_call(
        depth_kernel,
        out_shape=(triple, triple),
        in_specs=[vmem()] * 4 + [hbm()] * 2,
        out_specs=(hbm(), hbm()),
        scratch_shapes=[pltpu.VMEM((slices, width), f32)] * 2
        + [pltpu.SemaphoreType.DMA((2,))],
        input_output_aliases={4: 0, 5: 1},
        compiler_params=params(),
        name="depth",
    )(field, ahead, dual_var, limits, new_split, new_dual)
    return new_volume, new_split, new_dual


def solution(mesh):
    return jax.shard_map(
        shards,
        mesh=mesh,
        in_specs=(
            P(("parts", "slab"), "tile"),
            P(None, ("parts", "slab"), "tile"),
            P(None, ("parts", "slab"), "tile"),
            P(("tile", "rep"), ("parts", "slab"), None),
            P(("tile", "rep"), None, None),
            P(("tile", "rep")),
            P(("tile", "rep")),
            P(("tile", "rep")),
            P(),
        ),
        out_specs=(
            P(("parts", "slab"), "tile"),
            P(None, ("parts", "slab"), "tile"),
            P(None, ("parts", "slab"), "tile"),
        ),
        check_vma=False,
    )
```

```python
import functools

import jax
import jax.numpy as jnp
from jax import lax
from jax.experimental import pallas as pl
from jax.experimental.pallas import tpu as pltpu
from jax.sharding import PartitionSpec as P

TV = 64
TR = 128
TAU = 0.5
GROUP = 4
CUTS = (0, 2, 5, 8)
VMEM_LIMIT = 16 * 1024 * 1024


def iotas(shape):
    row = lax.broadcasted_iota(jnp.int32, shape, 0)
    lane = lax.broadcasted_iota(jnp.int32, shape, 1)
    return row, lane


def tile_copies(proj_hbm, tiles, sems):
    eighth = proj_hbm.shape[0] // CUTS[-1]
    copies = {}
    for c, (low, high) in enumerate(zip(CUTS, CUTS[1:])):
        part = pl.ds(low * eighth, (high - low) * eighth)
        copies[low * eighth] = pltpu.make_async_copy(
            proj_hbm.at[part], tiles.at[part], sems.at[c]
        )
    return copies


def plane_masks(lane):
    return (lane % TV) // 8 < 7, lane % 8 < 7


def rows8(start):
    return pl.ds(pl.multiple_of(start, 8), 8)


def add_rows(accs, starts, values):
    held = [acc[rows8(start), :] for acc, start in zip(accs, starts)]
    for acc, start, old, value in zip(accs, starts, held, values):
        acc[rows8(start), :] = old + value


def forward_kernel(
    count, ray_hbm, voxel_hbm, vol_hbm, sino_hbm, proj_hbm,
    partial_out, index_out, tiles,
    ray, voxel, vol, sino, double, table, acc0, acc1, acc2, acc3,
    sems, tile_sems,
):
    slots = proj_hbm.shape[0]
    lines = ray.shape[0]
    rays = acc0.shape[0] // 8 - 1
    owned = sino.shape[0]
    width = vol.shape[1]
    pairs = [
        (voxel_hbm, voxel), (ray_hbm, ray), (vol_hbm, vol), (sino_hbm, sino),
        (voxel_hbm, index_out.at[pl.ds(0, lines)]), (ray_hbm, index_out.at[pl.ds(lines, lines)]),
    ]
    loads = [
        pltpu.make_async_copy(source, target, sems.at[i]) for i, (source, target) in enumerate(pairs)
    ]
    copies = tile_copies(proj_hbm, tiles, tile_sems)
    loads[2].start()
    loads[0].start()
    copies[0].start()
    loads[1].start()
    used = count[0]
    for n in copies:
        if n > 0:
            pl.when(used > n)(copies[n].start)
    for load in loads[3:]:
        load.start()
    accs = (acc0, acc1, acc2, acc3)
    for acc in accs:
        acc[...] = jnp.zeros_like(acc)
    row, lane = iotas((8, 128))
    low, top = lane < TV, row < 4

    loads[2].wait()
    field = vol[...]
    double[0:4, :] = field
    double[4:8, :] = field
    for j in range(width // 128):
        x = double[:, 128 * j:128 * j + 128].astype(jnp.bfloat16).astype(jnp.float32)
        turned = pltpu.roll(x, TV, axis=1)
        zero = jnp.zeros_like(x)
        first = jnp.where(jnp.logical_and(top, low), x, zero)
        second = jnp.where(jnp.logical_and(top, low), turned, zero)
        other = jnp.logical_not(jnp.logical_or(top, low))
        table[16 * j:16 * j + 8, :] = jnp.where(other, turned, first)
        table[16 * j + 8:16 * j + 16, :] = jnp.where(other, x, second)

    loads[0].wait()
    loads[1].wait()

    def add_part(low, high):
        copies[low].wait()
        for n in range(low, high, GROUP):
            at = [divmod(n + i, 128) for i in range(GROUP)]
            picked = [table[rows8(voxel[line, place] * 8), :] for line, place in at]
            pairs = [jnp.where(top, picked[2 * i], picked[2 * i + 1]) for i in range(2)]
            zero = jnp.zeros_like(pairs[0])
            left = jnp.concatenate([pairs[0], zero], axis=0).astype(jnp.bfloat16)
            right = jnp.concatenate([zero, pairs[1]], axis=0).astype(jnp.bfloat16)
            sums = jnp.dot(
                jnp.concatenate([left, right], axis=1),
                tiles[n:n + GROUP].reshape(GROUP * TV, TR),
                preferred_element_type=jnp.float32,
            )
            add_rows(
                accs,
                [
                    jnp.where(n + i < used, ray[line, place], rays) * 8
                    for i, (line, place) in enumerate(at)
                ],
                [sums[0:8], sums[0:8], sums[8:16], sums[8:16]],
            )

    lows = [*copies, slots]
    add_part(0, lows[1])
    for low, high in zip(lows[1:], lows[2:]):
        pl.when(used > low)(functools.partial(add_part, low, high))

    loads[3].wait()
    mine = (lax.axis_index("tile") * lax.axis_size("rep") + lax.axis_index("rep")) * owned
    for r in range(owned):
        at = pl.ds(pl.multiple_of((mine + r) * 8, 8), 4)
        acc0[at, :] = acc0[at, :] - sino[r]
    loads[4].wait()
    loads[5].wait()
    for q in range(rays // 4):
        halves = []
        for r in (4 * q, 4 * q + 2):
            at = [slice(8 * (r + k), 8 * (r + k) + 8) for k in range(2)]
            even = [acc0[at[k], :] + acc2[at[k], :] for k in range(2)]
            odd = [acc1[at[k], :] + acc3[at[k], :] for k in range(2)]
            halves.append(
                jnp.where(top, even[0], odd[1])
                + pltpu.roll(jnp.where(top, even[1], odd[0]), 4, axis=0)
            )
        partial_out[16 * q:16 * q + 16, :] = jnp.concatenate(halves, axis=0).astype(jnp.bfloat16)


def edges_kernel(vol, split, dual, edge_out, halo_out):
    start = lax.axis_index("slab") == 0
    for j in range(vol.shape[1] // 128):
        at = slice(128 * j, 128 * j + 128)
        edge = vol[3:4, at] - dual[0, 3:4, at] + split[0, 3:4, at]
        edge_out[:, at] = edge
        halo_out[:, at] = jnp.broadcast_to(jnp.where(start, edge, vol[0:1, at]), (4, 128))


def local_kernel(rho, vol, split, dual, edge, from_next, from_previous, base_out):
    slab, slabs = lax.axis_index("slab"), lax.axis_size("slab")
    factor = TAU * rho[0]
    row, lane = iotas((8, 128))
    row_mask, col_mask = plane_masks(lane)
    for j in range(vol.shape[1] // 128):
        at = slice(128 * j, 128 * j + 128)
        x = jnp.concatenate([vol[:, at]] * 2, axis=0)
        gap = [
            jnp.concatenate([dual[k, :, at] - split[k, :, at]] * 2, axis=0) for k in range(3)
        ]
        above = jnp.where(slab == slabs - 1, 0.0, from_next[0:1, at] - edge[:, at])
        below = jnp.where(slab == 0, 0.0, x[0:1] - from_previous[0:1, at])
        depth = jnp.where(row < 3, pltpu.roll(x, 7, axis=0) - x + gap[0], above)
        across = jnp.where(row_mask, pltpu.roll(x, 120, axis=1) - x + gap[1], 0.0)
        along = jnp.where(col_mask, pltpu.roll(x, 127, axis=1) - x + gap[2], 0.0)
        adjoint = jnp.where(row == 0, below, pltpu.roll(depth, 1, axis=0)) - depth
        adjoint += jnp.where((lane % TV) >= 8, pltpu.roll(across, 8, axis=1), 0.0) - across
        adjoint += jnp.where(lane % 8 >= 1, pltpu.roll(along, 1, axis=1), 0.0) - along
        base_out[:, at] = (x - factor * adjoint)[0:4]


def backward_kernel(
    count, indices, tiles, part, moved, grad_out,
    index, table, acc0, acc1, acc2, acc3, sem,
):
    slots = tiles.shape[0]
    lines = indices.shape[0] // 2
    rays = table.shape[0] // 8
    voxel_tiles = acc0.shape[0] // 8 - 1
    to_scalar = pltpu.make_async_copy(indices, index, sem)
    to_scalar.start()
    accs = (acc0, acc1, acc2, acc3)
    for acc in accs:
        acc[...] = jnp.zeros_like(acc)
    row, lane = iotas((8, 128))
    low, top = lane < TV, row < 4
    for q in range(rays // 4):
        at = slice(16 * q, 16 * q + 16)
        total = part[at, :].astype(jnp.float32) + moved[at, :].astype(jnp.float32)
        for k in range(2):
            x = total[8 * k:8 * k + 8]
            turned = pltpu.roll(x, 4, axis=0)
            r = 8 * (4 * q + 2 * k)
            table[r:r + 8, :] = jnp.where(top, x, turned)
            table[r + 8:r + 16, :] = jnp.where(top, turned, x)

    to_scalar.wait()
    used = count[0]

    def add_part(low, high):
        for n in range(low, high, GROUP):
            at = [divmod(n + i, 128) for i in range(GROUP)]
            picked = [table[rows8(index[lines + line, place] * 8), :] for line, place in at]
            rows = jnp.concatenate(
                [jnp.where(top, picked[2 * i], picked[2 * i + 1]) for i in range(2)], axis=0
            )
            back = lax.dot_general(
                rows.astype(jnp.bfloat16),
                tiles[n:n + GROUP].reshape(GROUP * TV, TR),
                (((1,), (1,)), ((), ())),
                preferred_element_type=jnp.float32,
            )
            add_rows(
                accs,
                [
                    jnp.where(n + i < used, index[line, place], voxel_tiles) * 8
                    for i, (line, place) in enumerate(at)
                ],
                [back[8 * k:8 * k + 8, 128 * k:128 * k + 128] for k in (0, 0, 1, 1)],
            )

    cut = slots * CUTS[-2] // CUTS[-1]
    add_part(0, cut)
    pl.when(used > cut)(functools.partial(add_part, cut, slots))

    for j in range(voxel_tiles // 2):
        at = [slice(16 * j + 8 * k, 16 * j + 8 * k + 8) for k in range(2)]
        even = [acc0[at[k], :] + acc2[at[k], :] for k in range(2)]
        odd = [acc1[at[k], :] + acc3[at[k], :] for k in range(2)]
        turned = pltpu.roll(jnp.where(top, even[1], odd[0]), TV, axis=1)
        both = jnp.where(top == low, jnp.where(top, even[0], odd[1]), turned)
        grad_out[:, 128 * j:128 * j + 128] = (both + pltpu.roll(both, 4, axis=0))[0:4]


def plane_kernel(
    grad, grad_other, base, dual, limits,
    field_out, volume_hbm, split_hbm, dual_hbm,
    split, clipped, sems,
):
    row, lane = iotas((4, 128))
    row_mask, col_mask = plane_masks(lane)
    for j in range(dual.shape[2] // 128):
        at = slice(128 * j, 128 * j + 128)
        limit = limits[:, at]
        field = base[:, at] - TAU * (grad[:, at] + grad_other[:, at])
        field_out[:, at] = field
        x = jnp.concatenate([field] * 2, axis=0)
        steps = (
            jnp.where(row_mask, pltpu.roll(x, 120, axis=1)[0:4] - field, 0.0),
            jnp.where(col_mask, pltpu.roll(x, 127, axis=1)[0:4] - field, 0.0),
        )
        for k in range(2):
            mixed = steps[k] + dual[k + 1, :, at]
            bounded = jnp.clip(mixed, -limit, limit)
            clipped[k, :, at] = bounded
            split[k, :, at] = mixed - bounded
    copies = [
        pltpu.make_async_copy(split, split_hbm.at[pl.ds(1, 2)], sems.at[0]),
        pltpu.make_async_copy(clipped, dual_hbm.at[pl.ds(1, 2)], sems.at[1]),
        pltpu.make_async_copy(field_out, volume_hbm, sems.at[2]),
    ]
    for copy in copies:
        copy.start()
    for copy in copies:
        copy.wait()


def depth_kernel(
    field_in, ahead, dual, limits, split_in, dual_in,
    split_hbm, dual_hbm,
    split, clipped, sems,
):
    del split_in, dual_in
    last = lax.axis_index("slab") == lax.axis_size("slab") - 1
    row, lane = iotas((8, 128))
    inner = jnp.logical_or(row < 3, jnp.logical_not(last))
    for j in range(dual.shape[2] // 128):
        at = slice(128 * j, 128 * j + 128)
        limit = limits[:, at]
        x = jnp.concatenate([field_in[:, at]] * 2, axis=0)
        following = jnp.where(row < 3, pltpu.roll(x, 7, axis=0), ahead[:, at])
        mixed = jnp.where(inner, following - x, 0.0)[0:4] + dual[0, :, at]
        bounded = jnp.clip(mixed, -limit, limit)
        clipped[:, at] = bounded
        split[:, at] = mixed - bounded
    copies = [
        pltpu.make_async_copy(split, split_hbm.at[0], sems.at[0]),
        pltpu.make_async_copy(clipped, dual_hbm.at[0], sems.at[1]),
    ]
    for copy in copies:
        copy.start()
    for copy in copies:
        copy.wait()


def vmem():
    return pl.BlockSpec(memory_space=pltpu.VMEM)


def smem():
    return pl.BlockSpec(memory_space=pltpu.SMEM)


def hbm():
    return pl.BlockSpec(memory_space=pltpu.HBM)


def params():
    return pltpu.CompilerParams(vmem_limit_bytes=VMEM_LIMIT)


def shards(
    volume, split_var, dual_var, sinogram, proj_tiles, ray_index, voxel_index, tile_count, rho
):
    f32, bf16 = jnp.float32, jnp.bfloat16
    slices, width = volume.shape
    slots = ray_index.shape[0]
    owned = sinogram.shape[0]
    group = lax.axis_size(("tile", "rep"))
    reps = lax.axis_size("rep")
    slabs = lax.axis_size("slab")
    rays = owned * group
    voxel_tiles = width // TV
    lines = slots // 128
    ray_index, voxel_index = ray_index.reshape(lines, 128), voxel_index.reshape(lines, 128)
    sources = [
        pltpu.with_memory_space_constraint(x, pltpu.HBM)
        for x in (ray_index, voxel_index, volume, sinogram, proj_tiles)
    ]

    partial, indices, tiles = pl.pallas_call(
        forward_kernel,
        out_shape=(
            jax.ShapeDtypeStruct((rays * slices, TR), bf16),
            jax.ShapeDtypeStruct((2 * lines, 128), jnp.int32),
            jax.ShapeDtypeStruct(proj_tiles.shape, bf16),
        ),
        in_specs=[smem()] + [hbm()] * 5,
        out_specs=(vmem(),) * 3,
        scratch_shapes=[
            pltpu.SMEM((lines, 128), jnp.int32),
            pltpu.SMEM((lines, 128), jnp.int32),
            pltpu.VMEM((slices, width), f32),
            pltpu.VMEM(sinogram.shape, f32),
            pltpu.VMEM((8, width), f32),
            pltpu.VMEM((voxel_tiles * 8, 128), f32),
        ]
        + [pltpu.VMEM((rays * 8 + 8, 128), f32)] * 4
        + [pltpu.SemaphoreType.DMA((6,)), pltpu.SemaphoreType.DMA((len(CUTS) - 1,))],
        compiler_params=params(),
        name="forward",
    )(tile_count, *sources)

    row = jax.ShapeDtypeStruct((1, width), f32)
    edge, halo = pl.pallas_call(
        edges_kernel,
        out_shape=(row, jax.ShapeDtypeStruct((4, width), f32)),
        in_specs=[vmem()] * 3,
        out_specs=(vmem(),) * 2,
        compiler_params=params(),
        name="edges",
    )(volume, split_var, dual_var)
    across = [(i, i ^ 3) for i in range(2 * reps)]
    down = [(i, i - 1) for i in range(1, slabs)]
    if slabs == 2:
        from_next = from_previous = lax.ppermute(halo, ("slab", "rep"), across)
    else:
        from_next = lax.ppermute(volume[0:1], "slab", down)
        from_previous = lax.ppermute(edge, "slab", [(i - 1, i) for i in range(1, slabs)])
    swap = [(i, i ^ 1) for i in range(reps)]
    moved = lax.ppermute(partial, "rep", swap)
    step = reps
    while step < group:
        partial = (partial.astype(f32) + moved.astype(f32)).astype(bf16)
        moved = lax.ppermute(
            partial, ("tile", "rep"), [(i, i ^ (step + 1)) for i in range(group)]
        )
        step *= 2
    limits = jnp.broadcast_to((1.0 / rho)[:, None], (1, width))
    moved, from_next, from_previous, limits = lax.optimization_barrier(
        (moved, from_next, from_previous, limits)
    )

    base = pl.pallas_call(
        local_kernel,
        out_shape=jax.ShapeDtypeStruct((slices, width), f32),
        in_specs=[smem()] + [vmem()] * 6,
        out_specs=vmem(),
        compiler_params=params(),
        name="local",
    )(rho, volume, split_var, dual_var, edge, from_next, from_previous)

    grad = pl.pallas_call(
        backward_kernel,
        out_shape=jax.ShapeDtypeStruct((slices, width), f32),
        in_specs=[smem()] + [vmem()] * 4,
        out_specs=vmem(),
        scratch_shapes=[
            pltpu.SMEM((2 * lines, 128), jnp.int32),
            pltpu.VMEM((rays * 8, 128), f32),
        ]
        + [pltpu.VMEM((voxel_tiles * 8 + 8, 128), f32)] * 4
        + [pltpu.SemaphoreType.DMA],
        compiler_params=params(),
        name="backward",
    )(tile_count, indices, tiles, partial, moved)
    grad_other = lax.ppermute(grad, "rep", swap)
    ahead = base[0:1] - TAU * (grad[0:1] + grad_other[0:1])
    if slabs == 2:
        ahead = lax.ppermute(ahead, ("slab", "rep"), across)
    else:
        ahead = lax.ppermute(ahead, "slab", down)

    whole = jax.ShapeDtypeStruct((slices, width), f32)
    triple = jax.ShapeDtypeStruct((3, slices, width), f32)
    field, new_volume, new_split, new_dual = pl.pallas_call(
        plane_kernel,
        out_shape=(whole, whole, triple, triple),
        in_specs=[vmem()] * 5,
        out_specs=(vmem(), hbm(), hbm(), hbm()),
        scratch_shapes=[pltpu.VMEM((2, slices, width), f32)] * 2
        + [pltpu.SemaphoreType.DMA((3,))],
        compiler_params=params(),
        name="plane",
    )(grad, grad_other, base, dual_var, limits)
    new_split, new_dual = pl.pallas_call(
        depth_kernel,
        out_shape=(triple, triple),
        in_specs=[vmem()] * 4 + [hbm()] * 2,
        out_specs=(hbm(), hbm()),
        scratch_shapes=[pltpu.VMEM((slices, width), f32)] * 2
        + [pltpu.SemaphoreType.DMA((2,))],
        input_output_aliases={4: 0, 5: 1},
        compiler_params=params(),
        name="depth",
    )(field, ahead, dual_var, limits, new_split, new_dual)
    return new_volume, new_split, new_dual


def solution(mesh):
    return jax.shard_map(
        shards,
        mesh=mesh,
        in_specs=(
            P(("parts", "slab"), "tile"),
            P(None, ("parts", "slab"), "tile"),
            P(None, ("parts", "slab"), "tile"),
            P(("tile", "rep"), ("parts", "slab"), None),
            P(("tile", "rep"), None, None),
            P(("tile", "rep")),
            P(("tile", "rep")),
            P(("tile", "rep")),
            P(),
        ),
        out_specs=(
            P(("parts", "slab"), "tile"),
            P(None, ("parts", "slab"), "tile"),
            P(None, ("parts", "slab"), "tile"),
        ),
        check_vma=False,
    )
```

```python
import functools

import jax
import jax.numpy as jnp
from jax import lax
from jax.experimental import pallas as pl
from jax.experimental.pallas import tpu as pltpu
from jax.sharding import PartitionSpec as P

TV = 64
TR = 128
TAU = 0.5
GROUP = 4
CUTS = (0, 2, 5, 8)
VMEM_LIMIT = 16 * 1024 * 1024


def iotas(shape):
    row = lax.broadcasted_iota(jnp.int32, shape, 0)
    lane = lax.broadcasted_iota(jnp.int32, shape, 1)
    return row, lane


def tile_copies(proj_hbm, tiles, sems):
    eighth = proj_hbm.shape[0] // CUTS[-1]
    copies = {}
    for c, (low, high) in enumerate(zip(CUTS, CUTS[1:])):
        part = pl.ds(low * eighth, (high - low) * eighth)
        copies[low * eighth] = pltpu.make_async_copy(
            proj_hbm.at[part], tiles.at[part], sems.at[c]
        )
    return copies


def plane_masks(lane):
    return (lane % TV) // 8 < 7, lane % 8 < 7


def rows8(start):
    return pl.ds(pl.multiple_of(start, 8), 8)


def add_rows(accs, starts, values):
    held = [acc[rows8(start), :] for acc, start in zip(accs, starts)]
    for acc, start, old, value in zip(accs, starts, held, values):
        acc[rows8(start), :] = old + value


def forward_kernel(
    count, ray_hbm, voxel_hbm, vol_hbm, sino_hbm, proj_hbm,
    partial_out, tiles,
    ray, voxel, vol, sino, double, table, acc0, acc1, acc2, acc3,
    sems, tile_sems,
):
    slots = proj_hbm.shape[0]
    rays = acc0.shape[0] // 8 - 1
    owned = sino.shape[0]
    width = vol.shape[1]
    pairs = [(voxel_hbm, voxel), (ray_hbm, ray), (vol_hbm, vol), (sino_hbm, sino)]
    loads = [
        pltpu.make_async_copy(source, target, sems.at[i]) for i, (source, target) in enumerate(pairs)
    ]
    copies = tile_copies(proj_hbm, tiles, tile_sems)
    loads[2].start()
    loads[0].start()
    copies[0].start()
    loads[1].start()
    used = count[0]
    for n in copies:
        if n > 0:
            pl.when(used > n)(copies[n].start)
    for load in loads[3:]:
        load.start()
    accs = (acc0, acc1, acc2, acc3)
    for acc in accs:
        acc[...] = jnp.zeros_like(acc)
    row, lane = iotas((8, 128))
    low, top = lane < TV, row < 4

    loads[2].wait()
    field = vol[...]
    double[0:4, :] = field
    double[4:8, :] = field
    for j in range(width // 128):
        x = double[:, 128 * j:128 * j + 128].astype(jnp.bfloat16).astype(jnp.float32)
        turned = pltpu.roll(x, TV, axis=1)
        zero = jnp.zeros_like(x)
        first = jnp.where(jnp.logical_and(top, low), x, zero)
        second = jnp.where(jnp.logical_and(top, low), turned, zero)
        other = jnp.logical_not(jnp.logical_or(top, low))
        table[16 * j:16 * j + 8, :] = jnp.where(other, turned, first)
        table[16 * j + 8:16 * j + 16, :] = jnp.where(other, x, second)

    loads[0].wait()
    loads[1].wait()

    def add_part(low, high):
        copies[low].wait()
        for n in range(low, high, GROUP):
            at = [divmod(n + i, 128) for i in range(GROUP)]
            picked = [table[rows8(voxel[line, place] * 8), :] for line, place in at]
            pairs = [jnp.where(top, picked[2 * i], picked[2 * i + 1]) for i in range(2)]
            zero = jnp.zeros_like(pairs[0])
            left = jnp.concatenate([pairs[0], zero], axis=0).astype(jnp.bfloat16)
            right = jnp.concatenate([zero, pairs[1]], axis=0).astype(jnp.bfloat16)
            sums = jnp.dot(
                jnp.concatenate([left, right], axis=1),
                tiles[n:n + GROUP].reshape(GROUP * TV, TR),
                preferred_element_type=jnp.float32,
            )
            add_rows(
                accs,
                [
                    jnp.where(n + i < used, ray[line, place], rays) * 8
                    for i, (line, place) in enumerate(at)
                ],
                [sums[0:8], sums[0:8], sums[8:16], sums[8:16]],
            )

    lows = [*copies, slots]
    add_part(0, lows[1])
    for low, high in zip(lows[1:], lows[2:]):
        pl.when(used > low)(functools.partial(add_part, low, high))

    loads[3].wait()
    mine = (lax.axis_index("tile") * lax.axis_size("rep") + lax.axis_index("rep")) * owned
    for r in range(owned):
        at = pl.ds(pl.multiple_of((mine + r) * 8, 8), 4)
        acc0[at, :] = acc0[at, :] - sino[r]
    for q in range(rays // 4):
        halves = []
        for r in (4 * q, 4 * q + 2):
            at = [slice(8 * (r + k), 8 * (r + k) + 8) for k in range(2)]
            even = [acc0[at[k], :] + acc2[at[k], :] for k in range(2)]
            odd = [acc1[at[k], :] + acc3[at[k], :] for k in range(2)]
            halves.append(
                jnp.where(top, even[0], odd[1])
                + pltpu.roll(jnp.where(top, even[1], odd[0]), 4, axis=0)
            )
        partial_out[16 * q:16 * q + 16, :] = jnp.concatenate(halves, axis=0).astype(jnp.bfloat16)


def index_kernel(ray_hbm, voxel_hbm, index_out, sems):
    lines = ray_hbm.shape[0]
    copies = [
        pltpu.make_async_copy(voxel_hbm, index_out.at[pl.ds(0, lines)], sems.at[0]),
        pltpu.make_async_copy(ray_hbm, index_out.at[pl.ds(lines, lines)], sems.at[1]),
    ]
    for copy in copies:
        copy.start()
    for copy in copies:
        copy.wait()


def edges_kernel(vol, split, dual, edge_out, halo_out):
    start = lax.axis_index("slab") == 0
    for j in range(vol.shape[1] // 128):
        at = slice(128 * j, 128 * j + 128)
        edge = vol[3:4, at] - dual[0, 3:4, at] + split[0, 3:4, at]
        edge_out[:, at] = edge
        halo_out[:, at] = jnp.broadcast_to(jnp.where(start, edge, vol[0:1, at]), (4, 128))


def local_kernel(rho, vol, split, dual, edge, from_next, from_previous, base_out):
    slab, slabs = lax.axis_index("slab"), lax.axis_size("slab")
    factor = TAU * rho[0]
    row, lane = iotas((8, 128))
    row_mask, col_mask = plane_masks(lane)
    for j in range(vol.shape[1] // 128):
        at = slice(128 * j, 128 * j + 128)
        x = jnp.concatenate([vol[:, at]] * 2, axis=0)
        gap = [
            jnp.concatenate([dual[k, :, at] - split[k, :, at]] * 2, axis=0) for k in range(3)
        ]
        above = jnp.where(slab == slabs - 1, 0.0, from_next[0:1, at] - edge[:, at])
        below = jnp.where(slab == 0, 0.0, x[0:1] - from_previous[0:1, at])
        depth = jnp.where(row < 3, pltpu.roll(x, 7, axis=0) - x + gap[0], above)
        across = jnp.where(row_mask, pltpu.roll(x, 120, axis=1) - x + gap[1], 0.0)
        along = jnp.where(col_mask, pltpu.roll(x, 127, axis=1) - x + gap[2], 0.0)
        adjoint = jnp.where(row == 0, below, pltpu.roll(depth, 1, axis=0)) - depth
        adjoint += jnp.where((lane % TV) >= 8, pltpu.roll(across, 8, axis=1), 0.0) - across
        adjoint += jnp.where(lane % 8 >= 1, pltpu.roll(along, 1, axis=1), 0.0) - along
        base_out[:, at] = (x - factor * adjoint)[0:4]


def backward_kernel(
    count, indices, tiles, part, moved, grad_out,
    index, table, acc0, acc1, acc2, acc3, sem,
):
    slots = tiles.shape[0]
    lines = indices.shape[0] // 2
    rays = table.shape[0] // 8
    voxel_tiles = acc0.shape[0] // 8 - 1
    to_scalar = pltpu.make_async_copy(indices, index, sem)
    to_scalar.start()
    accs = (acc0, acc1, acc2, acc3)
    for acc in accs:
        acc[...] = jnp.zeros_like(acc)
    row, lane = iotas((8, 128))
    low, top = lane < TV, row < 4
    for q in range(rays // 4):
        at = slice(16 * q, 16 * q + 16)
        total = part[at, :].astype(jnp.float32) + moved[at, :].astype(jnp.float32)
        for k in range(2):
            x = total[8 * k:8 * k + 8]
            turned = pltpu.roll(x, 4, axis=0)
            r = 8 * (4 * q + 2 * k)
            table[r:r + 8, :] = jnp.where(top, x, turned)
            table[r + 8:r + 16, :] = jnp.where(top, turned, x)

    to_scalar.wait()
    used = count[0]
    for n in range(0, slots, GROUP):
        at = [divmod(n + i, 128) for i in range(GROUP)]
        picked = [table[rows8(index[lines + line, place] * 8), :] for line, place in at]
        rows = jnp.concatenate(
            [jnp.where(top, picked[2 * i], picked[2 * i + 1]) for i in range(2)], axis=0
        )
        back = lax.dot_general(
            rows.astype(jnp.bfloat16),
            tiles[n:n + GROUP].reshape(GROUP * TV, TR),
            (((1,), (1,)), ((), ())),
            preferred_element_type=jnp.float32,
        )
        add_rows(
            accs,
            [
                jnp.where(n + i < used, index[line, place], voxel_tiles) * 8
                for i, (line, place) in enumerate(at)
            ],
            [back[8 * k:8 * k + 8, 128 * k:128 * k + 128] for k in (0, 0, 1, 1)],
        )
    for j in range(voxel_tiles // 2):
        at = [slice(16 * j + 8 * k, 16 * j + 8 * k + 8) for k in range(2)]
        even = [acc0[at[k], :] + acc2[at[k], :] for k in range(2)]
        odd = [acc1[at[k], :] + acc3[at[k], :] for k in range(2)]
        turned = pltpu.roll(jnp.where(top, even[1], odd[0]), TV, axis=1)
        both = jnp.where(top == low, jnp.where(top, even[0], odd[1]), turned)
        grad_out[:, 128 * j:128 * j + 128] = (both + pltpu.roll(both, 4, axis=0))[0:4]


def plane_kernel(
    grad, grad_other, base, dual, limits,
    field_out, volume_hbm, split_hbm, dual_hbm,
    split, clipped, sems,
):
    row, lane = iotas((4, 128))
    row_mask, col_mask = plane_masks(lane)
    for j in range(dual.shape[2] // 128):
        at = slice(128 * j, 128 * j + 128)
        limit = limits[:, at]
        field = base[:, at] - TAU * (grad[:, at] + grad_other[:, at])
        field_out[:, at] = field
        x = jnp.concatenate([field] * 2, axis=0)
        steps = (
            jnp.where(row_mask, pltpu.roll(x, 120, axis=1)[0:4] - field, 0.0),
            jnp.where(col_mask, pltpu.roll(x, 127, axis=1)[0:4] - field, 0.0),
        )
        for k in range(2):
            mixed = steps[k] + dual[k + 1, :, at]
            bounded = jnp.clip(mixed, -limit, limit)
            clipped[k, :, at] = bounded
            split[k, :, at] = mixed - bounded
    copies = [
        pltpu.make_async_copy(split, split_hbm.at[pl.ds(1, 2)], sems.at[0]),
        pltpu.make_async_copy(clipped, dual_hbm.at[pl.ds(1, 2)], sems.at[1]),
        pltpu.make_async_copy(field_out, volume_hbm, sems.at[2]),
    ]
    for copy in copies:
        copy.start()
    for copy in copies:
        copy.wait()


def depth_kernel(
    field_in, ahead, dual, limits, split_in, dual_in,
    split_hbm, dual_hbm,
    split, clipped, sems,
):
    del split_in, dual_in
    last = lax.axis_index("slab") == lax.axis_size("slab") - 1
    row, lane = iotas((8, 128))
    inner = jnp.logical_or(row < 3, jnp.logical_not(last))
    for j in range(dual.shape[2] // 128):
        at = slice(128 * j, 128 * j + 128)
        limit = limits[:, at]
        x = jnp.concatenate([field_in[:, at]] * 2, axis=0)
        following = jnp.where(row < 3, pltpu.roll(x, 7, axis=0), ahead[:, at])
        mixed = jnp.where(inner, following - x, 0.0)[0:4] + dual[0, :, at]
        bounded = jnp.clip(mixed, -limit, limit)
        clipped[:, at] = bounded
        split[:, at] = mixed - bounded
    copies = [
        pltpu.make_async_copy(split, split_hbm.at[0], sems.at[0]),
        pltpu.make_async_copy(clipped, dual_hbm.at[0], sems.at[1]),
    ]
    for copy in copies:
        copy.start()
    for copy in copies:
        copy.wait()


def vmem():
    return pl.BlockSpec(memory_space=pltpu.VMEM)


def smem():
    return pl.BlockSpec(memory_space=pltpu.SMEM)


def hbm():
    return pl.BlockSpec(memory_space=pltpu.HBM)


def params():
    return pltpu.CompilerParams(vmem_limit_bytes=VMEM_LIMIT)


def shards(
    volume, split_var, dual_var, sinogram, proj_tiles, ray_index, voxel_index, tile_count, rho
):
    f32, bf16 = jnp.float32, jnp.bfloat16
    slices, width = volume.shape
    slots = ray_index.shape[0]
    owned = sinogram.shape[0]
    group = lax.axis_size(("tile", "rep"))
    reps = lax.axis_size("rep")
    slabs = lax.axis_size("slab")
    rays = owned * group
    voxel_tiles = width // TV
    lines = slots // 128
    ray_index, voxel_index = ray_index.reshape(lines, 128), voxel_index.reshape(lines, 128)
    sources = [
        pltpu.with_memory_space_constraint(x, pltpu.HBM)
        for x in (ray_index, voxel_index, volume, sinogram, proj_tiles)
    ]

    partial, tiles = pl.pallas_call(
        forward_kernel,
        out_shape=(
            jax.ShapeDtypeStruct((rays * slices, TR), bf16),
            jax.ShapeDtypeStruct(proj_tiles.shape, bf16),
        ),
        in_specs=[smem()] + [hbm()] * 5,
        out_specs=(vmem(),) * 2,
        scratch_shapes=[
            pltpu.SMEM((lines, 128), jnp.int32),
            pltpu.SMEM((lines, 128), jnp.int32),
            pltpu.VMEM((slices, width), f32),
            pltpu.VMEM(sinogram.shape, f32),
            pltpu.VMEM((8, width), f32),
            pltpu.VMEM((voxel_tiles * 8, 128), f32),
        ]
        + [pltpu.VMEM((rays * 8 + 8, 128), f32)] * 4
        + [pltpu.SemaphoreType.DMA((4,)), pltpu.SemaphoreType.DMA((len(CUTS) - 1,))],
        compiler_params=params(),
        name="forward",
    )(tile_count, *sources)

    row = jax.ShapeDtypeStruct((1, width), f32)
    edge, halo = pl.pallas_call(
        edges_kernel,
        out_shape=(row, jax.ShapeDtypeStruct((4, width), f32)),
        in_specs=[vmem()] * 3,
        out_specs=(vmem(),) * 2,
        compiler_params=params(),
        name="edges",
    )(volume, split_var, dual_var)
    across = [(i, i ^ 3) for i in range(2 * reps)]
    down = [(i, i - 1) for i in range(1, slabs)]
    if slabs == 2:
        from_next = from_previous = lax.ppermute(halo, ("slab", "rep"), across)
    else:
        from_next = lax.ppermute(volume[0:1], "slab", down)
        from_previous = lax.ppermute(edge, "slab", [(i - 1, i) for i in range(1, slabs)])
    swap = [(i, i ^ 1) for i in range(reps)]
    moved = lax.ppermute(partial, "rep", swap)
    step = reps
    while step < group:
        partial = (partial.astype(f32) + moved.astype(f32)).astype(bf16)
        moved = lax.ppermute(
            partial, ("tile", "rep"), [(i, i ^ (step + 1)) for i in range(group)]
        )
        step *= 2
    indices = pl.pallas_call(
        index_kernel,
        out_shape=jax.ShapeDtypeStruct((2 * lines, 128), jnp.int32),
        in_specs=[hbm()] * 2,
        out_specs=vmem(),
        scratch_shapes=[pltpu.SemaphoreType.DMA((2,))],
        compiler_params=params(),
        name="indices",
    )(*sources[:2])
    limits = jnp.broadcast_to((1.0 / rho)[:, None], (1, width))
    moved, from_next, from_previous, limits, indices = lax.optimization_barrier(
        (moved, from_next, from_previous, limits, indices)
    )

    base = pl.pallas_call(
        local_kernel,
        out_shape=jax.ShapeDtypeStruct((slices, width), f32),
        in_specs=[smem()] + [vmem()] * 6,
        out_specs=vmem(),
        compiler_params=params(),
        name="local",
    )(rho, volume, split_var, dual_var, edge, from_next, from_previous)

    grad = pl.pallas_call(
        backward_kernel,
        out_shape=jax.ShapeDtypeStruct((slices, width), f32),
        in_specs=[smem()] + [vmem()] * 4,
        out_specs=vmem(),
        scratch_shapes=[
            pltpu.SMEM((2 * lines, 128), jnp.int32),
            pltpu.VMEM((rays * 8, 128), f32),
        ]
        + [pltpu.VMEM((voxel_tiles * 8 + 8, 128), f32)] * 4
        + [pltpu.SemaphoreType.DMA],
        compiler_params=params(),
        name="backward",
    )(tile_count, indices, tiles, partial, moved)
    grad_other = lax.ppermute(grad, "rep", swap)
    ahead = base[0:1] - TAU * (grad[0:1] + grad_other[0:1])
    if slabs == 2:
        ahead = lax.ppermute(ahead, ("slab", "rep"), across)
    else:
        ahead = lax.ppermute(ahead, "slab", down)

    whole = jax.ShapeDtypeStruct((slices, width), f32)
    triple = jax.ShapeDtypeStruct((3, slices, width), f32)
    field, new_volume, new_split, new_dual = pl.pallas_call(
        plane_kernel,
        out_shape=(whole, whole, triple, triple),
        in_specs=[vmem()] * 5,
        out_specs=(vmem(), hbm(), hbm(), hbm()),
        scratch_shapes=[pltpu.VMEM((2, slices, width), f32)] * 2
        + [pltpu.SemaphoreType.DMA((3,))],
        compiler_params=params(),
        name="plane",
    )(grad, grad_other, base, dual_var, limits)
    new_split, new_dual = pl.pallas_call(
        depth_kernel,
        out_shape=(triple, triple),
        in_specs=[vmem()] * 4 + [hbm()] * 2,
        out_specs=(hbm(), hbm()),
        scratch_shapes=[pltpu.VMEM((slices, width), f32)] * 2
        + [pltpu.SemaphoreType.DMA((2,))],
        input_output_aliases={4: 0, 5: 1},
        compiler_params=params(),
        name="depth",
    )(field, ahead, dual_var, limits, new_split, new_dual)
    return new_volume, new_split, new_dual


def solution(mesh):
    return jax.shard_map(
        shards,
        mesh=mesh,
        in_specs=(
            P(("parts", "slab"), "tile"),
            P(None, ("parts", "slab"), "tile"),
            P(None, ("parts", "slab"), "tile"),
            P(("tile", "rep"), ("parts", "slab"), None),
            P(("tile", "rep"), None, None),
            P(("tile", "rep")),
            P(("tile", "rep")),
            P(("tile", "rep")),
            P(),
        ),
        out_specs=(
            P(("parts", "slab"), "tile"),
            P(None, ("parts", "slab"), "tile"),
            P(None, ("parts", "slab"), "tile"),
        ),
        check_vma=False,
    )
```

```python
import functools

import jax
import jax.numpy as jnp
from jax import lax
from jax.experimental import pallas as pl
from jax.experimental.pallas import tpu as pltpu
from jax.sharding import PartitionSpec as P

TV = 64
TR = 128
TAU = 0.5
GROUP = 4
CUTS = (0, 2, 4, 6, 8)
VMEM_LIMIT = 16 * 1024 * 1024


def iotas(shape):
    row = lax.broadcasted_iota(jnp.int32, shape, 0)
    lane = lax.broadcasted_iota(jnp.int32, shape, 1)
    return row, lane


def tile_copies(proj_hbm, tiles, sems):
    eighth = proj_hbm.shape[0] // CUTS[-1]
    copies = {}
    for c, (low, high) in enumerate(zip(CUTS, CUTS[1:])):
        part = pl.ds(low * eighth, (high - low) * eighth)
        copies[low * eighth] = pltpu.make_async_copy(
            proj_hbm.at[part], tiles.at[part], sems.at[c]
        )
    return copies


def plane_masks(lane):
    return (lane % TV) // 8 < 7, lane % 8 < 7


def rows8(start):
    return pl.ds(pl.multiple_of(start, 8), 8)


def add_rows(accs, starts, values):
    held = [acc[rows8(start), :] for acc, start in zip(accs, starts)]
    for acc, start, old, value in zip(accs, starts, held, values):
        acc[rows8(start), :] = old + value


def forward_kernel(
    count, ray_hbm, voxel_hbm, vol_hbm, sino_hbm, proj_hbm,
    partial_out, index_out, tiles,
    ray, voxel, vol, sino, double, table, acc0, acc1, acc2, acc3,
    sems, tile_sems,
):
    slots = proj_hbm.shape[0]
    lines = ray.shape[0]
    rays = acc0.shape[0] // 8 - 1
    owned = sino.shape[0]
    width = vol.shape[1]
    pairs = [
        (voxel_hbm, voxel), (ray_hbm, ray), (vol_hbm, vol), (sino_hbm, sino),
        (voxel_hbm, index_out.at[pl.ds(0, lines)]), (ray_hbm, index_out.at[pl.ds(lines, lines)]),
    ]
    loads = [
        pltpu.make_async_copy(source, target, sems.at[i]) for i, (source, target) in enumerate(pairs)
    ]
    copies = tile_copies(proj_hbm, tiles, tile_sems)
    loads[2].start()
    loads[0].start()
    copies[0].start()
    loads[1].start()
    used = count[0]
    for n in copies:
        if n > 0:
            pl.when(used > n)(copies[n].start)
    for load in loads[3:]:
        load.start()
    accs = (acc0, acc1, acc2, acc3)
    for acc in accs:
        acc[...] = jnp.zeros_like(acc)
    row, lane = iotas((8, 128))
    low, top = lane < TV, row < 4

    loads[2].wait()
    field = vol[...]
    double[0:4, :] = field
    double[4:8, :] = field
    for j in range(width // 128):
        x = double[:, 128 * j:128 * j + 128].astype(jnp.bfloat16).astype(jnp.float32)
        turned = pltpu.roll(x, TV, axis=1)
        zero = jnp.zeros_like(x)
        first = jnp.where(jnp.logical_and(top, low), x, zero)
        second = jnp.where(jnp.logical_and(top, low), turned, zero)
        other = jnp.logical_not(jnp.logical_or(top, low))
        table[16 * j:16 * j + 8, :] = jnp.where(other, turned, first)
        table[16 * j + 8:16 * j + 16, :] = jnp.where(other, x, second)

    loads[0].wait()
    loads[1].wait()

    def add_part(low, high):
        copies[low].wait()
        for n in range(low, high, GROUP):
            at = [divmod(n + i, 128) for i in range(GROUP)]
            picked = [table[rows8(voxel[line, place] * 8), :] for line, place in at]
            pairs = [jnp.where(top, picked[2 * i], picked[2 * i + 1]) for i in range(2)]
            zero = jnp.zeros_like(pairs[0])
            left = jnp.concatenate([pairs[0], zero], axis=0).astype(jnp.bfloat16)
            right = jnp.concatenate([zero, pairs[1]], axis=0).astype(jnp.bfloat16)
            sums = jnp.dot(
                jnp.concatenate([left, right], axis=1),
                tiles[n:n + GROUP].reshape(GROUP * TV, TR),
                preferred_element_type=jnp.float32,
            )
            add_rows(
                accs,
                [
                    jnp.where(n + i < used, ray[line, place], rays) * 8
                    for i, (line, place) in enumerate(at)
                ],
                [sums[0:8], sums[0:8], sums[8:16], sums[8:16]],
            )

    lows = [*copies, slots]
    add_part(0, lows[1])
    for low, high in zip(lows[1:], lows[2:]):
        pl.when(used > low)(functools.partial(add_part, low, high))

    loads[3].wait()
    mine = (lax.axis_index("tile") * lax.axis_size("rep") + lax.axis_index("rep")) * owned
    for r in range(owned):
        at = pl.ds(pl.multiple_of((mine + r) * 8, 8), 4)
        acc0[at, :] = acc0[at, :] - sino[r]
    loads[4].wait()
    loads[5].wait()
    for q in range(rays // 4):
        halves = []
        for r in (4 * q, 4 * q + 2):
            at = [slice(8 * (r + k), 8 * (r + k) + 8) for k in range(2)]
            even = [acc0[at[k], :] + acc2[at[k], :] for k in range(2)]
            odd = [acc1[at[k], :] + acc3[at[k], :] for k in range(2)]
            halves.append(
                jnp.where(top, even[0], odd[1])
                + pltpu.roll(jnp.where(top, even[1], odd[0]), 4, axis=0)
            )
        partial_out[16 * q:16 * q + 16, :] = jnp.concatenate(halves, axis=0).astype(jnp.bfloat16)


def edges_kernel(vol, split, dual, edge_out, halo_out):
    start = lax.axis_index("slab") == 0
    for j in range(vol.shape[1] // 128):
        at = slice(128 * j, 128 * j + 128)
        edge = vol[3:4, at] - dual[0, 3:4, at] + split[0, 3:4, at]
        edge_out[:, at] = edge
        halo_out[:, at] = jnp.broadcast_to(jnp.where(start, edge, vol[0:1, at]), (4, 128))


def local_kernel(rho, vol, split, dual, edge, from_next, from_previous, base_out):
    slab, slabs = lax.axis_index("slab"), lax.axis_size("slab")
    factor = TAU * rho[0]
    row, lane = iotas((8, 128))
    row_mask, col_mask = plane_masks(lane)
    for j in range(vol.shape[1] // 128):
        at = slice(128 * j, 128 * j + 128)
        x = jnp.concatenate([vol[:, at]] * 2, axis=0)
        gap = [
            jnp.concatenate([dual[k, :, at] - split[k, :, at]] * 2, axis=0) for k in range(3)
        ]
        above = jnp.where(slab == slabs - 1, 0.0, from_next[0:1, at] - edge[:, at])
        below = jnp.where(slab == 0, 0.0, x[0:1] - from_previous[0:1, at])
        depth = jnp.where(row < 3, pltpu.roll(x, 7, axis=0) - x + gap[0], above)
        across = jnp.where(row_mask, pltpu.roll(x, 120, axis=1) - x + gap[1], 0.0)
        along = jnp.where(col_mask, pltpu.roll(x, 127, axis=1) - x + gap[2], 0.0)
        adjoint = jnp.where(row == 0, below, pltpu.roll(depth, 1, axis=0)) - depth
        adjoint += jnp.where((lane % TV) >= 8, pltpu.roll(across, 8, axis=1), 0.0) - across
        adjoint += jnp.where(lane % 8 >= 1, pltpu.roll(along, 1, axis=1), 0.0) - along
        base_out[:, at] = (x - factor * adjoint)[0:4]


def backward_kernel(
    count, indices, tiles, part, moved, grad_out,
    index, table, acc0, acc1, acc2, acc3, sem,
):
    slots = tiles.shape[0]
    lines = indices.shape[0] // 2
    rays = table.shape[0] // 8
    voxel_tiles = acc0.shape[0] // 8 - 1
    to_scalar = pltpu.make_async_copy(indices, index, sem)
    to_scalar.start()
    accs = (acc0, acc1, acc2, acc3)
    for acc in accs:
        acc[...] = jnp.zeros_like(acc)
    row, lane = iotas((8, 128))
    low, top = lane < TV, row < 4
    for q in range(rays // 4):
        at = slice(16 * q, 16 * q + 16)
        total = part[at, :].astype(jnp.float32) + moved[at, :].astype(jnp.float32)
        for k in range(2):
            x = total[8 * k:8 * k + 8]
            turned = pltpu.roll(x, 4, axis=0)
            r = 8 * (4 * q + 2 * k)
            table[r:r + 8, :] = jnp.where(top, x, turned)
            table[r + 8:r + 16, :] = jnp.where(top, turned, x)

    to_scalar.wait()
    used = count[0]
    for n in range(0, slots, GROUP):
        at = [divmod(n + i, 128) for i in range(GROUP)]
        picked = [table[rows8(index[lines + line, place] * 8), :] for line, place in at]
        rows = jnp.concatenate(
            [jnp.where(top, picked[2 * i], picked[2 * i + 1]) for i in range(2)], axis=0
        )
        back = lax.dot_general(
            rows.astype(jnp.bfloat16),
            tiles[n:n + GROUP].reshape(GROUP * TV, TR),
            (((1,), (1,)), ((), ())),
            preferred_element_type=jnp.float32,
        )
        add_rows(
            accs,
            [
                jnp.where(n + i < used, index[line, place], voxel_tiles) * 8
                for i, (line, place) in enumerate(at)
            ],
            [back[8 * k:8 * k + 8, 128 * k:128 * k + 128] for k in (0, 0, 1, 1)],
        )
    for j in range(voxel_tiles // 2):
        at = [slice(16 * j + 8 * k, 16 * j + 8 * k + 8) for k in range(2)]
        even = [acc0[at[k], :] + acc2[at[k], :] for k in range(2)]
        odd = [acc1[at[k], :] + acc3[at[k], :] for k in range(2)]
        turned = pltpu.roll(jnp.where(top, even[1], odd[0]), TV, axis=1)
        both = jnp.where(top == low, jnp.where(top, even[0], odd[1]), turned)
        grad_out[:, 128 * j:128 * j + 128] = (both + pltpu.roll(both, 4, axis=0))[0:4]


def plane_kernel(
    grad, grad_other, base, dual, limits,
    field_out, volume_hbm, split_hbm, dual_hbm,
    split, clipped, sems,
):
    row, lane = iotas((4, 128))
    row_mask, col_mask = plane_masks(lane)
    for j in range(dual.shape[2] // 128):
        at = slice(128 * j, 128 * j + 128)
        limit = limits[:, at]
        field = base[:, at] - TAU * (grad[:, at] + grad_other[:, at])
        field_out[:, at] = field
        x = jnp.concatenate([field] * 2, axis=0)
        steps = (
            jnp.where(row_mask, pltpu.roll(x, 120, axis=1)[0:4] - field, 0.0),
            jnp.where(col_mask, pltpu.roll(x, 127, axis=1)[0:4] - field, 0.0),
        )
        for k in range(2):
            mixed = steps[k] + dual[k + 1, :, at]
            bounded = jnp.clip(mixed, -limit, limit)
            clipped[k, :, at] = bounded
            split[k, :, at] = mixed - bounded
    copies = [
        pltpu.make_async_copy(split, split_hbm.at[pl.ds(1, 2)], sems.at[0]),
        pltpu.make_async_copy(clipped, dual_hbm.at[pl.ds(1, 2)], sems.at[1]),
        pltpu.make_async_copy(field_out, volume_hbm, sems.at[2]),
    ]
    for copy in copies:
        copy.start()
    for copy in copies:
        copy.wait()


def depth_kernel(
    field_in, ahead, dual, limits, split_in, dual_in,
    split_hbm, dual_hbm,
    split, clipped, sems,
):
    del split_in, dual_in
    last = lax.axis_index("slab") == lax.axis_size("slab") - 1
    row, lane = iotas((8, 128))
    inner = jnp.logical_or(row < 3, jnp.logical_not(last))
    for j in range(dual.shape[2] // 128):
        at = slice(128 * j, 128 * j + 128)
        limit = limits[:, at]
        x = jnp.concatenate([field_in[:, at]] * 2, axis=0)
        following = jnp.where(row < 3, pltpu.roll(x, 7, axis=0), ahead[:, at])
        mixed = jnp.where(inner, following - x, 0.0)[0:4] + dual[0, :, at]
        bounded = jnp.clip(mixed, -limit, limit)
        clipped[:, at] = bounded
        split[:, at] = mixed - bounded
    copies = [
        pltpu.make_async_copy(split, split_hbm.at[0], sems.at[0]),
        pltpu.make_async_copy(clipped, dual_hbm.at[0], sems.at[1]),
    ]
    for copy in copies:
        copy.start()
    for copy in copies:
        copy.wait()


def vmem():
    return pl.BlockSpec(memory_space=pltpu.VMEM)


def smem():
    return pl.BlockSpec(memory_space=pltpu.SMEM)


def hbm():
    return pl.BlockSpec(memory_space=pltpu.HBM)


def params():
    return pltpu.CompilerParams(vmem_limit_bytes=VMEM_LIMIT)


def shards(
    volume, split_var, dual_var, sinogram, proj_tiles, ray_index, voxel_index, tile_count, rho
):
    f32, bf16 = jnp.float32, jnp.bfloat16
    slices, width = volume.shape
    slots = ray_index.shape[0]
    owned = sinogram.shape[0]
    group = lax.axis_size(("tile", "rep"))
    reps = lax.axis_size("rep")
    slabs = lax.axis_size("slab")
    rays = owned * group
    voxel_tiles = width // TV
    lines = slots // 128
    ray_index, voxel_index = ray_index.reshape(lines, 128), voxel_index.reshape(lines, 128)
    sources = [
        pltpu.with_memory_space_constraint(x, pltpu.HBM)
        for x in (ray_index, voxel_index, volume, sinogram, proj_tiles)
    ]

    partial, indices, tiles = pl.pallas_call(
        forward_kernel,
        out_shape=(
            jax.ShapeDtypeStruct((rays * slices, TR), bf16),
            jax.ShapeDtypeStruct((2 * lines, 128), jnp.int32),
            jax.ShapeDtypeStruct(proj_tiles.shape, bf16),
        ),
        in_specs=[smem()] + [hbm()] * 5,
        out_specs=(vmem(),) * 3,
        scratch_shapes=[
            pltpu.SMEM((lines, 128), jnp.int32),
            pltpu.SMEM((lines, 128), jnp.int32),
            pltpu.VMEM((slices, width), f32),
            pltpu.VMEM(sinogram.shape, f32),
            pltpu.VMEM((8, width), f32),
            pltpu.VMEM((voxel_tiles * 8, 128), f32),
        ]
        + [pltpu.VMEM((rays * 8 + 8, 128), f32)] * 4
        + [pltpu.SemaphoreType.DMA((6,)), pltpu.SemaphoreType.DMA((len(CUTS) - 1,))],
        compiler_params=params(),
        name="forward",
    )(tile_count, *sources)

    row = jax.ShapeDtypeStruct((1, width), f32)
    edge, halo = pl.pallas_call(
        edges_kernel,
        out_shape=(row, jax.ShapeDtypeStruct((4, width), f32)),
        in_specs=[vmem()] * 3,
        out_specs=(vmem(),) * 2,
        compiler_params=params(),
        name="edges",
    )(volume, split_var, dual_var)
    across = [(i, i ^ 3) for i in range(2 * reps)]
    down = [(i, i - 1) for i in range(1, slabs)]
    if slabs == 2:
        from_next = from_previous = lax.ppermute(halo, ("slab", "rep"), across)
    else:
        from_next = lax.ppermute(volume[0:1], "slab", down)
        from_previous = lax.ppermute(edge, "slab", [(i - 1, i) for i in range(1, slabs)])
    swap = [(i, i ^ 1) for i in range(reps)]
    moved = lax.ppermute(partial, "rep", swap)
    step = reps
    while step < group:
        partial = (partial.astype(f32) + moved.astype(f32)).astype(bf16)
        moved = lax.ppermute(
            partial, ("tile", "rep"), [(i, i ^ (step + 1)) for i in range(group)]
        )
        step *= 2
    limits = jnp.broadcast_to((1.0 / rho)[:, None], (1, width))
    moved, from_next, from_previous, limits = lax.optimization_barrier(
        (moved, from_next, from_previous, limits)
    )

    base = pl.pallas_call(
        local_kernel,
        out_shape=jax.ShapeDtypeStruct((slices, width), f32),
        in_specs=[smem()] + [vmem()] * 6,
        out_specs=vmem(),
        compiler_params=params(),
        name="local",
    )(rho, volume, split_var, dual_var, edge, from_next, from_previous)

    grad = pl.pallas_call(
        backward_kernel,
        out_shape=jax.ShapeDtypeStruct((slices, width), f32),
        in_specs=[smem()] + [vmem()] * 4,
        out_specs=vmem(),
        scratch_shapes=[
            pltpu.SMEM((2 * lines, 128), jnp.int32),
            pltpu.VMEM((rays * 8, 128), f32),
        ]
        + [pltpu.VMEM((voxel_tiles * 8 + 8, 128), f32)] * 4
        + [pltpu.SemaphoreType.DMA],
        compiler_params=params(),
        name="backward",
    )(tile_count, indices, tiles, partial, moved)
    grad_other = lax.ppermute(grad, "rep", swap)
    ahead = base[0:1] - TAU * (grad[0:1] + grad_other[0:1])
    if slabs == 2:
        ahead = lax.ppermute(ahead, ("slab", "rep"), across)
    else:
        ahead = lax.ppermute(ahead, "slab", down)

    whole = jax.ShapeDtypeStruct((slices, width), f32)
    triple = jax.ShapeDtypeStruct((3, slices, width), f32)
    field, new_volume, new_split, new_dual = pl.pallas_call(
        plane_kernel,
        out_shape=(whole, whole, triple, triple),
        in_specs=[vmem()] * 5,
        out_specs=(vmem(), hbm(), hbm(), hbm()),
        scratch_shapes=[pltpu.VMEM((2, slices, width), f32)] * 2
        + [pltpu.SemaphoreType.DMA((3,))],
        compiler_params=params(),
        name="plane",
    )(grad, grad_other, base, dual_var, limits)
    new_split, new_dual = pl.pallas_call(
        depth_kernel,
        out_shape=(triple, triple),
        in_specs=[vmem()] * 4 + [hbm()] * 2,
        out_specs=(hbm(), hbm()),
        scratch_shapes=[pltpu.VMEM((slices, width), f32)] * 2
        + [pltpu.SemaphoreType.DMA((2,))],
        input_output_aliases={4: 0, 5: 1},
        compiler_params=params(),
        name="depth",
    )(field, ahead, dual_var, limits, new_split, new_dual)
    return new_volume, new_split, new_dual


def solution(mesh):
    return jax.shard_map(
        shards,
        mesh=mesh,
        in_specs=(
            P(("parts", "slab"), "tile"),
            P(None, ("parts", "slab"), "tile"),
            P(None, ("parts", "slab"), "tile"),
            P(("tile", "rep"), ("parts", "slab"), None),
            P(("tile", "rep"), None, None),
            P(("tile", "rep")),
            P(("tile", "rep")),
            P(("tile", "rep")),
            P(),
        ),
        out_specs=(
            P(("parts", "slab"), "tile"),
            P(None, ("parts", "slab"), "tile"),
            P(None, ("parts", "slab"), "tile"),
        ),
        check_vma=False,
    )
```

```python
import functools

import jax
import jax.numpy as jnp
from jax import lax
from jax.experimental import pallas as pl
from jax.experimental.pallas import tpu as pltpu
from jax.sharding import PartitionSpec as P

TV = 64
TR = 128
TAU = 0.5
GROUP = 4
CUTS = (0, 2, 4, 8)
VMEM_LIMIT = 16 * 1024 * 1024


def iotas(shape):
    row = lax.broadcasted_iota(jnp.int32, shape, 0)
    lane = lax.broadcasted_iota(jnp.int32, shape, 1)
    return row, lane


def tile_copies(proj_hbm, tiles, sems):
    eighth = proj_hbm.shape[0] // CUTS[-1]
    copies = {}
    for c, (low, high) in enumerate(zip(CUTS, CUTS[1:])):
        part = pl.ds(low * eighth, (high - low) * eighth)
        copies[low * eighth] = pltpu.make_async_copy(
            proj_hbm.at[part], tiles.at[part], sems.at[c]
        )
    return copies


def plane_masks(lane):
    return (lane % TV) // 8 < 7, lane % 8 < 7


def rows8(start):
    return pl.ds(pl.multiple_of(start, 8), 8)


def add_rows(accs, starts, values):
    held = [acc[rows8(start), :] for acc, start in zip(accs, starts)]
    for acc, start, old, value in zip(accs, starts, held, values):
        acc[rows8(start), :] = old + value


def forward_kernel(
    count, ray_hbm, voxel_hbm, vol_hbm, sino_hbm, proj_hbm,
    partial_out, index_out, tiles,
    ray, voxel, vol, sino, double, table, acc0, acc1, acc2, acc3,
    sems, tile_sems,
):
    slots = proj_hbm.shape[0]
    lines = ray.shape[0]
    rays = acc0.shape[0] // 8 - 1
    owned = sino.shape[0]
    width = vol.shape[1]
    pairs = [
        (voxel_hbm, voxel), (ray_hbm, ray), (vol_hbm, vol), (sino_hbm, sino),
        (voxel_hbm, index_out.at[pl.ds(0, lines)]), (ray_hbm, index_out.at[pl.ds(lines, lines)]),
    ]
    loads = [
        pltpu.make_async_copy(source, target, sems.at[i]) for i, (source, target) in enumerate(pairs)
    ]
    copies = tile_copies(proj_hbm, tiles, tile_sems)
    loads[2].start()
    loads[0].start()
    copies[0].start()
    loads[1].start()
    used = count[0]
    for n in copies:
        if n > 0:
            pl.when(used > n)(copies[n].start)
    for load in loads[3:]:
        load.start()
    accs = (acc0, acc1, acc2, acc3)
    for acc in accs:
        acc[...] = jnp.zeros_like(acc)
    row, lane = iotas((8, 128))
    low, top = lane < TV, row < 4

    loads[2].wait()
    field = vol[...]
    double[0:4, :] = field
    double[4:8, :] = field
    for j in range(width // 128):
        x = double[:, 128 * j:128 * j + 128].astype(jnp.bfloat16).astype(jnp.float32)
        turned = pltpu.roll(x, TV, axis=1)
        zero = jnp.zeros_like(x)
        first = jnp.where(jnp.logical_and(top, low), x, zero)
        second = jnp.where(jnp.logical_and(top, low), turned, zero)
        other = jnp.logical_not(jnp.logical_or(top, low))
        table[16 * j:16 * j + 8, :] = jnp.where(other, turned, first)
        table[16 * j + 8:16 * j + 16, :] = jnp.where(other, x, second)

    loads[0].wait()
    loads[1].wait()

    def add_part(low, high):
        copies[low].wait()
        for n in range(low, high, GROUP):
            at = [divmod(n + i, 128) for i in range(GROUP)]
            picked = [table[rows8(voxel[line, place] * 8), :] for line, place in at]
            pairs = [jnp.where(top, picked[2 * i], picked[2 * i + 1]) for i in range(2)]
            zero = jnp.zeros_like(pairs[0])
            left = jnp.concatenate([pairs[0], zero], axis=0).astype(jnp.bfloat16)
            right = jnp.concatenate([zero, pairs[1]], axis=0).astype(jnp.bfloat16)
            sums = jnp.dot(
                jnp.concatenate([left, right], axis=1),
                tiles[n:n + GROUP].reshape(GROUP * TV, TR),
                preferred_element_type=jnp.float32,
            )
            add_rows(
                accs,
                [
                    jnp.where(n + i < used, ray[line, place], rays) * 8
                    for i, (line, place) in enumerate(at)
                ],
                [sums[0:8], sums[0:8], sums[8:16], sums[8:16]],
            )

    lows = [*copies, slots]
    add_part(0, lows[1])
    for low, high in zip(lows[1:], lows[2:]):
        pl.when(used > low)(functools.partial(add_part, low, high))

    loads[3].wait()
    mine = (lax.axis_index("tile") * lax.axis_size("rep") + lax.axis_index("rep")) * owned
    for r in range(owned):
        at = pl.ds(pl.multiple_of((mine + r) * 8, 8), 4)
        acc0[at, :] = acc0[at, :] - sino[r]
    loads[4].wait()
    loads[5].wait()
    for q in range(rays // 4):
        halves = []
        for r in (4 * q, 4 * q + 2):
            at = [slice(8 * (r + k), 8 * (r + k) + 8) for k in range(2)]
            even = [acc0[at[k], :] + acc2[at[k], :] for k in range(2)]
            odd = [acc1[at[k], :] + acc3[at[k], :] for k in range(2)]
            halves.append(
                jnp.where(top, even[0], odd[1])
                + pltpu.roll(jnp.where(top, even[1], odd[0]), 4, axis=0)
            )
        partial_out[16 * q:16 * q + 16, :] = jnp.concatenate(halves, axis=0).astype(jnp.bfloat16)


def edges_kernel(vol, split, dual, edge_out, halo_out):
    start = lax.axis_index("slab") == 0
    for j in range(vol.shape[1] // 128):
        at = slice(128 * j, 128 * j + 128)
        edge = vol[3:4, at] - dual[0, 3:4, at] + split[0, 3:4, at]
        edge_out[:, at] = edge
        halo_out[:, at] = jnp.broadcast_to(jnp.where(start, edge, vol[0:1, at]), (4, 128))


def local_kernel(rho, vol, split, dual, edge, from_next, from_previous, base_out):
    slab, slabs = lax.axis_index("slab"), lax.axis_size("slab")
    factor = TAU * rho[0]
    row, lane = iotas((8, 128))
    row_mask, col_mask = plane_masks(lane)
    for j in range(vol.shape[1] // 128):
        at = slice(128 * j, 128 * j + 128)
        x = jnp.concatenate([vol[:, at]] * 2, axis=0)
        gap = [
            jnp.concatenate([dual[k, :, at] - split[k, :, at]] * 2, axis=0) for k in range(3)
        ]
        above = jnp.where(slab == slabs - 1, 0.0, from_next[0:1, at] - edge[:, at])
        below = jnp.where(slab == 0, 0.0, x[0:1] - from_previous[0:1, at])
        depth = jnp.where(row < 3, pltpu.roll(x, 7, axis=0) - x + gap[0], above)
        across = jnp.where(row_mask, pltpu.roll(x, 120, axis=1) - x + gap[1], 0.0)
        along = jnp.where(col_mask, pltpu.roll(x, 127, axis=1) - x + gap[2], 0.0)
        adjoint = jnp.where(row == 0, below, pltpu.roll(depth, 1, axis=0)) - depth
        adjoint += jnp.where((lane % TV) >= 8, pltpu.roll(across, 8, axis=1), 0.0) - across
        adjoint += jnp.where(lane % 8 >= 1, pltpu.roll(along, 1, axis=1), 0.0) - along
        base_out[:, at] = (x - factor * adjoint)[0:4]


def backward_kernel(
    count, indices, tiles, part, moved, grad_out,
    index, table, acc0, acc1, acc2, acc3, sem,
):
    slots = tiles.shape[0]
    lines = indices.shape[0] // 2
    rays = table.shape[0] // 8
    voxel_tiles = acc0.shape[0] // 8 - 1
    to_scalar = pltpu.make_async_copy(indices, index, sem)
    to_scalar.start()
    accs = (acc0, acc1, acc2, acc3)
    for acc in accs:
        acc[...] = jnp.zeros_like(acc)
    row, lane = iotas((8, 128))
    low, top = lane < TV, row < 4
    for q in range(rays // 4):
        at = slice(16 * q, 16 * q + 16)
        total = part[at, :].astype(jnp.float32) + moved[at, :].astype(jnp.float32)
        for k in range(2):
            x = total[8 * k:8 * k + 8]
            turned = pltpu.roll(x, 4, axis=0)
            r = 8 * (4 * q + 2 * k)
            table[r:r + 8, :] = jnp.where(top, x, turned)
            table[r + 8:r + 16, :] = jnp.where(top, turned, x)

    to_scalar.wait()
    used = count[0]
    for n in range(0, slots, GROUP):
        at = [divmod(n + i, 128) for i in range(GROUP)]
        picked = [table[rows8(index[lines + line, place] * 8), :] for line, place in at]
        rows = jnp.concatenate(
            [jnp.where(top, picked[2 * i], picked[2 * i + 1]) for i in range(2)], axis=0
        )
        back = lax.dot_general(
            rows.astype(jnp.bfloat16),
            tiles[n:n + GROUP].reshape(GROUP * TV, TR),
            (((1,), (1,)), ((), ())),
            preferred_element_type=jnp.float32,
        )
        add_rows(
            accs,
            [
                jnp.where(n + i < used, index[line, place], voxel_tiles) * 8
                for i, (line, place) in enumerate(at)
            ],
            [back[8 * k:8 * k + 8, 128 * k:128 * k + 128] for k in (0, 0, 1, 1)],
        )
    for j in range(voxel_tiles // 2):
        at = [slice(16 * j + 8 * k, 16 * j + 8 * k + 8) for k in range(2)]
        even = [acc0[at[k], :] + acc2[at[k], :] for k in range(2)]
        odd = [acc1[at[k], :] + acc3[at[k], :] for k in range(2)]
        turned = pltpu.roll(jnp.where(top, even[1], odd[0]), TV, axis=1)
        both = jnp.where(top == low, jnp.where(top, even[0], odd[1]), turned)
        grad_out[:, 128 * j:128 * j + 128] = (both + pltpu.roll(both, 4, axis=0))[0:4]


def plane_kernel(
    grad, grad_other, base, dual, limits,
    field_out, volume_hbm, split_hbm, dual_hbm,
    split, clipped, sems,
):
    row, lane = iotas((4, 128))
    row_mask, col_mask = plane_masks(lane)
    for j in range(dual.shape[2] // 128):
        at = slice(128 * j, 128 * j + 128)
        limit = limits[:, at]
        field = base[:, at] - TAU * (grad[:, at] + grad_other[:, at])
        field_out[:, at] = field
        x = jnp.concatenate([field] * 2, axis=0)
        steps = (
            jnp.where(row_mask, pltpu.roll(x, 120, axis=1)[0:4] - field, 0.0),
            jnp.where(col_mask, pltpu.roll(x, 127, axis=1)[0:4] - field, 0.0),
        )
        for k in range(2):
            mixed = steps[k] + dual[k + 1, :, at]
            bounded = jnp.clip(mixed, -limit, limit)
            clipped[k, :, at] = bounded
            split[k, :, at] = mixed - bounded
    copies = [
        pltpu.make_async_copy(split, split_hbm.at[pl.ds(1, 2)], sems.at[0]),
        pltpu.make_async_copy(clipped, dual_hbm.at[pl.ds(1, 2)], sems.at[1]),
        pltpu.make_async_copy(field_out, volume_hbm, sems.at[2]),
    ]
    for copy in copies:
        copy.start()
    for copy in copies:
        copy.wait()


def depth_kernel(
    field_in, ahead, dual, limits, split_in, dual_in,
    split_hbm, dual_hbm,
    split, clipped, sems,
):
    del split_in, dual_in
    last = lax.axis_index("slab") == lax.axis_size("slab") - 1
    row, lane = iotas((8, 128))
    inner = jnp.logical_or(row < 3, jnp.logical_not(last))
    for j in range(dual.shape[2] // 128):
        at = slice(128 * j, 128 * j + 128)
        limit = limits[:, at]
        x = jnp.concatenate([field_in[:, at]] * 2, axis=0)
        following = jnp.where(row < 3, pltpu.roll(x, 7, axis=0), ahead[:, at])
        mixed = jnp.where(inner, following - x, 0.0)[0:4] + dual[0, :, at]
        bounded = jnp.clip(mixed, -limit, limit)
        clipped[:, at] = bounded
        split[:, at] = mixed - bounded
    copies = [
        pltpu.make_async_copy(split, split_hbm.at[0], sems.at[0]),
        pltpu.make_async_copy(clipped, dual_hbm.at[0], sems.at[1]),
    ]
    for copy in copies:
        copy.start()
    for copy in copies:
        copy.wait()


def vmem():
    return pl.BlockSpec(memory_space=pltpu.VMEM)


def smem():
    return pl.BlockSpec(memory_space=pltpu.SMEM)


def hbm():
    return pl.BlockSpec(memory_space=pltpu.HBM)


def params():
    return pltpu.CompilerParams(vmem_limit_bytes=VMEM_LIMIT)


def shards(
    volume, split_var, dual_var, sinogram, proj_tiles, ray_index, voxel_index, tile_count, rho
):
    f32, bf16 = jnp.float32, jnp.bfloat16
    slices, width = volume.shape
    slots = ray_index.shape[0]
    owned = sinogram.shape[0]
    group = lax.axis_size(("tile", "rep"))
    reps = lax.axis_size("rep")
    slabs = lax.axis_size("slab")
    rays = owned * group
    voxel_tiles = width // TV
    lines = slots // 128
    ray_index, voxel_index = ray_index.reshape(lines, 128), voxel_index.reshape(lines, 128)
    sources = [
        pltpu.with_memory_space_constraint(x, pltpu.HBM)
        for x in (ray_index, voxel_index, volume, sinogram, proj_tiles)
    ]

    partial, indices, tiles = pl.pallas_call(
        forward_kernel,
        out_shape=(
            jax.ShapeDtypeStruct((rays * slices, TR), bf16),
            jax.ShapeDtypeStruct((2 * lines, 128), jnp.int32),
            jax.ShapeDtypeStruct(proj_tiles.shape, bf16),
        ),
        in_specs=[smem()] + [hbm()] * 5,
        out_specs=(vmem(),) * 3,
        scratch_shapes=[
            pltpu.SMEM((lines, 128), jnp.int32),
            pltpu.SMEM((lines, 128), jnp.int32),
            pltpu.VMEM((slices, width), f32),
            pltpu.VMEM(sinogram.shape, f32),
            pltpu.VMEM((8, width), f32),
            pltpu.VMEM((voxel_tiles * 8, 128), f32),
        ]
        + [pltpu.VMEM((rays * 8 + 8, 128), f32)] * 4
        + [pltpu.SemaphoreType.DMA((6,)), pltpu.SemaphoreType.DMA((len(CUTS) - 1,))],
        compiler_params=params(),
        name="forward",
    )(tile_count, *sources)

    row = jax.ShapeDtypeStruct((1, width), f32)
    edge, halo = pl.pallas_call(
        edges_kernel,
        out_shape=(row, jax.ShapeDtypeStruct((4, width), f32)),
        in_specs=[vmem()] * 3,
        out_specs=(vmem(),) * 2,
        compiler_params=params(),
        name="edges",
    )(volume, split_var, dual_var)
    across = [(i, i ^ 3) for i in range(2 * reps)]
    down = [(i, i - 1) for i in range(1, slabs)]
    if slabs == 2:
        from_next = from_previous = lax.ppermute(halo, ("slab", "rep"), across)
    else:
        from_next = lax.ppermute(volume[0:1], "slab", down)
        from_previous = lax.ppermute(edge, "slab", [(i - 1, i) for i in range(1, slabs)])
    swap = [(i, i ^ 1) for i in range(reps)]
    moved = lax.ppermute(partial, "rep", swap)
    step = reps
    while step < group:
        partial = (partial.astype(f32) + moved.astype(f32)).astype(bf16)
        moved = lax.ppermute(
            partial, ("tile", "rep"), [(i, i ^ (step + 1)) for i in range(group)]
        )
        step *= 2
    limits = jnp.broadcast_to((1.0 / rho)[:, None], (1, width))
    moved, from_next, from_previous, limits = lax.optimization_barrier(
        (moved, from_next, from_previous, limits)
    )

    base = pl.pallas_call(
        local_kernel,
        out_shape=jax.ShapeDtypeStruct((slices, width), f32),
        in_specs=[smem()] + [vmem()] * 6,
        out_specs=vmem(),
        compiler_params=params(),
        name="local",
    )(rho, volume, split_var, dual_var, edge, from_next, from_previous)

    grad = pl.pallas_call(
        backward_kernel,
        out_shape=jax.ShapeDtypeStruct((slices, width), f32),
        in_specs=[smem()] + [vmem()] * 4,
        out_specs=vmem(),
        scratch_shapes=[
            pltpu.SMEM((2 * lines, 128), jnp.int32),
            pltpu.VMEM((rays * 8, 128), f32),
        ]
        + [pltpu.VMEM((voxel_tiles * 8 + 8, 128), f32)] * 4
        + [pltpu.SemaphoreType.DMA],
        compiler_params=params(),
        name="backward",
    )(tile_count, indices, tiles, partial, moved)
    grad_other = lax.ppermute(grad, "rep", swap)
    ahead = base[0:1] - TAU * (grad[0:1] + grad_other[0:1])
    if slabs == 2:
        ahead = lax.ppermute(ahead, ("slab", "rep"), across)
    else:
        ahead = lax.ppermute(ahead, "slab", down)

    whole = jax.ShapeDtypeStruct((slices, width), f32)
    triple = jax.ShapeDtypeStruct((3, slices, width), f32)
    field, new_volume, new_split, new_dual = pl.pallas_call(
        plane_kernel,
        out_shape=(whole, whole, triple, triple),
        in_specs=[vmem()] * 5,
        out_specs=(vmem(), hbm(), hbm(), hbm()),
        scratch_shapes=[pltpu.VMEM((2, slices, width), f32)] * 2
        + [pltpu.SemaphoreType.DMA((3,))],
        compiler_params=params(),
        name="plane",
    )(grad, grad_other, base, dual_var, limits)
    new_split, new_dual = pl.pallas_call(
        depth_kernel,
        out_shape=(triple, triple),
        in_specs=[vmem()] * 4 + [hbm()] * 2,
        out_specs=(hbm(), hbm()),
        scratch_shapes=[pltpu.VMEM((slices, width), f32)] * 2
        + [pltpu.SemaphoreType.DMA((2,))],
        input_output_aliases={4: 0, 5: 1},
        compiler_params=params(),
        name="depth",
    )(field, ahead, dual_var, limits, new_split, new_dual)
    return new_volume, new_split, new_dual


def solution(mesh):
    return jax.shard_map(
        shards,
        mesh=mesh,
        in_specs=(
            P(("parts", "slab"), "tile"),
            P(None, ("parts", "slab"), "tile"),
            P(None, ("parts", "slab"), "tile"),
            P(("tile", "rep"), ("parts", "slab"), None),
            P(("tile", "rep"), None, None),
            P(("tile", "rep")),
            P(("tile", "rep")),
            P(("tile", "rep")),
            P(),
        ),
        out_specs=(
            P(("parts", "slab"), "tile"),
            P(None, ("parts", "slab"), "tile"),
            P(None, ("parts", "slab"), "tile"),
        ),
        check_vma=False,
    )
```
